32 devices in a mesh: fsdp: 32 (over z, y, x, core).
Axes of the slice: x: 2, y: 2, z: 4, core: 2. Of those that a mesh axis runs over, the one named last changes fastest.
Arguments:
- patches: bfloat16 [64, 197, 768], P('fsdp'), may hold values from -6 to 6
- live_count: int32 [32], P('fsdp'), may hold values from 1 to 2, 48 in all
- expert_ids: int32 [12608, 2], P('fsdp'), may hold values from 0 to 3, all different within a row; in each aligned block of 394 rows (0 to 393, 394 to 787, ...) at most 247 rows name the same one
- attn_gain: bfloat16 [768, 2], P('fsdp'), may hold values from 0.099609375 to 1.8984375
- attn_qkv: bfloat16 [768, 2, 2304], P('fsdp'), may hold values from -0.21875 to 0.21875
- attn_out: bfloat16 [768, 2, 768], P('fsdp'), may hold values from -1.25 to 1.25
- mlp_gain: bfloat16 [768], P('fsdp'), may hold values from 0.099609375 to 1.8984375
- mlp_in: bfloat16 [768, 3072], P('fsdp'), may hold values from -0.21875 to 0.21875
- mlp_out: bfloat16 [3072, 768], P('fsdp'), may hold values from -0.15625 to 0.15625
- moe_gain: bfloat16 [768], P('fsdp'), may hold values from 0.099609375 to 1.8984375
- router: bfloat16 [768, 4], P('fsdp'), may hold values from -0.15625 to 0.15625
- expert_in: bfloat16 [768, 4, 3072], P('fsdp'), may hold values from -0.21875 to 0.21875
- expert_out: bfloat16 [3072, 4, 768], P('fsdp'), may hold values from -0.21875 to 0.21875
- cotangent: bfloat16 [64, 197, 768], P('fsdp'), may hold values from -6 to 6
Outputs:
- block_out: bfloat16 [64, 197, 768], P('fsdp')
- input_grad: float32 [64, 197, 768], P('fsdp')
- grad_attn_gain: float32 [768, 2], P('fsdp')
- grad_attn_qkv: float32 [768, 2, 2304], P('fsdp')
- grad_attn_out: float32 [768, 2, 768], P('fsdp')
- grad_mlp_gain: float32 [768], P('fsdp')
- grad_mlp_in: float32 [768, 3072], P('fsdp')
- grad_mlp_out: float32 [3072, 768], P('fsdp')
- grad_moe_gain: float32 [768], P('fsdp')
- grad_router: float32 [768, 4], P('fsdp')
- grad_expert_in: float32 [768, 4, 3072], P('fsdp')
- grad_expert_out: float32 [3072, 4, 768], P('fsdp')
The draws below stay inside these ranges and needn't reach their ends.
Inputs may be any that keep to these rules, and one draw needn't show every extreme that they name: `live_count`: each device holds 1 to 2 live images in its first slots, 48 in all, and some device holds 2. `expert_ids`: each token names 2 different experts; of the 394 tokens of one device at most 247 name the same expert, and some device reaches 247.
All inputs are finite; a program needn't handle non-finite values.
Results may differ from the reference program's by a relative error of at most 0.023.
Values may be sent and summed in bfloat16 or wider, within the bound.
A program may use at most 384 MiB of HBM per device.

```python
import math
import jax
import jax.numpy as jnp
import numpy as np
from jax import lax

D = 768
HEADS = 12
HEAD_DIM = 64
FF = 3072
EXPERTS = 4
TOP = 2
SEQ = 197
SLOTS = 2
IMAGE_SLOTS = 64
IMAGES = 48
TOKENS = 12608
CAP = 247
DEVICES = 32


def level_of(stream_key, extent, pieces, least, top_value):
    gain = 1.0
    for position, shards_of in pieces:
        steps = jax.random.uniform(jax.random.fold_in(jax.random.fold_in(stream_key, 6), position), (shards_of,), jnp.float32, least / len(pieces), top_value / len(pieces))
        gain = gain * jnp.repeat(jnp.exp(steps), extent[position] // shards_of).reshape((-1,) + (1,) * (len(extent) - 1 - position))
    return gain


def length_profile(count, total, limit, slope):
    loads = [(1 << 20) // math.isqrt(standing ** slope) + 1 for standing in range(2, count + 1)]
    rest, counts = total - limit - (count - 1), [1] * (count - 1)
    while rest > 0:
        free = [i for i in range(count - 1) if counts[i] < limit]
        pool, left = sum([loads[i] for i in free]), rest
        for i in free:
            extra = min(limit - counts[i], max(1, left * loads[i] // pool), rest)
            counts[i] = counts[i] + extra
            rest = rest - extra
    return np.array([limit] + counts)


def uneven(stream_key, count, total, reach, skew):
    if count == 2:
        one = jax.random.randint(stream_key, (), max(1, total - reach), min(reach, total - 1) + 1)
        return jnp.stack([one, total - one])
    lengths = jnp.asarray(length_profile(count, total, reach, skew), jnp.int32)
    twos = (count - 1) // 2
    giver, sink = lengths[1:1 + 2 * twos:2], lengths[2:2 + 2 * twos:2]
    slack = jnp.minimum(giver - 1, reach - sink)
    shifted = jax.random.randint(jax.random.fold_in(stream_key, 1), (twos,), 0, 1 << 20) % (slack + 1)
    lengths = lengths.at[1:1 + 2 * twos:2].set(giver - shifted).at[2:2 + 2 * twos:2].set(sink + shifted)
    return lengths[jax.random.permutation(jax.random.fold_in(stream_key, 2), count)]


def shared_out(rng, own, number, rows, count, top, bound, skew):
    ranking = jax.random.permutation(rng, count)
    packed, common = shares(count, rows * top, bound, skew, True), shares(count, rows * top, bound, skew, False)
    places = jnp.arange(count)

    def named(sizes, offset_by):
        used = int((sizes > 0).sum())
        fixed = max(1, used // 4)
        passed = fixed + (places - fixed + offset_by * (used - fixed)) % max(1, count - fixed)
        return jnp.zeros((count,), jnp.int32).at[ranking[jnp.where(places < fixed, places, passed)]].set(jnp.asarray(sizes, jnp.int32))

    sizes = jnp.where(number % 4 == 0, named(packed, number // 4), named(common, number - number // 4 - 1))
    mixed = jax.random.permutation(jax.random.fold_in(own, 3), count)
    source_of, taker = mixed[0:count // 2 * 2:2], mixed[1:count // 2 * 2:2]
    margin = jnp.minimum(sizes[source_of] - 1, bound - sizes[taker]) // 2
    margin = jnp.where((source_of == ranking[0]) | (taker == ranking[0]) | (sizes[taker] == 0), 0, jnp.maximum(margin, 0))
    passed = jax.random.randint(jax.random.fold_in(own, 4), (count // 2,), 0, 1 << 20) % (margin + 1)
    sizes = sizes.at[source_of].add(-passed).at[taker].add(passed)
    members = jnp.searchsorted(jnp.cumsum(sizes), jnp.arange(rows * top), side="right").astype(jnp.int32)
    listing = members.reshape(top, rows).T
    listing = listing[jax.random.permutation(jax.random.fold_in(own, 1), rows)]
    offset_by = jax.random.randint(jax.random.fold_in(own, 2), (rows, 1), 0, top)
    return jnp.take_along_axis(listing, (jnp.arange(top)[None, :] + offset_by) % top, axis=1)


def shares(amount, total, reach, slope, full):
    portions = [(1 << 20) // math.isqrt(rank ** slope) + 1 for rank in range(1, amount + 1)]
    largest = reach if full else min(reach, max(-(-total // amount), total * portions[0] // sum(portions)))
    least = 1 if total - largest >= amount - 1 else 0
    holding, surplus = [largest] + [least] * (amount - 1), total - largest - least * (amount - 1)
    while surplus > 0:
        candidates = [i for i in range(1, amount) if holding[i] < largest] or [i for i in range(1, amount) if holding[i] < reach]
        pool, budget = sum([portions[i] for i in candidates]), surplus
        for i in candidates:
            addition = min(reach - holding[i], max(1, budget * portions[i] // pool), surplus)
            holding[i] = holding[i] + addition
            surplus = surplus - addition
    return np.array(holding)


def noise(rng, extent, scale, reach, split=(), kind=jnp.bfloat16):
    level = level_of(rng, extent, split, -0.22, 0.18) if split else 1.0
    values = jax.random.normal(rng, extent, jnp.float32) * scale * level
    return jnp.minimum(jnp.maximum(values, -reach), reach).astype(kind)


def setup_inputs(seed: int = 0) -> dict:
    key_of = jax.random.split(jax.random.key(seed), 15)
    patches = noise(key_of[0], (IMAGE_SLOTS, SEQ, D), 1.0, 6.0, ((0, 32),))
    live_count = uneven(key_of[1], DEVICES, IMAGES, SLOTS, 0).astype(jnp.int32)
    expert_ids_keys = jax.random.split(jax.random.fold_in(key_of[2], 1), TOKENS // (SLOTS * SEQ))
    expert_ids_turns = jax.random.permutation(jax.random.fold_in(key_of[2], 3), TOKENS // (SLOTS * SEQ))
    expert_ids = jax.vmap(lambda own, number: shared_out(jax.random.fold_in(key_of[2], 2), own, number, SLOTS * SEQ, EXPERTS, TOP, CAP, 1))(expert_ids_keys, expert_ids_turns).reshape((TOKENS, TOP))
    attn_gain = jnp.clip(1.0 + 0.18 * jax.random.normal(key_of[3], (D, 2), jnp.float32), 0.099609375, 1.8984375).astype(jnp.bfloat16)
    attn_qkv = noise(key_of[4], (D, 2, 3 * D), D ** -0.5, 0.21875, ((0, 32),))
    attn_out = noise(key_of[5], (D, 2, D), (D // 32) ** -0.5, 1.25, ((0, 32),))
    mlp_gain = jnp.clip(1.0 + 0.18 * jax.random.normal(key_of[6], (D,), jnp.float32), 0.099609375, 1.8984375).astype(jnp.bfloat16)
    mlp_in = noise(key_of[7], (D, FF), D ** -0.5, 0.21875, ((0, 32),))
    mlp_out = noise(key_of[8], (FF, D), (FF // 2) ** -0.5, 0.15625, ((0, 32),))
    moe_gain = jnp.clip(1.0 + 0.18 * jax.random.normal(key_of[9], (D,), jnp.float32), 0.099609375, 1.8984375).astype(jnp.bfloat16)
    router = noise(key_of[10], (D, EXPERTS), (2 * D) ** -0.5, 0.15625, ((0, 32),))
    expert_in = noise(key_of[11], (D, EXPERTS, FF), D ** -0.5, 0.21875, ((0, 32),))
    expert_out = noise(key_of[12], (FF, EXPERTS, D), (FF // 4) ** -0.5, 0.21875, ((0, 32),))
    cotangent = noise(key_of[13], (IMAGE_SLOTS, SEQ, D), 1.0, 6.0, ((0, 32),))
    return dict(patches=patches, live_count=live_count, expert_ids=expert_ids, attn_gain=attn_gain, attn_qkv=attn_qkv, attn_out=attn_out, mlp_gain=mlp_gain, mlp_in=mlp_in, mlp_out=mlp_out, moe_gain=moe_gain, router=router, expert_in=expert_in, expert_out=expert_out, cotangent=cotangent)


NORM_EPSILON = 1e-06
HIGHEST = lax.Precision.HIGHEST

@jax.custom_vjp
def low(v):
    return lax.optimization_barrier(v.astype(jnp.bfloat16)).astype(jnp.float32)

@jax.custom_vjp
def low_back(v):
    return v

def low_keep(v):
    return (low(v), None)

def low_pass(kept, grad):
    return (grad,)

def back_keep(v):
    return (v, None)

def back_low(kept, grad):
    return (low(grad),)
low.defvjp(low_keep, low_pass)
low_back.defvjp(back_keep, back_low)

def layer_norm(residual, norm_gain):
    center = residual - lax.optimization_barrier(jnp.mean(residual, -1, keepdims=True))
    spread = lax.optimization_barrier(jnp.mean(center * center, -1, keepdims=True))
    return center * lax.rsqrt(spread + NORM_EPSILON) * norm_gain

def gelu_tanh(values):
    return jax.nn.gelu(values, approximate=True)

def attention(residual, norm_gain, w_qkv, w_out):
    images = residual.shape[0]
    normed = low(layer_norm(residual, norm_gain))
    mixed_qkv = low_back(low(jnp.einsum('gsd,de->gse', normed, w_qkv, precision=HIGHEST)))
    split_qkv = mixed_qkv.reshape(images, SEQ, 3, HEADS, HEAD_DIM)
    queries = split_qkv[:, :, 0]
    key_rows = split_qkv[:, :, 1]
    value_rows = split_qkv[:, :, 2]
    scores = low_back(jnp.einsum('gqhd,gkhd->ghqk', queries, key_rows, precision=HIGHEST) * HEAD_DIM ** (-0.5))
    attn_probs = low(jax.nn.softmax(scores, axis=-1))
    context = jnp.einsum('ghqk,gkhd->gqhd', attn_probs, value_rows, precision=HIGHEST).reshape(images, SEQ, D)
    context = low_back(low(context))
    return low_back(jnp.einsum('gsd,de->gse', context, w_out, precision=HIGHEST))

def dense_mlp(residual, norm_gain, w_in, w_out):
    normed = low(layer_norm(residual, norm_gain))
    hidden = low_back(jnp.einsum('gsd,df->gsf', normed, w_in, precision=HIGHEST))
    active = low(gelu_tanh(hidden))
    return low_back(jnp.einsum('gsf,fd->gsd', active, w_out, precision=HIGHEST))

def expert_mlp(residual, route_ids, norm_gain, router, w_in, w_out):
    normed = low(layer_norm(residual, norm_gain))
    logits = low_back(jnp.einsum('gsd,de->gse', normed, router, precision=HIGHEST))
    chances = jax.nn.softmax(logits, axis=-1)
    chosen = (route_ids[..., None] == jnp.arange(EXPERTS, dtype=jnp.int32)).astype(jnp.float32)
    gate_values = lax.optimization_barrier(jnp.sum(chances[..., None, :] * chosen, axis=-1))
    weight_of = lax.optimization_barrier(jnp.sum(gate_values[..., None] * chosen, axis=-2))
    combined = jnp.zeros_like(residual)
    for expert in range(EXPERTS):
        hidden = low_back(jnp.einsum('gsd,df->gsf', normed, w_in[:, expert], precision=HIGHEST))
        active = low(gelu_tanh(hidden))
        produced = low_back(low(jnp.einsum('gsf,fd->gsd', active, w_out[:, expert], precision=HIGHEST)))
        combined = combined + weight_of[..., expert:expert + 1] * produced
    return combined

def whole_block(residual, route_ids, alive_mask, params):
    attn_gain, attn_qkv, attn_out, mlp_gain, mlp_in, mlp_out, moe_gain, router, expert_in, expert_out = params
    residual = residual + attention(residual, attn_gain[:, 0], attn_qkv[:, 0], attn_out[:, 0])
    residual = residual + dense_mlp(residual, mlp_gain, mlp_in, mlp_out)
    residual = residual + attention(residual, attn_gain[:, 1], attn_qkv[:, 1], attn_out[:, 1])
    residual = residual + expert_mlp(residual, route_ids, moe_gain, router, expert_in, expert_out)
    return residual * alive_mask

def reference(patches, live_count, expert_ids, attn_gain, attn_qkv, attn_out, mlp_gain, mlp_in, mlp_out, moe_gain, router, expert_in, expert_out, cotangent):
    slots_all = patches.shape[0]
    group_size = math.gcd(slots_all, 16)
    group_count = slots_all // group_size
    slot_index = jnp.arange(slots_all, dtype=jnp.int32)
    alive_mask = (slot_index % SLOTS < live_count[slot_index // SLOTS]).astype(jnp.float32)
    inputs = patches.astype(jnp.float32).reshape(group_count, group_size, SEQ, D)
    routes = expert_ids.reshape(group_count, group_size, SEQ, TOP)
    alive_groups = alive_mask.reshape(group_count, group_size, 1, 1)
    params = tuple((weight.astype(jnp.float32) for weight in (attn_gain, attn_qkv, attn_out, mlp_gain, mlp_in, mlp_out, moe_gain, router, expert_in, expert_out)))

    def forward(inputs, params):

        def one_group(items):
            return jax.checkpoint(whole_block)(items[0], items[1], items[2], params)
        return lax.map(one_group, (inputs, routes, alive_groups))
    result, pullback = jax.vjp(forward, inputs, params)
    grad_input, grads = pullback(cotangent.astype(jnp.float32).reshape(group_count, group_size, SEQ, D))
    return (result.reshape(slots_all, SEQ, D).astype(jnp.bfloat16), grad_input.reshape(slots_all, SEQ, D), grads[0], grads[1], grads[2], grads[3], grads[4], grads[5], grads[6], grads[7], grads[8], grads[9])
```

```python
import functools

import jax
import jax.numpy as jnp
from jax import lax
from jax.experimental import pallas as pl
from jax.experimental.pallas import tpu as pltpu
from jax.sharding import PartitionSpec as P

HEADS = 12
HEAD_DIM = 64
EXPERTS = 4
CAP = 247
SLOT = 256
WIDTH = 768
HIDDEN = 3072
NORM_EPSILON = 1e-06
VMEM_BYTES = 60 << 20
F32 = jnp.float32
BF16 = jnp.bfloat16


def nn(left, right):
    return lax.dot_general(left, right, (((1,), (0,)), ((), ())), preferred_element_type=F32)


def nt(left, right):
    return lax.dot_general(left, right, (((1,), (1,)), ((), ())), preferred_element_type=F32)


def tn(left, right):
    return lax.dot_general(left, right, (((0,), (0,)), ((), ())), preferred_element_type=F32)


def tile(index, size):
    return pl.ds(pl.multiple_of(index * size, size), size)


def loop(count, body):
    pl.loop(0, count)(body)


def norm_parts(values):
    center = values - jnp.mean(values, -1, keepdims=True)
    spread = jnp.mean(center * center, -1, keepdims=True)
    scale = lax.rsqrt(spread + NORM_EPSILON)
    return center * scale, scale


def norm_rows(x_ref, gain, out_ref, block=32):
    def body(i):
        rows = tile(i, block)
        unit, _ = norm_parts(x_ref[rows, :])
        out_ref[rows, :] = (unit * gain).astype(BF16)

    loop(x_ref.shape[0] // block, body)


def norm_back(x_ref, gain, dn_ref, g_ref, dgain_ref, row, block=32):
    def body(i, total):
        rows = tile(i, block)
        unit, scale = norm_parts(x_ref[rows, :])
        dn = dn_ref[rows, :]
        scaled = dn * gain
        mean_one = jnp.mean(scaled, -1, keepdims=True)
        mean_two = jnp.mean(scaled * unit, -1, keepdims=True)
        g_ref[rows, :] = g_ref[rows, :] + scale * (scaled - mean_one - unit * mean_two)
        return total + jnp.sum((dn * unit).reshape(block // 8, 8, WIDTH), 0)

    total = lax.fori_loop(0, x_ref.shape[0] // block, body, jnp.zeros((8, WIDTH), F32))
    dgain_ref[row : row + 1, :] = jnp.sum(total, 0, keepdims=True)


def gelu_both(u):
    c = 0.7978845608
    square = u * u
    t = jnp.tanh(c * u * (1.0 + 0.044715 * square))
    half = 0.5 * (1.0 + t)
    slope = half + 0.5 * u * (1.0 - t * t) * (c + (3 * 0.044715 * c) * square)
    return u * half, slope


def halves(shape):
    lane = lax.broadcasted_iota(jnp.int32, shape, 1)
    return lane < HEAD_DIM


def head_probs(q, k, seq):
    scores = nt(q, k) * HEAD_DIM ** (-0.5)
    key = lax.broadcasted_iota(jnp.int32, scores.shape, 1)
    scores = jnp.where(key < seq, scores, -1e30)
    top = jnp.max(scores, -1, keepdims=True)
    e = jnp.exp(scores - top)
    return e / jnp.sum(e, -1, keepdims=True)


def attention_heads(qkv_ref, o_ref, images, seq):
    rows_of = qkv_ref.shape[0] // images
    for image in range(images):
        rows = pl.ds(image * rows_of, rows_of)

        def pair(p, rows=rows):
            q = qkv_ref[rows, tile(p, 128)]
            k = qkv_ref[rows, tile(p + 6, 128)]
            v = qkv_ref[rows, tile(p + 12, 128)]
            first = halves(q.shape)
            zero = jnp.zeros_like(q)
            p0 = head_probs(jnp.where(first, q, zero), k, seq).astype(BF16)
            p1 = head_probs(jnp.where(first, zero, q), k, seq).astype(BF16)
            out = nn(p0, jnp.where(first, v, zero)) + nn(p1, jnp.where(first, zero, v))
            o_ref[rows, tile(p, 128)] = out.astype(BF16)

        loop(6, pair)


def attention_forward(x_ref, gain, w_ref, xo_ref, an_ref, qkv_ref, o_ref, images, seq):
    norm_rows(x_ref, gain, an_ref)

    def project(n):
        qkv_ref[:, tile(n, 256)] = nn(an_ref[...], w_ref[:, tile(n, 256)]).astype(BF16)

    loop(9, project)
    attention_heads(qkv_ref, o_ref, images, seq)

    def outward(n):
        cols = tile(n, 256)
        xo_ref[:, cols] = x_ref[:, cols] + nn(o_ref[...], w_ref[:, tile(n + 9, 256)])

    loop(3, outward)


def attention_backward(
    g_ref, x_ref, gain, w_ref, an_ref, qkv_ref, o_ref, dw_ref, dgain_ref, row, images, seq,
    low_ref, do_ref, dqkv_ref, dn_ref,
):
    rows_of = qkv_ref.shape[0] // images
    low_ref[...] = g_ref[...].astype(BF16)

    def outward(n):
        dw_ref[:, tile(n + 9, 256)] = tn(o_ref[...], low_ref[:, tile(n, 256)]).astype(BF16)
        do_ref[:, tile(n, 256)] = nt(low_ref[...], w_ref[tile(n, 256), 2304:]).astype(BF16)

    loop(3, outward)
    for image in range(images):
        rows = pl.ds(image * rows_of, rows_of)

        def pair(p, rows=rows):
            q = qkv_ref[rows, tile(p, 128)]
            k = qkv_ref[rows, tile(p + 6, 128)]
            v = qkv_ref[rows, tile(p + 12, 128)]
            d = do_ref[rows, tile(p, 128)]
            first = halves(q.shape)
            zero = jnp.zeros_like(q)
            dq = dk = dv = None
            for mine in (first, ~first):
                qm, km, dm = (jnp.where(mine, t, zero) for t in (q, k, d))
                probs = head_probs(qm, k, seq)
                dp = nt(dm, v)
                inner = jnp.sum(dp * probs, -1, keepdims=True)
                ds = (probs * (dp - inner)).astype(BF16)
                one = (nn(ds, km), tn(ds, qm), tn(probs.astype(BF16), dm))
                dq, dk, dv = one if dq is None else (dq + one[0], dk + one[1], dv + one[2])
            scale = HEAD_DIM ** (-0.5)
            dqkv_ref[rows, tile(p, 128)] = (dq * scale).astype(BF16)
            dqkv_ref[rows, tile(p + 6, 128)] = (dk * scale).astype(BF16)
            dqkv_ref[rows, tile(p + 12, 128)] = dv.astype(BF16)

        loop(6, pair)

    def inward(n):
        dw_ref[:, tile(n, 256)] = tn(an_ref[...], dqkv_ref[:, tile(n, 256)]).astype(BF16)

    loop(9, inward)

    def normed(n):
        dn_ref[:, tile(n, 256)] = nt(dqkv_ref[...], w_ref[tile(n, 256), :2304])

    loop(3, normed)
    norm_back(x_ref, gain, dn_ref, g_ref, dgain_ref, row)


def forward_kernel(
    images, seq,
    x0_ref, g4_ref, ids_ref, small_ref, wa0_ref, wmi_ref, wmo_ref, wa1_ref,
    x1_ref, x2_ref, x3_ref, an0_ref, qkv0_ref, o0_ref, mn_ref, slope_ref, ma_ref,
    an1_ref, qkv1_ref, o1_ref, en_ref, aux_ref, g0_ref, g1_ref, rx_ref, rd_ref,
    xf_ref,
):
    rows = x0_ref.shape[0]
    xf_ref[...] = x0_ref[...].astype(F32)
    attention_forward(
        xf_ref, small_ref[0:1, :], wa0_ref, x1_ref, an0_ref, qkv0_ref, o0_ref, images, seq
    )
    norm_rows(x1_ref, small_ref[2:3, :], mn_ref)
    x2_ref[...] = x1_ref[...]

    def dense(n):
        cols = tile(n, 512)
        active, slope = gelu_both(nn(mn_ref[...], wmi_ref[:, cols]))
        slope_ref[:, cols] = slope.astype(BF16)
        active = active.astype(BF16)
        ma_ref[:, cols] = active
        x2_ref[...] += nn(active, wmo_ref[cols, :])

    loop(6, dense)
    attention_forward(
        x2_ref, small_ref[1:2, :], wa1_ref, x3_ref, an1_ref, qkv1_ref, o1_ref, images, seq
    )
    norm_rows(x3_ref, small_ref[3:4, :], en_ref)
    logits = nt(en_ref[...], small_ref[8:136, :].astype(BF16))
    lane = lax.broadcasted_iota(jnp.int32, logits.shape, 1)
    logits = jnp.where(lane < EXPERTS, logits, -1e30)
    e = jnp.exp(logits - jnp.max(logits, -1, keepdims=True))
    chances = e / jnp.sum(e, -1, keepdims=True)
    ids = ids_ref[...]
    chosen = [(ids[:, j : j + 1] == lane).astype(F32) for j in range(2)]
    row_i = lax.broadcasted_iota(jnp.int32, (rows, rows), 0)
    row_j = lax.broadcasted_iota(jnp.int32, (rows, rows), 1)
    earlier = nn((row_j < row_i).astype(BF16), (chosen[0] + chosen[1]).astype(BF16))
    place = lax.broadcasted_iota(jnp.int32, (rows, EXPERTS * SLOT), 1)
    gates = []
    for j, pick_ref in ((0, g0_ref), (1, g1_ref)):
        gates.append(jnp.sum(chances * chosen[j], -1, keepdims=True))
        inside = jnp.sum(earlier * chosen[j], -1, keepdims=True).astype(jnp.int32)
        slot = jnp.where(ids[:, j : j + 1] >= 0, ids[:, j : j + 1] * SLOT + inside, -1)
        pick_ref[...] = (slot == place).astype(BF16)
    aux = jnp.where(lane < EXPERTS, chances, 0.0)
    aux = jnp.where(lane == 8, gates[0], aux)
    aux_ref[...] = jnp.where(lane == 9, gates[1], aux)

    def fill(n):
        cols = tile(n, 256)
        both = g0_ref[:, cols] + g1_ref[:, cols]
        rx_ref[cols, :] = tn(both, en_ref[...]).astype(BF16)
        g4 = g4_ref[...].astype(F32)
        one = tn(g0_ref[:, cols], (g4 * gates[0]).astype(BF16))
        two = tn(g1_ref[:, cols], (g4 * gates[1]).astype(BF16))
        rd_ref[cols, :] = (one + two).astype(BF16)

    loop(EXPERTS, fill)


def expert_kernel(x_ref, d_ref, wi_ref, wo_ref, y_ref, dx_ref, dwi_ref, dwo_ref, yf_ref, df_ref):
    yf_ref[...] = jnp.zeros_like(yf_ref)
    df_ref[...] = jnp.zeros_like(df_ref)

    def body(n):
        cols = tile(n, 512)
        active, slope = gelu_both(nn(x_ref[...], wi_ref[:, cols]))
        active = active.astype(BF16)
        yf_ref[...] += nn(active, wo_ref[cols, :])
        dwo_ref[cols, :] = tn(active, d_ref[...]).astype(BF16)
        dh = (slope * nt(d_ref[...], wo_ref[cols, :])).astype(BF16)
        df_ref[...] += nt(dh, wi_ref[:, cols])
        dwi_ref[:, cols] = tn(x_ref[...], dh).astype(BF16)

    loop(6, body)
    y_ref[...] = yf_ref[...].astype(BF16)
    dx_ref[...] = df_ref[...].astype(BF16)


def combine_kernel(
    g4_ref, small_ref, x3_ref, en_ref, aux_ref, g0_ref, g1_ref, yr_ref, dr_ref,
    x4_ref, g_ref, ds_ref,
    dn_ref,
):
    aux = aux_ref[...]
    lane = lax.broadcasted_iota(jnp.int32, aux.shape, 1)
    g_ref[...] = g4_ref[...].astype(F32)
    x4_ref[...] = x3_ref[...]
    dgates = []
    chosen = []
    expert_of = lax.broadcasted_iota(jnp.int32, (EXPERTS * SLOT, 128), 0) // SLOT
    spread = (expert_of == lax.broadcasted_iota(jnp.int32, expert_of.shape, 1)).astype(BF16)
    for j, pick_ref in ((0, g0_ref), (1, g1_ref)):
        picked = nn(pick_ref[...], yr_ref[...])
        x4_ref[...] += aux[:, 8 + j : 9 + j] * picked
        dgates.append(jnp.sum(g_ref[...] * picked, -1, keepdims=True))
        chosen.append(nn(pick_ref[...], spread))
    dr = dgates[0] * chosen[0] + dgates[1] * chosen[1]
    chances = jnp.where(lane < EXPERTS, aux, 0.0)
    dlogits = chances * (dr - jnp.sum(chances * dr, -1, keepdims=True))
    dlogits = jnp.where(lane < EXPERTS, dlogits, 0.0).astype(BF16)
    ds_ref[...] = jnp.zeros_like(ds_ref)
    ds_ref[4:8, :] = tn(dlogits, en_ref[...])[0:4, :]
    dn_ref[...] = nn(dlogits, small_ref[8:136, :].astype(BF16)) + nn(
        g0_ref[...] + g1_ref[...], dr_ref[...]
    )
    norm_back(x3_ref, small_ref[3:4, :], dn_ref, g_ref, ds_ref, 3)


def attention_back_kernel(
    images, seq, row,
    g_in_ref, small_ref, x_ref, w_ref, an_ref, qkv_ref, o_ref,
    g_ref, dw_ref, ds_ref,
    xf_ref, low_ref, do_ref, dqkv_ref, dn_ref,
):
    g_ref[...] = g_in_ref[...]
    xf_ref[...] = x_ref[...].astype(F32)
    ds_ref[...] = jnp.zeros_like(ds_ref)
    attention_backward(
        g_ref, xf_ref, small_ref[row : row + 1, :], w_ref, an_ref, qkv_ref, o_ref, dw_ref,
        ds_ref, row, images, seq, low_ref, do_ref, dqkv_ref, dn_ref,
    )


def dense_back_kernel(
    g_in_ref, small_ref, x1_ref, wmi_ref, wmo_ref, mn_ref, slope_ref, ma_ref,
    g_ref, dwmi_ref, dwmo_ref, ds_ref,
    low_ref, dn_ref,
):
    g_ref[...] = g_in_ref[...]
    ds_ref[...] = jnp.zeros_like(ds_ref)
    low_ref[...] = g_ref[...].astype(BF16)
    dn_ref[...] = jnp.zeros_like(dn_ref)

    def dense(n):
        cols = tile(n, 512)
        dwmo_ref[cols, :] = tn(ma_ref[:, cols], low_ref[...]).astype(BF16)
        dact = nt(low_ref[...], wmo_ref[cols, :])
        dh = (slope_ref[:, cols].astype(F32) * dact).astype(BF16)
        dwmi_ref[:, cols] = tn(mn_ref[...], dh).astype(BF16)
        dn_ref[...] += nt(dh, wmi_ref[:, cols])

    loop(6, dense)
    norm_back(x1_ref, small_ref[2:3, :], dn_ref, g_ref, ds_ref, 2)


def struct(shape, dtype):
    return jax.ShapeDtypeStruct(shape, dtype)


def call(body, outs, scratch, args, flops):
    total = sum(a.size * a.dtype.itemsize for a in list(args) + list(outs))
    return pl.pallas_call(
        body,
        out_shape=outs,
        in_specs=[pl.BlockSpec(memory_space=pltpu.VMEM)] * len(args),
        out_specs=[pl.BlockSpec(memory_space=pltpu.VMEM)] * len(outs),
        scratch_shapes=scratch,
        compiler_params=pltpu.CompilerParams(vmem_limit_bytes=VMEM_BYTES),
        cost_estimate=pl.CostEstimate(flops=flops, bytes_accessed=total, transcendentals=0),
    )(*args)


def run_forward(images, seq, x0, g4, ids, small, wa0, wmi, wmo, wa1):
    rows = x0.shape[0]
    act = struct((rows, WIDTH), F32)
    low = struct((rows, WIDTH), BF16)
    qkv = struct((rows, 3 * WIDTH), BF16)
    hid = struct((rows, HIDDEN), BF16)
    pick = struct((rows, EXPERTS * SLOT), BF16)
    buf = struct((EXPERTS * SLOT, WIDTH), BF16)
    outs = [act, act, act, low, qkv, low, low, hid, hid, low, qkv, low, low,
            struct((rows, 128), F32), pick, pick, buf, buf]
    return call(
        functools.partial(forward_kernel, images, seq), outs,
        [pltpu.VMEM((rows, WIDTH), F32)],
        [x0, g4, ids, small, wa0, wmi, wmo, wa1], 8_000_000_000,
    )


def run_expert(x, d, wi, wo):
    outs = [struct(x.shape, BF16), struct(x.shape, BF16), struct(wi.shape, BF16), struct(wo.shape, BF16)]
    return call(
        expert_kernel, outs, [pltpu.VMEM(x.shape, F32), pltpu.VMEM(x.shape, F32)],
        [x, d, wi, wo], 30_000_000_000,
    )


def run_backward(images, seq, x0, g4, small, weights, saved, y_back, d_back):
    rows = x0.shape[0]
    act = struct((rows, WIDTH), F32)
    wide, tall = struct((WIDTH, HIDDEN), BF16), struct((HIDDEN, WIDTH), BF16)
    row = struct((8, WIDTH), F32)
    wa0, wmi, wmo, wa1 = weights
    x1, x2, x3, an0, qkv0, o0, mn, slope, ma, an1, qkv1, o1, en, aux, p0, p1 = saved
    full = pltpu.VMEM((rows, WIDTH), F32)
    low = pltpu.VMEM((rows, WIDTH), BF16)
    mixed = pltpu.VMEM((rows, 3 * WIDTH), BF16)
    x4, g, s0 = call(
        combine_kernel, [act, act, row], [full],
        [g4, small, x3, en, aux, p0, p1, y_back, d_back], 3_000_000_000,
    )
    g, dwa1, s1 = call(
        functools.partial(attention_back_kernel, images, seq, 1), [act, wide, row],
        [full, low, low, mixed, full], [g, small, x2, wa1, an1, qkv1, o1], 5_000_000_000,
    )
    g, dwmi, dwmo, s2 = call(
        dense_back_kernel, [act, wide, tall, row], [low, full],
        [g, small, x1, wmi, wmo, mn, slope, ma], 8_000_000_000,
    )
    g, dwa0, s3 = call(
        functools.partial(attention_back_kernel, images, seq, 0), [act, wide, row],
        [full, low, low, mixed, full], [g, small, x0, wa0, an0, qkv0, o0], 5_000_000_000,
    )
    return x4, g, dwa0, dwmi, dwmo, dwa1, s0 + s1 + s2 + s3


def gather_rows(piece):
    return lax.all_gather(piece, "fsdp", axis=0, tiled=True)


def shift(values, steps):
    count = lax.axis_size("fsdp")
    return lax.ppermute(values, "fsdp", [(s, (s + steps) % count) for s in range(count)])


def group_exchange(rows, group_size, group_id):
    out = jnp.zeros_like(rows)
    for offset in range(EXPERTS):
        piece = lax.dynamic_index_in_dim(rows, (group_id + offset) % EXPERTS, 0, keepdims=False)
        if offset:
            piece = shift(piece, offset * group_size)
        out = lax.dynamic_update_index_in_dim(out, piece, (group_id - offset) % EXPERTS, 0)
    return out


def plain_gather(smalls, wide, tall, e_in, e_out):
    n = lax.axis_size("fsdp")
    group_size = n // EXPERTS
    group = lax.axis_index("fsdp") // group_size
    small = gather_rows(smalls)
    wides = [gather_rows(w) for w in wide]
    talls = [gather_rows(w) for w in tall]
    big_in = lax.dynamic_index_in_dim(gather_rows(e_in), group, 1, keepdims=False)
    big_out = lax.dynamic_index_in_dim(gather_rows(e_out), group, 1, keepdims=False)
    return small, wides, talls, big_in, big_out


def plain_reduce(grad):
    return lax.psum_scatter(grad, "fsdp", scatter_dimension=0, tiled=True)


def plain_reduce_expert(grad):
    n = lax.axis_size("fsdp")
    group_size = n // EXPERTS
    group = lax.axis_index("fsdp") // group_size
    full = jnp.zeros((grad.shape[0], EXPERTS, grad.shape[1]), BF16)
    full = lax.dynamic_update_index_in_dim(full, grad, group, 1)
    return plain_reduce(full)

MESH_ID = pl.DeviceIdType.MESH


class Place:
    def __init__(self):
        self.me = lax.axis_index("fsdp")
        self.core = self.me % 2
        self.x = self.me // 2 % 2
        self.y = self.me // 4 % 2
        self.z = self.me // 8
        self.sibling = self.me + 1 - 2 * self.core
        self.across_x = self.me + 2 - 4 * self.x
        self.across_y = self.me + 4 - 8 * self.y
        self.across_both = self.across_x + 4 - 8 * self.y
        self.chip = self.me // 2 % 4


def remote(src, dst, send, recv, device):
    return pltpu.make_async_remote_copy(
        src_ref=src, dst_ref=dst, send_sem=send, recv_sem=recv,
        device_id=(device,), device_id_type=MESH_ID,
    )


def greet_all(place, count):
    barrier = pltpu.get_barrier_semaphore()

    def hello(i):
        pl.semaphore_signal(
            barrier, inc=1, device_id=((place.me + i) % count,), device_id_type=MESH_ID
        )

    pl.loop(1, count)(hello)
    pl.semaphore_wait(barrier, count - 1)


DENSE = ("wide", "wide", "tall", "wide")


def part(ref, kind, z, y, x, core, half):
    if kind == "wide":
        return ref.at[z, y, x, :, pl.ds(pl.multiple_of(core * 1536 + half * 768, 128), 768)]
    return ref.at[z, y, x, pl.ds(pl.multiple_of(core * 96 + half * 48, 16), 48), :]


def own_part(mine, kind, half):
    if kind == "wide":
        return mine.at[:, pl.ds(half * 768, 768)]
    return mine.at[pl.ds(half * 48, 48), :]


class Gather:
    def __init__(self, place, kind, mine, out, sems):
        self.p, self.kind, self.mine, self.out, self.sems = place, kind, mine, out, sems

    def _z(self, half, source, up):
        p = self.p
        where = part(self.out, self.kind, source, p.y, p.x, p.core, half)
        return where, 0 if up else 1

    def _slot(self, half, source):
        return half * 4 + source

    def start_own(self):
        p, s = self.p, self.sems
        for half in range(2):
            there = part(self.out, self.kind, p.z, p.y, p.x, p.core, half)
            src = own_part(self.mine, self.kind, half)
            pltpu.make_async_copy(src, there, s["own"].at[half]).start()
            self._along_z(half, p.z, src, True, True)

    def _copy_z(self, half, source, src, up):
        p, s = self.p, self.sems
        slot = self._slot(half, source)
        there = part(self.out, self.kind, source, p.y, p.x, p.core, half)
        name = "zu" if up else "zd"
        return remote(there if src is None else src, there, s[name].at[slot], s["zr"].at[slot],
                      p.me + 8 if up else p.me - 8)

    def _along_z(self, half, source, src, up, down):
        p = self.p
        if up:
            pl.when(p.z < 3)(lambda: self._copy_z(half, source, src, True).start())
        if down:
            pl.when(p.z > 0)(lambda: self._copy_z(half, source, src, False).start())

    def _first(self, half, source, src=None):
        p, s = self.p, self.sems
        slot = self._slot(half, source)
        there = part(self.out, self.kind, source, p.y, p.x, p.core, half)
        return remote(there if src is None else src, there, s["fs"].at[slot], s["fr"].at[slot],
                      p.across_y if half else p.across_x)

    def _line(self, half, source):
        p = self.p
        if self.kind == "wide":
            rows, cols = slice(None), pl.ds(pl.multiple_of(p.core * 1536 + half * 768, 128), 768)
        else:
            rows, cols = pl.ds(pl.multiple_of(p.core * 96 + half * 48, 16), 48), slice(None)
        if half:
            return self.out.at[source, :, p.x, rows, cols]
        return self.out.at[source, p.y, :, rows, cols]

    def _second(self, half, source):
        p, s = self.p, self.sems
        slot = self._slot(half, source)
        line = self._line(half, source)
        return remote(line, line, s["ss"].at[slot], s["sr"].at[slot],
                      p.across_x if half else p.across_y)

    def _hand(self, half, source):
        p, s = self.p, self.sems
        slot = self._slot(half, source)
        if self.kind == "wide":
            rows, cols = slice(None), pl.ds(pl.multiple_of(p.core * 1536 + half * 768, 128), 768)
        else:
            rows, cols = pl.ds(pl.multiple_of(p.core * 96 + half * 48, 16), 48), slice(None)
        plane = self.out.at[source, :, :, rows, cols]
        return remote(plane, plane, s["hs"].at[slot], s["hr"].at[slot], p.sibling)

    def valid(self, k):
        z = self.p.z + k
        return (z >= 0) & (z <= 3)

    def stage_one(self, half, k):
        source = self.p.z + k

        def run():
            if k == 0:
                src = own_part(self.mine, self.kind, half)
                self._first(half, source, src).start()
                there = part(self.out, self.kind, source, self.p.y, self.p.x, self.p.core, half)
                pltpu.make_async_copy(src, there, self.sems["own"].at[half]).wait()
                return
            self._copy_z(half, source, None, k < 0).wait_recv()
            self._along_z(half, source, None, k < 0, k > 0)
            self._first(half, source).start()

        pl.when(self.valid(k))(run)

    def stage_two(self, half, k):
        source = self.p.z + k

        def run():
            self._first(half, source).wait_recv()
            self._second(half, source).start()

        pl.when(self.valid(k))(run)

    def stage_three(self, half, k):
        source = self.p.z + k

        def run():
            self._second(half, source).wait_recv()
            self._hand(half, source).start()

        pl.when(self.valid(k))(run)

    def arrived(self):
        for half in range(2):
            for source in range(4):
                self._hand(half, source).wait_recv()

    def finish(self):
        p = self.p
        for half in range(2):
            for source in range(4):
                self._first(half, source).wait_send()
                self._second(half, source).wait_send()
                self._hand(half, source).wait_send()
                up = (source <= p.z) & (p.z < 3)
                down = (source >= p.z) & (p.z > 0)
                pl.when(up)(lambda: self._copy_z(half, source, None, True).wait_send())
                pl.when(down)(lambda: self._copy_z(half, source, None, False).wait_send())


GATHER_SEMS = ("zu", "zd", "zr", "fs", "fr", "ss", "sr", "hs", "hr")


def expert_block(ref, kind, z, y, core):
    if kind == "wide":
        return ref.at[z, y, :, :, pl.ds(pl.multiple_of(core * 1536, 128), 1536)]
    return ref.at[z, y, :, pl.ds(pl.multiple_of(core * 96, 16), 96), :]


def expert_piece(ref, kind, z, y, x, core):
    if kind == "wide":
        return ref.at[z, y, x, :, pl.ds(pl.multiple_of(core * 1536, 128), 1536)]
    return ref.at[z, y, x, pl.ds(pl.multiple_of(core * 96, 16), 96), :]


class ExpertGather:
    def __init__(self, place, kind, mine, out, sems):
        self.p, self.kind, self.mine, self.out, self.sems = place, kind, mine, out, sems

    def _cross(self, i):
        p, s = self.p, self.sems
        there = expert_piece(self.out, self.kind, p.z, p.y, p.x, p.core)
        device = (p.across_x, p.across_y, p.across_both)[i]
        expert = device // 2 % 4
        return remote(self.mine.at[expert], there, s["cs"].at[i], s["cr"].at[i], device)

    def _own(self):
        p = self.p
        there = expert_piece(self.out, self.kind, p.z, p.y, p.x, p.core)
        return pltpu.make_async_copy(self.mine.at[p.chip], there, self.sems["own"].at[0])

    def start_own(self):
        self._own().start()
        for i in range(3):
            self._cross(i).start()

    def _copy_z(self, y, source, up):
        p, s = self.p, self.sems
        slot = y * 4 + source
        block = expert_block(self.out, self.kind, source, y, p.core)
        return remote(block, block, s["zu" if up else "zd"].at[slot], s["zr"].at[slot],
                      p.me + 8 if up else p.me - 8)

    def _hand(self, y, source):
        p, s = self.p, self.sems
        slot = y * 4 + source
        block = expert_block(self.out, self.kind, source, y, p.core)
        return remote(block, block, s["hs"].at[slot], s["hr"].at[slot], p.sibling)

    def crossed(self):
        p = self.p
        self._own().wait()
        for i in range(3):
            self._cross(i).wait_recv()
        for y in range(2):
            pl.when(p.z < 3)(lambda: self._copy_z(y, p.z, True).start())
            pl.when(p.z > 0)(lambda: self._copy_z(y, p.z, False).start())
            self._hand(y, p.z).start()

    def stage(self, y, k):
        p = self.p
        source = p.z + k

        def run():
            self._copy_z(y, source, k < 0).wait_recv()
            if k < 0:
                pl.when(p.z < 3)(lambda: self._copy_z(y, source, True).start())
            else:
                pl.when(p.z > 0)(lambda: self._copy_z(y, source, False).start())
            self._hand(y, source).start()

        pl.when((source >= 0) & (source <= 3))(run)

    def arrived(self):
        for y in range(2):
            for source in range(4):
                self._hand(y, source).wait_recv()

    def finish(self):
        p = self.p
        for i in range(3):
            self._cross(i).wait_send()
        for y in range(2):
            for source in range(4):
                self._hand(y, source).wait_send()
                up = (source <= p.z) & (p.z < 3)
                down = (source >= p.z) & (p.z > 0)
                pl.when(up)(lambda: self._copy_z(y, source, True).wait_send())
                pl.when(down)(lambda: self._copy_z(y, source, False).wait_send())


EXPERT_SEMS = ("zu", "zd", "zr", "hs", "hr")
STEPS = (0, -1, 1, -2, 2, -3, 3)


def gather_kernel(
    small_in, wide_in, tall_in,
    small_out, wa0, wmi, wmo, wa1, ein, eout,
    wide_mine, expert_mine, from_sibling, meet, small_sems, gather_sems, own_sems, expert_sems,
    cross_sems,
):
    p = Place()
    greet_all(p, 32)
    swap = remote(wide_in.at[1 - p.core], from_sibling, meet.at[0], meet.at[1], p.sibling)
    swap.start()

    def spread(i):
        remote(small_in, small_out.at[p.me], small_sems.at[0, i], small_sems.at[1, p.me],
               (p.me + i) % 32).start()

    pl.loop(1, 32)(spread)
    small_out[p.me] = small_in[...]
    outs = (wa0, wmi, wmo, wa1)
    dense = []
    for m, kind in enumerate(DENSE):
        sems = {name: gather_sems.at[m, i] for i, name in enumerate(GATHER_SEMS)}
        sems["own"] = own_sems.at[m]
        mine = tall_in.at[0] if kind == "tall" else wide_mine.at[(0, 1, None, 2)[m]]
        dense.append(Gather(p, kind, mine, outs[m], sems))
    experts = []
    for m, kind in enumerate(("wide", "tall")):
        sems = {name: expert_sems.at[m, i] for i, name in enumerate(EXPERT_SEMS)}
        sems["cs"], sems["cr"], sems["own"] = (
            cross_sems.at[m, 0], cross_sems.at[m, 1], cross_sems.at[m, 2])
        mine = tall_in.at[pl.ds(1, 4)] if kind == "tall" else expert_mine
        experts.append(ExpertGather(p, kind, mine, (ein, eout)[m], sems))
    dense[2].start_own()
    experts[1].start_own()
    swap.wait_recv()

    def merge(m, out):
        cols = pl.ds(m * 1536, 1536)
        kept = wide_in[p.core, :, cols]
        came = from_sibling[:, cols]
        upper = jnp.where(p.core == 0, kept, came)
        lower = jnp.where(p.core == 0, came, kept)
        out[...] = jnp.concatenate([upper, lower], 0).astype(BF16)

    merge(0, wide_mine.at[0])
    dense[0].start_own()
    for e in range(4):
        merge(3 + e, expert_mine.at[e])
    experts[0].start_own()
    merge(1, wide_mine.at[1])
    dense[1].start_own()
    merge(2, wide_mine.at[2])
    dense[3].start_own()

    order = [(m, k, half) for m in (0, 1, 2, 3) for k in STEPS for half in range(2)]
    pumps = []
    for i in range(len(order) + 16):
        for stage, lag in ((0, 0), (1, 8), (2, 16)):
            if 0 <= i - lag < len(order):
                pumps.append((stage,) + order[i - lag])
    turns = [(y, k, m) for k in STEPS[1:] for m in (1, 0) for y in range(2)]
    at = {8 + j * (len(pumps) - 10) // len(turns): turn for j, turn in enumerate(turns)}
    for i, (stage, m, k, half) in enumerate(pumps):
        if i == 6:
            experts[1].crossed()
            experts[0].crossed()
        if i in at:
            y, kk, mm = at[i]
            experts[mm].stage(y, kk)
        job = dense[m]
        (job.stage_one, job.stage_two, job.stage_three)[stage](half, k)
    for job in dense + experts:
        job.arrived()
    for job in dense + experts:
        job.finish()
    swap.wait_send()

    def spread_done(i):
        remote(small_in, small_out.at[(p.me + i) % 32], small_sems.at[0, i],
               small_sems.at[1, (p.me + i) % 32], (p.me + i) % 32).wait()

    pl.loop(1, 32)(spread_done)


def run_gather(small, wide, tall):
    any_space = pl.BlockSpec(memory_space=pl.ANY)
    vmem = pl.BlockSpec(memory_space=pltpu.VMEM)
    wide_out = struct((4, 2, 2, 48, 3072), BF16)
    tall_out = struct((4, 2, 2, 192, 768), BF16)
    dma = pltpu.SemaphoreType.DMA
    return pl.pallas_call(
        gather_kernel,
        out_shape=[struct((32, 8, 128), F32), wide_out, wide_out, tall_out, wide_out,
                   wide_out, tall_out],
        in_specs=[vmem, vmem, vmem],
        out_specs=[vmem] + [any_space] * 6,
        scratch_shapes=[
            pltpu.VMEM((3, 48, 1536), BF16),
            pltpu.VMEM((4, 48, 1536), BF16),
            pltpu.VMEM((24, 7 * 1536), F32),
            dma((2,)),
            dma((2, 32)),
            dma((4, len(GATHER_SEMS), 8)),
            dma((4, 2)),
            dma((2, len(EXPERT_SEMS), 8)),
            dma((2, 3, 3)),
        ],
        compiler_params=pltpu.CompilerParams(
            collective_id=0, has_side_effects=True, vmem_limit_bytes=VMEM_BYTES),
        cost_estimate=pl.CostEstimate(flops=0, bytes_accessed=60_000_000, transcendentals=0),
    )(small, wide, tall)

KINDS = ("wide", "tall", "wide", "tall", "wide", "wide")
WIDE_AT = {2: 2, 4: 1, 5: 0}
FAR_FIRST = (-3, 3, -2, 2, -1, 1, 0)


def plane_part(ref, kind, z, core, half):
    if kind == "wide":
        return ref.at[z, :, :, :, pl.ds(pl.multiple_of(core * 1536 + half * 768, 128), 768)]
    return ref.at[z, :, :, pl.ds(pl.multiple_of(core * 96 + half * 48, 16), 48), :]


def add_into(kept, came, pieces):
    def body(i):
        rows = pl.ds(pl.multiple_of(i % 3 * 16, 16), 16)
        a, b = kept(i // 3), came(i // 3)
        a[rows, :] = (a[rows, :].astype(F32) + b[rows, :].astype(F32)).astype(BF16)

    loop(pieces * 3, body)


class Reduce:
    def __init__(self, place, m, ref, own, near, bufs, sems, sink):
        self.p, self.m, self.kind, self.ref = place, m, KINDS[m], ref
        self.own, self.near, self.bufs, self.sems, self.sink = own, near, bufs, sems, sink

    def _load(self, half, z):
        src = plane_part(self.ref, self.kind, z, self.p.core, half)
        return pltpu.make_async_copy(src, self.own.at[z, half], self.sems["load"].at[z, half])

    def _pair(self, half, z):
        p, s = self.p, self.sems
        src = plane_part(self.ref, self.kind, z, 1 - p.core, half)
        return remote(src, self.near.at[z, half], s["ps"].at[z, half], s["pr"].at[z, half], p.sibling)

    def start(self, k):
        z = self.p.z + k

        def run():
            for half in range(2):
                self._load(half, z).start()
                self._pair(half, z).start()

        pl.when(self.valid(k))(run)

    def valid(self, k):
        z = self.p.z + k
        return (z >= 0) & (z <= 3)

    def pair_sum(self, half, k):
        z = self.p.z + k
        self._load(half, z).wait()
        self._pair(half, z).wait_recv()
        own, near = self.own.at[z, half], self.near.at[z, half]
        add_into(lambda i: own.at[i // 2, i % 2], lambda i: near.at[i // 2, i % 2], 4)

    def _block(self, half, z):
        raise NotImplementedError

    def _send_z(self, half, z, up):
        p, s = self.p, self.sems
        side = 0 if up else 1
        return remote(self._block(half, z), self.bufs["z"].at[half, z, side], s["zs"].at[half, z],
                      s["zr"].at[half, z, side], p.me + 8 if up else p.me - 8)

    def _wait_z(self, half, z, up):
        p, s = self.p, self.sems
        side = 0 if up else 1
        remote(self._block(half, z), self.bufs["z"].at[half, z, side], s["zs"].at[half, z],
               s["zr"].at[half, z, side], p.me).wait_recv()

    def along_z(self, half, k):
        p = self.p
        z = p.z + k
        if k == 0:
            self.end_z(half)
            return
        up = k > 0

        def join():
            self._wait_z(half, z, up)
            self._add_z(half, z, 0 if up else 1)

        pl.when(p.z > 0 if up else p.z < 3)(join)
        self._send_z(half, z, up).start()

    def finish(self):
        p = self.p
        for half in range(2):
            for z in range(4):
                self._pair(half, z).wait_send()
                pl.when(p.z != z)(lambda: self._send_z(half, z, True).wait_send())


class DenseReduce(Reduce):
    def _block(self, half, z):
        return self.own.at[z, half, self.p.y, self.p.x]

    def _add_z(self, half, z, side):
        kept, came = self._block(half, z), self.bufs["z"].at[half, z, side]
        add_into(lambda i: kept, lambda i: came, 1)

    def _first(self, half, z):
        p, s = self.p, self.sems
        src = self.own.at[z, half, :, 1 - p.x] if half else self.own.at[z, half, 1 - p.y]
        return remote(src, self.bufs["first"].at[z, half], s["fs"].at[z, half], s["fr"].at[z, half],
                      p.across_x if half else p.across_y)

    def _second(self, half, z):
        p, s = self.p, self.sems
        src = self.own.at[z, half, 1 - p.y, p.x] if half else self.own.at[z, half, p.y, 1 - p.x]
        return remote(src, self.bufs["second"].at[z, half], s["ss"].at[z, half],
                      s["sr"].at[z, half], p.across_y if half else p.across_x)

    def stage_one(self, half, k):
        def run():
            self.pair_sum(half, k)
            self._first(half, self.p.z + k).start()

        pl.when(self.valid(k))(run)

    def stage_two(self, half, k):
        p = self.p
        z = p.z + k

        def run():
            self._first(half, z).wait_recv()
            own, came = self.own.at[z, half], self.bufs["first"].at[z, half]
            if half:
                add_into(lambda i: own.at[i, p.x], lambda i: came.at[i], 2)
            else:
                add_into(lambda i: own.at[p.y, i], lambda i: came.at[i], 2)
            self._second(half, z).start()

        pl.when(self.valid(k))(run)

    def stage_three(self, half, k):
        z = self.p.z + k

        def run():
            self._second(half, z).wait_recv()
            kept, came = self._block(half, z), self.bufs["second"].at[z, half]
            add_into(lambda i: kept, lambda i: came, 1)
            self.along_z(half, k)

        pl.when(self.valid(k))(run)

    def end_z(self, half):
        p = self.p
        kept, got = self._block(half, p.z), self.bufs["z"]
        out = self.sink(half)
        out[...] = kept[...].astype(F32)

        def join(side):
            self._wait_z(half, p.z, side == 0)
            out[...] += got[half, p.z, side].astype(F32)

        pl.when(p.z > 0)(lambda: join(0))
        pl.when(p.z < 3)(lambda: join(1))

    def finish(self):
        super().finish()
        for half in range(2):
            for z in range(4):
                self._first(half, z).wait_send()
                self._second(half, z).wait_send()


class ExpertReduce(Reduce):
    def _block(self, half, z):
        return self.own.at[z, half]

    def _add_z(self, half, z, side):
        kept, came = self._block(half, z), self.bufs["z"].at[half, z, side]
        add_into(lambda i: kept.at[i // 2, i % 2], lambda i: came.at[i // 2, i % 2], 4)

    def stage_one(self, half, k):
        def run():
            self.pair_sum(half, k)
            self.along_z(half, k)

        pl.when(self.valid(k))(run)

    def _cross(self, half, i):
        p, s = self.p, self.sems
        device = (p.across_x, p.across_y, p.across_both)[i]
        chip = device // 2 % 4
        src = self.own.at[p.z, half, chip // 2, chip % 2]
        return remote(src, self.bufs["cross"].at[half, i], s["cs"].at[half, i], s["cr"].at[half, i], device)

    def end_z(self, half):
        p = self.p
        pl.when(p.z > 0)(lambda: (self._wait_z(half, p.z, True), self._add_z(half, p.z, 0)) and None)
        pl.when(p.z < 3)(lambda: (self._wait_z(half, p.z, False), self._add_z(half, p.z, 1)) and None)
        for i in range(3):
            self._cross(half, i).start()

    def crossed(self, half):
        p = self.p
        self.sink(half, p.chip)[...] = self.own[p.z, half, p.y, p.x].astype(F32)
        for i in range(3):
            self._cross(half, i).wait_recv()
            device = (p.across_x, p.across_y, p.across_both)[i]
            self.sink(half, device // 2 % 4)[...] = self.bufs["cross"][half, i].astype(F32)

    def finish(self):
        super().finish()
        for half in range(2):
            for i in range(3):
                self._cross(half, i).wait_send()


def reduce_kernel(
    small_in, ein, eout, wa1, wmo, wmi, wa0,
    small_out, wide_out, tall_out,
    own, near, first, second, z_dense, z_expert, cross, done, small_got,
    load_sems, pair_sems, plane_sems, zs_sems, zr_sems, cross_sems, small_sems, meet,
):
    p = Place()
    greet_all(p, 32)
    jobs = []
    for m, ref in enumerate((ein, eout, wa1, wmo, wmi, wa0)):
        sems = {"load": load_sems.at[m], "ps": pair_sems.at[m, 0], "pr": pair_sems.at[m, 1],
                "zs": zs_sems.at[m], "zr": zr_sems.at[m]}
        if m < 2:
            sems.update(cs=cross_sems.at[m, 0], cr=cross_sems.at[m, 1])
            bufs = {"z": z_expert.at[m], "cross": cross.at[m]}
            if m == 0:
                def sink(half, e):
                    return done.at[3 + e, :, pl.ds(half * 768, 768)]
            else:
                def sink(half, e):
                    return tall_out.at[1 + e, pl.ds(half * 48, 48), :]
            jobs.append(ExpertReduce(p, m, ref, own.at[m], near.at[m], bufs, sems, sink))
            continue
        for i, name in enumerate(("fs", "fr", "ss", "sr")):
            sems[name] = plane_sems.at[m - 2, i]
        bufs = {"z": z_dense.at[m - 2], "first": first.at[m - 2], "second": second.at[m - 2]}
        if m in WIDE_AT:
            def sink(half, m=m):
                return done.at[WIDE_AT[m], :, pl.ds(half * 768, 768)]
        else:
            def sink(half):
                return tall_out.at[0, pl.ds(half * 48, 48), :]
        jobs.append(DenseReduce(p, m, ref, own.at[m], near.at[m], bufs, sems, sink))

    def spread(i):
        to = (p.me + i) % 32
        remote(small_in.at[to], small_got.at[p.me], small_sems.at[0, i], small_sems.at[1, p.me], to).start()

    pl.loop(1, 32)(spread)
    for k in FAR_FIRST:
        for m in (0, 2, 1, 3, 4, 5):
            jobs[m].start(k)
    experts = [("e", m, k, h) for k in FAR_FIRST for m in (0, 1) for h in range(2)]
    dense = [(m, k, h) for m in (2, 3, 4, 5) for k in FAR_FIRST for h in range(2)]
    pumps = []
    for i in range(len(dense) + 16):
        for stage, lag in ((0, 0), (1, 8), (2, 16)):
            if 0 <= i - lag < len(dense):
                pumps.append((stage,) + dense[i - lag])
    at = {j * len(pumps) // len(experts): e for j, e in enumerate(experts)}
    for i, (stage, m, k, half) in enumerate(pumps):
        if i in at:
            _, em, ek, eh = at[i]
            jobs[em].stage_one(eh, ek)
        job = jobs[m]
        (job.stage_one, job.stage_two, job.stage_three)[stage](half, k)
    for m in range(2):
        for half in range(2):
            jobs[m].crossed(half)
    swap = remote(
        done.at[:, pl.ds(pl.multiple_of((1 - p.core) * 24, 8), 24), :], wide_out.at[p.core],
        meet.at[0], meet.at[1], p.sibling)
    swap.start()
    wide_out[p.core] = done[:, pl.ds(pl.multiple_of(p.core * 24, 8), 24), :]

    def spread_done(i):
        to = (p.me + i) % 32
        remote(small_in.at[to], small_got.at[to], small_sems.at[0, i], small_sems.at[1, to], to).wait()

    pl.loop(1, 32)(spread_done)
    small_got[p.me] = small_in[p.me]
    small_out[...] = jnp.sum(small_got[...], 0)
    for job in jobs:
        job.finish()
    swap.wait()


def run_reduce(small, ein, eout, wa1, wmo, wmi, wa0):
    any_space = pl.BlockSpec(memory_space=pl.ANY)
    vmem = pl.BlockSpec(memory_space=pltpu.VMEM)
    dma = pltpu.SemaphoreType.DMA
    piece = (48, 768)
    return pl.pallas_call(
        reduce_kernel,
        out_shape=[struct((8, 128), F32), struct((2, 7, 24, 1536), F32), struct((5, 96, 768), F32)],
        in_specs=[vmem] + [any_space] * 6,
        out_specs=[vmem] * 3,
        scratch_shapes=[
            pltpu.VMEM((6, 4, 2, 2, 2) + piece, BF16),
            pltpu.VMEM((6, 4, 2, 2, 2) + piece, BF16),
            pltpu.VMEM((4, 4, 2, 2) + piece, BF16),
            pltpu.VMEM((4, 4, 2) + piece, BF16),
            pltpu.VMEM((4, 2, 4, 2) + piece, BF16),
            pltpu.VMEM((2, 2, 4, 2, 2, 2) + piece, BF16),
            pltpu.VMEM((2, 2, 3) + piece, BF16),
            pltpu.VMEM((7, 48, 1536), F32),
            pltpu.VMEM((32, 8, 128), F32),
            dma((6, 4, 2)),
            dma((6, 2, 4, 2)),
            dma((4, 4, 4, 2)),
            dma((6, 2, 4)),
            dma((6, 2, 4, 2)),
            dma((2, 2, 2, 3)),
            dma((2, 32)),
            dma((2,)),
        ],
        compiler_params=pltpu.CompilerParams(
            collective_id=1, has_side_effects=True, vmem_limit_bytes=62 << 20),
        cost_estimate=pl.CostEstimate(flops=0, bytes_accessed=60_000_000, transcendentals=0),
    )(small, ein, eout, wa1, wmo, wmi, wa0)


def fast_reduce(dsmall, de_in, de_out, d0, dmi, dmo, d1):
    small = jnp.pad(dsmall.reshape(8, 32, 24).transpose(1, 0, 2), ((0, 0), (0, 0), (0, 104)))
    w = lambda g: g.reshape(4, 2, 2, 48, HIDDEN)
    t = lambda g: g.reshape(4, 2, 2, 192, WIDTH)
    small, wide, tall = run_reduce(small, w(de_in), t(de_out), w(d1), t(dmo), w(dmi), w(d0))
    wide = wide.transpose(1, 2, 0, 3).reshape(7, 24, HIDDEN)
    return (small[:, :24].T, wide[0], wide[1], tall[0], wide[2],
            wide[3:].transpose(1, 0, 2), tall[1:].transpose(1, 0, 2))


def exchange_kernel(a, b, out_a, out_b, sems, own_sems):
    p = Place()
    greet_all(p, 32)
    copies = []
    for m, (src, dst) in enumerate(((a, out_a), (b, out_b))):
        for i, device in enumerate((p.across_x, p.across_y, p.across_both)):
            copy = remote(src.at[device // 2 % 4], dst.at[p.chip], sems.at[m, 0, i],
                          sems.at[m, 1, i], device)
            copy.start()
            copies.append(copy)
        copy = pltpu.make_async_copy(src.at[p.chip], dst.at[p.chip], own_sems.at[m])
        copy.start()
        copies.append(copy)
    for copy in copies:
        copy.wait()


def run_exchange(a, b, which):
    any_space = pl.BlockSpec(memory_space=pl.ANY)
    shape = (EXPERTS, SLOT, WIDTH)
    out = pl.pallas_call(
        exchange_kernel,
        out_shape=[struct(shape, BF16)] * 2,
        in_specs=[any_space] * 2,
        out_specs=[any_space] * 2,
        scratch_shapes=[pltpu.SemaphoreType.DMA((2, 2, 3)), pltpu.SemaphoreType.DMA((2,))],
        compiler_params=pltpu.CompilerParams(collective_id=2 + which, has_side_effects=True),
    )(a.reshape(shape), b.reshape(shape))
    return [o.reshape(EXPERTS * SLOT, WIDTH) for o in out]


def fast_gather(smalls, wide, mlp_out, expert_in, expert_out):
    width = smalls.shape[0] * 32
    small = jnp.pad(smalls.astype(F32).T, ((0, 0), (0, 128 - smalls.shape[0])))
    packed = jnp.concatenate(wide + [expert_in[:, e] for e in range(EXPERTS)], 1).astype(F32)
    packed = packed.reshape(24, 7, 2, 1536).transpose(2, 0, 1, 3).reshape(2, 24, 7 * 1536)
    tall = jnp.concatenate([mlp_out[None], expert_out.transpose(1, 0, 2)], 0)
    small, wa0, wmi, wmo, wa1, ein, eout = run_gather(small, packed, tall)
    small = small[:, :, : smalls.shape[0]].transpose(1, 0, 2).reshape(8, width)
    flat = [w.reshape(width, HIDDEN) for w in (wa0, wmi, wa1, ein)]
    return small, flat[:2] + [flat[2]], [wmo.reshape(HIDDEN, width)], flat[3], eout.reshape(HIDDEN, width)


def local(
    patches, live_count, expert_ids, attn_gain, attn_qkv, attn_out, mlp_gain, mlp_in, mlp_out,
    moe_gain, router, expert_in, expert_out, cotangent,
):
    images, seq, width = patches.shape
    padded = -(-seq // 16) * 16
    n = lax.axis_size("fsdp")
    group_size = n // EXPERTS
    group = lax.axis_index("fsdp") // group_size
    alive = jnp.arange(images, dtype=jnp.int32) < live_count[0]

    def pad(values, fill=0):
        values = values.reshape(images, seq, -1)
        values = jnp.pad(values, ((0, 0), (0, padded - seq), (0, 0)), constant_values=fill)
        return values.reshape(images * padded, -1)

    x0 = pad(patches)
    g4 = pad(jnp.where(alive[:, None, None], cotangent, jnp.zeros_like(cotangent)))
    ids = pad(expert_ids, -1)
    smalls = jnp.concatenate(
        [attn_gain, mlp_gain[:, None], moe_gain[:, None], router], 1
    )
    wide = [jnp.concatenate([attn_qkv[:, 0], attn_out[:, 0]], 1), mlp_in,
            jnp.concatenate([attn_qkv[:, 1], attn_out[:, 1]], 1)]
    if n == 32:
        small, wides, talls, w_in, w_out = fast_gather(smalls, wide, mlp_out, expert_in, expert_out)
    else:
        small, wides, talls, w_in, w_out = plain_gather(
            smalls, wide, [mlp_out], expert_in, expert_out)
        small = small.astype(F32).T
    small = jnp.concatenate(
        [small[:4], jnp.zeros((4, width), F32), small[4:], jnp.zeros((124, width), F32)], 0
    )
    weights = (wides[0], wides[1], talls[0], wides[2])
    out = run_forward(images, seq, x0, g4, ids, small, *weights)
    saved, rows_x, rows_d = out[:16], out[16], out[17]

    def exchange(first, second, which):
        if n == 32:
            return run_exchange(first, second, which)
        return exchange_one(first), exchange_one(second)

    def exchange_one(rows):
        rows = rows.reshape(EXPERTS, SLOT, width)
        return group_exchange(rows, group_size, group).reshape(EXPERTS * SLOT, width)

    y, dx, dw_in, dw_out = run_expert(*exchange(rows_x, rows_d, 0), w_in, w_out)
    x4, grad, d0, dmi, dmo, d1, dsmall = run_backward(
        images, seq, x0, g4, small, weights, saved, *exchange(y, dx, 1)
    )

    def unpad(values):
        return values.reshape(images, padded, width)[:, :seq]

    block_out = jnp.where(alive[:, None, None], unpad(x4), 0.0).astype(BF16)
    if n == 32:
        dsmall, d0, dmi, dmo, d1, de_in, de_out = fast_reduce(
            dsmall, dw_in, dw_out, d0, dmi, dmo, d1)
    else:
        d0, dmi, dmo, d1 = (plain_reduce(g).astype(F32) for g in (d0, dmi, dmo, d1))
        de_in, de_out = (plain_reduce_expert(g).astype(F32) for g in (dw_in, dw_out))
        dsmall = lax.psum_scatter(dsmall.T, "fsdp", scatter_dimension=0, tiled=True)
    return (
        block_out,
        unpad(grad),
        dsmall[:, 0:2],
        jnp.stack([d0[:, :2304], d1[:, :2304]], 1),
        jnp.stack([d0[:, 2304:], d1[:, 2304:]], 1),
        dsmall[:, 2],
        dmi,
        dmo,
        dsmall[:, 3],
        dsmall[:, 4:8],
        de_in,
        de_out,
    )


def solution(mesh):
    def lead(rank):
        return P("fsdp", *([None] * (rank - 1)))

    return jax.shard_map(
        local,
        mesh=mesh,
        in_specs=tuple(lead(r) for r in (3, 1, 2, 2, 3, 3, 1, 2, 2, 1, 2, 3, 3, 3)),
        out_specs=tuple(lead(r) for r in (3, 3, 2, 3, 3, 1, 2, 2, 1, 2, 3, 3)),
        check_vma=False,
    )
```

```python
import functools

import jax
import jax.numpy as jnp
from jax import lax
from jax.experimental import pallas as pl
from jax.experimental.pallas import tpu as pltpu
from jax.sharding import PartitionSpec as P

HEADS = 12
HEAD_DIM = 64
EXPERTS = 4
CAP = 247
SLOT = 256
WIDTH = 768
HIDDEN = 3072
NORM_EPSILON = 1e-06
VMEM_BYTES = 60 << 20
F32 = jnp.float32
BF16 = jnp.bfloat16


def nn(left, right):
    return lax.dot_general(left, right, (((1,), (0,)), ((), ())), preferred_element_type=F32)


def nt(left, right):
    return lax.dot_general(left, right, (((1,), (1,)), ((), ())), preferred_element_type=F32)


def tn(left, right):
    return lax.dot_general(left, right, (((0,), (0,)), ((), ())), preferred_element_type=F32)


def tile(index, size):
    return pl.ds(pl.multiple_of(index * size, size), size)


def loop(count, body):
    pl.loop(0, count)(body)


def norm_parts(values):
    center = values - jnp.mean(values, -1, keepdims=True)
    spread = jnp.mean(center * center, -1, keepdims=True)
    scale = lax.rsqrt(spread + NORM_EPSILON)
    return center * scale, scale


def norm_rows(x_ref, gain, out_ref, block=32):
    def body(i):
        rows = tile(i, block)
        unit, _ = norm_parts(x_ref[rows, :])
        out_ref[rows, :] = (unit * gain).astype(BF16)

    loop(x_ref.shape[0] // block, body)


def norm_back(x_ref, gain, dn_ref, g_ref, dgain_ref, row, block=32):
    def body(i, total):
        rows = tile(i, block)
        unit, scale = norm_parts(x_ref[rows, :])
        dn = dn_ref[rows, :]
        scaled = dn * gain
        mean_one = jnp.mean(scaled, -1, keepdims=True)
        mean_two = jnp.mean(scaled * unit, -1, keepdims=True)
        g_ref[rows, :] = g_ref[rows, :] + scale * (scaled - mean_one - unit * mean_two)
        return total + jnp.sum((dn * unit).reshape(block // 8, 8, WIDTH), 0)

    total = lax.fori_loop(0, x_ref.shape[0] // block, body, jnp.zeros((8, WIDTH), F32))
    dgain_ref[row : row + 1, :] = jnp.sum(total, 0, keepdims=True)


def gelu_both(u):
    c = 0.7978845608
    square = u * u
    t = jnp.tanh(c * u * (1.0 + 0.044715 * square))
    half = 0.5 * (1.0 + t)
    slope = half + 0.5 * u * (1.0 - t * t) * (c + (3 * 0.044715 * c) * square)
    return u * half, slope


def halves(shape):
    lane = lax.broadcasted_iota(jnp.int32, shape, 1)
    return lane < HEAD_DIM


def head_probs(q, k, seq):
    scores = nt(q, k) * HEAD_DIM ** (-0.5)
    key = lax.broadcasted_iota(jnp.int32, scores.shape, 1)
    scores = jnp.where(key < seq, scores, -1e30)
    top = jnp.max(scores, -1, keepdims=True)
    e = jnp.exp(scores - top)
    return e / jnp.sum(e, -1, keepdims=True)


def attention_heads(qkv_ref, o_ref, images, seq):
    rows_of = qkv_ref.shape[0] // images
    for image in range(images):
        rows = pl.ds(image * rows_of, rows_of)

        def pair(p, rows=rows):
            q = qkv_ref[rows, tile(p, 128)]
            k = qkv_ref[rows, tile(p + 6, 128)]
            v = qkv_ref[rows, tile(p + 12, 128)]
            first = halves(q.shape)
            zero = jnp.zeros_like(q)
            p0 = head_probs(jnp.where(first, q, zero), k, seq).astype(BF16)
            p1 = head_probs(jnp.where(first, zero, q), k, seq).astype(BF16)
            out = nn(p0, jnp.where(first, v, zero)) + nn(p1, jnp.where(first, zero, v))
            o_ref[rows, tile(p, 128)] = out.astype(BF16)

        loop(6, pair)


def attention_forward(x_ref, gain, w_ref, xo_ref, an_ref, qkv_ref, o_ref, images, seq):
    norm_rows(x_ref, gain, an_ref)

    def project(n):
        qkv_ref[:, tile(n, 256)] = nn(an_ref[...], w_ref[:, tile(n, 256)]).astype(BF16)

    loop(9, project)
    attention_heads(qkv_ref, o_ref, images, seq)

    def outward(n):
        cols = tile(n, 256)
        xo_ref[:, cols] = x_ref[:, cols] + nn(o_ref[...], w_ref[:, tile(n + 9, 256)])

    loop(3, outward)


def attention_backward(
    g_ref, x_ref, gain, w_ref, an_ref, qkv_ref, o_ref, dw_ref, dgain_ref, row, images, seq,
    low_ref, do_ref, dqkv_ref, dn_ref,
):
    rows_of = qkv_ref.shape[0] // images
    low_ref[...] = g_ref[...].astype(BF16)

    def outward(n):
        dw_ref[:, tile(n + 9, 256)] = tn(o_ref[...], low_ref[:, tile(n, 256)]).astype(BF16)
        do_ref[:, tile(n, 256)] = nt(low_ref[...], w_ref[tile(n, 256), 2304:]).astype(BF16)

    loop(3, outward)
    for image in range(images):
        rows = pl.ds(image * rows_of, rows_of)

        def pair(p, rows=rows):
            q = qkv_ref[rows, tile(p, 128)]
            k = qkv_ref[rows, tile(p + 6, 128)]
            v = qkv_ref[rows, tile(p + 12, 128)]
            d = do_ref[rows, tile(p, 128)]
            first = halves(q.shape)
            zero = jnp.zeros_like(q)
            dq = dk = dv = None
            for mine in (first, ~first):
                qm, km, dm = (jnp.where(mine, t, zero) for t in (q, k, d))
                probs = head_probs(qm, k, seq)
                dp = nt(dm, v)
                inner = jnp.sum(dp * probs, -1, keepdims=True)
                ds = (probs * (dp - inner)).astype(BF16)
                one = (nn(ds, km), tn(ds, qm), tn(probs.astype(BF16), dm))
                dq, dk, dv = one if dq is None else (dq + one[0], dk + one[1], dv + one[2])
            scale = HEAD_DIM ** (-0.5)
            dqkv_ref[rows, tile(p, 128)] = (dq * scale).astype(BF16)
            dqkv_ref[rows, tile(p + 6, 128)] = (dk * scale).astype(BF16)
            dqkv_ref[rows, tile(p + 12, 128)] = dv.astype(BF16)

        loop(6, pair)

    def inward(n):
        dw_ref[:, tile(n, 256)] = tn(an_ref[...], dqkv_ref[:, tile(n, 256)]).astype(BF16)

    loop(9, inward)

    def normed(n):
        dn_ref[:, tile(n, 256)] = nt(dqkv_ref[...], w_ref[tile(n, 256), :2304])

    loop(3, normed)
    norm_back(x_ref, gain, dn_ref, g_ref, dgain_ref, row)


def forward_kernel(
    images, seq,
    x0_ref, g4_ref, ids_ref, small_ref, wa0_ref, wmi_ref, wmo_ref, wa1_ref,
    x1_ref, x2_ref, x3_ref, an0_ref, qkv0_ref, o0_ref, mn_ref, slope_ref, ma_ref,
    an1_ref, qkv1_ref, o1_ref, en_ref, aux_ref, g0_ref, g1_ref, rx_ref, rd_ref,
    xf_ref,
):
    rows = x0_ref.shape[0]
    xf_ref[...] = x0_ref[...].astype(F32)
    attention_forward(
        xf_ref, small_ref[0:1, :], wa0_ref, x1_ref, an0_ref, qkv0_ref, o0_ref, images, seq
    )
    norm_rows(x1_ref, small_ref[2:3, :], mn_ref)
    x2_ref[...] = x1_ref[...]

    def dense(n):
        cols = tile(n, 512)
        active, slope = gelu_both(nn(mn_ref[...], wmi_ref[:, cols]))
        slope_ref[:, cols] = slope.astype(BF16)
        active = active.astype(BF16)
        ma_ref[:, cols] = active
        x2_ref[...] += nn(active, wmo_ref[cols, :])

    loop(6, dense)
    attention_forward(
        x2_ref, small_ref[1:2, :], wa1_ref, x3_ref, an1_ref, qkv1_ref, o1_ref, images, seq
    )
    norm_rows(x3_ref, small_ref[3:4, :], en_ref)
    logits = nt(en_ref[...], small_ref[8:136, :].astype(BF16))
    lane = lax.broadcasted_iota(jnp.int32, logits.shape, 1)
    logits = jnp.where(lane < EXPERTS, logits, -1e30)
    e = jnp.exp(logits - jnp.max(logits, -1, keepdims=True))
    chances = e / jnp.sum(e, -1, keepdims=True)
    ids = ids_ref[...]
    chosen = [(ids[:, j : j + 1] == lane).astype(F32) for j in range(2)]
    row_i = lax.broadcasted_iota(jnp.int32, (rows, rows), 0)
    row_j = lax.broadcasted_iota(jnp.int32, (rows, rows), 1)
    earlier = nn((row_j < row_i).astype(BF16), (chosen[0] + chosen[1]).astype(BF16))
    place = lax.broadcasted_iota(jnp.int32, (rows, EXPERTS * SLOT), 1)
    gates = []
    for j, pick_ref in ((0, g0_ref), (1, g1_ref)):
        gates.append(jnp.sum(chances * chosen[j], -1, keepdims=True))
        inside = jnp.sum(earlier * chosen[j], -1, keepdims=True).astype(jnp.int32)
        slot = jnp.where(ids[:, j : j + 1] >= 0, ids[:, j : j + 1] * SLOT + inside, -1)
        pick_ref[...] = (slot == place).astype(BF16)
    aux = jnp.where(lane < EXPERTS, chances, 0.0)
    aux = jnp.where(lane == 8, gates[0], aux)
    aux_ref[...] = jnp.where(lane == 9, gates[1], aux)

    def fill(n):
        cols = tile(n, 256)
        both = g0_ref[:, cols] + g1_ref[:, cols]
        rx_ref[cols, :] = tn(both, en_ref[...]).astype(BF16)
        g4 = g4_ref[...].astype(F32)
        one = tn(g0_ref[:, cols], (g4 * gates[0]).astype(BF16))
        two = tn(g1_ref[:, cols], (g4 * gates[1]).astype(BF16))
        rd_ref[cols, :] = (one + two).astype(BF16)

    loop(EXPERTS, fill)


def expert_kernel(x_ref, d_ref, wi_ref, wo_ref, y_ref, dx_ref, dwi_ref, dwo_ref, yf_ref, df_ref):
    yf_ref[...] = jnp.zeros_like(yf_ref)
    df_ref[...] = jnp.zeros_like(df_ref)

    def body(n):
        cols = tile(n, 512)
        active, slope = gelu_both(nn(x_ref[...], wi_ref[:, cols]))
        active = active.astype(BF16)
        yf_ref[...] += nn(active, wo_ref[cols, :])
        dwo_ref[cols, :] = tn(active, d_ref[...]).astype(BF16)
        dh = (slope * nt(d_ref[...], wo_ref[cols, :])).astype(BF16)
        df_ref[...] += nt(dh, wi_ref[:, cols])
        dwi_ref[:, cols] = tn(x_ref[...], dh).astype(BF16)

    loop(6, body)
    y_ref[...] = yf_ref[...].astype(BF16)
    dx_ref[...] = df_ref[...].astype(BF16)


def combine_kernel(
    g4_ref, small_ref, x3_ref, en_ref, aux_ref, g0_ref, g1_ref, yr_ref, dr_ref,
    x4_ref, g_ref, ds_ref,
    dn_ref,
):
    aux = aux_ref[...]
    lane = lax.broadcasted_iota(jnp.int32, aux.shape, 1)
    g_ref[...] = g4_ref[...].astype(F32)
    x4_ref[...] = x3_ref[...]
    dgates = []
    chosen = []
    expert_of = lax.broadcasted_iota(jnp.int32, (EXPERTS * SLOT, 128), 0) // SLOT
    spread = (expert_of == lax.broadcasted_iota(jnp.int32, expert_of.shape, 1)).astype(BF16)
    for j, pick_ref in ((0, g0_ref), (1, g1_ref)):
        picked = nn(pick_ref[...], yr_ref[...])
        x4_ref[...] += aux[:, 8 + j : 9 + j] * picked
        dgates.append(jnp.sum(g_ref[...] * picked, -1, keepdims=True))
        chosen.append(nn(pick_ref[...], spread))
    dr = dgates[0] * chosen[0] + dgates[1] * chosen[1]
    chances = jnp.where(lane < EXPERTS, aux, 0.0)
    dlogits = chances * (dr - jnp.sum(chances * dr, -1, keepdims=True))
    dlogits = jnp.where(lane < EXPERTS, dlogits, 0.0).astype(BF16)
    ds_ref[...] = jnp.zeros_like(ds_ref)
    ds_ref[4:8, :] = tn(dlogits, en_ref[...])[0:4, :]
    dn_ref[...] = nn(dlogits, small_ref[8:136, :].astype(BF16)) + nn(
        g0_ref[...] + g1_ref[...], dr_ref[...]
    )
    norm_back(x3_ref, small_ref[3:4, :], dn_ref, g_ref, ds_ref, 3)


def attention_back_kernel(
    images, seq, row,
    g_in_ref, small_ref, x_ref, w_ref, an_ref, qkv_ref, o_ref,
    g_ref, dw_ref, ds_ref,
    xf_ref, low_ref, do_ref, dqkv_ref, dn_ref,
):
    g_ref[...] = g_in_ref[...]
    xf_ref[...] = x_ref[...].astype(F32)
    ds_ref[...] = jnp.zeros_like(ds_ref)
    attention_backward(
        g_ref, xf_ref, small_ref[row : row + 1, :], w_ref, an_ref, qkv_ref, o_ref, dw_ref,
        ds_ref, row, images, seq, low_ref, do_ref, dqkv_ref, dn_ref,
    )


def dense_back_kernel(
    g_in_ref, small_ref, x1_ref, wmi_ref, wmo_ref, mn_ref, slope_ref, ma_ref,
    g_ref, dwmi_ref, dwmo_ref, ds_ref,
    low_ref, dn_ref,
):
    g_ref[...] = g_in_ref[...]
    ds_ref[...] = jnp.zeros_like(ds_ref)
    low_ref[...] = g_ref[...].astype(BF16)
    dn_ref[...] = jnp.zeros_like(dn_ref)

    def dense(n):
        cols = tile(n, 512)
        dwmo_ref[cols, :] = tn(ma_ref[:, cols], low_ref[...]).astype(BF16)
        dact = nt(low_ref[...], wmo_ref[cols, :])
        dh = (slope_ref[:, cols].astype(F32) * dact).astype(BF16)
        dwmi_ref[:, cols] = tn(mn_ref[...], dh).astype(BF16)
        dn_ref[...] += nt(dh, wmi_ref[:, cols])

    loop(6, dense)
    norm_back(x1_ref, small_ref[2:3, :], dn_ref, g_ref, ds_ref, 2)


def struct(shape, dtype):
    return jax.ShapeDtypeStruct(shape, dtype)


def call(body, outs, scratch, args, flops):
    total = sum(a.size * a.dtype.itemsize for a in list(args) + list(outs))
    return pl.pallas_call(
        body,
        out_shape=outs,
        in_specs=[pl.BlockSpec(memory_space=pltpu.VMEM)] * len(args),
        out_specs=[pl.BlockSpec(memory_space=pltpu.VMEM)] * len(outs),
        scratch_shapes=scratch,
        compiler_params=pltpu.CompilerParams(vmem_limit_bytes=VMEM_BYTES),
        cost_estimate=pl.CostEstimate(flops=flops, bytes_accessed=total, transcendentals=0),
    )(*args)


def run_forward(images, seq, x0, g4, ids, small, wa0, wmi, wmo, wa1):
    rows = x0.shape[0]
    act = struct((rows, WIDTH), F32)
    low = struct((rows, WIDTH), BF16)
    qkv = struct((rows, 3 * WIDTH), BF16)
    hid = struct((rows, HIDDEN), BF16)
    pick = struct((rows, EXPERTS * SLOT), BF16)
    buf = struct((EXPERTS * SLOT, WIDTH), BF16)
    outs = [act, act, act, low, qkv, low, low, hid, hid, low, qkv, low, low,
            struct((rows, 128), F32), pick, pick, buf, buf]
    return call(
        functools.partial(forward_kernel, images, seq), outs,
        [pltpu.VMEM((rows, WIDTH), F32)],
        [x0, g4, ids, small, wa0, wmi, wmo, wa1], 8_000_000_000,
    )


def run_expert(x, d, wi, wo):
    outs = [struct(x.shape, BF16), struct(x.shape, BF16), struct(wi.shape, BF16), struct(wo.shape, BF16)]
    return call(
        expert_kernel, outs, [pltpu.VMEM(x.shape, F32), pltpu.VMEM(x.shape, F32)],
        [x, d, wi, wo], 30_000_000_000,
    )


def run_backward(images, seq, x0, g4, small, weights, saved, y_back, d_back):
    rows = x0.shape[0]
    act = struct((rows, WIDTH), F32)
    wide, tall = struct((WIDTH, HIDDEN), BF16), struct((HIDDEN, WIDTH), BF16)
    row = struct((8, WIDTH), F32)
    wa0, wmi, wmo, wa1 = weights
    x1, x2, x3, an0, qkv0, o0, mn, slope, ma, an1, qkv1, o1, en, aux, p0, p1 = saved
    full = pltpu.VMEM((rows, WIDTH), F32)
    low = pltpu.VMEM((rows, WIDTH), BF16)
    mixed = pltpu.VMEM((rows, 3 * WIDTH), BF16)
    x4, g, s0 = call(
        combine_kernel, [act, act, row], [full],
        [g4, small, x3, en, aux, p0, p1, y_back, d_back], 3_000_000_000,
    )
    g, dwa1, s1 = call(
        functools.partial(attention_back_kernel, images, seq, 1), [act, wide, row],
        [full, low, low, mixed, full], [g, small, x2, wa1, an1, qkv1, o1], 5_000_000_000,
    )
    g, dwmi, dwmo, s2 = call(
        dense_back_kernel, [act, wide, tall, row], [low, full],
        [g, small, x1, wmi, wmo, mn, slope, ma], 8_000_000_000,
    )
    g, dwa0, s3 = call(
        functools.partial(attention_back_kernel, images, seq, 0), [act, wide, row],
        [full, low, low, mixed, full], [g, small, x0, wa0, an0, qkv0, o0], 5_000_000_000,
    )
    return x4, g, dwa0, dwmi, dwmo, dwa1, s0 + s1 + s2 + s3


def gather_rows(piece):
    return lax.all_gather(piece, "fsdp", axis=0, tiled=True)


def shift(values, steps):
    count = lax.axis_size("fsdp")
    return lax.ppermute(values, "fsdp", [(s, (s + steps) % count) for s in range(count)])


def group_exchange(rows, group_size, group_id):
    out = jnp.zeros_like(rows)
    for offset in range(EXPERTS):
        piece = lax.dynamic_index_in_dim(rows, (group_id + offset) % EXPERTS, 0, keepdims=False)
        if offset:
            piece = shift(piece, offset * group_size)
        out = lax.dynamic_update_index_in_dim(out, piece, (group_id - offset) % EXPERTS, 0)
    return out


def plain_gather(smalls, wide, tall, e_in, e_out):
    n = lax.axis_size("fsdp")
    group_size = n // EXPERTS
    group = lax.axis_index("fsdp") // group_size
    small = gather_rows(smalls)
    wides = [gather_rows(w) for w in wide]
    talls = [gather_rows(w) for w in tall]
    big_in = lax.dynamic_index_in_dim(gather_rows(e_in), group, 1, keepdims=False)
    big_out = lax.dynamic_index_in_dim(gather_rows(e_out), group, 1, keepdims=False)
    return small, wides, talls, big_in, big_out


def plain_reduce(grad):
    return lax.psum_scatter(grad, "fsdp", scatter_dimension=0, tiled=True)


def plain_reduce_expert(grad):
    n = lax.axis_size("fsdp")
    group_size = n // EXPERTS
    group = lax.axis_index("fsdp") // group_size
    full = jnp.zeros((grad.shape[0], EXPERTS, grad.shape[1]), BF16)
    full = lax.dynamic_update_index_in_dim(full, grad, group, 1)
    return plain_reduce(full)

MESH_ID = pl.DeviceIdType.MESH


class Place:
    def __init__(self):
        self.me = lax.axis_index("fsdp")
        self.core = self.me % 2
        self.x = self.me // 2 % 2
        self.y = self.me // 4 % 2
        self.z = self.me // 8
        self.sibling = self.me + 1 - 2 * self.core
        self.across_x = self.me + 2 - 4 * self.x
        self.across_y = self.me + 4 - 8 * self.y
        self.across_both = self.across_x + 4 - 8 * self.y
        self.chip = self.me // 2 % 4


def remote(src, dst, send, recv, device):
    return pltpu.make_async_remote_copy(
        src_ref=src, dst_ref=dst, send_sem=send, recv_sem=recv,
        device_id=(device,), device_id_type=MESH_ID,
    )


def greet_all(place, count):
    barrier = pltpu.get_barrier_semaphore()

    def hello(i):
        pl.semaphore_signal(
            barrier, inc=1, device_id=((place.me + i) % count,), device_id_type=MESH_ID
        )

    pl.loop(1, count)(hello)
    pl.semaphore_wait(barrier, count - 1)


DENSE = ("wide", "wide", "tall", "wide")


def part(ref, kind, z, y, x, core, half):
    if kind == "wide":
        return ref.at[z, y, x, :, pl.ds(pl.multiple_of(core * 1536 + half * 768, 128), 768)]
    return ref.at[z, y, x, pl.ds(pl.multiple_of(core * 96 + half * 48, 16), 48), :]


def own_part(mine, kind, half):
    if kind == "wide":
        return mine.at[:, pl.ds(half * 768, 768)]
    return mine.at[pl.ds(half * 48, 48), :]


class Gather:
    def __init__(self, place, kind, mine, out, sems):
        self.p, self.kind, self.mine, self.out, self.sems = place, kind, mine, out, sems

    def _z(self, half, source, up):
        p = self.p
        where = part(self.out, self.kind, source, p.y, p.x, p.core, half)
        return where, 0 if up else 1

    def _slot(self, half, source):
        return half * 4 + source

    def start_own(self):
        p, s = self.p, self.sems
        for half in range(2):
            there = part(self.out, self.kind, p.z, p.y, p.x, p.core, half)
            src = own_part(self.mine, self.kind, half)
            pltpu.make_async_copy(src, there, s["own"].at[half]).start()
            self._along_z(half, p.z, src, True, True)

    def _copy_z(self, half, source, src, up):
        p, s = self.p, self.sems
        slot = self._slot(half, source)
        there = part(self.out, self.kind, source, p.y, p.x, p.core, half)
        name = "zu" if up else "zd"
        return remote(there if src is None else src, there, s[name].at[slot], s["zr"].at[slot],
                      p.me + 8 if up else p.me - 8)

    def _along_z(self, half, source, src, up, down):
        p = self.p
        if up:
            pl.when(p.z < 3)(lambda: self._copy_z(half, source, src, True).start())
        if down:
            pl.when(p.z > 0)(lambda: self._copy_z(half, source, src, False).start())

    def _first(self, half, source, src=None):
        p, s = self.p, self.sems
        slot = self._slot(half, source)
        there = part(self.out, self.kind, source, p.y, p.x, p.core, half)
        return remote(there if src is None else src, there, s["fs"].at[slot], s["fr"].at[slot],
                      p.across_y if half else p.across_x)

    def _line(self, half, source):
        p = self.p
        if self.kind == "wide":
            rows, cols = slice(None), pl.ds(pl.multiple_of(p.core * 1536 + half * 768, 128), 768)
        else:
            rows, cols = pl.ds(pl.multiple_of(p.core * 96 + half * 48, 16), 48), slice(None)
        if half:
            return self.out.at[source, :, p.x, rows, cols]
        return self.out.at[source, p.y, :, rows, cols]

    def _second(self, half, source):
        p, s = self.p, self.sems
        slot = self._slot(half, source)
        line = self._line(half, source)
        return remote(line, line, s["ss"].at[slot], s["sr"].at[slot],
                      p.across_x if half else p.across_y)

    def _hand(self, half, source):
        p, s = self.p, self.sems
        slot = self._slot(half, source)
        if self.kind == "wide":
            rows, cols = slice(None), pl.ds(pl.multiple_of(p.core * 1536 + half * 768, 128), 768)
        else:
            rows, cols = pl.ds(pl.multiple_of(p.core * 96 + half * 48, 16), 48), slice(None)
        plane = self.out.at[source, :, :, rows, cols]
        return remote(plane, plane, s["hs"].at[slot], s["hr"].at[slot], p.sibling)

    def valid(self, k):
        z = self.p.z + k
        return (z >= 0) & (z <= 3)

    def stage_one(self, half, k):
        source = self.p.z + k

        def run():
            if k == 0:
                src = own_part(self.mine, self.kind, half)
                self._first(half, source, src).start()
                there = part(self.out, self.kind, source, self.p.y, self.p.x, self.p.core, half)
                pltpu.make_async_copy(src, there, self.sems["own"].at[half]).wait()
                return
            self._copy_z(half, source, None, k < 0).wait_recv()
            self._along_z(half, source, None, k < 0, k > 0)
            self._first(half, source).start()

        pl.when(self.valid(k))(run)

    def stage_two(self, half, k):
        source = self.p.z + k

        def run():
            self._first(half, source).wait_recv()
            self._second(half, source).start()

        pl.when(self.valid(k))(run)

    def stage_three(self, half, k):
        source = self.p.z + k

        def run():
            self._second(half, source).wait_recv()
            self._hand(half, source).start()

        pl.when(self.valid(k))(run)

    def arrived(self):
        for half in range(2):
            for source in range(4):
                self._hand(half, source).wait_recv()

    def finish(self):
        p = self.p
        for half in range(2):
            for source in range(4):
                self._first(half, source).wait_send()
                self._second(half, source).wait_send()
                self._hand(half, source).wait_send()
                up = (source <= p.z) & (p.z < 3)
                down = (source >= p.z) & (p.z > 0)
                pl.when(up)(lambda: self._copy_z(half, source, None, True).wait_send())
                pl.when(down)(lambda: self._copy_z(half, source, None, False).wait_send())


GATHER_SEMS = ("zu", "zd", "zr", "fs", "fr", "ss", "sr", "hs", "hr")


def expert_block(ref, kind, z, y, core):
    if kind == "wide":
        return ref.at[z, y, :, :, pl.ds(pl.multiple_of(core * 1536, 128), 1536)]
    return ref.at[z, y, :, pl.ds(pl.multiple_of(core * 96, 16), 96), :]


def expert_piece(ref, kind, z, y, x, core):
    if kind == "wide":
        return ref.at[z, y, x, :, pl.ds(pl.multiple_of(core * 1536, 128), 1536)]
    return ref.at[z, y, x, pl.ds(pl.multiple_of(core * 96, 16), 96), :]


class ExpertGather:
    def __init__(self, place, kind, mine, out, sems):
        self.p, self.kind, self.mine, self.out, self.sems = place, kind, mine, out, sems

    def _cross(self, i):
        p, s = self.p, self.sems
        there = expert_piece(self.out, self.kind, p.z, p.y, p.x, p.core)
        device = (p.across_x, p.across_y, p.across_both)[i]
        expert = device // 2 % 4
        return remote(self.mine.at[expert], there, s["cs"].at[i], s["cr"].at[i], device)

    def _own(self):
        p = self.p
        there = expert_piece(self.out, self.kind, p.z, p.y, p.x, p.core)
        return pltpu.make_async_copy(self.mine.at[p.chip], there, self.sems["own"].at[0])

    def start_own(self):
        self._own().start()
        for i in range(3):
            self._cross(i).start()

    def _copy_z(self, y, source, up):
        p, s = self.p, self.sems
        slot = y * 4 + source
        block = expert_block(self.out, self.kind, source, y, p.core)
        return remote(block, block, s["zu" if up else "zd"].at[slot], s["zr"].at[slot],
                      p.me + 8 if up else p.me - 8)

    def _hand(self, y, source):
        p, s = self.p, self.sems
        slot = y * 4 + source
        block = expert_block(self.out, self.kind, source, y, p.core)
        return remote(block, block, s["hs"].at[slot], s["hr"].at[slot], p.sibling)

    def crossed(self):
        p = self.p
        self._own().wait()
        for i in range(3):
            self._cross(i).wait_recv()
        for y in range(2):
            pl.when(p.z < 3)(lambda: self._copy_z(y, p.z, True).start())
            pl.when(p.z > 0)(lambda: self._copy_z(y, p.z, False).start())
            self._hand(y, p.z).start()

    def stage(self, y, k):
        p = self.p
        source = p.z + k

        def run():
            self._copy_z(y, source, k < 0).wait_recv()
            if k < 0:
                pl.when(p.z < 3)(lambda: self._copy_z(y, source, True).start())
            else:
                pl.when(p.z > 0)(lambda: self._copy_z(y, source, False).start())
            self._hand(y, source).start()

        pl.when((source >= 0) & (source <= 3))(run)

    def arrived(self):
        for y in range(2):
            for source in range(4):
                self._hand(y, source).wait_recv()

    def finish(self):
        p = self.p
        for i in range(3):
            self._cross(i).wait_send()
        for y in range(2):
            for source in range(4):
                self._hand(y, source).wait_send()
                up = (source <= p.z) & (p.z < 3)
                down = (source >= p.z) & (p.z > 0)
                pl.when(up)(lambda: self._copy_z(y, source, True).wait_send())
                pl.when(down)(lambda: self._copy_z(y, source, False).wait_send())


EXPERT_SEMS = ("zu", "zd", "zr", "hs", "hr")
STEPS = (0, -1, 1, -2, 2, -3, 3)


def gather_kernel(
    small_in, wide_in, tall_in,
    small_out, wa0, wmi, wmo, wa1, ein, eout,
    wide_mine, expert_mine, from_sibling, meet, small_sems, gather_sems, own_sems, expert_sems,
    cross_sems,
):
    p = Place()
    greet_all(p, 32)
    swap = remote(wide_in.at[1 - p.core], from_sibling, meet.at[0], meet.at[1], p.sibling)
    swap.start()

    def spread(i):
        remote(small_in, small_out.at[p.me], small_sems.at[0, i], small_sems.at[1, p.me],
               (p.me + i) % 32).start()

    pl.loop(1, 32)(spread)
    small_out[p.me] = small_in[...]
    outs = (wa0, wmi, wmo, wa1)
    dense = []
    for m, kind in enumerate(DENSE):
        sems = {name: gather_sems.at[m, i] for i, name in enumerate(GATHER_SEMS)}
        sems["own"] = own_sems.at[m]
        mine = tall_in.at[0] if kind == "tall" else wide_mine.at[(0, 1, None, 2)[m]]
        dense.append(Gather(p, kind, mine, outs[m], sems))
    experts = []
    for m, kind in enumerate(("wide", "tall")):
        sems = {name: expert_sems.at[m, i] for i, name in enumerate(EXPERT_SEMS)}
        sems["cs"], sems["cr"], sems["own"] = (
            cross_sems.at[m, 0], cross_sems.at[m, 1], cross_sems.at[m, 2])
        mine = tall_in.at[pl.ds(1, 4)] if kind == "tall" else expert_mine
        experts.append(ExpertGather(p, kind, mine, (ein, eout)[m], sems))
    dense[2].start_own()
    experts[1].start_own()
    swap.wait_recv()

    def merge(m, out):
        cols = pl.ds(m * 1536, 1536)
        kept = wide_in[p.core, :, cols]
        came = from_sibling[:, cols]
        upper = jnp.where(p.core == 0, kept, came)
        lower = jnp.where(p.core == 0, came, kept)
        out[...] = jnp.concatenate([upper, lower], 0).astype(BF16)

    merge(0, wide_mine.at[0])
    dense[0].start_own()
    for e in range(4):
        merge(3 + e, expert_mine.at[e])
    experts[0].start_own()
    merge(1, wide_mine.at[1])
    dense[1].start_own()
    merge(2, wide_mine.at[2])
    dense[3].start_own()

    order = [(m, k, half) for m in (0, 1, 2, 3) for k in STEPS for half in range(2)]
    pumps = []
    for i in range(len(order) + 16):
        for stage, lag in ((0, 0), (1, 8), (2, 16)):
            if 0 <= i - lag < len(order):
                pumps.append((stage,) + order[i - lag])
    turns = [(y, k, m) for k in STEPS[1:] for m in (1, 0) for y in range(2)]
    at = {8 + j * (len(pumps) - 10) // len(turns): turn for j, turn in enumerate(turns)}
    for i, (stage, m, k, half) in enumerate(pumps):
        if i == 6:
            experts[1].crossed()
            experts[0].crossed()
        if i in at:
            y, kk, mm = at[i]
            experts[mm].stage(y, kk)
        job = dense[m]
        (job.stage_one, job.stage_two, job.stage_three)[stage](half, k)
    for job in dense + experts:
        job.arrived()
    for job in dense + experts:
        job.finish()
    swap.wait_send()

    def spread_done(i):
        remote(small_in, small_out.at[(p.me + i) % 32], small_sems.at[0, i],
               small_sems.at[1, (p.me + i) % 32], (p.me + i) % 32).wait()

    pl.loop(1, 32)(spread_done)


def run_gather(small, wide, tall):
    any_space = pl.BlockSpec(memory_space=pl.ANY)
    vmem = pl.BlockSpec(memory_space=pltpu.VMEM)
    wide_out = struct((4, 2, 2, 48, 3072), BF16)
    tall_out = struct((4, 2, 2, 192, 768), BF16)
    dma = pltpu.SemaphoreType.DMA
    return pl.pallas_call(
        gather_kernel,
        out_shape=[struct((32, 8, 128), F32), wide_out, wide_out, tall_out, wide_out,
                   wide_out, tall_out],
        in_specs=[vmem, vmem, vmem],
        out_specs=[vmem] + [any_space] * 6,
        scratch_shapes=[
            pltpu.VMEM((3, 48, 1536), BF16),
            pltpu.VMEM((4, 48, 1536), BF16),
            pltpu.VMEM((24, 7 * 1536), F32),
            dma((2,)),
            dma((2, 32)),
            dma((4, len(GATHER_SEMS), 8)),
            dma((4, 2)),
            dma((2, len(EXPERT_SEMS), 8)),
            dma((2, 3, 3)),
        ],
        compiler_params=pltpu.CompilerParams(
            collective_id=0, has_side_effects=True, vmem_limit_bytes=VMEM_BYTES),
        cost_estimate=pl.CostEstimate(flops=0, bytes_accessed=60_000_000, transcendentals=0),
    )(small, wide, tall)

KINDS = ("wide", "tall", "wide", "tall", "wide", "wide")
WIDE_AT = {2: 2, 4: 1, 5: 0}
FAR_FIRST = (-3, 3, -2, 2, -1, 1, 0)


def plane_part(ref, kind, z, core, half):
    if kind == "wide":
        return ref.at[z, :, :, :, pl.ds(pl.multiple_of(core * 1536 + half * 768, 128), 768)]
    return ref.at[z, :, :, pl.ds(pl.multiple_of(core * 96 + half * 48, 16), 48), :]


def add_into(kept, came, pieces):
    def body(i):
        rows = pl.ds(pl.multiple_of(i % 3 * 16, 16), 16)
        a, b = kept(i // 3), came(i // 3)
        a[rows, :] = (a[rows, :].astype(F32) + b[rows, :].astype(F32)).astype(BF16)

    loop(pieces * 3, body)


class Reduce:
    def __init__(self, place, m, ref, own, near, bufs, sems, sink):
        self.p, self.m, self.kind, self.ref = place, m, KINDS[m], ref
        self.own, self.near, self.bufs, self.sems, self.sink = own, near, bufs, sems, sink

    def _load(self, half, z):
        src = plane_part(self.ref, self.kind, z, self.p.core, half)
        return pltpu.make_async_copy(src, self.own.at[z, half], self.sems["load"].at[z, half])

    def _pair(self, half, z):
        p, s = self.p, self.sems
        src = plane_part(self.ref, self.kind, z, 1 - p.core, half)
        return remote(src, self.near.at[z, half], s["ps"].at[z, half], s["pr"].at[z, half], p.sibling)

    def start(self, k):
        z = self.p.z + k

        def run():
            for half in range(2):
                self._load(half, z).start()
                self._pair(half, z).start()

        pl.when(self.valid(k))(run)

    def valid(self, k):
        z = self.p.z + k
        return (z >= 0) & (z <= 3)

    def pair_sum(self, half, k):
        z = self.p.z + k
        self._load(half, z).wait()
        self._pair(half, z).wait_recv()
        own, near = self.own.at[z, half], self.near.at[z, half]
        add_into(lambda i: own.at[i // 2, i % 2], lambda i: near.at[i // 2, i % 2], 4)

    def _block(self, half, z):
        raise NotImplementedError

    def _send_z(self, half, z, up):
        p, s = self.p, self.sems
        side = 0 if up else 1
        return remote(self._block(half, z), self.bufs["z"].at[half, z, side], s["zs"].at[half, z],
                      s["zr"].at[half, z, side], p.me + 8 if up else p.me - 8)

    def _wait_z(self, half, z, up):
        p, s = self.p, self.sems
        side = 0 if up else 1
        remote(self._block(half, z), self.bufs["z"].at[half, z, side], s["zs"].at[half, z],
               s["zr"].at[half, z, side], p.me).wait_recv()

    def along_z(self, half, k):
        p = self.p
        z = p.z + k
        if k == 0:
            self.end_z(half)
            return
        up = k > 0

        def join():
            self._wait_z(half, z, up)
            self._add_z(half, z, 0 if up else 1)

        pl.when(p.z > 0 if up else p.z < 3)(join)
        self._send_z(half, z, up).start()

    def finish(self):
        p = self.p
        for half in range(2):
            for z in range(4):
                if self.m > 1:
                    self._pair(half, z).wait_send()
                pl.when(p.z != z)(lambda: self._send_z(half, z, True).wait_send())


class DenseReduce(Reduce):
    def _block(self, half, z):
        return self.own.at[z, half, self.p.y, self.p.x]

    def _add_z(self, half, z, side):
        kept, came = self._block(half, z), self.bufs["z"].at[half, z, side]
        add_into(lambda i: kept, lambda i: came, 1)

    def _first(self, half, z):
        p, s = self.p, self.sems
        src = self.own.at[z, half, :, 1 - p.x] if half else self.own.at[z, half, 1 - p.y]
        return remote(src, self.bufs["first"].at[z, half], s["fs"].at[z, half], s["fr"].at[z, half],
                      p.across_x if half else p.across_y)

    def _second(self, half, z):
        p, s = self.p, self.sems
        src = self.own.at[z, half, 1 - p.y, p.x] if half else self.own.at[z, half, p.y, 1 - p.x]
        return remote(src, self.bufs["second"].at[z, half], s["ss"].at[z, half],
                      s["sr"].at[z, half], p.across_y if half else p.across_x)

    def stage_one(self, half, k):
        def run():
            self.pair_sum(half, k)
            self._first(half, self.p.z + k).start()

        pl.when(self.valid(k))(run)

    def stage_two(self, half, k):
        p = self.p
        z = p.z + k

        def run():
            self._first(half, z).wait_recv()
            own, came = self.own.at[z, half], self.bufs["first"].at[z, half]
            if half:
                add_into(lambda i: own.at[i, p.x], lambda i: came.at[i], 2)
            else:
                add_into(lambda i: own.at[p.y, i], lambda i: came.at[i], 2)
            self._second(half, z).start()

        pl.when(self.valid(k))(run)

    def stage_three(self, half, k):
        z = self.p.z + k

        def run():
            self._second(half, z).wait_recv()
            kept, came = self._block(half, z), self.bufs["second"].at[z, half]
            add_into(lambda i: kept, lambda i: came, 1)
            self.along_z(half, k)

        pl.when(self.valid(k))(run)

    def end_z(self, half):
        p = self.p
        kept, got = self._block(half, p.z), self.bufs["z"]
        out = self.sink(half)
        out[...] = kept[...].astype(F32)

        def join(side):
            self._wait_z(half, p.z, side == 0)
            out[...] += got[half, p.z, side].astype(F32)

        pl.when(p.z > 0)(lambda: join(0))
        pl.when(p.z < 3)(lambda: join(1))

    def finish(self):
        super().finish()
        for half in range(2):
            for z in range(4):
                self._first(half, z).wait_send()
                self._second(half, z).wait_send()


class ExpertReduce(Reduce):
    def _load(self, half, z):
        return pltpu.make_async_copy(
            self.ref.at[z, half], self.own.at[z, half], self.sems["load"].at[z, half])

    def start(self, k):
        z = self.p.z + k

        def run():
            for half in range(2):
                self._load(half, z).start()

        pl.when(self.valid(k))(run)

    def _block(self, half, z):
        return self.own.at[z, half]

    def _add_z(self, half, z, side):
        kept, came = self._block(half, z), self.bufs["z"].at[half, z, side]
        add_into(lambda i: kept.at[i // 2, i % 2], lambda i: came.at[i // 2, i % 2], 4)

    def stage_one(self, half, k):
        def run():
            self._load(half, self.p.z + k).wait()
            self.along_z(half, k)

        pl.when(self.valid(k))(run)

    def _cross(self, half, i):
        p, s = self.p, self.sems
        device = (p.across_x, p.across_y, p.across_both)[i]
        chip = device // 2 % 4
        src = self.own.at[p.z, half, chip // 2, chip % 2]
        return remote(src, self.bufs["cross"].at[half, i], s["cs"].at[half, i], s["cr"].at[half, i], device)

    def end_z(self, half):
        p = self.p
        pl.when(p.z > 0)(lambda: (self._wait_z(half, p.z, True), self._add_z(half, p.z, 0)) and None)
        pl.when(p.z < 3)(lambda: (self._wait_z(half, p.z, False), self._add_z(half, p.z, 1)) and None)
        for i in range(3):
            self._cross(half, i).start()

    def crossed(self, half):
        p = self.p
        self.sink(half, p.chip)[...] = self.own[p.z, half, p.y, p.x].astype(F32)
        for i in range(3):
            self._cross(half, i).wait_recv()
            device = (p.across_x, p.across_y, p.across_both)[i]
            self.sink(half, device // 2 % 4)[...] = self.bufs["cross"][half, i].astype(F32)

    def finish(self):
        super().finish()
        for half in range(2):
            for i in range(3):
                self._cross(half, i).wait_send()


def reduce_kernel(
    small_in, sums, wa1, wmo, wmi, wa0,
    small_out, wide_out, tall_out,
    own, near, first, second, z_dense, z_expert, cross, done, small_got,
    load_sems, pair_sems, plane_sems, zs_sems, zr_sems, cross_sems, small_sems, meet,
):
    p = Place()
    greet_all(p, 32)
    jobs = []
    for m, ref in enumerate((sums.at[0], sums.at[1], wa1, wmo, wmi, wa0)):
        sems = {"load": load_sems.at[m], "ps": pair_sems.at[m, 0], "pr": pair_sems.at[m, 1],
                "zs": zs_sems.at[m], "zr": zr_sems.at[m]}
        if m < 2:
            sems.update(cs=cross_sems.at[m, 0], cr=cross_sems.at[m, 1])
            bufs = {"z": z_expert.at[m], "cross": cross.at[m]}
            if m == 0:
                def sink(half, e):
                    return done.at[3 + e, :, pl.ds(half * 768, 768)]
            else:
                def sink(half, e):
                    return tall_out.at[1 + e, pl.ds(half * 48, 48), :]
            jobs.append(ExpertReduce(p, m, ref, own.at[m], None, bufs, sems, sink))
            continue
        for i, name in enumerate(("fs", "fr", "ss", "sr")):
            sems[name] = plane_sems.at[m - 2, i]
        bufs = {"z": z_dense.at[m - 2], "first": first.at[m - 2], "second": second.at[m - 2]}
        if m in WIDE_AT:
            def sink(half, m=m):
                return done.at[WIDE_AT[m], :, pl.ds(half * 768, 768)]
        else:
            def sink(half):
                return tall_out.at[0, pl.ds(half * 48, 48), :]
        jobs.append(DenseReduce(p, m, ref, own.at[m], near.at[m - 2], bufs, sems, sink))

    def spread(i):
        to = (p.me + i) % 32
        remote(small_in.at[to], small_got.at[p.me], small_sems.at[0, i], small_sems.at[1, p.me], to).start()

    pl.loop(1, 32)(spread)
    for k in FAR_FIRST:
        for m in (0, 2, 1, 3, 4, 5):
            jobs[m].start(k)
    experts = [("e", m, k, h) for k in FAR_FIRST for m in (0, 1) for h in range(2)]
    dense = [(m, k, h) for m in (2, 3, 4, 5) for k in FAR_FIRST for h in range(2)]
    pumps = []
    for i in range(len(dense) + 16):
        for stage, lag in ((0, 0), (1, 8), (2, 16)):
            if 0 <= i - lag < len(dense):
                pumps.append((stage,) + dense[i - lag])
    at = {j * len(pumps) // len(experts): e for j, e in enumerate(experts)}
    for i, (stage, m, k, half) in enumerate(pumps):
        if i in at:
            _, em, ek, eh = at[i]
            jobs[em].stage_one(eh, ek)
        job = jobs[m]
        (job.stage_one, job.stage_two, job.stage_three)[stage](half, k)
    for m in range(2):
        for half in range(2):
            jobs[m].crossed(half)
    swap = remote(
        done.at[:, pl.ds(pl.multiple_of((1 - p.core) * 24, 8), 24), :], wide_out.at[p.core],
        meet.at[0], meet.at[1], p.sibling)
    swap.start()
    wide_out[p.core] = done[:, pl.ds(pl.multiple_of(p.core * 24, 8), 24), :]

    def spread_done(i):
        to = (p.me + i) % 32
        remote(small_in.at[to], small_got.at[to], small_sems.at[0, i], small_sems.at[1, to], to).wait()

    pl.loop(1, 32)(spread_done)
    small_got[p.me] = small_in[p.me]
    small_out[...] = jnp.sum(small_got[...], 0)
    for job in jobs:
        job.finish()
    swap.wait()


def run_reduce(small, sums, wa1, wmo, wmi, wa0):
    any_space = pl.BlockSpec(memory_space=pl.ANY)
    vmem = pl.BlockSpec(memory_space=pltpu.VMEM)
    dma = pltpu.SemaphoreType.DMA
    piece = (48, 768)
    return pl.pallas_call(
        reduce_kernel,
        out_shape=[struct((8, 128), F32), struct((2, 7, 24, 1536), F32), struct((5, 96, 768), F32)],
        in_specs=[vmem] + [any_space] * 5,
        out_specs=[vmem] * 3,
        scratch_shapes=[
            pltpu.VMEM((6, 4, 2, 2, 2) + piece, BF16),
            pltpu.VMEM((4, 4, 2, 2, 2) + piece, BF16),
            pltpu.VMEM((4, 4, 2, 2) + piece, BF16),
            pltpu.VMEM((4, 4, 2) + piece, BF16),
            pltpu.VMEM((4, 2, 4, 2) + piece, BF16),
            pltpu.VMEM((2, 2, 4, 2, 2, 2) + piece, BF16),
            pltpu.VMEM((2, 2, 3) + piece, BF16),
            pltpu.VMEM((7, 48, 1536), F32),
            pltpu.VMEM((32, 8, 128), F32),
            dma((6, 4, 2)),
            dma((6, 2, 4, 2)),
            dma((4, 4, 4, 2)),
            dma((6, 2, 4)),
            dma((6, 2, 4, 2)),
            dma((2, 2, 2, 3)),
            dma((2, 32)),
            dma((2,)),
        ],
        compiler_params=pltpu.CompilerParams(
            collective_id=1, has_side_effects=True, vmem_limit_bytes=62 << 20),
        cost_estimate=pl.CostEstimate(flops=0, bytes_accessed=60_000_000, transcendentals=0),
    )(small, sums, wa1, wmo, wmi, wa0)


def fast_reduce(dsmall, sums, d0, dmi, dmo, d1):
    small = jnp.pad(dsmall.reshape(8, 32, 24).transpose(1, 0, 2), ((0, 0), (0, 0), (0, 104)))
    w = lambda g: g.reshape(4, 2, 2, 48, HIDDEN)
    t = lambda g: g.reshape(4, 2, 2, 192, WIDTH)
    small, wide, tall = run_reduce(small, sums, w(d1), t(dmo), w(dmi), w(d0))
    wide = wide.transpose(1, 2, 0, 3).reshape(7, 24, HIDDEN)
    return (small[:, :24].T, wide[0], wide[1], tall[0], wide[2],
            wide[3:].transpose(1, 0, 2), tall[1:].transpose(1, 0, 2))


def expert_step(
    rows_x, rows_d, ein, eout,
    y_back, d_back, sums,
    wi, wo, got_x, got_d, active, slope, y_out, d_out, acc, dwi, dwo, near,
    load_sems, own_sems, move_sems, pair_sems, sum_sems,
):
    p = Place()
    greet_all(p, 32)
    chips = [device // 2 % 4 for device in (p.me, p.across_x, p.across_y, p.across_both)]
    devices = (None, p.across_x, p.across_y, p.across_both)
    loads = [pltpu.make_async_copy(src, dst, load_sems.at[i])
             for i, (src, dst) in enumerate(((ein, wi), (eout, wo)))]

    def inward(t, i):
        src, dst = ((rows_x, got_x), (rows_d, got_d))[t]
        if i == 0:
            return pltpu.make_async_copy(src.at[p.chip], dst.at[p.chip], own_sems.at[t])
        return remote(src.at[chips[i]], dst.at[p.chip], move_sems.at[t, 0, i], move_sems.at[t, 1, i],
                      devices[i])

    def outward(t, i):
        src, dst = ((y_out, y_back), (d_out, d_back))[t]
        if i == 0:
            return pltpu.make_async_copy(src.at[p.chip], dst.at[p.chip], own_sems.at[2 + t])
        return remote(src.at[chips[i]], dst.at[p.chip], move_sems.at[2 + t, 0, i],
                      move_sems.at[2 + t, 1, i], devices[i])

    for i in range(4):
        inward(0, i).start()
    for copy in loads:
        copy.start()
    inward(1, 0).start()
    for copy in loads:
        copy.wait()
    wide = wi.reshape(WIDTH, HIDDEN)
    tall = wo.reshape(HIDDEN, WIDTH)
    for i in range(4):
        chip = chips[i]
        if i == 0:
            inward(0, 0).wait()
        else:
            inward(0, i).wait_recv()
        if i == 1:
            for j in range(1, 4):
                inward(1, j).start()
        acc[...] = jnp.zeros_like(acc)

        def forward(n):
            cols = tile(n, 512)
            ea, sl = gelu_both(nn(got_x[chip], wide[:, cols]))
            ea = ea.astype(BF16)
            active[chip, :, cols] = ea
            slope[chip, :, cols] = sl.astype(BF16)
            acc[...] += nn(ea, tall[cols, :])

        loop(6, forward)
        y_out[chip] = acc[...].astype(BF16)
        outward(0, i).start()
    for i in range(4):
        chip = chips[i]
        if i == 0:
            inward(1, 0).wait()
        else:
            inward(1, i).wait_recv()
        acc[...] = jnp.zeros_like(acc)

        def backward(n):
            cols = tile(n, 512)
            dh = slope[chip, :, cols].astype(F32) * nt(got_d[chip], tall[cols, :])
            dh = dh.astype(BF16)
            slope[chip, :, cols] = dh
            acc[...] += nt(dh, wide[:, cols])

        loop(6, backward)
        d_out[chip] = acc[...].astype(BF16)
        outward(1, i).start()
    every = EXPERTS * SLOT
    x_all, d_all = got_x.reshape(every, WIDTH), got_d.reshape(every, WIDTH)
    ea_all, dh_all = active.reshape(every, HIDDEN), slope.reshape(every, HIDDEN)
    dwi_all, dwo_all = dwi.reshape(WIDTH, HIDDEN), dwo.reshape(HIDDEN, WIDTH)

    def weights(n):
        cols = tile(n, 512)
        dwo_all[cols, :] = tn(ea_all[:, cols], d_all[...]).astype(BF16)
        dwi_all[:, cols] = tn(x_all[...], dh_all[:, cols]).astype(BF16)

    loop(6, weights)
    pairs = [(m, z, half) for z in range(4) for m in range(2) for half in range(2)]

    def pair(m, z, half):
        src = plane_part((dwi, dwo)[m], KINDS[m], z, 1 - p.core, half)
        return remote(src, near.at[m, z, half], pair_sems.at[m, z, half, 0],
                      pair_sems.at[m, z, half, 1], p.sibling)

    def result(m, z, half):
        return pltpu.make_async_copy(near.at[m, z, half], sums.at[m, z, half], sum_sems.at[m, z, half])

    for one in pairs:
        pair(*one).start()
    for m, z, half in pairs:
        pair(m, z, half).wait_recv()
        own = plane_part((dwi, dwo)[m], KINDS[m], z, p.core, half)
        came = near.at[m, z, half]
        add_into(lambda i: came.at[i // 2, i % 2], lambda i: own.at[i // 2, i % 2], 4)
        result(m, z, half).start()
    for one in pairs:
        result(*one).wait()
        pair(*one).wait_send()
    for t in range(2):
        outward(t, 0).wait()
        for i in range(1, 4):
            inward(t, i).wait_send()
            outward(t, i).wait()


def run_expert_step(rows_x, rows_d, ein, eout):
    any_space = pl.BlockSpec(memory_space=pl.ANY)
    dma = pltpu.SemaphoreType.DMA
    rows = (EXPERTS, SLOT, WIDTH)
    y, d, sums = pl.pallas_call(
        expert_step,
        out_shape=[struct(rows, BF16)] * 2 + [struct((2, 4, 2, 2, 2, 48, 768), BF16)],
        in_specs=[any_space] * 4,
        out_specs=[any_space] * 3,
        scratch_shapes=[
            pltpu.VMEM((4, 2, 2, 48, HIDDEN), BF16),
            pltpu.VMEM((4, 2, 2, 192, WIDTH), BF16),
            pltpu.VMEM(rows, BF16),
            pltpu.VMEM(rows, BF16),
            pltpu.VMEM((EXPERTS, SLOT, HIDDEN), BF16),
            pltpu.VMEM((EXPERTS, SLOT, HIDDEN), BF16),
            pltpu.VMEM(rows, BF16),
            pltpu.VMEM(rows, BF16),
            pltpu.VMEM((SLOT, WIDTH), F32),
            pltpu.VMEM((4, 2, 2, 48, HIDDEN), BF16),
            pltpu.VMEM((4, 2, 2, 192, WIDTH), BF16),
            pltpu.VMEM((2, 4, 2, 2, 2, 48, 768), BF16),
            dma((2,)),
            dma((4,)),
            dma((4, 2, 4)),
            dma((2, 4, 2, 2)),
            dma((2, 4, 2)),
        ],
        compiler_params=pltpu.CompilerParams(
            collective_id=2, has_side_effects=True, vmem_limit_bytes=VMEM_BYTES),
        cost_estimate=pl.CostEstimate(
            flops=30_000_000_000, bytes_accessed=40_000_000, transcendentals=0),
    )(rows_x.reshape(rows), rows_d.reshape(rows), ein, eout)
    flat = (EXPERTS * SLOT, WIDTH)
    return y.reshape(flat), d.reshape(flat), sums


def fast_gather(smalls, wide, mlp_out, expert_in, expert_out):
    width = smalls.shape[0] * 32
    small = jnp.pad(smalls.astype(F32).T, ((0, 0), (0, 128 - smalls.shape[0])))
    packed = jnp.concatenate(wide + [expert_in[:, e] for e in range(EXPERTS)], 1).astype(F32)
    packed = packed.reshape(24, 7, 2, 1536).transpose(2, 0, 1, 3).reshape(2, 24, 7 * 1536)
    tall = jnp.concatenate([mlp_out[None], expert_out.transpose(1, 0, 2)], 0)
    small, wa0, wmi, wmo, wa1, ein, eout = run_gather(small, packed, tall)
    small = small[:, :, : smalls.shape[0]].transpose(1, 0, 2).reshape(8, width)
    flat = [w.reshape(width, HIDDEN) for w in (wa0, wmi, wa1)]
    return small, flat[:2] + [flat[2]], [wmo.reshape(HIDDEN, width)], ein, eout


def local(
    patches, live_count, expert_ids, attn_gain, attn_qkv, attn_out, mlp_gain, mlp_in, mlp_out,
    moe_gain, router, expert_in, expert_out, cotangent,
):
    images, seq, width = patches.shape
    padded = -(-seq // 16) * 16
    n = lax.axis_size("fsdp")
    group_size = n // EXPERTS
    group = lax.axis_index("fsdp") // group_size
    alive = jnp.arange(images, dtype=jnp.int32) < live_count[0]

    def pad(values, fill=0):
        values = values.reshape(images, seq, -1)
        values = jnp.pad(values, ((0, 0), (0, padded - seq), (0, 0)), constant_values=fill)
        return values.reshape(images * padded, -1)

    x0 = pad(patches)
    g4 = pad(jnp.where(alive[:, None, None], cotangent, jnp.zeros_like(cotangent)))
    ids = pad(expert_ids, -1)
    smalls = jnp.concatenate(
        [attn_gain, mlp_gain[:, None], moe_gain[:, None], router], 1
    )
    wide = [jnp.concatenate([attn_qkv[:, 0], attn_out[:, 0]], 1), mlp_in,
            jnp.concatenate([attn_qkv[:, 1], attn_out[:, 1]], 1)]
    if n == 32:
        small, wides, talls, w_in, w_out = fast_gather(smalls, wide, mlp_out, expert_in, expert_out)
    else:
        small, wides, talls, w_in, w_out = plain_gather(
            smalls, wide, [mlp_out], expert_in, expert_out)
        small = small.astype(F32).T
    small = jnp.concatenate(
        [small[:4], jnp.zeros((4, width), F32), small[4:], jnp.zeros((124, width), F32)], 0
    )
    weights = (wides[0], wides[1], talls[0], wides[2])
    out = run_forward(images, seq, x0, g4, ids, small, *weights)
    saved, rows_x, rows_d = out[:16], out[16], out[17]

    def exchange(rows):
        rows = rows.reshape(EXPERTS, SLOT, width)
        return group_exchange(rows, group_size, group).reshape(EXPERTS * SLOT, width)

    if n == 32:
        y_back, d_back, sums = run_expert_step(rows_x, rows_d, w_in, w_out)
    else:
        y, dx, dw_in, dw_out = run_expert(exchange(rows_x), exchange(rows_d), w_in, w_out)
        y_back, d_back = exchange(y), exchange(dx)
    x4, grad, d0, dmi, dmo, d1, dsmall = run_backward(
        images, seq, x0, g4, small, weights, saved, y_back, d_back
    )

    def unpad(values):
        return values.reshape(images, padded, width)[:, :seq]

    block_out = jnp.where(alive[:, None, None], unpad(x4), 0.0).astype(BF16)
    if n == 32:
        dsmall, d0, dmi, dmo, d1, de_in, de_out = fast_reduce(
            dsmall, sums, d0, dmi, dmo, d1)
    else:
        d0, dmi, dmo, d1 = (plain_reduce(g).astype(F32) for g in (d0, dmi, dmo, d1))
        de_in, de_out = (plain_reduce_expert(g).astype(F32) for g in (dw_in, dw_out))
        dsmall = lax.psum_scatter(dsmall.T, "fsdp", scatter_dimension=0, tiled=True)
    return (
        block_out,
        unpad(grad),
        dsmall[:, 0:2],
        jnp.stack([d0[:, :2304], d1[:, :2304]], 1),
        jnp.stack([d0[:, 2304:], d1[:, 2304:]], 1),
        dsmall[:, 2],
        dmi,
        dmo,
        dsmall[:, 3],
        dsmall[:, 4:8],
        de_in,
        de_out,
    )


def solution(mesh):
    def lead(rank):
        return P("fsdp", *([None] * (rank - 1)))

    return jax.shard_map(
        local,
        mesh=mesh,
        in_specs=tuple(lead(r) for r in (3, 1, 2, 2, 3, 3, 1, 2, 2, 1, 2, 3, 3, 3)),
        out_specs=tuple(lead(r) for r in (3, 3, 2, 3, 3, 1, 2, 2, 1, 2, 3, 3)),
        check_vma=False,
    )
```

```python
import functools

import jax
import jax.numpy as jnp
from jax import lax
from jax.experimental import pallas as pl
from jax.experimental.pallas import tpu as pltpu
from jax.sharding import PartitionSpec as P

HEADS = 12
HEAD_DIM = 64
EXPERTS = 4
CAP = 247
SLOT = 256
WIDTH = 768
HIDDEN = 3072
NORM_EPSILON = 1e-06
VMEM_BYTES = 60 << 20
F32 = jnp.float32
BF16 = jnp.bfloat16


def nn(left, right):
    return lax.dot_general(left, right, (((1,), (0,)), ((), ())), preferred_element_type=F32)


def nt(left, right):
    return lax.dot_general(left, right, (((1,), (1,)), ((), ())), preferred_element_type=F32)


def tn(left, right):
    return lax.dot_general(left, right, (((0,), (0,)), ((), ())), preferred_element_type=F32)


def tile(index, size):
    return pl.ds(pl.multiple_of(index * size, size), size)


def loop(count, body):
    pl.loop(0, count)(body)


def norm_parts(values):
    center = values - jnp.mean(values, -1, keepdims=True)
    spread = jnp.mean(center * center, -1, keepdims=True)
    scale = lax.rsqrt(spread + NORM_EPSILON)
    return center * scale, scale


def norm_rows(x_ref, gain, out_ref, block=32):
    def body(i):
        rows = tile(i, block)
        unit, _ = norm_parts(x_ref[rows, :])
        out_ref[rows, :] = (unit * gain).astype(BF16)

    loop(x_ref.shape[0] // block, body)


def norm_back(x_ref, gain, dn_ref, g_ref, dgain_ref, row, block=32):
    def body(i, total):
        rows = tile(i, block)
        unit, scale = norm_parts(x_ref[rows, :])
        dn = dn_ref[rows, :]
        scaled = dn * gain
        mean_one = jnp.mean(scaled, -1, keepdims=True)
        mean_two = jnp.mean(scaled * unit, -1, keepdims=True)
        g_ref[rows, :] = g_ref[rows, :] + scale * (scaled - mean_one - unit * mean_two)
        return total + jnp.sum((dn * unit).reshape(block // 8, 8, WIDTH), 0)

    total = lax.fori_loop(0, x_ref.shape[0] // block, body, jnp.zeros((8, WIDTH), F32))
    dgain_ref[row : row + 1, :] = jnp.sum(total, 0, keepdims=True)


def gelu_both(u):
    c = 0.7978845608
    square = u * u
    t = jnp.tanh(c * u * (1.0 + 0.044715 * square))
    half = 0.5 * (1.0 + t)
    slope = half + 0.5 * u * (1.0 - t * t) * (c + (3 * 0.044715 * c) * square)
    return u * half, slope


def halves(shape):
    lane = lax.broadcasted_iota(jnp.int32, shape, 1)
    return lane < HEAD_DIM


def head_probs(q, k, seq):
    scores = nt(q, k) * HEAD_DIM ** (-0.5)
    key = lax.broadcasted_iota(jnp.int32, scores.shape, 1)
    scores = jnp.where(key < seq, scores, -1e30)
    top = jnp.max(scores, -1, keepdims=True)
    e = jnp.exp(scores - top)
    return e / jnp.sum(e, -1, keepdims=True)


def attention_heads(qkv_ref, o_ref, images, seq):
    rows_of = qkv_ref.shape[0] // images
    for image in range(images):
        rows = pl.ds(image * rows_of, rows_of)

        def pair(p, rows=rows):
            q = qkv_ref[rows, tile(p, 128)]
            k = qkv_ref[rows, tile(p + 6, 128)]
            v = qkv_ref[rows, tile(p + 12, 128)]
            first = halves(q.shape)
            zero = jnp.zeros_like(q)
            p0 = head_probs(jnp.where(first, q, zero), k, seq).astype(BF16)
            p1 = head_probs(jnp.where(first, zero, q), k, seq).astype(BF16)
            out = nn(p0, jnp.where(first, v, zero)) + nn(p1, jnp.where(first, zero, v))
            o_ref[rows, tile(p, 128)] = out.astype(BF16)

        loop(6, pair)


def attention_forward(x_ref, gain, w_ref, xo_ref, an_ref, qkv_ref, o_ref, images, seq):
    norm_rows(x_ref, gain, an_ref)

    def project(n):
        qkv_ref[:, tile(n, 256)] = nn(an_ref[...], w_ref[:, tile(n, 256)]).astype(BF16)

    loop(9, project)
    attention_heads(qkv_ref, o_ref, images, seq)

    def outward(n):
        cols = tile(n, 256)
        xo_ref[:, cols] = x_ref[:, cols] + nn(o_ref[...], w_ref[:, tile(n + 9, 256)])

    loop(3, outward)


def attention_backward(
    g_ref, x_ref, gain, w_ref, an_ref, qkv_ref, o_ref, dw_ref, dgain_ref, row, images, seq,
    low_ref, do_ref, dqkv_ref, dn_ref, weights_here=lambda: None, ready=lambda: None,
    pump=lambda: None,
):
    rows_of = qkv_ref.shape[0] // images
    low_ref[...] = g_ref[...].astype(BF16)

    def outward(n):
        dw_ref[:, tile(n + 9, 256)] = tn(o_ref[...], low_ref[:, tile(n, 256)]).astype(BF16)

    loop(3, outward)
    pump()
    weights_here()

    def outward_rows(n):
        do_ref[:, tile(n, 256)] = nt(low_ref[...], w_ref[tile(n, 256), 2304:]).astype(BF16)

    loop(3, outward_rows)
    pump()
    for image in range(images):
        rows = pl.ds(image * rows_of, rows_of)

        def pair(p, rows=rows):
            q = qkv_ref[rows, tile(p, 128)]
            k = qkv_ref[rows, tile(p + 6, 128)]
            v = qkv_ref[rows, tile(p + 12, 128)]
            d = do_ref[rows, tile(p, 128)]
            first = halves(q.shape)
            zero = jnp.zeros_like(q)
            dq = dk = dv = None
            for mine in (first, ~first):
                qm, km, dm = (jnp.where(mine, t, zero) for t in (q, k, d))
                probs = head_probs(qm, k, seq)
                dp = nt(dm, v)
                inner = jnp.sum(dp * probs, -1, keepdims=True)
                ds = (probs * (dp - inner)).astype(BF16)
                one = (nn(ds, km), tn(ds, qm), tn(probs.astype(BF16), dm))
                dq, dk, dv = one if dq is None else (dq + one[0], dk + one[1], dv + one[2])
            scale = HEAD_DIM ** (-0.5)
            dqkv_ref[rows, tile(p, 128)] = (dq * scale).astype(BF16)
            dqkv_ref[rows, tile(p + 6, 128)] = (dk * scale).astype(BF16)
            dqkv_ref[rows, tile(p + 12, 128)] = dv.astype(BF16)

        loop(3, pair)
        pump()
        loop(3, lambda p, pair=pair: pair(p + 3))
        pump()

    for third in range(3):

        def inward(n, third=third):
            cols = tile(n + third * 3, 256)
            dw_ref[:, cols] = tn(an_ref[...], dqkv_ref[:, cols]).astype(BF16)

        loop(3, inward)
        pump()
    ready()

    def normed(n):
        dn_ref[:, tile(n, 256)] = nt(dqkv_ref[...], w_ref[tile(n, 256), :2304])

    loop(3, normed)
    pump()
    norm_back(x_ref, gain, dn_ref, g_ref, dgain_ref, row)
    pump()


def forward_kernel(
    images, seq,
    x0_ref, g4_ref, ids_ref, small_ref, wa0_ref, wmi_ref, wmo_ref, wa1_ref,
    x1_ref, x2_ref, x3_ref, an0_ref, qkv0_ref, o0_ref, mn_ref, slope_ref, ma_ref,
    an1_ref, qkv1_ref, o1_ref, en_ref, aux_ref, g0_ref, g1_ref, rx_ref, rd_ref,
    xf_ref,
):
    rows = x0_ref.shape[0]
    xf_ref[...] = x0_ref[...].astype(F32)
    attention_forward(
        xf_ref, small_ref[0:1, :], wa0_ref, x1_ref, an0_ref, qkv0_ref, o0_ref, images, seq
    )
    norm_rows(x1_ref, small_ref[2:3, :], mn_ref)
    x2_ref[...] = x1_ref[...]

    def dense(n):
        cols = tile(n, 512)
        active, slope = gelu_both(nn(mn_ref[...], wmi_ref[:, cols]))
        slope_ref[:, cols] = slope.astype(BF16)
        active = active.astype(BF16)
        ma_ref[:, cols] = active
        x2_ref[...] += nn(active, wmo_ref[cols, :])

    loop(6, dense)
    attention_forward(
        x2_ref, small_ref[1:2, :], wa1_ref, x3_ref, an1_ref, qkv1_ref, o1_ref, images, seq
    )
    norm_rows(x3_ref, small_ref[3:4, :], en_ref)
    logits = nt(en_ref[...], small_ref[8:136, :].astype(BF16))
    lane = lax.broadcasted_iota(jnp.int32, logits.shape, 1)
    logits = jnp.where(lane < EXPERTS, logits, -1e30)
    e = jnp.exp(logits - jnp.max(logits, -1, keepdims=True))
    chances = e / jnp.sum(e, -1, keepdims=True)
    ids = ids_ref[...]
    chosen = [(ids[:, j : j + 1] == lane).astype(F32) for j in range(2)]
    row_i = lax.broadcasted_iota(jnp.int32, (rows, rows), 0)
    row_j = lax.broadcasted_iota(jnp.int32, (rows, rows), 1)
    earlier = nn((row_j < row_i).astype(BF16), (chosen[0] + chosen[1]).astype(BF16))
    place = lax.broadcasted_iota(jnp.int32, (rows, EXPERTS * SLOT), 1)
    gates = []
    for j, pick_ref in ((0, g0_ref), (1, g1_ref)):
        gates.append(jnp.sum(chances * chosen[j], -1, keepdims=True))
        inside = jnp.sum(earlier * chosen[j], -1, keepdims=True).astype(jnp.int32)
        slot = jnp.where(ids[:, j : j + 1] >= 0, ids[:, j : j + 1] * SLOT + inside, -1)
        pick_ref[...] = (slot == place).astype(BF16)
    aux = jnp.where(lane < EXPERTS, chances, 0.0)
    aux = jnp.where(lane == 8, gates[0], aux)
    aux_ref[...] = jnp.where(lane == 9, gates[1], aux)

    def fill(n):
        cols = tile(n, 256)
        both = g0_ref[:, cols] + g1_ref[:, cols]
        rx_ref[cols, :] = tn(both, en_ref[...]).astype(BF16)
        g4 = g4_ref[...].astype(F32)
        one = tn(g0_ref[:, cols], (g4 * gates[0]).astype(BF16))
        two = tn(g1_ref[:, cols], (g4 * gates[1]).astype(BF16))
        rd_ref[cols, :] = (one + two).astype(BF16)

    loop(EXPERTS, fill)


def expert_kernel(x_ref, d_ref, wi_ref, wo_ref, y_ref, dx_ref, dwi_ref, dwo_ref, yf_ref, df_ref):
    yf_ref[...] = jnp.zeros_like(yf_ref)
    df_ref[...] = jnp.zeros_like(df_ref)

    def body(n):
        cols = tile(n, 512)
        active, slope = gelu_both(nn(x_ref[...], wi_ref[:, cols]))
        active = active.astype(BF16)
        yf_ref[...] += nn(active, wo_ref[cols, :])
        dwo_ref[cols, :] = tn(active, d_ref[...]).astype(BF16)
        dh = (slope * nt(d_ref[...], wo_ref[cols, :])).astype(BF16)
        df_ref[...] += nt(dh, wi_ref[:, cols])
        dwi_ref[:, cols] = tn(x_ref[...], dh).astype(BF16)

    loop(6, body)
    y_ref[...] = yf_ref[...].astype(BF16)
    dx_ref[...] = df_ref[...].astype(BF16)


def combine_kernel(
    g4_ref, small_ref, x3_ref, en_ref, aux_ref, g0_ref, g1_ref, yr_ref, dr_ref,
    x4_ref, g_ref, ds_ref,
    dn_ref,
):
    aux = aux_ref[...]
    lane = lax.broadcasted_iota(jnp.int32, aux.shape, 1)
    g_ref[...] = g4_ref[...].astype(F32)
    x4_ref[...] = x3_ref[...]
    dgates = []
    chosen = []
    expert_of = lax.broadcasted_iota(jnp.int32, (EXPERTS * SLOT, 128), 0) // SLOT
    spread = (expert_of == lax.broadcasted_iota(jnp.int32, expert_of.shape, 1)).astype(BF16)
    for j, pick_ref in ((0, g0_ref), (1, g1_ref)):
        picked = nn(pick_ref[...], yr_ref[...])
        x4_ref[...] += aux[:, 8 + j : 9 + j] * picked
        dgates.append(jnp.sum(g_ref[...] * picked, -1, keepdims=True))
        chosen.append(nn(pick_ref[...], spread))
    dr = dgates[0] * chosen[0] + dgates[1] * chosen[1]
    chances = jnp.where(lane < EXPERTS, aux, 0.0)
    dlogits = chances * (dr - jnp.sum(chances * dr, -1, keepdims=True))
    dlogits = jnp.where(lane < EXPERTS, dlogits, 0.0).astype(BF16)
    ds_ref[...] = jnp.zeros_like(ds_ref)
    ds_ref[4:8, :] = tn(dlogits, en_ref[...])[0:4, :]
    dn_ref[...] = nn(dlogits, small_ref[8:136, :].astype(BF16)) + nn(
        g0_ref[...] + g1_ref[...], dr_ref[...]
    )
    norm_back(x3_ref, small_ref[3:4, :], dn_ref, g_ref, ds_ref, 3)


def attention_back_kernel(
    images, seq, row,
    g_in_ref, small_ref, x_ref, w_ref, an_ref, qkv_ref, o_ref,
    g_ref, dw_ref, ds_ref,
    xf_ref, low_ref, do_ref, dqkv_ref, dn_ref,
):
    g_ref[...] = g_in_ref[...]
    xf_ref[...] = x_ref[...].astype(F32)
    ds_ref[...] = jnp.zeros_like(ds_ref)
    attention_backward(
        g_ref, xf_ref, small_ref[row : row + 1, :], w_ref, an_ref, qkv_ref, o_ref, dw_ref,
        ds_ref, row, images, seq, low_ref, do_ref, dqkv_ref, dn_ref,
    )


def dense_back_kernel(
    g_in_ref, small_ref, x1_ref, wmi_ref, wmo_ref, mn_ref, slope_ref, ma_ref,
    g_ref, dwmi_ref, dwmo_ref, ds_ref,
    low_ref, dn_ref,
):
    g_ref[...] = g_in_ref[...]
    ds_ref[...] = jnp.zeros_like(ds_ref)
    low_ref[...] = g_ref[...].astype(BF16)
    dn_ref[...] = jnp.zeros_like(dn_ref)

    def dense(n):
        cols = tile(n, 512)
        dwmo_ref[cols, :] = tn(ma_ref[:, cols], low_ref[...]).astype(BF16)
        dact = nt(low_ref[...], wmo_ref[cols, :])
        dh = (slope_ref[:, cols].astype(F32) * dact).astype(BF16)
        dwmi_ref[:, cols] = tn(mn_ref[...], dh).astype(BF16)
        dn_ref[...] += nt(dh, wmi_ref[:, cols])

    loop(6, dense)
    norm_back(x1_ref, small_ref[2:3, :], dn_ref, g_ref, ds_ref, 2)


def struct(shape, dtype):
    return jax.ShapeDtypeStruct(shape, dtype)


def call(body, outs, scratch, args, flops):
    total = sum(a.size * a.dtype.itemsize for a in list(args) + list(outs))
    return pl.pallas_call(
        body,
        out_shape=outs,
        in_specs=[pl.BlockSpec(memory_space=pltpu.VMEM)] * len(args),
        out_specs=[pl.BlockSpec(memory_space=pltpu.VMEM)] * len(outs),
        scratch_shapes=scratch,
        compiler_params=pltpu.CompilerParams(vmem_limit_bytes=VMEM_BYTES),
        cost_estimate=pl.CostEstimate(flops=flops, bytes_accessed=total, transcendentals=0),
    )(*args)


def run_forward(images, seq, x0, g4, ids, small, wa0, wmi, wmo, wa1):
    rows = x0.shape[0]
    act = struct((rows, WIDTH), F32)
    low = struct((rows, WIDTH), BF16)
    qkv = struct((rows, 3 * WIDTH), BF16)
    hid = struct((rows, HIDDEN), BF16)
    pick = struct((rows, EXPERTS * SLOT), BF16)
    buf = struct((EXPERTS * SLOT, WIDTH), BF16)
    outs = [act, act, act, low, qkv, low, low, hid, hid, low, qkv, low, low,
            struct((rows, 128), F32), pick, pick, buf, buf]
    return call(
        functools.partial(forward_kernel, images, seq), outs,
        [pltpu.VMEM((rows, WIDTH), F32)],
        [x0, g4, ids, small, wa0, wmi, wmo, wa1], 8_000_000_000,
    )


def run_expert(x, d, wi, wo):
    outs = [struct(x.shape, BF16), struct(x.shape, BF16), struct(wi.shape, BF16), struct(wo.shape, BF16)]
    return call(
        expert_kernel, outs, [pltpu.VMEM(x.shape, F32), pltpu.VMEM(x.shape, F32)],
        [x, d, wi, wo], 30_000_000_000,
    )


def run_backward(images, seq, x0, g4, small, weights, saved, y_back, d_back):
    rows = x0.shape[0]
    act = struct((rows, WIDTH), F32)
    wide, tall = struct((WIDTH, HIDDEN), BF16), struct((HIDDEN, WIDTH), BF16)
    row = struct((8, WIDTH), F32)
    wa0, wmi, wmo, wa1 = weights
    x1, x2, x3, an0, qkv0, o0, mn, slope, ma, an1, qkv1, o1, en, aux, p0, p1 = saved
    full = pltpu.VMEM((rows, WIDTH), F32)
    low = pltpu.VMEM((rows, WIDTH), BF16)
    mixed = pltpu.VMEM((rows, 3 * WIDTH), BF16)
    x4, g, s0 = call(
        combine_kernel, [act, act, row], [full],
        [g4, small, x3, en, aux, p0, p1, y_back, d_back], 3_000_000_000,
    )
    g, dwa1, s1 = call(
        functools.partial(attention_back_kernel, images, seq, 1), [act, wide, row],
        [full, low, low, mixed, full], [g, small, x2, wa1, an1, qkv1, o1], 5_000_000_000,
    )
    g, dwmi, dwmo, s2 = call(
        dense_back_kernel, [act, wide, tall, row], [low, full],
        [g, small, x1, wmi, wmo, mn, slope, ma], 8_000_000_000,
    )
    g, dwa0, s3 = call(
        functools.partial(attention_back_kernel, images, seq, 0), [act, wide, row],
        [full, low, low, mixed, full], [g, small, x0, wa0, an0, qkv0, o0], 5_000_000_000,
    )
    return x4, g, dwa0, dwmi, dwmo, dwa1, s0 + s1 + s2 + s3


def gather_rows(piece):
    return lax.all_gather(piece, "fsdp", axis=0, tiled=True)


def shift(values, steps):
    count = lax.axis_size("fsdp")
    return lax.ppermute(values, "fsdp", [(s, (s + steps) % count) for s in range(count)])


def group_exchange(rows, group_size, group_id):
    out = jnp.zeros_like(rows)
    for offset in range(EXPERTS):
        piece = lax.dynamic_index_in_dim(rows, (group_id + offset) % EXPERTS, 0, keepdims=False)
        if offset:
            piece = shift(piece, offset * group_size)
        out = lax.dynamic_update_index_in_dim(out, piece, (group_id - offset) % EXPERTS, 0)
    return out


def plain_gather(smalls, wide, tall, e_in, e_out):
    n = lax.axis_size("fsdp")
    group_size = n // EXPERTS
    group = lax.axis_index("fsdp") // group_size
    small = gather_rows(smalls)
    wides = [gather_rows(w) for w in wide]
    talls = [gather_rows(w) for w in tall]
    big_in = lax.dynamic_index_in_dim(gather_rows(e_in), group, 1, keepdims=False)
    big_out = lax.dynamic_index_in_dim(gather_rows(e_out), group, 1, keepdims=False)
    return small, wides, talls, big_in, big_out


def plain_reduce(grad):
    return lax.psum_scatter(grad, "fsdp", scatter_dimension=0, tiled=True)


def plain_reduce_expert(grad):
    n = lax.axis_size("fsdp")
    group_size = n // EXPERTS
    group = lax.axis_index("fsdp") // group_size
    full = jnp.zeros((grad.shape[0], EXPERTS, grad.shape[1]), BF16)
    full = lax.dynamic_update_index_in_dim(full, grad, group, 1)
    return plain_reduce(full)

MESH_ID = pl.DeviceIdType.MESH


class Place:
    def __init__(self):
        self.me = lax.axis_index("fsdp")
        self.core = self.me % 2
        self.x = self.me // 2 % 2
        self.y = self.me // 4 % 2
        self.z = self.me // 8
        self.sibling = self.me + 1 - 2 * self.core
        self.across_x = self.me + 2 - 4 * self.x
        self.across_y = self.me + 4 - 8 * self.y
        self.across_both = self.across_x + 4 - 8 * self.y
        self.chip = self.me // 2 % 4


def remote(src, dst, send, recv, device):
    return pltpu.make_async_remote_copy(
        src_ref=src, dst_ref=dst, send_sem=send, recv_sem=recv,
        device_id=(device,), device_id_type=MESH_ID,
    )


def greet_all(place, count):
    barrier = pltpu.get_barrier_semaphore()

    def hello(i):
        pl.semaphore_signal(
            barrier, inc=1, device_id=((place.me + i) % count,), device_id_type=MESH_ID
        )

    pl.loop(1, count)(hello)
    pl.semaphore_wait(barrier, count - 1)


DENSE = ("wide", "wide", "tall", "wide")


def part(ref, kind, z, y, x, core, half):
    if kind == "wide":
        return ref.at[z, y, x, :, pl.ds(pl.multiple_of(core * 1536 + half * 768, 128), 768)]
    return ref.at[z, y, x, pl.ds(pl.multiple_of(core * 96 + half * 48, 16), 48), :]


def own_part(mine, kind, half):
    if kind == "wide":
        return mine.at[:, pl.ds(half * 768, 768)]
    return mine.at[pl.ds(half * 48, 48), :]


class Gather:
    def __init__(self, place, kind, mine, out, sems):
        self.p, self.kind, self.mine, self.out, self.sems = place, kind, mine, out, sems

    def _z(self, half, source, up):
        p = self.p
        where = part(self.out, self.kind, source, p.y, p.x, p.core, half)
        return where, 0 if up else 1

    def _slot(self, half, source):
        return half * 4 + source

    def start_own(self):
        p, s = self.p, self.sems
        for half in range(2):
            there = part(self.out, self.kind, p.z, p.y, p.x, p.core, half)
            src = own_part(self.mine, self.kind, half)
            pltpu.make_async_copy(src, there, s["own"].at[half]).start()
            self._along_z(half, p.z, src, True, True)

    def _copy_z(self, half, source, src, up):
        p, s = self.p, self.sems
        slot = self._slot(half, source)
        there = part(self.out, self.kind, source, p.y, p.x, p.core, half)
        name = "zu" if up else "zd"
        return remote(there if src is None else src, there, s[name].at[slot], s["zr"].at[slot],
                      p.me + 8 if up else p.me - 8)

    def _along_z(self, half, source, src, up, down):
        p = self.p
        if up:
            pl.when(p.z < 3)(lambda: self._copy_z(half, source, src, True).start())
        if down:
            pl.when(p.z > 0)(lambda: self._copy_z(half, source, src, False).start())

    def _first(self, half, source, src=None):
        p, s = self.p, self.sems
        slot = self._slot(half, source)
        there = part(self.out, self.kind, source, p.y, p.x, p.core, half)
        return remote(there if src is None else src, there, s["fs"].at[slot], s["fr"].at[slot],
                      p.across_y if half else p.across_x)

    def _line(self, half, source):
        p = self.p
        if self.kind == "wide":
            rows, cols = slice(None), pl.ds(pl.multiple_of(p.core * 1536 + half * 768, 128), 768)
        else:
            rows, cols = pl.ds(pl.multiple_of(p.core * 96 + half * 48, 16), 48), slice(None)
        if half:
            return self.out.at[source, :, p.x, rows, cols]
        return self.out.at[source, p.y, :, rows, cols]

    def _second(self, half, source):
        p, s = self.p, self.sems
        slot = self._slot(half, source)
        line = self._line(half, source)
        return remote(line, line, s["ss"].at[slot], s["sr"].at[slot],
                      p.across_x if half else p.across_y)

    def _hand(self, half, source):
        p, s = self.p, self.sems
        slot = self._slot(half, source)
        if self.kind == "wide":
            rows, cols = slice(None), pl.ds(pl.multiple_of(p.core * 1536 + half * 768, 128), 768)
        else:
            rows, cols = pl.ds(pl.multiple_of(p.core * 96 + half * 48, 16), 48), slice(None)
        plane = self.out.at[source, :, :, rows, cols]
        return remote(plane, plane, s["hs"].at[slot], s["hr"].at[slot], p.sibling)

    def valid(self, k):
        z = self.p.z + k
        return (z >= 0) & (z <= 3)

    def stage_one(self, half, k):
        source = self.p.z + k

        def run():
            if k == 0:
                src = own_part(self.mine, self.kind, half)
                self._first(half, source, src).start()
                there = part(self.out, self.kind, source, self.p.y, self.p.x, self.p.core, half)
                pltpu.make_async_copy(src, there, self.sems["own"].at[half]).wait()
                return
            self._copy_z(half, source, None, k < 0).wait_recv()
            self._along_z(half, source, None, k < 0, k > 0)
            self._first(half, source).start()

        pl.when(self.valid(k))(run)

    def stage_two(self, half, k):
        source = self.p.z + k

        def run():
            self._first(half, source).wait_recv()
            self._second(half, source).start()

        pl.when(self.valid(k))(run)

    def stage_three(self, half, k):
        source = self.p.z + k

        def run():
            self._second(half, source).wait_recv()
            self._hand(half, source).start()

        pl.when(self.valid(k))(run)

    def arrived(self):
        for half in range(2):
            for source in range(4):
                self._hand(half, source).wait_recv()

    def finish(self):
        p = self.p
        for half in range(2):
            for source in range(4):
                self._first(half, source).wait_send()
                self._second(half, source).wait_send()
                self._hand(half, source).wait_send()
                up = (source <= p.z) & (p.z < 3)
                down = (source >= p.z) & (p.z > 0)
                pl.when(up)(lambda: self._copy_z(half, source, None, True).wait_send())
                pl.when(down)(lambda: self._copy_z(half, source, None, False).wait_send())


GATHER_SEMS = ("zu", "zd", "zr", "fs", "fr", "ss", "sr", "hs", "hr")


def expert_block(ref, kind, z, y, core):
    if kind == "wide":
        return ref.at[z, y, :, :, pl.ds(pl.multiple_of(core * 1536, 128), 1536)]
    return ref.at[z, y, :, pl.ds(pl.multiple_of(core * 96, 16), 96), :]


def expert_piece(ref, kind, z, y, x, core):
    if kind == "wide":
        return ref.at[z, y, x, :, pl.ds(pl.multiple_of(core * 1536, 128), 1536)]
    return ref.at[z, y, x, pl.ds(pl.multiple_of(core * 96, 16), 96), :]


class ExpertGather:
    def __init__(self, place, kind, mine, out, sems):
        self.p, self.kind, self.mine, self.out, self.sems = place, kind, mine, out, sems

    def _cross(self, i):
        p, s = self.p, self.sems
        there = expert_piece(self.out, self.kind, p.z, p.y, p.x, p.core)
        device = (p.across_x, p.across_y, p.across_both)[i]
        expert = device // 2 % 4
        return remote(self.mine.at[expert], there, s["cs"].at[i], s["cr"].at[i], device)

    def _own(self):
        p = self.p
        there = expert_piece(self.out, self.kind, p.z, p.y, p.x, p.core)
        return pltpu.make_async_copy(self.mine.at[p.chip], there, self.sems["own"].at[0])

    def start_own(self):
        self._own().start()
        for i in range(3):
            self._cross(i).start()

    def _copy_z(self, y, source, up):
        p, s = self.p, self.sems
        slot = y * 4 + source
        block = expert_block(self.out, self.kind, source, y, p.core)
        return remote(block, block, s["zu" if up else "zd"].at[slot], s["zr"].at[slot],
                      p.me + 8 if up else p.me - 8)

    def _hand(self, y, source):
        p, s = self.p, self.sems
        slot = y * 4 + source
        block = expert_block(self.out, self.kind, source, y, p.core)
        return remote(block, block, s["hs"].at[slot], s["hr"].at[slot], p.sibling)

    def crossed(self):
        p = self.p
        self._own().wait()
        for i in range(3):
            self._cross(i).wait_recv()
        for y in range(2):
            pl.when(p.z < 3)(lambda: self._copy_z(y, p.z, True).start())
            pl.when(p.z > 0)(lambda: self._copy_z(y, p.z, False).start())
            self._hand(y, p.z).start()

    def stage(self, y, k):
        p = self.p
        source = p.z + k

        def run():
            self._copy_z(y, source, k < 0).wait_recv()
            if k < 0:
                pl.when(p.z < 3)(lambda: self._copy_z(y, source, True).start())
            else:
                pl.when(p.z > 0)(lambda: self._copy_z(y, source, False).start())
            self._hand(y, source).start()

        pl.when((source >= 0) & (source <= 3))(run)

    def arrived(self):
        for y in range(2):
            for source in range(4):
                self._hand(y, source).wait_recv()

    def finish(self):
        p = self.p
        for i in range(3):
            self._cross(i).wait_send()
        for y in range(2):
            for source in range(4):
                self._hand(y, source).wait_send()
                up = (source <= p.z) & (p.z < 3)
                down = (source >= p.z) & (p.z > 0)
                pl.when(up)(lambda: self._copy_z(y, source, True).wait_send())
                pl.when(down)(lambda: self._copy_z(y, source, False).wait_send())


EXPERT_SEMS = ("zu", "zd", "zr", "hs", "hr")
STEPS = (0, -1, 1, -2, 2, -3, 3)


def gather_kernel(
    small_in, wide_in, tall_in,
    small_out, wa0, wmi, wmo, wa1, ein, eout,
    wide_mine, expert_mine, from_sibling, meet, small_sems, gather_sems, own_sems, expert_sems,
    cross_sems,
):
    p = Place()
    greet_all(p, 32)
    swap = remote(wide_in.at[1 - p.core], from_sibling, meet.at[0], meet.at[1], p.sibling)
    swap.start()

    def spread(i):
        remote(small_in, small_out.at[p.me], small_sems.at[0, i], small_sems.at[1, p.me],
               (p.me + i) % 32).start()

    pl.loop(1, 32)(spread)
    small_out[p.me] = small_in[...]
    outs = (wa0, wmi, wmo, wa1)
    dense = []
    for m, kind in enumerate(DENSE):
        sems = {name: gather_sems.at[m, i] for i, name in enumerate(GATHER_SEMS)}
        sems["own"] = own_sems.at[m]
        mine = tall_in.at[0] if kind == "tall" else wide_mine.at[(0, 1, None, 2)[m]]
        dense.append(Gather(p, kind, mine, outs[m], sems))
    experts = []
    for m, kind in enumerate(("wide", "tall")):
        sems = {name: expert_sems.at[m, i] for i, name in enumerate(EXPERT_SEMS)}
        sems["cs"], sems["cr"], sems["own"] = (
            cross_sems.at[m, 0], cross_sems.at[m, 1], cross_sems.at[m, 2])
        mine = tall_in.at[pl.ds(1, 4)] if kind == "tall" else expert_mine
        experts.append(ExpertGather(p, kind, mine, (ein, eout)[m], sems))
    dense[2].start_own()
    experts[1].start_own()
    swap.wait_recv()

    def merge(m, out):
        cols = pl.ds(m * 1536, 1536)
        kept = wide_in[p.core, :, cols]
        came = from_sibling[:, cols]
        upper = jnp.where(p.core == 0, kept, came)
        lower = jnp.where(p.core == 0, came, kept)
        out[...] = jnp.concatenate([upper, lower], 0).astype(BF16)

    merge(0, wide_mine.at[0])
    dense[0].start_own()
    for e in range(4):
        merge(3 + e, expert_mine.at[e])
    experts[0].start_own()
    merge(1, wide_mine.at[1])
    dense[1].start_own()
    merge(2, wide_mine.at[2])
    dense[3].start_own()

    order = [(m, k, half) for m in (0, 1, 2, 3) for k in STEPS for half in range(2)]
    pumps = []
    for i in range(len(order) + 16):
        for stage, lag in ((0, 0), (1, 8), (2, 16)):
            if 0 <= i - lag < len(order):
                pumps.append((stage,) + order[i - lag])
    turns = [(y, k, m) for k in STEPS[1:] for m in (1, 0) for y in range(2)]
    at = {8 + j * (len(pumps) - 10) // len(turns): turn for j, turn in enumerate(turns)}
    for i, (stage, m, k, half) in enumerate(pumps):
        if i == 6:
            experts[1].crossed()
            experts[0].crossed()
        if i in at:
            y, kk, mm = at[i]
            experts[mm].stage(y, kk)
        job = dense[m]
        (job.stage_one, job.stage_two, job.stage_three)[stage](half, k)
    for job in dense + experts:
        job.arrived()
    for job in dense + experts:
        job.finish()
    swap.wait_send()

    def spread_done(i):
        remote(small_in, small_out.at[(p.me + i) % 32], small_sems.at[0, i],
               small_sems.at[1, (p.me + i) % 32], (p.me + i) % 32).wait()

    pl.loop(1, 32)(spread_done)


def run_gather(small, wide, tall):
    any_space = pl.BlockSpec(memory_space=pl.ANY)
    vmem = pl.BlockSpec(memory_space=pltpu.VMEM)
    wide_out = struct((4, 2, 2, 48, 3072), BF16)
    tall_out = struct((4, 2, 2, 192, 768), BF16)
    dma = pltpu.SemaphoreType.DMA
    return pl.pallas_call(
        gather_kernel,
        out_shape=[struct((32, 8, 128), F32), wide_out, wide_out, tall_out, wide_out,
                   wide_out, tall_out],
        in_specs=[vmem, vmem, vmem],
        out_specs=[vmem] + [any_space] * 6,
        scratch_shapes=[
            pltpu.VMEM((3, 48, 1536), BF16),
            pltpu.VMEM((4, 48, 1536), BF16),
            pltpu.VMEM((24, 7 * 1536), F32),
            dma((2,)),
            dma((2, 32)),
            dma((4, len(GATHER_SEMS), 8)),
            dma((4, 2)),
            dma((2, len(EXPERT_SEMS), 8)),
            dma((2, 3, 3)),
        ],
        compiler_params=pltpu.CompilerParams(
            collective_id=0, has_side_effects=True, vmem_limit_bytes=VMEM_BYTES),
        cost_estimate=pl.CostEstimate(flops=0, bytes_accessed=60_000_000, transcendentals=0),
    )(small, wide, tall)

KINDS = ("wide", "tall", "wide", "tall", "wide", "wide")
WIDE_AT = {2: 2, 4: 1, 5: 0}
LAG = 3
AHEAD = 4
PACE = ((0.65, 0), (0.65, 1.2), (0.65, 1.3), (2, 1))


def plane_part(ref, kind, z, core, half):
    if kind == "wide":
        return ref.at[z, :, :, :, pl.ds(pl.multiple_of(core * 1536 + half * 768, 128), 768)]
    return ref.at[z, :, :, pl.ds(pl.multiple_of(core * 96 + half * 48, 16), 48), :]


def add_into(kept, came, pieces):
    def body(i):
        a, b = kept(i), came(i)
        a[...] = a[...] + b[...]

    if pieces == 1:
        body(0)
    else:
        loop(pieces, body)


class Reduce:
    def __init__(self, place, m, ref, bufs, sems, sink):
        self.p, self.m, self.kind, self.ref = place, m, KINDS[m], ref
        self.bufs, self.sems, self.sink = bufs, sems, sink

    def goal(self, stop):
        z = self.p.z
        if stop == 3:
            return z
        table = ((3, 3, 0, 0), (2, 0, 3, 1), (1, 2, 1, 2))[stop]
        low = jnp.where(z == 0, table[0], table[1])
        return jnp.where(z < 2, low, jnp.where(z == 2, table[2], table[3]))

    def joins(self, stop):
        z = self.p.z
        return (z > 0) & (z < 3) if stop < 3 else z >= 0

    def _send_z(self, half, stop, src):
        p, s = self.p, self.sems
        z = self.goal(stop)
        up = z > p.z
        slot = jnp.where(up | (z != p.z - 1), z, 4)
        return remote(src, self.bufs["z"].at[half, slot], s["zs"].at[half, stop],
                      s["zr"].at[half, slot], jnp.where(up, p.me + 8, p.me - 8))

    def _came(self, half, src, slot):
        p, s = self.p, self.sems
        came = self.bufs["z"].at[half, slot]
        remote(src, came, s["zs"].at[half, 0], s["zr"].at[half, slot], p.sibling).wait_recv()
        return came


class DenseReduce(Reduce):
    def _plane(self, half, stop):
        return plane_part(self.ref, self.kind, self.goal(stop), self.p.core, half)

    def _block(self, half, stop):
        return self._plane(half, stop).at[self.p.y, self.p.x]

    def _pair(self, half, stop):
        p, s = self.p, self.sems
        src = plane_part(self.ref, self.kind, self.goal(stop), 1 - p.core, half)
        return remote(src, self.bufs["near"].at[stop, half], s["ps"].at[stop, half],
                      s["pr"].at[stop, half], p.sibling)

    def start(self):
        for unit in range(3):
            self._pair(unit % 2, unit // 2).start()

    def _first(self, half, stop):
        p, s = self.p, self.sems
        plane = self._plane(half, stop)
        src = plane.at[:, 1 - p.x] if half else plane.at[1 - p.y]
        return remote(src, self.bufs["first"].at[stop, half], s["fs"].at[stop, half],
                      s["fr"].at[stop, half], p.across_x if half else p.across_y)

    def _second(self, half, stop):
        p, s = self.p, self.sems
        plane = self._plane(half, stop)
        src = plane.at[1 - p.y, p.x] if half else plane.at[p.y, 1 - p.x]
        return remote(src, self.bufs["second"].at[stop, half], s["ss"].at[stop, half],
                      s["sr"].at[stop, half], p.across_y if half else p.across_x)

    def stage_one(self, half, stop):
        self._pair(half, stop).wait_recv()
        later = stop * 2 + half + 3
        if later < 8:
            self._pair(later % 2, later // 2).start()
        own, near = self._plane(half, stop), self.bufs["near"].at[stop, half]
        add_into(lambda i: own.at[i // 2, i % 2], lambda i: near.at[i // 2, i % 2], 4)
        self._first(half, stop).start()

    def stage_two(self, half, stop):
        p = self.p
        self._first(half, stop).wait_recv()
        own, came = self._plane(half, stop), self.bufs["first"].at[stop, half]
        if half:
            add_into(lambda i: own.at[i, p.x], lambda i: came.at[i], 2)
        else:
            add_into(lambda i: own.at[p.y, i], lambda i: came.at[i], 2)
        self._second(half, stop).start()

    def stage_three(self, half, stop):
        self._second(half, stop).wait_recv()
        kept, came = self._block(half, stop), self.bufs["second"].at[stop, half]
        add_into(lambda i: kept, lambda i: came, 1)

    def stage_four(self, half, stop):
        p = self.p
        block = self._block(half, stop)
        if stop < 3:

            def join():
                came = self._came(half, block, self.goal(stop))
                add_into(lambda i: block, lambda i: came, 1)

            pl.when(self.joins(stop))(join)
            self._send_z(half, stop, block).start()
            return
        out = self.sink(half)
        out[...] = block[...].astype(F32)

        def last(slot):
            out[...] += self._came(half, block, slot)[...].astype(F32)

        pl.when(p.z > 0)(lambda: last(p.z))
        pl.when(p.z < 3)(lambda: last(4))

    def z_events(self):
        return [functools.partial(self.stage_four, half, stop)
                for stop in range(4) for half in range(2)]

    def finish(self):
        for half in range(2):
            for stop in range(4):
                self._pair(half, stop).wait_send()
                self._first(half, stop).wait_send()
                self._second(half, stop).wait_send()
                if stop < 3:
                    self._send_z(half, stop, self._block(half, stop)).wait_send()


class ExpertReduce(Reduce):
    def _source(self, half, stop):
        return self.ref.at[self.goal(stop), half]

    def _load(self, half, stop):
        return pltpu.make_async_copy(
            self._source(half, stop), self.bufs["own"].at[half], self.sems["load"].at[half])

    def start_load(self, half, stop):
        pl.when(self.joins(stop))(lambda: self._load(half, stop).start())

    def begin(self):
        for half in range(2):
            self.start_load(half, 0)

    def plain_send(self, half, stop):
        p = self.p
        pl.when((p.z == 0) | (p.z == 3))(
            lambda: self._send_z(half, stop, self._source(half, stop)).start())

    def stage_one(self, half, stop):
        p = self.p
        own = self.bufs["own"].at[half]

        def join(slot, into_own):
            came = self._came(half, self._source(half, stop), slot)
            kept, added = (own, came) if into_own else (came, own)
            add_into(lambda i: kept.at[i // 2, i % 2], lambda i: added.at[i // 2, i % 2], 4)

        def middle():
            z = self.goal(stop)
            self._load(half, stop).wait()
            join(z, False)
            self._send_z(half, stop, self.bufs["z"].at[half, z]).start()

        if stop < 3:
            pl.when(self.joins(stop))(middle)
            self.start_load(half, stop + 1)
            return
        self._load(half, stop).wait()
        pl.when(p.z > 0)(lambda: join(p.z, True))
        pl.when(p.z < 3)(lambda: join(4, True))
        for i in range(3):
            self._cross(half, i).start()

    def _cross(self, half, i):
        p, s = self.p, self.sems
        device = (p.across_x, p.across_y, p.across_both)[i]
        chip = device // 2 % 4
        src = self.bufs["own"].at[half, chip // 2, chip % 2]
        return remote(src, self.bufs["cross"].at[half, i], s["cs"].at[half, i], s["cr"].at[half, i], device)

    def crossed(self, half):
        p = self.p
        self.sink(half, p.chip)[...] = self.bufs["own"][half, p.y, p.x].astype(F32)
        for i in range(3):
            self._cross(half, i).wait_recv()
            device = (p.across_x, p.across_y, p.across_both)[i]
            self.sink(half, device // 2 % 4)[...] = self.bufs["cross"][half, i].astype(F32)

    def finish(self):
        for half in range(2):
            for i in range(3):
                self._cross(half, i).wait_send()
            for stop in range(3):
                self._send_z(half, stop, self._source(half, stop)).wait_send()


class Pump:
    def __init__(self):
        self.queue, self.due = [], 0.0

    def add(self, events):
        self.queue += events

    def run(self, count):
        self.due = min(self.due + count, 8.0)
        while self.due >= 1 and self.step():
            self.due -= 1

    def step(self):
        if self.queue:
            self.queue.pop(0)()
            return True
        return False


class Belt(Pump):
    def __init__(self, lag, after):
        super().__init__()
        self.units, self.done, self.lag, self.after = [], [0, 0, 0, 0], lag, after

    def add(self, job):
        self.units += [(job, half, stop) for stop in range(4) for half in range(2)]

    def step(self):
        moved = False
        for stage in range(4):
            ahead = self.done[stage - 1] if stage else len(self.units)
            mine = self.done[stage]
            flush = ahead == len(self.units)
            if mine < ahead and (stage == 0 or flush or ahead - mine > self.lag):
                job, half, stop = self.units[mine]
                self.done[stage] += 1
                moved = True
                if stage < 3:
                    (job.stage_one, job.stage_two, job.stage_three)[stage](half, stop)
                else:
                    self.after(job, half, stop)
        return moved


def window(device):
    return jnp.minimum(device * 24 // 128, 4) * 128


def backward_step(
    images, seq,
    g_in, small, small_grad_in, x2, x1, x0, an1, qkv1, o1, mn, slope, ma, an0, qkv0, o0,
    wa1, wmo, wmi, wa0, sums,
    g_ref, small_out, wide_out, tall_out,
    xf, low, do, dqkv, dn, an_buf, mix_buf, ds,
    dw_wide, dw_tall, near, first, second, z_dense, own, z_expert, cross, done, small_got,
    load_sems, expert_load_sems, pair_sems, plane_sems, zs_sems, zr_sems, cross_sems, small_sems,
    meet, stream_sems, credit,
):
    p = Place()
    greet_all(p, 32)
    jobs = []
    sets = {2: 0, 3: 1, 4: 2, 5: 0}
    refs = {2: dw_wide.at[0], 3: dw_tall, 4: dw_wide.at[1], 5: dw_wide.at[2]}
    for m in range(6):
        sems = {"zs": zs_sems.at[m], "zr": zr_sems.at[m]}
        if m < 2:
            sems.update(cs=cross_sems.at[m, 0], cr=cross_sems.at[m, 1], load=expert_load_sems.at[m])
            bufs = {"z": z_expert.at[m], "cross": cross.at[m], "own": own.at[m]}
            if m == 0:
                def sink(half, e):
                    return done.at[3 + e, :, pl.ds(half * 768, 768)]
            else:
                def sink(half, e):
                    return tall_out.at[1 + e, pl.ds(half * 48, 48), :]
            jobs.append(ExpertReduce(p, m, sums.at[m], bufs, sems, sink))
            continue
        sems.update(ps=pair_sems.at[m - 2, 0], pr=pair_sems.at[m - 2, 1])
        for i, name in enumerate(("fs", "fr", "ss", "sr")):
            sems[name] = plane_sems.at[m - 2, i]
        s = sets[m]
        bufs = {"z": z_dense.at[m - 2], "first": first.at[s], "second": second.at[s], "near": near.at[s]}
        if m in WIDE_AT:
            def sink(half, m=m):
                return done.at[WIDE_AT[m], :, pl.ds(half * 768, 768)]
        else:
            def sink(half):
                return tall_out.at[0, pl.ds(half * 48, 48), :]
        jobs.append(DenseReduce(p, m, refs[m], bufs, sems, sink))
    for m in range(2):
        jobs[m].begin()

    experts = Pump()

    def along(job, half, stop):
        experts.add([functools.partial(job.stage_four, half, stop)])
        if job.m == 2 and (half, stop) == (1, 3):
            for device in (p.sibling, p.across_x, p.across_y):
                pl.semaphore_signal(credit, inc=1, device_id=(device,), device_id_type=MESH_ID)

    dense = Belt(LAG, along)
    units = [(m, half, stop) for stop in range(4) for m in range(2) for half in range(2)]

    def expert_event(i):
        if i + AHEAD < 12:
            m, half, stop = units[i + AHEAD]
            jobs[m].plain_send(half, stop)
        m, half, stop = units[i]
        jobs[m].stage_one(half, stop)

    for m, half, stop in units[:AHEAD]:
        jobs[m].plain_send(half, stop)
    experts.add([functools.partial(expert_event, i) for i in range(16)])
    experts.add([functools.partial(jobs[m].crossed, half) for m in range(2) for half in range(2)])

    def pump(e=1, d=0):
        experts.run(e)
        dense.run(d)

    def load(pairs, sems):
        copies = [pltpu.make_async_copy(src, dst, sems.at[i]) for i, (src, dst) in enumerate(pairs)]
        for copy in copies:
            copy.start()
        return copies

    def attention(w_src, x_src, an_src, qkv_src, o_src, dw, row, ready, pump):
        def scope(w_buf):
            qkv, o = mix_buf.at[:, pl.ds(0, 2304)], mix_buf.at[:, pl.ds(2304, 768)]
            x_to = xf if x_src.dtype == F32 else low
            copies = load([(x_src, x_to), (o_src, o), (an_src, an_buf), (qkv_src, qkv),
                           (w_src.reshape(WIDTH, HIDDEN), w_buf)], load_sems)
            for copy in copies[:2]:
                copy.wait()
            if x_src.dtype != F32:
                xf[...] = low[...].astype(F32)

            def weights_here():
                for copy in copies[2:]:
                    copy.wait()

            attention_backward(
                g_ref, xf, small[row : row + 1, :], w_buf, an_buf, qkv, o, dw, ds, row, images, seq,
                low, do, dqkv, dn, weights_here, ready, pump,
            )

        pl.run_scoped(scope, pltpu.VMEM((WIDTH, HIDDEN), BF16))

    g_ref[...] = g_in[...]
    ds[...] = small_grad_in[...]
    attention(wa1, x2, an1, qkv1, o1, dw_wide.at[0].reshape(WIDTH, HIDDEN), 1, jobs[2].start,
              lambda: pump(*PACE[0]))
    dense.add(jobs[2])

    def feed_forward(wo_buf, wi_buf, slope_buf, ma_buf):
        wo, wi = wmo.reshape(HIDDEN, WIDTH), wmi.reshape(WIDTH, HIDDEN)
        dwo, dwi = dw_tall.reshape(HIDDEN, WIDTH), dw_wide.at[1].reshape(WIDTH, HIDDEN)
        first_loads = load([(x1, xf), (mn, an_buf)], load_sems)

        def chunk(n):
            cols = pl.ds(n * 512, 512)
            slot = n % 2
            return load([(wo.at[cols, :], wo_buf.at[slot]), (wi.at[:, cols], wi_buf.at[slot]),
                         (slope.at[:, cols], slope_buf.at[slot]), (ma.at[:, cols], ma_buf.at[slot])],
                        stream_sems.at[slot])

        coming = chunk(0)
        low[...] = g_ref[...].astype(BF16)
        dn[...] = jnp.zeros_like(dn)
        for copy in first_loads:
            copy.wait()
        for n in range(6):
            for copy in coming:
                copy.wait()
            if n < 5:
                coming = chunk(n + 1)
            slot = n % 2
            cols = pl.ds(n * 512, 512)
            dwo[cols, :] = tn(ma_buf[slot], low[...]).astype(BF16)
            dact = nt(low[...], wo_buf[slot])
            dh = (slope_buf[slot].astype(F32) * dact).astype(BF16)
            dwi[:, cols] = tn(an_buf[...], dh).astype(BF16)
            dn[...] += nt(dh, wi_buf[slot])
            pump(*PACE[1])
        jobs[3].start()
        jobs[4].start()
        norm_back(x1_buf, small[2:3, :], dn, g_ref, ds, 2)

    x1_buf = xf
    rows = g_ref.shape[0]
    pl.run_scoped(
        feed_forward, pltpu.VMEM((2, 512, WIDTH), BF16), pltpu.VMEM((2, WIDTH, 512), BF16),
        pltpu.VMEM((2, rows, 512), BF16), pltpu.VMEM((2, rows, 512), BF16))
    dense.add(jobs[3])
    dense.add(jobs[4])

    def last_ready():
        assert dense.done[3] >= 8
        pl.semaphore_wait(credit, 3)
        jobs[5].start()

    attention(wa0, x0, an0, qkv0, o0, dw_wide.at[2].reshape(WIDTH, HIDDEN), 0, last_ready,
              lambda: pump(*PACE[2]))

    def small_copy(to, i, source):
        return remote(ds.at[:, pl.ds(pl.multiple_of(window(to), 128), 256)], small_got.at[source],
                      small_sems.at[0, i], small_sems.at[1, source], to)

    pl.loop(1, 32)(lambda i: small_copy((p.me + i) % 32, i, p.me).start())
    dense.add(jobs[5])
    while dense.done[3] < len(dense.units) or experts.queue:
        pump(*PACE[3])
    swap = remote(
        done.at[:, pl.ds(pl.multiple_of((1 - p.core) * 24, 8), 24), :], wide_out.at[p.core],
        meet.at[0], meet.at[1], p.sibling)
    swap.start()
    keep = pltpu.make_async_copy(
        done.at[:, pl.ds(pl.multiple_of(p.core * 24, 8), 24), :], wide_out.at[p.core], meet.at[2])
    keep.start()
    pl.loop(1, 32)(lambda i: small_copy((p.me + i) % 32, i, (p.me + i) % 32).wait())
    small_got[p.me] = ds[:, pl.ds(pl.multiple_of(window(p.me), 128), 256)]
    small_out[...] = jnp.sum(small_got[...], 0)
    for m in range(6):
        jobs[m].finish()
    keep.wait()
    swap.wait()


def run_backward_step(images, seq, args):
    any_space = pl.BlockSpec(memory_space=pl.ANY)
    vmem = pl.BlockSpec(memory_space=pltpu.VMEM)
    dma = pltpu.SemaphoreType.DMA
    piece = (48, 768)
    rows = args[0].shape[0]
    act, low = pltpu.VMEM((rows, WIDTH), F32), pltpu.VMEM((rows, WIDTH), BF16)
    return pl.pallas_call(
        functools.partial(backward_step, images, seq),
        out_shape=[struct((rows, WIDTH), F32), struct((8, 256), F32),
                   struct((2, 7, 24, 1536), F32), struct((5, 96, 768), F32)],
        in_specs=[vmem] * 3 + [any_space] * (len(args) - 3),
        out_specs=[vmem, vmem, any_space, vmem],
        scratch_shapes=[
            act, low, low, pltpu.VMEM((rows, 3 * WIDTH), BF16), act, low,
            pltpu.VMEM((rows, HIDDEN), BF16), pltpu.VMEM((8, WIDTH), F32),
            pltpu.VMEM((3, 4, 2, 2, 48, HIDDEN), BF16),
            pltpu.VMEM((4, 2, 2, 192, WIDTH), BF16),
            pltpu.VMEM((3, 4, 2, 2, 2) + piece, BF16),
            pltpu.VMEM((3, 4, 2, 2) + piece, BF16),
            pltpu.VMEM((3, 4, 2) + piece, BF16),
            pltpu.VMEM((4, 2, 5) + piece, BF16),
            pltpu.VMEM((2, 2, 2, 2) + piece, BF16),
            pltpu.VMEM((2, 2, 5, 2, 2) + piece, BF16),
            pltpu.VMEM((2, 2, 3) + piece, BF16),
            pltpu.VMEM((7, 48, 1536), F32),
            pltpu.VMEM((32, 8, 256), F32),
            dma((5,)),
            dma((2, 2)),
            dma((4, 2, 4, 2)),
            dma((4, 4, 4, 2)),
            dma((6, 2, 4)),
            dma((6, 2, 5)),
            dma((2, 2, 2, 3)),
            dma((2, 32)),
            dma((3,)),
            dma((2, 4)),
            pltpu.SemaphoreType.REGULAR,
        ],
        compiler_params=pltpu.CompilerParams(
            collective_id=1, has_side_effects=True, vmem_limit_bytes=63 << 20),
        cost_estimate=pl.CostEstimate(
            flops=20_000_000_000, bytes_accessed=60_000_000, transcendentals=0),
    )(*args)


def fast_backward(images, seq, x0, g4, small, weights, saved, y_back, d_back, sums):
    rows = x0.shape[0]
    act = struct((rows, WIDTH), F32)
    wa0, wmi, wmo, wa1 = weights
    x1, x2, x3, an0, qkv0, o0, mn, slope, ma, an1, qkv1, o1, en, aux, p0, p1 = saved
    x4, g, ds = call(
        combine_kernel, [act, act, struct((8, WIDTH), F32)], [pltpu.VMEM((rows, WIDTH), F32)],
        [g4, small, x3, en, aux, p0, p1, y_back, d_back], 3_000_000_000,
    )
    w = lambda g: g.reshape(4, 2, 2, 48, HIDDEN)
    t = lambda g: g.reshape(4, 2, 2, 192, WIDTH)
    g, dsmall, wide, tall = run_backward_step(images, seq, [
        g, small, ds, x2, x1, x0, an1, qkv1, o1, mn, slope, ma, an0, qkv0, o0,
        w(wa1), t(wmo), w(wmi), w(wa0), sums])
    me = lax.axis_index("fsdp")
    dsmall = lax.dynamic_slice(dsmall, (0, me * 24 - window(me)), (8, 24))
    wide = wide.transpose(1, 2, 0, 3).reshape(7, 24, HIDDEN)
    return x4, g, (dsmall.T, wide[0], wide[1], tall[0], wide[2],
                   wide[3:].transpose(1, 0, 2), tall[1:].transpose(1, 0, 2))


def expert_step(
    rows_x, rows_d, ein, eout,
    y_back, d_back, sums,
    wi, wo, got_x, got_d, active, slope, y_out, d_out, acc, dwi, dwo, near,
    load_sems, own_sems, move_sems, pair_sems, sum_sems,
):
    p = Place()
    greet_all(p, 32)
    chips = [device // 2 % 4 for device in (p.me, p.across_x, p.across_y, p.across_both)]
    devices = (None, p.across_x, p.across_y, p.across_both)
    loads = [pltpu.make_async_copy(src, dst, load_sems.at[i])
             for i, (src, dst) in enumerate(((ein, wi), (eout, wo)))]

    def inward(t, i):
        src, dst = ((rows_x, got_x), (rows_d, got_d))[t]
        if i == 0:
            return pltpu.make_async_copy(src.at[p.chip], dst.at[p.chip], own_sems.at[t])
        return remote(src.at[chips[i]], dst.at[p.chip], move_sems.at[t, 0, i], move_sems.at[t, 1, i],
                      devices[i])

    def outward(t, i):
        src, dst = ((y_out, y_back), (d_out, d_back))[t]
        if i == 0:
            return pltpu.make_async_copy(src.at[p.chip], dst.at[p.chip], own_sems.at[2 + t])
        return remote(src.at[chips[i]], dst.at[p.chip], move_sems.at[2 + t, 0, i],
                      move_sems.at[2 + t, 1, i], devices[i])

    for i in range(4):
        inward(0, i).start()
    for copy in loads:
        copy.start()
    inward(1, 0).start()
    for copy in loads:
        copy.wait()
    wide = wi.reshape(WIDTH, HIDDEN)
    tall = wo.reshape(HIDDEN, WIDTH)
    for i in range(4):
        chip = chips[i]
        if i == 0:
            inward(0, 0).wait()
        else:
            inward(0, i).wait_recv()
        if i == 1:
            for j in range(1, 4):
                inward(1, j).start()
        acc[...] = jnp.zeros_like(acc)

        def forward(n):
            cols = tile(n, 512)
            ea, sl = gelu_both(nn(got_x[chip], wide[:, cols]))
            ea = ea.astype(BF16)
            active[chip, :, cols] = ea
            slope[chip, :, cols] = sl.astype(BF16)
            acc[...] += nn(ea, tall[cols, :])

        loop(6, forward)
        y_out[chip] = acc[...].astype(BF16)
        outward(0, i).start()
    for i in range(4):
        chip = chips[i]
        if i == 0:
            inward(1, 0).wait()
        else:
            inward(1, i).wait_recv()
        acc[...] = jnp.zeros_like(acc)

        def backward(n):
            cols = tile(n, 512)
            dh = slope[chip, :, cols].astype(F32) * nt(got_d[chip], tall[cols, :])
            dh = dh.astype(BF16)
            slope[chip, :, cols] = dh
            acc[...] += nt(dh, wide[:, cols])

        loop(6, backward)
        d_out[chip] = acc[...].astype(BF16)
        outward(1, i).start()
    every = EXPERTS * SLOT
    x_all, d_all = got_x.reshape(every, WIDTH), got_d.reshape(every, WIDTH)
    ea_all, dh_all = active.reshape(every, HIDDEN), slope.reshape(every, HIDDEN)
    dwi_all, dwo_all = dwi.reshape(WIDTH, HIDDEN), dwo.reshape(HIDDEN, WIDTH)

    def weights(n):
        cols = tile(n, 512)
        dwo_all[cols, :] = tn(ea_all[:, cols], d_all[...]).astype(BF16)
        dwi_all[:, cols] = tn(x_all[...], dh_all[:, cols]).astype(BF16)

    loop(6, weights)
    pairs = [(m, z, half) for z in range(4) for m in range(2) for half in range(2)]

    def pair(m, z, half):
        src = plane_part((dwi, dwo)[m], KINDS[m], z, 1 - p.core, half)
        return remote(src, near.at[m, z, half], pair_sems.at[m, z, half, 0],
                      pair_sems.at[m, z, half, 1], p.sibling)

    def result(m, z, half):
        return pltpu.make_async_copy(near.at[m, z, half], sums.at[m, z, half], sum_sems.at[m, z, half])

    for one in pairs:
        pair(*one).start()
    for m, z, half in pairs:
        pair(m, z, half).wait_recv()
        own = plane_part((dwi, dwo)[m], KINDS[m], z, p.core, half)
        came = near.at[m, z, half]
        add_into(lambda i: came.at[i // 2, i % 2], lambda i: own.at[i // 2, i % 2], 4)
        result(m, z, half).start()
    for one in pairs:
        result(*one).wait()
        pair(*one).wait_send()
    for t in range(2):
        outward(t, 0).wait()
        for i in range(1, 4):
            inward(t, i).wait_send()
            outward(t, i).wait()


def run_expert_step(rows_x, rows_d, ein, eout):
    any_space = pl.BlockSpec(memory_space=pl.ANY)
    dma = pltpu.SemaphoreType.DMA
    rows = (EXPERTS, SLOT, WIDTH)
    y, d, sums = pl.pallas_call(
        expert_step,
        out_shape=[struct(rows, BF16)] * 2 + [struct((2, 4, 2, 2, 2, 48, 768), BF16)],
        in_specs=[any_space] * 4,
        out_specs=[any_space] * 3,
        scratch_shapes=[
            pltpu.VMEM((4, 2, 2, 48, HIDDEN), BF16),
            pltpu.VMEM((4, 2, 2, 192, WIDTH), BF16),
            pltpu.VMEM(rows, BF16),
            pltpu.VMEM(rows, BF16),
            pltpu.VMEM((EXPERTS, SLOT, HIDDEN), BF16),
            pltpu.VMEM((EXPERTS, SLOT, HIDDEN), BF16),
            pltpu.VMEM(rows, BF16),
            pltpu.VMEM(rows, BF16),
            pltpu.VMEM((SLOT, WIDTH), F32),
            pltpu.VMEM((4, 2, 2, 48, HIDDEN), BF16),
            pltpu.VMEM((4, 2, 2, 192, WIDTH), BF16),
            pltpu.VMEM((2, 4, 2, 2, 2, 48, 768), BF16),
            dma((2,)),
            dma((4,)),
            dma((4, 2, 4)),
            dma((2, 4, 2, 2)),
            dma((2, 4, 2)),
        ],
        compiler_params=pltpu.CompilerParams(
            collective_id=2, has_side_effects=True, vmem_limit_bytes=VMEM_BYTES),
        cost_estimate=pl.CostEstimate(
            flops=30_000_000_000, bytes_accessed=40_000_000, transcendentals=0),
    )(rows_x.reshape(rows), rows_d.reshape(rows), ein, eout)
    flat = (EXPERTS * SLOT, WIDTH)
    return y.reshape(flat), d.reshape(flat), sums


def fast_gather(smalls, wide, mlp_out, expert_in, expert_out):
    width = smalls.shape[0] * 32
    small = jnp.pad(smalls.astype(F32).T, ((0, 0), (0, 128 - smalls.shape[0])))
    packed = jnp.concatenate(wide + [expert_in[:, e] for e in range(EXPERTS)], 1).astype(F32)
    packed = packed.reshape(24, 7, 2, 1536).transpose(2, 0, 1, 3).reshape(2, 24, 7 * 1536)
    tall = jnp.concatenate([mlp_out[None], expert_out.transpose(1, 0, 2)], 0)
    small, wa0, wmi, wmo, wa1, ein, eout = run_gather(small, packed, tall)
    small = small[:, :, : smalls.shape[0]].transpose(1, 0, 2).reshape(8, width)
    flat = [w.reshape(width, HIDDEN) for w in (wa0, wmi, wa1)]
    return small, flat[:2] + [flat[2]], [wmo.reshape(HIDDEN, width)], ein, eout


def local(
    patches, live_count, expert_ids, attn_gain, attn_qkv, attn_out, mlp_gain, mlp_in, mlp_out,
    moe_gain, router, expert_in, expert_out, cotangent,
):
    images, seq, width = patches.shape
    padded = -(-seq // 16) * 16
    n = lax.axis_size("fsdp")
    group_size = n // EXPERTS
    group = lax.axis_index("fsdp") // group_size
    alive = jnp.arange(images, dtype=jnp.int32) < live_count[0]

    def pad(values, fill=0):
        values = values.reshape(images, seq, -1)
        values = jnp.pad(values, ((0, 0), (0, padded - seq), (0, 0)), constant_values=fill)
        return values.reshape(images * padded, -1)

    x0 = pad(patches)
    g4 = pad(jnp.where(alive[:, None, None], cotangent, jnp.zeros_like(cotangent)))
    ids = pad(expert_ids, -1)
    smalls = jnp.concatenate(
        [attn_gain, mlp_gain[:, None], moe_gain[:, None], router], 1
    )
    wide = [jnp.concatenate([attn_qkv[:, 0], attn_out[:, 0]], 1), mlp_in,
            jnp.concatenate([attn_qkv[:, 1], attn_out[:, 1]], 1)]
    if n == 32:
        small, wides, talls, w_in, w_out = fast_gather(smalls, wide, mlp_out, expert_in, expert_out)
    else:
        small, wides, talls, w_in, w_out = plain_gather(
            smalls, wide, [mlp_out], expert_in, expert_out)
        small = small.astype(F32).T
    small = jnp.concatenate(
        [small[:4], jnp.zeros((4, width), F32), small[4:], jnp.zeros((124, width), F32)], 0
    )
    weights = (wides[0], wides[1], talls[0], wides[2])
    out = run_forward(images, seq, x0, g4, ids, small, *weights)
    saved, rows_x, rows_d = out[:16], out[16], out[17]

    def exchange(rows):
        rows = rows.reshape(EXPERTS, SLOT, width)
        return group_exchange(rows, group_size, group).reshape(EXPERTS * SLOT, width)

    if n == 32:
        y_back, d_back, sums = run_expert_step(rows_x, rows_d, w_in, w_out)
        x4, grad, shards = fast_backward(
            images, seq, x0, g4, small, weights, saved, y_back, d_back, sums)
        dsmall, d0, dmi, dmo, d1, de_in, de_out = shards
    else:
        y, dx, dw_in, dw_out = run_expert(exchange(rows_x), exchange(rows_d), w_in, w_out)
        x4, grad, d0, dmi, dmo, d1, dsmall = run_backward(
            images, seq, x0, g4, small, weights, saved, exchange(y), exchange(dx)
        )
        d0, dmi, dmo, d1 = (plain_reduce(g).astype(F32) for g in (d0, dmi, dmo, d1))
        de_in, de_out = (plain_reduce_expert(g).astype(F32) for g in (dw_in, dw_out))
        dsmall = lax.psum_scatter(dsmall.T, "fsdp", scatter_dimension=0, tiled=True)

    def unpad(values):
        return values.reshape(images, padded, width)[:, :seq]

    block_out = jnp.where(alive[:, None, None], unpad(x4), 0.0).astype(BF16)
    return (
        block_out,
        unpad(grad),
        dsmall[:, 0:2],
        jnp.stack([d0[:, :2304], d1[:, :2304]], 1),
        jnp.stack([d0[:, 2304:], d1[:, 2304:]], 1),
        dsmall[:, 2],
        dmi,
        dmo,
        dsmall[:, 3],
        dsmall[:, 4:8],
        de_in,
        de_out,
    )


def solution(mesh):
    def lead(rank):
        return P("fsdp", *([None] * (rank - 1)))

    return jax.shard_map(
        local,
        mesh=mesh,
        in_specs=tuple(lead(r) for r in (3, 1, 2, 2, 3, 3, 1, 2, 2, 1, 2, 3, 3, 3)),
        out_specs=tuple(lead(r) for r in (3, 3, 2, 3, 3, 1, 2, 2, 1, 2, 3, 3)),
        check_vma=False,
    )
```

```python
import functools

import jax
import jax.numpy as jnp
from jax import lax
from jax.experimental import pallas as pl
from jax.experimental.pallas import tpu as pltpu
from jax.sharding import PartitionSpec as P

HEADS = 12
HEAD_DIM = 64
EXPERTS = 4
CAP = 247
SLOT = 256
WIDTH = 768
HIDDEN = 3072
NORM_EPSILON = 1e-06
VMEM_BYTES = 60 << 20
F32 = jnp.float32
BF16 = jnp.bfloat16


def nn(left, right):
    return lax.dot_general(left, right, (((1,), (0,)), ((), ())), preferred_element_type=F32)


def nt(left, right):
    return lax.dot_general(left, right, (((1,), (1,)), ((), ())), preferred_element_type=F32)


def tn(left, right):
    return lax.dot_general(left, right, (((0,), (0,)), ((), ())), preferred_element_type=F32)


def tile(index, size):
    return pl.ds(pl.multiple_of(index * size, size), size)


def loop(count, body):
    pl.loop(0, count)(body)


def norm_parts(values):
    center = values - jnp.mean(values, -1, keepdims=True)
    spread = jnp.mean(center * center, -1, keepdims=True)
    scale = lax.rsqrt(spread + NORM_EPSILON)
    return center * scale, scale


def norm_rows(x_ref, gain, out_ref, block=32):
    def body(i):
        rows = tile(i, block)
        unit, _ = norm_parts(x_ref[rows, :])
        out_ref[rows, :] = (unit * gain).astype(BF16)

    loop(x_ref.shape[0] // block, body)


def norm_back(x_ref, gain, dn_ref, g_ref, dgain_ref, row, block=32):
    def body(i, total):
        rows = tile(i, block)
        unit, scale = norm_parts(x_ref[rows, :])
        dn = dn_ref[rows, :]
        scaled = dn * gain
        mean_one = jnp.mean(scaled, -1, keepdims=True)
        mean_two = jnp.mean(scaled * unit, -1, keepdims=True)
        g_ref[rows, :] = g_ref[rows, :] + scale * (scaled - mean_one - unit * mean_two)
        return total + jnp.sum((dn * unit).reshape(block // 8, 8, WIDTH), 0)

    total = lax.fori_loop(0, x_ref.shape[0] // block, body, jnp.zeros((8, WIDTH), F32))
    dgain_ref[row : row + 1, :] = jnp.sum(total, 0, keepdims=True)


def gelu_both(u):
    c = 0.7978845608
    square = u * u
    t = jnp.tanh(c * u * (1.0 + 0.044715 * square))
    half = 0.5 * (1.0 + t)
    slope = half + 0.5 * u * (1.0 - t * t) * (c + (3 * 0.044715 * c) * square)
    return u * half, slope


def halves(shape):
    lane = lax.broadcasted_iota(jnp.int32, shape, 1)
    return lane < HEAD_DIM


def head_probs(q, k, seq):
    scores = nt(q, k) * HEAD_DIM ** (-0.5)
    key = lax.broadcasted_iota(jnp.int32, scores.shape, 1)
    scores = jnp.where(key < seq, scores, -1e30)
    top = jnp.max(scores, -1, keepdims=True)
    e = jnp.exp(scores - top)
    return e / jnp.sum(e, -1, keepdims=True)


def attention_heads(qkv_ref, o_ref, images, seq):
    rows_of = qkv_ref.shape[0] // images
    for image in range(images):
        rows = pl.ds(image * rows_of, rows_of)

        def pair(p, rows=rows):
            q = qkv_ref[rows, tile(p, 128)]
            k = qkv_ref[rows, tile(p + 6, 128)]
            v = qkv_ref[rows, tile(p + 12, 128)]
            first = halves(q.shape)
            zero = jnp.zeros_like(q)
            p0 = head_probs(jnp.where(first, q, zero), k, seq).astype(BF16)
            p1 = head_probs(jnp.where(first, zero, q), k, seq).astype(BF16)
            out = nn(p0, jnp.where(first, v, zero)) + nn(p1, jnp.where(first, zero, v))
            o_ref[rows, tile(p, 128)] = out.astype(BF16)

        loop(6, pair)


def attention_forward(x_ref, gain, w_ref, xo_ref, an_ref, qkv_ref, o_ref, images, seq):
    norm_rows(x_ref, gain, an_ref)

    def project(n):
        qkv_ref[:, tile(n, 256)] = nn(an_ref[...], w_ref[:, tile(n, 256)]).astype(BF16)

    loop(9, project)
    attention_heads(qkv_ref, o_ref, images, seq)

    def outward(n):
        cols = tile(n, 256)
        xo_ref[:, cols] = x_ref[:, cols] + nn(o_ref[...], w_ref[:, tile(n + 9, 256)])

    loop(3, outward)


def attention_backward(
    g_ref, x_ref, gain, w_ref, an_ref, qkv_ref, o_ref, dw_ref, dgain_ref, row, images, seq,
    low_ref, do_ref, dqkv_ref, dn_ref, weights_here=lambda: None, ready=lambda: None,
    pump=lambda: None,
):
    rows_of = qkv_ref.shape[0] // images
    low_ref[...] = g_ref[...].astype(BF16)

    def outward(n):
        dw_ref[:, tile(n + 9, 256)] = tn(o_ref[...], low_ref[:, tile(n, 256)]).astype(BF16)

    loop(3, outward)
    pump()
    weights_here()

    def outward_rows(n):
        do_ref[:, tile(n, 256)] = nt(low_ref[...], w_ref[tile(n, 256), 2304:]).astype(BF16)

    loop(3, outward_rows)
    pump()
    for image in range(images):
        rows = pl.ds(image * rows_of, rows_of)

        def pair(p, rows=rows):
            q = qkv_ref[rows, tile(p, 128)]
            k = qkv_ref[rows, tile(p + 6, 128)]
            v = qkv_ref[rows, tile(p + 12, 128)]
            d = do_ref[rows, tile(p, 128)]
            first = halves(q.shape)
            zero = jnp.zeros_like(q)
            dq = dk = dv = None
            for mine in (first, ~first):
                qm, km, dm = (jnp.where(mine, t, zero) for t in (q, k, d))
                probs = head_probs(qm, k, seq)
                dp = nt(dm, v)
                inner = jnp.sum(dp * probs, -1, keepdims=True)
                ds = (probs * (dp - inner)).astype(BF16)
                one = (nn(ds, km), tn(ds, qm), tn(probs.astype(BF16), dm))
                dq, dk, dv = one if dq is None else (dq + one[0], dk + one[1], dv + one[2])
            scale = HEAD_DIM ** (-0.5)
            dqkv_ref[rows, tile(p, 128)] = (dq * scale).astype(BF16)
            dqkv_ref[rows, tile(p + 6, 128)] = (dk * scale).astype(BF16)
            dqkv_ref[rows, tile(p + 12, 128)] = dv.astype(BF16)

        loop(3, pair)
        pump()
        loop(3, lambda p, pair=pair: pair(p + 3))
        pump()

    for third in range(3):

        def inward(n, third=third):
            cols = tile(n + third * 3, 256)
            dw_ref[:, cols] = tn(an_ref[...], dqkv_ref[:, cols]).astype(BF16)

        loop(3, inward)
        pump()
    ready()

    def normed(n):
        dn_ref[:, tile(n, 256)] = nt(dqkv_ref[...], w_ref[tile(n, 256), :2304])

    loop(3, normed)
    pump()
    norm_back(x_ref, gain, dn_ref, g_ref, dgain_ref, row)
    pump()


def route_rows(g4_ref, ids_ref, small_ref, en_ref, aux_ref, g0_ref, g1_ref, rx_ref, rd_ref, pump):
    rows = en_ref.shape[0]
    logits = nt(en_ref[...], small_ref[8:136, :].astype(BF16))
    lane = lax.broadcasted_iota(jnp.int32, logits.shape, 1)
    logits = jnp.where(lane < EXPERTS, logits, -1e30)
    e = jnp.exp(logits - jnp.max(logits, -1, keepdims=True))
    chances = e / jnp.sum(e, -1, keepdims=True)
    ids = ids_ref[...]
    chosen = [(ids[:, j : j + 1] == lane).astype(F32) for j in range(2)]
    row_i = lax.broadcasted_iota(jnp.int32, (rows, rows), 0)
    row_j = lax.broadcasted_iota(jnp.int32, (rows, rows), 1)
    earlier = nn((row_j < row_i).astype(BF16), (chosen[0] + chosen[1]).astype(BF16))
    place = lax.broadcasted_iota(jnp.int32, (rows, EXPERTS * SLOT), 1)
    gates = []
    for j, pick_ref in ((0, g0_ref), (1, g1_ref)):
        gates.append(jnp.sum(chances * chosen[j], -1, keepdims=True))
        inside = jnp.sum(earlier * chosen[j], -1, keepdims=True).astype(jnp.int32)
        slot = jnp.where(ids[:, j : j + 1] >= 0, ids[:, j : j + 1] * SLOT + inside, -1)
        pick_ref[...] = (slot == place).astype(BF16)
    aux = jnp.where(lane < EXPERTS, chances, 0.0)
    aux = jnp.where(lane == 8, gates[0], aux)
    aux_ref[...] = jnp.where(lane == 9, gates[1], aux)

    def fill(n):
        cols = tile(n, 256)
        both = g0_ref[:, cols] + g1_ref[:, cols]
        rx_ref[cols, :] = tn(both, en_ref[...]).astype(BF16)
        g4 = g4_ref[...].astype(F32)
        one = tn(g0_ref[:, cols], (g4 * gates[0]).astype(BF16))
        two = tn(g1_ref[:, cols], (g4 * gates[1]).astype(BF16))
        rd_ref[cols, :] = (one + two).astype(BF16)

    pump()
    loop(2, fill)
    pump()
    loop(2, lambda n: fill(n + 2))
    pump()


def forward_kernel(
    images, seq,
    x0_ref, g4_ref, ids_ref, small_ref, wa0_ref, wmi_ref, wmo_ref, wa1_ref,
    x1_ref, x2_ref, x3_ref, an0_ref, qkv0_ref, o0_ref, mn_ref, slope_ref, ma_ref,
    an1_ref, qkv1_ref, o1_ref, en_ref, aux_ref, g0_ref, g1_ref, rx_ref, rd_ref,
    xf_ref,
):
    xf_ref[...] = x0_ref[...].astype(F32)
    attention_forward(
        xf_ref, small_ref[0:1, :], wa0_ref, x1_ref, an0_ref, qkv0_ref, o0_ref, images, seq
    )
    norm_rows(x1_ref, small_ref[2:3, :], mn_ref)
    x2_ref[...] = x1_ref[...]

    def dense(n):
        cols = tile(n, 512)
        active, slope = gelu_both(nn(mn_ref[...], wmi_ref[:, cols]))
        slope_ref[:, cols] = slope.astype(BF16)
        active = active.astype(BF16)
        ma_ref[:, cols] = active
        x2_ref[...] += nn(active, wmo_ref[cols, :])

    loop(6, dense)
    attention_forward(
        x2_ref, small_ref[1:2, :], wa1_ref, x3_ref, an1_ref, qkv1_ref, o1_ref, images, seq
    )
    norm_rows(x3_ref, small_ref[3:4, :], en_ref)
    route_rows(
        g4_ref, ids_ref, small_ref, en_ref, aux_ref, g0_ref, g1_ref, rx_ref, rd_ref, lambda: None
    )


def expert_kernel(x_ref, d_ref, wi_ref, wo_ref, y_ref, dx_ref, dwi_ref, dwo_ref, yf_ref, df_ref):
    yf_ref[...] = jnp.zeros_like(yf_ref)
    df_ref[...] = jnp.zeros_like(df_ref)

    def body(n):
        cols = tile(n, 512)
        active, slope = gelu_both(nn(x_ref[...], wi_ref[:, cols]))
        active = active.astype(BF16)
        yf_ref[...] += nn(active, wo_ref[cols, :])
        dwo_ref[cols, :] = tn(active, d_ref[...]).astype(BF16)
        dh = (slope * nt(d_ref[...], wo_ref[cols, :])).astype(BF16)
        df_ref[...] += nt(dh, wi_ref[:, cols])
        dwi_ref[:, cols] = tn(x_ref[...], dh).astype(BF16)

    loop(6, body)
    y_ref[...] = yf_ref[...].astype(BF16)
    dx_ref[...] = df_ref[...].astype(BF16)


def combine_kernel(
    g4_ref, small_ref, x3_ref, en_ref, aux_ref, g0_ref, g1_ref, yr_ref, dr_ref,
    x4_ref, g_ref, ds_ref,
    dn_ref,
):
    aux = aux_ref[...]
    lane = lax.broadcasted_iota(jnp.int32, aux.shape, 1)
    g_ref[...] = g4_ref[...].astype(F32)
    x4_ref[...] = x3_ref[...]
    dgates = []
    chosen = []
    expert_of = lax.broadcasted_iota(jnp.int32, (EXPERTS * SLOT, 128), 0) // SLOT
    spread = (expert_of == lax.broadcasted_iota(jnp.int32, expert_of.shape, 1)).astype(BF16)
    for j, pick_ref in ((0, g0_ref), (1, g1_ref)):
        picked = nn(pick_ref[...], yr_ref[...])
        x4_ref[...] += aux[:, 8 + j : 9 + j] * picked
        dgates.append(jnp.sum(g_ref[...] * picked, -1, keepdims=True))
        chosen.append(nn(pick_ref[...], spread))
    dr = dgates[0] * chosen[0] + dgates[1] * chosen[1]
    chances = jnp.where(lane < EXPERTS, aux, 0.0)
    dlogits = chances * (dr - jnp.sum(chances * dr, -1, keepdims=True))
    dlogits = jnp.where(lane < EXPERTS, dlogits, 0.0).astype(BF16)
    ds_ref[...] = jnp.zeros_like(ds_ref)
    ds_ref[4:8, :] = tn(dlogits, en_ref[...])[0:4, :]
    dn_ref[...] = nn(dlogits, small_ref[8:136, :].astype(BF16)) + nn(
        g0_ref[...] + g1_ref[...], dr_ref[...]
    )
    norm_back(x3_ref, small_ref[3:4, :], dn_ref, g_ref, ds_ref, 3)


def attention_back_kernel(
    images, seq, row,
    g_in_ref, small_ref, x_ref, w_ref, an_ref, qkv_ref, o_ref,
    g_ref, dw_ref, ds_ref,
    xf_ref, low_ref, do_ref, dqkv_ref, dn_ref,
):
    g_ref[...] = g_in_ref[...]
    xf_ref[...] = x_ref[...].astype(F32)
    ds_ref[...] = jnp.zeros_like(ds_ref)
    attention_backward(
        g_ref, xf_ref, small_ref[row : row + 1, :], w_ref, an_ref, qkv_ref, o_ref, dw_ref,
        ds_ref, row, images, seq, low_ref, do_ref, dqkv_ref, dn_ref,
    )


def dense_back_kernel(
    g_in_ref, small_ref, x1_ref, wmi_ref, wmo_ref, mn_ref, slope_ref, ma_ref,
    g_ref, dwmi_ref, dwmo_ref, ds_ref,
    low_ref, dn_ref,
):
    g_ref[...] = g_in_ref[...]
    ds_ref[...] = jnp.zeros_like(ds_ref)
    low_ref[...] = g_ref[...].astype(BF16)
    dn_ref[...] = jnp.zeros_like(dn_ref)

    def dense(n):
        cols = tile(n, 512)
        dwmo_ref[cols, :] = tn(ma_ref[:, cols], low_ref[...]).astype(BF16)
        dact = nt(low_ref[...], wmo_ref[cols, :])
        dh = (slope_ref[:, cols].astype(F32) * dact).astype(BF16)
        dwmi_ref[:, cols] = tn(mn_ref[...], dh).astype(BF16)
        dn_ref[...] += nt(dh, wmi_ref[:, cols])

    loop(6, dense)
    norm_back(x1_ref, small_ref[2:3, :], dn_ref, g_ref, ds_ref, 2)


def struct(shape, dtype):
    return jax.ShapeDtypeStruct(shape, dtype)


def call(body, outs, scratch, args, flops):
    total = sum(a.size * a.dtype.itemsize for a in list(args) + list(outs))
    return pl.pallas_call(
        body,
        out_shape=outs,
        in_specs=[pl.BlockSpec(memory_space=pltpu.VMEM)] * len(args),
        out_specs=[pl.BlockSpec(memory_space=pltpu.VMEM)] * len(outs),
        scratch_shapes=scratch,
        compiler_params=pltpu.CompilerParams(vmem_limit_bytes=VMEM_BYTES),
        cost_estimate=pl.CostEstimate(flops=flops, bytes_accessed=total, transcendentals=0),
    )(*args)


def run_forward(images, seq, x0, g4, ids, small, wa0, wmi, wmo, wa1):
    rows = x0.shape[0]
    act = struct((rows, WIDTH), F32)
    low = struct((rows, WIDTH), BF16)
    qkv = struct((rows, 3 * WIDTH), BF16)
    hid = struct((rows, HIDDEN), BF16)
    pick = struct((rows, EXPERTS * SLOT), BF16)
    buf = struct((EXPERTS * SLOT, WIDTH), BF16)
    outs = [act, act, act, low, qkv, low, low, hid, hid, low, qkv, low, low,
            struct((rows, 128), F32), pick, pick, buf, buf]
    return call(
        functools.partial(forward_kernel, images, seq), outs,
        [pltpu.VMEM((rows, WIDTH), F32)],
        [x0, g4, ids, small, wa0, wmi, wmo, wa1], 8_000_000_000,
    )


def run_expert(x, d, wi, wo):
    outs = [struct(x.shape, BF16), struct(x.shape, BF16), struct(wi.shape, BF16), struct(wo.shape, BF16)]
    return call(
        expert_kernel, outs, [pltpu.VMEM(x.shape, F32), pltpu.VMEM(x.shape, F32)],
        [x, d, wi, wo], 30_000_000_000,
    )


def run_backward(images, seq, x0, g4, small, weights, saved, y_back, d_back):
    rows = x0.shape[0]
    act = struct((rows, WIDTH), F32)
    wide, tall = struct((WIDTH, HIDDEN), BF16), struct((HIDDEN, WIDTH), BF16)
    row = struct((8, WIDTH), F32)
    wa0, wmi, wmo, wa1 = weights
    x1, x2, x3, an0, qkv0, o0, mn, slope, ma, an1, qkv1, o1, en, aux, p0, p1 = saved
    full = pltpu.VMEM((rows, WIDTH), F32)
    low = pltpu.VMEM((rows, WIDTH), BF16)
    mixed = pltpu.VMEM((rows, 3 * WIDTH), BF16)
    x4, g, s0 = call(
        combine_kernel, [act, act, row], [full],
        [g4, small, x3, en, aux, p0, p1, y_back, d_back], 3_000_000_000,
    )
    g, dwa1, s1 = call(
        functools.partial(attention_back_kernel, images, seq, 1), [act, wide, row],
        [full, low, low, mixed, full], [g, small, x2, wa1, an1, qkv1, o1], 5_000_000_000,
    )
    g, dwmi, dwmo, s2 = call(
        dense_back_kernel, [act, wide, tall, row], [low, full],
        [g, small, x1, wmi, wmo, mn, slope, ma], 8_000_000_000,
    )
    g, dwa0, s3 = call(
        functools.partial(attention_back_kernel, images, seq, 0), [act, wide, row],
        [full, low, low, mixed, full], [g, small, x0, wa0, an0, qkv0, o0], 5_000_000_000,
    )
    return x4, g, dwa0, dwmi, dwmo, dwa1, s0 + s1 + s2 + s3


def gather_rows(piece):
    return lax.all_gather(piece, "fsdp", axis=0, tiled=True)


def shift(values, steps):
    count = lax.axis_size("fsdp")
    return lax.ppermute(values, "fsdp", [(s, (s + steps) % count) for s in range(count)])


def group_exchange(rows, group_size, group_id):
    out = jnp.zeros_like(rows)
    for offset in range(EXPERTS):
        piece = lax.dynamic_index_in_dim(rows, (group_id + offset) % EXPERTS, 0, keepdims=False)
        if offset:
            piece = shift(piece, offset * group_size)
        out = lax.dynamic_update_index_in_dim(out, piece, (group_id - offset) % EXPERTS, 0)
    return out


def plain_gather(smalls, wide, tall, e_in, e_out):
    n = lax.axis_size("fsdp")
    group_size = n // EXPERTS
    group = lax.axis_index("fsdp") // group_size
    small = gather_rows(smalls)
    wides = [gather_rows(w) for w in wide]
    talls = [gather_rows(w) for w in tall]
    big_in = lax.dynamic_index_in_dim(gather_rows(e_in), group, 1, keepdims=False)
    big_out = lax.dynamic_index_in_dim(gather_rows(e_out), group, 1, keepdims=False)
    return small, wides, talls, big_in, big_out


def plain_reduce(grad):
    return lax.psum_scatter(grad, "fsdp", scatter_dimension=0, tiled=True)


def plain_reduce_expert(grad):
    n = lax.axis_size("fsdp")
    group_size = n // EXPERTS
    group = lax.axis_index("fsdp") // group_size
    full = jnp.zeros((grad.shape[0], EXPERTS, grad.shape[1]), BF16)
    full = lax.dynamic_update_index_in_dim(full, grad, group, 1)
    return plain_reduce(full)

MESH_ID = pl.DeviceIdType.MESH


class Place:
    def __init__(self):
        self.me = lax.axis_index("fsdp")
        self.core = self.me % 2
        self.x = self.me // 2 % 2
        self.y = self.me // 4 % 2
        self.z = self.me // 8
        self.sibling = self.me + 1 - 2 * self.core
        self.across_x = self.me + 2 - 4 * self.x
        self.across_y = self.me + 4 - 8 * self.y
        self.across_both = self.across_x + 4 - 8 * self.y
        self.chip = self.me // 2 % 4


def remote(src, dst, send, recv, device):
    return pltpu.make_async_remote_copy(
        src_ref=src, dst_ref=dst, send_sem=send, recv_sem=recv,
        device_id=(device,), device_id_type=MESH_ID,
    )


def greet_all(place, count):
    barrier = pltpu.get_barrier_semaphore()

    def hello(i):
        pl.semaphore_signal(
            barrier, inc=1, device_id=((place.me + i) % count,), device_id_type=MESH_ID
        )

    pl.loop(1, count)(hello)
    pl.semaphore_wait(barrier, count - 1)


DENSE = ("wide", "wide", "tall", "wide")


def part(ref, kind, z, y, x, core, half):
    if kind == "wide":
        return ref.at[z, y, x, :, pl.ds(pl.multiple_of(core * 1536 + half * 768, 128), 768)]
    return ref.at[z, y, x, pl.ds(pl.multiple_of(core * 96 + half * 48, 16), 48), :]


def own_part(mine, kind, half):
    if kind == "wide":
        return mine.at[:, pl.ds(half * 768, 768)]
    return mine.at[pl.ds(half * 48, 48), :]


class Gather:
    def __init__(self, place, kind, mine, out, sems):
        self.p, self.kind, self.mine, self.out, self.sems = place, kind, mine, out, sems

    def _z(self, half, source, up):
        p = self.p
        where = part(self.out, self.kind, source, p.y, p.x, p.core, half)
        return where, 0 if up else 1

    def _slot(self, half, source):
        return half * 4 + source

    def start_own(self):
        p, s = self.p, self.sems
        for half in range(2):
            there = part(self.out, self.kind, p.z, p.y, p.x, p.core, half)
            src = own_part(self.mine, self.kind, half)
            pltpu.make_async_copy(src, there, s["own"].at[half]).start()
            self._along_z(half, p.z, src, True, True)

    def _copy_z(self, half, source, src, up):
        p, s = self.p, self.sems
        slot = self._slot(half, source)
        there = part(self.out, self.kind, source, p.y, p.x, p.core, half)
        name = "zu" if up else "zd"
        return remote(there if src is None else src, there, s[name].at[slot], s["zr"].at[slot],
                      p.me + 8 if up else p.me - 8)

    def _along_z(self, half, source, src, up, down):
        p = self.p
        if up:
            pl.when(p.z < 3)(lambda: self._copy_z(half, source, src, True).start())
        if down:
            pl.when(p.z > 0)(lambda: self._copy_z(half, source, src, False).start())

    def _first(self, half, source, src=None):
        p, s = self.p, self.sems
        slot = self._slot(half, source)
        there = part(self.out, self.kind, source, p.y, p.x, p.core, half)
        return remote(there if src is None else src, there, s["fs"].at[slot], s["fr"].at[slot],
                      p.across_y if half else p.across_x)

    def _line(self, half, source):
        p = self.p
        if self.kind == "wide":
            rows, cols = slice(None), pl.ds(pl.multiple_of(p.core * 1536 + half * 768, 128), 768)
        else:
            rows, cols = pl.ds(pl.multiple_of(p.core * 96 + half * 48, 16), 48), slice(None)
        if half:
            return self.out.at[source, :, p.x, rows, cols]
        return self.out.at[source, p.y, :, rows, cols]

    def _second(self, half, source):
        p, s = self.p, self.sems
        slot = self._slot(half, source)
        line = self._line(half, source)
        return remote(line, line, s["ss"].at[slot], s["sr"].at[slot],
                      p.across_x if half else p.across_y)

    def _hand(self, half, source):
        p, s = self.p, self.sems
        slot = self._slot(half, source)
        if self.kind == "wide":
            rows, cols = slice(None), pl.ds(pl.multiple_of(p.core * 1536 + half * 768, 128), 768)
        else:
            rows, cols = pl.ds(pl.multiple_of(p.core * 96 + half * 48, 16), 48), slice(None)
        plane = self.out.at[source, :, :, rows, cols]
        return remote(plane, plane, s["hs"].at[slot], s["hr"].at[slot], p.sibling)

    def valid(self, k):
        z = self.p.z + k
        return (z >= 0) & (z <= 3)

    def stage_one(self, half, k):
        source = self.p.z + k

        def run():
            if k == 0:
                src = own_part(self.mine, self.kind, half)
                self._first(half, source, src).start()
                there = part(self.out, self.kind, source, self.p.y, self.p.x, self.p.core, half)
                pltpu.make_async_copy(src, there, self.sems["own"].at[half]).wait()
                return
            self._copy_z(half, source, None, k < 0).wait_recv()
            self._along_z(half, source, None, k < 0, k > 0)
            self._first(half, source).start()

        pl.when(self.valid(k))(run)

    def stage_two(self, half, k):
        source = self.p.z + k

        def run():
            self._first(half, source).wait_recv()
            self._second(half, source).start()

        pl.when(self.valid(k))(run)

    def stage_three(self, half, k):
        source = self.p.z + k

        def run():
            self._second(half, source).wait_recv()
            self._hand(half, source).start()

        pl.when(self.valid(k))(run)

    def arrived(self):
        for half in range(2):
            for source in range(4):
                self._hand(half, source).wait_recv()

    def finish(self):
        p = self.p
        for half in range(2):
            for source in range(4):
                self._first(half, source).wait_send()
                self._second(half, source).wait_send()
                self._hand(half, source).wait_send()
                up = (source <= p.z) & (p.z < 3)
                down = (source >= p.z) & (p.z > 0)
                pl.when(up)(lambda: self._copy_z(half, source, None, True).wait_send())
                pl.when(down)(lambda: self._copy_z(half, source, None, False).wait_send())


GATHER_SEMS = ("zu", "zd", "zr", "fs", "fr", "ss", "sr", "hs", "hr")


def expert_block(ref, kind, z, y, core):
    if kind == "wide":
        return ref.at[z, y, :, :, pl.ds(pl.multiple_of(core * 1536, 128), 1536)]
    return ref.at[z, y, :, pl.ds(pl.multiple_of(core * 96, 16), 96), :]


def expert_piece(ref, kind, z, y, x, core):
    if kind == "wide":
        return ref.at[z, y, x, :, pl.ds(pl.multiple_of(core * 1536, 128), 1536)]
    return ref.at[z, y, x, pl.ds(pl.multiple_of(core * 96, 16), 96), :]


class ExpertGather:
    def __init__(self, place, kind, mine, out, sems):
        self.p, self.kind, self.mine, self.out, self.sems = place, kind, mine, out, sems

    def _cross(self, i):
        p, s = self.p, self.sems
        there = expert_piece(self.out, self.kind, p.z, p.y, p.x, p.core)
        device = (p.across_x, p.across_y, p.across_both)[i]
        expert = device // 2 % 4
        return remote(self.mine.at[expert], there, s["cs"].at[i], s["cr"].at[i], device)

    def _own(self):
        p = self.p
        there = expert_piece(self.out, self.kind, p.z, p.y, p.x, p.core)
        return pltpu.make_async_copy(self.mine.at[p.chip], there, self.sems["own"].at[0])

    def start_own(self):
        self._own().start()
        for i in range(3):
            self._cross(i).start()

    def _copy_z(self, y, source, up):
        p, s = self.p, self.sems
        slot = y * 4 + source
        block = expert_block(self.out, self.kind, source, y, p.core)
        return remote(block, block, s["zu" if up else "zd"].at[slot], s["zr"].at[slot],
                      p.me + 8 if up else p.me - 8)

    def _hand(self, y, source):
        p, s = self.p, self.sems
        slot = y * 4 + source
        block = expert_block(self.out, self.kind, source, y, p.core)
        return remote(block, block, s["hs"].at[slot], s["hr"].at[slot], p.sibling)

    def crossed(self):
        p = self.p
        self._own().wait()
        for i in range(3):
            self._cross(i).wait_recv()
        for y in range(2):
            pl.when(p.z < 3)(lambda: self._copy_z(y, p.z, True).start())
            pl.when(p.z > 0)(lambda: self._copy_z(y, p.z, False).start())
            self._hand(y, p.z).start()

    def stage(self, y, k):
        p = self.p
        source = p.z + k

        def run():
            self._copy_z(y, source, k < 0).wait_recv()
            if k < 0:
                pl.when(p.z < 3)(lambda: self._copy_z(y, source, True).start())
            else:
                pl.when(p.z > 0)(lambda: self._copy_z(y, source, False).start())
            self._hand(y, source).start()

        pl.when((source >= 0) & (source <= 3))(run)

    def arrived(self):
        for y in range(2):
            for source in range(4):
                self._hand(y, source).wait_recv()

    def finish(self):
        p = self.p
        for i in range(3):
            self._cross(i).wait_send()
        for y in range(2):
            for source in range(4):
                self._hand(y, source).wait_send()
                up = (source <= p.z) & (p.z < 3)
                down = (source >= p.z) & (p.z > 0)
                pl.when(up)(lambda: self._copy_z(y, source, True).wait_send())
                pl.when(down)(lambda: self._copy_z(y, source, False).wait_send())


EXPERT_SEMS = ("zu", "zd", "zr", "hs", "hr")
STEPS = (0, -1, 1, -2, 2, -3, 3)

FRONT = (0.05, (0.3, 4.7), (0.4, 7), (0.4, 14), 1)


def front_kernel(
    images, seq,
    small_in, wide_in, tall_in, x0_ref, g4_ref, ids_ref,
    small, wa0, wmi, wmo, wa1, ein, eout, *rest,
):
    outs, mine, tools = rest[:18], rest[18:36], rest[36:]
    (x1, x2, x3, an0, qkv0, o0, mn, slope, ma, an1, qkv1, o1, en, aux_ref, pick0, pick1, rx, rd) = mine
    (xf, va0, vmi, vmo, va1, wide_mine, expert_mine, from_sibling, small_got,
     meet, small_sems, gather_sems, own_sems, expert_sems, cross_sems, out_sems, weight_sems) = tools
    p = Place()
    greet_all(p, 32)
    swap = remote(wide_in.at[1 - p.core], from_sibling, meet.at[0], meet.at[1], p.sibling)
    swap.start()

    def small_copy(to, i, source):
        return remote(small_in, small_got.at[source], small_sems.at[0, i], small_sems.at[1, source], to)

    pl.loop(1, 32)(lambda i: small_copy((p.me + i) % 32, i, p.me).start())
    small_got[p.me] = small_in[...]
    landing, weights = (va0, vmi, vmo, va1), (wa0, wmi, wmo, wa1)
    jobs = []
    for m, kind in enumerate(DENSE):
        sems = {name: gather_sems.at[m, i] for i, name in enumerate(GATHER_SEMS)}
        sems["own"] = own_sems.at[m]
        piece = tall_in.at[0] if kind == "tall" else wide_mine.at[(0, 1, None, 2)[m]]
        jobs.append(Gather(p, kind, piece, landing[m], sems))
    big = []
    for m, kind in enumerate(("wide", "tall")):
        sems = {name: expert_sems.at[m, i] for i, name in enumerate(EXPERT_SEMS)}
        sems["cs"], sems["cr"], sems["own"] = (
            cross_sems.at[m, 0], cross_sems.at[m, 1], cross_sems.at[m, 2])
        piece = tall_in.at[pl.ds(1, 4)] if kind == "tall" else expert_mine
        big.append(ExpertGather(p, kind, piece, (ein, eout)[m], sems))
    jobs[2].start_own()
    swap.wait_recv()

    def merge(m, out):
        cols = pl.ds(m * 1536, 1536)
        kept = wide_in[p.core, :, cols]
        came = from_sibling[:, cols]
        upper = jnp.where(p.core == 0, kept, came)
        lower = jnp.where(p.core == 0, came, kept)
        out[...] = jnp.concatenate([upper, lower], 0).astype(BF16)

    merge(0, wide_mine.at[0])
    jobs[0].start_own()
    big[1].start_own()
    for e in range(4):
        merge(3 + e, expert_mine.at[e])
    big[0].start_own()
    merge(1, wide_mine.at[1])
    jobs[1].start_own()
    merge(2, wide_mine.at[2])
    jobs[3].start_own()

    dense, experts = Pump(), Pump()
    order = [(m, k, half) for m in range(4) for k in STEPS for half in range(2)]
    done_at = {}
    for i in range(len(order) + 24):
        for stage, lag in ((0, 0), (1, 12), (2, 24)):
            if 0 <= i - lag < len(order):
                m, k, half = order[i - lag]
                name = ("stage_one", "stage_two", "stage_three")[stage]
                dense.add([functools.partial(getattr(jobs[m], name), half, k)])
                if stage == 2:
                    done_at[m] = len(dense.queue)
    total = len(dense.queue)

    def crossed():
        big[1].crossed()
        big[0].crossed()

    experts.add([crossed])
    experts.add([functools.partial(big[m].stage, y, k) for k in STEPS[1:] for m in (1, 0) for y in range(2)])

    def pump(pace=(0, 0)):
        experts.run(pace[0])
        dense.run(pace[1])

    def arrive(m):
        while total - len(dense.queue) < done_at[m]:
            pump((FRONT[0], 1))
        jobs[m].arrived()
        pltpu.make_async_copy(landing[m], weights[m], weight_sems.at[m]).start()

    copies = []

    def emit(i):
        copy = pltpu.make_async_copy(mine[i], outs[i], out_sems.at[i])
        copy.start()
        copies.append(copy)

    def attention(x, row, w_ref, xo, an, qkv, o, pace):
        norm_rows(x, small[row : row + 1, :], an)
        pump(pace)
        for third in range(3):

            def project(n, third=third):
                cols = tile(n + third * 3, 256)
                qkv[:, cols] = nn(an[...], w_ref[:, cols]).astype(BF16)

            loop(3, project)
            pump(pace)
        rows_of = qkv.shape[0] // images
        for image in range(images):
            rows = pl.ds(image * rows_of, rows_of)

            def pair(i, rows=rows):
                q = qkv[rows, tile(i, 128)]
                k = qkv[rows, tile(i + 6, 128)]
                v = qkv[rows, tile(i + 12, 128)]
                first = halves(q.shape)
                zero = jnp.zeros_like(q)
                p0 = head_probs(jnp.where(first, q, zero), k, seq).astype(BF16)
                p1 = head_probs(jnp.where(first, zero, q), k, seq).astype(BF16)
                out = nn(p0, jnp.where(first, v, zero)) + nn(p1, jnp.where(first, zero, v))
                o[rows, tile(i, 128)] = out.astype(BF16)

            for part in range(2):
                loop(3, lambda i, pair=pair, part=part: pair(i + 3 * part))
                pump(pace)

        def outward(n):
            cols = tile(n, 256)
            xo[:, cols] = x[:, cols] + nn(o[...], w_ref[:, tile(n + 9, 256)])

        loop(3, outward)
        pump(pace)

    xf[...] = x0_ref[...].astype(F32)
    arrive(0)
    pl.loop(1, 32)(lambda i: small_copy((p.me + i) % 32, i, (p.me + i) % 32).wait())
    small[...] = jnp.zeros_like(small)
    for d in range(32):
        lanes = slice(24 * d, 24 * d + 24)
        small[0:4, lanes] = small_got[d, 0:4, 0:24]
        small[8:12, lanes] = small_got[d, 4:8, 0:24]
    attention(xf, 0, va0.reshape(WIDTH, HIDDEN), x1, an0, qkv0, o0, FRONT[1])
    for i in (0, 3, 4, 5):
        emit(i)
    norm_rows(x1, small[2:3, :], mn)
    emit(6)
    arrive(1)
    wi = vmi.reshape(WIDTH, HIDDEN)
    for n in range(6):
        cols = pl.ds(n * 512, 512)
        active, bend = gelu_both(nn(mn[...], wi[:, cols]))
        slope[:, cols] = bend.astype(BF16)
        ma[:, cols] = active.astype(BF16)
        pump(FRONT[2])
    emit(7)
    emit(8)
    arrive(2)
    wo = vmo.reshape(HIDDEN, WIDTH)
    for n in range(3):
        cols = pl.ds(n * 256, 256)
        x2[:, cols] = x1[:, cols] + nn(ma[...], wo[:, cols])
        pump(FRONT[3])
    emit(1)
    arrive(3)
    attention(x2, 1, va1.reshape(WIDTH, HIDDEN), x3, an1, qkv1, o1, (FRONT[4], 0))
    for i in (2, 9, 10, 11):
        emit(i)
    norm_rows(x3, small[3:4, :], en)
    route_rows(g4_ref, ids_ref, small, en, aux_ref, pick0, pick1, rx, rd, lambda: pump((FRONT[4], 0)))
    for i in range(12, 18):
        emit(i)
    while experts.step():
        pass
    for job in big:
        job.arrived()
    for job in jobs + big:
        job.finish()
    swap.wait_send()
    for m in range(4):
        pltpu.make_async_copy(landing[m], weights[m], weight_sems.at[m]).wait()
    for copy in copies:
        copy.wait()


def run_front(images, seq, small, wide, tall, x0, g4, ids):
    any_space = pl.BlockSpec(memory_space=pl.ANY)
    vmem = pl.BlockSpec(memory_space=pltpu.VMEM)
    wide_out = struct((4, 2, 2, 48, HIDDEN), BF16)
    tall_out = struct((4, 2, 2, 192, WIDTH), BF16)
    dma = pltpu.SemaphoreType.DMA
    rows = x0.shape[0]
    act, low = struct((rows, WIDTH), F32), struct((rows, WIDTH), BF16)
    qkv, hid = struct((rows, 3 * WIDTH), BF16), struct((rows, HIDDEN), BF16)
    pick, buf = struct((rows, EXPERTS * SLOT), BF16), struct((EXPERTS * SLOT, WIDTH), BF16)
    kept = [act, act, act, low, qkv, low, low, hid, hid, low, qkv, low, low,
            struct((rows, 128), F32), pick, pick, buf, buf]

    def scratch(one):
        return pltpu.VMEM(one.shape, one.dtype)

    return pl.pallas_call(
        functools.partial(front_kernel, images, seq),
        out_shape=[struct((136, WIDTH), F32), wide_out, wide_out, tall_out, wide_out, wide_out,
                   tall_out] + kept,
        in_specs=[vmem] * 6,
        out_specs=[vmem] + [any_space] * 24,
        scratch_shapes=[scratch(one) for one in kept] + [
            scratch(act), scratch(wide_out), scratch(wide_out), scratch(tall_out), scratch(wide_out),
            pltpu.VMEM((3, 48, 1536), BF16),
            pltpu.VMEM((4, 48, 1536), BF16),
            pltpu.VMEM((24, 7 * 1536), F32),
            pltpu.VMEM((32, 8, 128), F32),
            dma((2,)),
            dma((2, 32)),
            dma((4, len(GATHER_SEMS), 8)),
            dma((4, 2)),
            dma((2, len(EXPERT_SEMS), 8)),
            dma((2, 3, 3)),
            dma((18,)),
            dma((4,)),
        ],
        compiler_params=pltpu.CompilerParams(
            collective_id=0, has_side_effects=True, vmem_limit_bytes=63 << 20),
        cost_estimate=pl.CostEstimate(
            flops=9_000_000_000, bytes_accessed=60_000_000, transcendentals=0),
    )(small, wide, tall, x0, g4, ids)


def fast_front(images, seq, smalls, wide, mlp_out, expert_in, expert_out, x0, g4, ids):
    small = jnp.pad(smalls.astype(F32).T, ((0, 0), (0, 128 - smalls.shape[0])))
    packed = jnp.concatenate(wide + [expert_in[:, e] for e in range(EXPERTS)], 1).astype(F32)
    packed = packed.reshape(24, 7, 2, 1536).transpose(2, 0, 1, 3).reshape(2, 24, 7 * 1536)
    tall = jnp.concatenate([mlp_out[None], expert_out.transpose(1, 0, 2)], 0)
    out = run_front(images, seq, small, packed, tall, x0, g4, ids)
    small, wa0, wmi, wmo, wa1, ein, eout = out[:7]
    return small, (wa0, wmi, wmo, wa1), ein, eout, out[7:23], out[23], out[24]

KINDS = ("wide", "tall", "wide", "tall", "wide", "wide")
WIDE_AT = {2: 2, 4: 1, 5: 0}
LAG = 3
AHEAD = 4
PACE = ((0.65, 0), (0.65, 1.2), (0.65, 1.3), (2, 1))


def plane_part(ref, kind, z, core, half):
    if kind == "wide":
        return ref.at[z, :, :, :, pl.ds(pl.multiple_of(core * 1536 + half * 768, 128), 768)]
    return ref.at[z, :, :, pl.ds(pl.multiple_of(core * 96 + half * 48, 16), 48), :]


def add_into(kept, came, pieces):
    def body(i):
        a, b = kept(i), came(i)
        a[...] = a[...] + b[...]

    if pieces == 1:
        body(0)
    else:
        loop(pieces, body)


class Reduce:
    def __init__(self, place, m, ref, bufs, sems, sink):
        self.p, self.m, self.kind, self.ref = place, m, KINDS[m], ref
        self.bufs, self.sems, self.sink = bufs, sems, sink

    def goal(self, stop):
        z = self.p.z
        if stop == 3:
            return z
        table = ((3, 3, 0, 0), (2, 0, 3, 1), (1, 2, 1, 2))[stop]
        low = jnp.where(z == 0, table[0], table[1])
        return jnp.where(z < 2, low, jnp.where(z == 2, table[2], table[3]))

    def joins(self, stop):
        z = self.p.z
        return (z > 0) & (z < 3) if stop < 3 else z >= 0

    def _send_z(self, half, stop, src):
        p, s = self.p, self.sems
        z = self.goal(stop)
        up = z > p.z
        slot = jnp.where(up | (z != p.z - 1), z, 4)
        return remote(src, self.bufs["z"].at[half, slot], s["zs"].at[half, stop],
                      s["zr"].at[half, slot], jnp.where(up, p.me + 8, p.me - 8))

    def _came(self, half, src, slot):
        p, s = self.p, self.sems
        came = self.bufs["z"].at[half, slot]
        remote(src, came, s["zs"].at[half, 0], s["zr"].at[half, slot], p.sibling).wait_recv()
        return came


class DenseReduce(Reduce):
    def _plane(self, half, stop):
        return plane_part(self.ref, self.kind, self.goal(stop), self.p.core, half)

    def _block(self, half, stop):
        return self._plane(half, stop).at[self.p.y, self.p.x]

    def _pair(self, half, stop):
        p, s = self.p, self.sems
        src = plane_part(self.ref, self.kind, self.goal(stop), 1 - p.core, half)
        return remote(src, self.bufs["near"].at[stop, half], s["ps"].at[stop, half],
                      s["pr"].at[stop, half], p.sibling)

    def start(self):
        for unit in range(3):
            self._pair(unit % 2, unit // 2).start()

    def _first(self, half, stop):
        p, s = self.p, self.sems
        plane = self._plane(half, stop)
        src = plane.at[:, 1 - p.x] if half else plane.at[1 - p.y]
        return remote(src, self.bufs["first"].at[stop, half], s["fs"].at[stop, half],
                      s["fr"].at[stop, half], p.across_x if half else p.across_y)

    def _second(self, half, stop):
        p, s = self.p, self.sems
        plane = self._plane(half, stop)
        src = plane.at[1 - p.y, p.x] if half else plane.at[p.y, 1 - p.x]
        return remote(src, self.bufs["second"].at[stop, half], s["ss"].at[stop, half],
                      s["sr"].at[stop, half], p.across_y if half else p.across_x)

    def stage_one(self, half, stop):
        self._pair(half, stop).wait_recv()
        later = stop * 2 + half + 3
        if later < 8:
            self._pair(later % 2, later // 2).start()
        own, near = self._plane(half, stop), self.bufs["near"].at[stop, half]
        add_into(lambda i: own.at[i // 2, i % 2], lambda i: near.at[i // 2, i % 2], 4)
        self._first(half, stop).start()

    def stage_two(self, half, stop):
        p = self.p
        self._first(half, stop).wait_recv()
        own, came = self._plane(half, stop), self.bufs["first"].at[stop, half]
        if half:
            add_into(lambda i: own.at[i, p.x], lambda i: came.at[i], 2)
        else:
            add_into(lambda i: own.at[p.y, i], lambda i: came.at[i], 2)
        self._second(half, stop).start()

    def stage_three(self, half, stop):
        self._second(half, stop).wait_recv()
        kept, came = self._block(half, stop), self.bufs["second"].at[stop, half]
        add_into(lambda i: kept, lambda i: came, 1)

    def stage_four(self, half, stop):
        p = self.p
        block = self._block(half, stop)
        if stop < 3:

            def join():
                came = self._came(half, block, self.goal(stop))
                add_into(lambda i: block, lambda i: came, 1)

            pl.when(self.joins(stop))(join)
            self._send_z(half, stop, block).start()
            return
        out = self.sink(half)
        out[...] = block[...].astype(F32)

        def last(slot):
            out[...] += self._came(half, block, slot)[...].astype(F32)

        pl.when(p.z > 0)(lambda: last(p.z))
        pl.when(p.z < 3)(lambda: last(4))

    def z_events(self):
        return [functools.partial(self.stage_four, half, stop)
                for stop in range(4) for half in range(2)]

    def finish(self):
        for half in range(2):
            for stop in range(4):
                self._pair(half, stop).wait_send()
                self._first(half, stop).wait_send()
                self._second(half, stop).wait_send()
                if stop < 3:
                    self._send_z(half, stop, self._block(half, stop)).wait_send()


class ExpertReduce(Reduce):
    def _source(self, half, stop):
        return self.ref.at[self.goal(stop), half]

    def _load(self, half, stop):
        return pltpu.make_async_copy(
            self._source(half, stop), self.bufs["own"].at[half], self.sems["load"].at[half])

    def start_load(self, half, stop):
        pl.when(self.joins(stop))(lambda: self._load(half, stop).start())

    def begin(self):
        for half in range(2):
            self.start_load(half, 0)

    def plain_send(self, half, stop):
        p = self.p
        pl.when((p.z == 0) | (p.z == 3))(
            lambda: self._send_z(half, stop, self._source(half, stop)).start())

    def stage_one(self, half, stop):
        p = self.p
        own = self.bufs["own"].at[half]

        def join(slot, into_own):
            came = self._came(half, self._source(half, stop), slot)
            kept, added = (own, came) if into_own else (came, own)
            add_into(lambda i: kept.at[i // 2, i % 2], lambda i: added.at[i // 2, i % 2], 4)

        def middle():
            z = self.goal(stop)
            self._load(half, stop).wait()
            join(z, False)
            self._send_z(half, stop, self.bufs["z"].at[half, z]).start()

        if stop < 3:
            pl.when(self.joins(stop))(middle)
            self.start_load(half, stop + 1)
            return
        self._load(half, stop).wait()
        pl.when(p.z > 0)(lambda: join(p.z, True))
        pl.when(p.z < 3)(lambda: join(4, True))
        for i in range(3):
            self._cross(half, i).start()

    def _cross(self, half, i):
        p, s = self.p, self.sems
        device = (p.across_x, p.across_y, p.across_both)[i]
        chip = device // 2 % 4
        src = self.bufs["own"].at[half, chip // 2, chip % 2]
        return remote(src, self.bufs["cross"].at[half, i], s["cs"].at[half, i], s["cr"].at[half, i], device)

    def crossed(self, half):
        p = self.p
        self.sink(half, p.chip)[...] = self.bufs["own"][half, p.y, p.x].astype(F32)
        for i in range(3):
            self._cross(half, i).wait_recv()
            device = (p.across_x, p.across_y, p.across_both)[i]
            self.sink(half, device // 2 % 4)[...] = self.bufs["cross"][half, i].astype(F32)

    def finish(self):
        for half in range(2):
            for i in range(3):
                self._cross(half, i).wait_send()
            for stop in range(3):
                self._send_z(half, stop, self._source(half, stop)).wait_send()


class Pump:
    def __init__(self):
        self.queue, self.due = [], 0.0

    def add(self, events):
        self.queue += events

    def run(self, count):
        self.due = min(self.due + count, count + 4.0)
        while self.due >= 1 and self.step():
            self.due -= 1

    def step(self):
        if self.queue:
            self.queue.pop(0)()
            return True
        return False


class Belt(Pump):
    def __init__(self, lag, after):
        super().__init__()
        self.units, self.done, self.lag, self.after = [], [0, 0, 0, 0], lag, after

    def add(self, job):
        self.units += [(job, half, stop) for stop in range(4) for half in range(2)]

    def step(self):
        moved = False
        for stage in range(4):
            ahead = self.done[stage - 1] if stage else len(self.units)
            mine = self.done[stage]
            flush = ahead == len(self.units)
            if mine < ahead and (stage == 0 or flush or ahead - mine > self.lag):
                job, half, stop = self.units[mine]
                self.done[stage] += 1
                moved = True
                if stage < 3:
                    (job.stage_one, job.stage_two, job.stage_three)[stage](half, stop)
                else:
                    self.after(job, half, stop)
        return moved


def window(device):
    return jnp.minimum(device * 24 // 128, 4) * 128


def backward_step(
    images, seq,
    g_in, small, small_grad_in, x2, x1, x0, an1, qkv1, o1, mn, slope, ma, an0, qkv0, o0,
    wa1, wmo, wmi, wa0, sums,
    g_ref, small_out, wide_out, tall_out,
    xf, low, do, dqkv, dn, an_buf, mix_buf, ds,
    dw_wide, dw_tall, near, first, second, z_dense, own, z_expert, cross, done, small_got,
    load_sems, expert_load_sems, pair_sems, plane_sems, zs_sems, zr_sems, cross_sems, small_sems,
    meet, stream_sems, credit,
):
    p = Place()
    greet_all(p, 32)
    jobs = []
    sets = {2: 0, 3: 1, 4: 2, 5: 0}
    refs = {2: dw_wide.at[0], 3: dw_tall, 4: dw_wide.at[1], 5: dw_wide.at[2]}
    for m in range(6):
        sems = {"zs": zs_sems.at[m], "zr": zr_sems.at[m]}
        if m < 2:
            sems.update(cs=cross_sems.at[m, 0], cr=cross_sems.at[m, 1], load=expert_load_sems.at[m])
            bufs = {"z": z_expert.at[m], "cross": cross.at[m], "own": own.at[m]}
            if m == 0:
                def sink(half, e):
                    return done.at[3 + e, :, pl.ds(half * 768, 768)]
            else:
                def sink(half, e):
                    return tall_out.at[1 + e, pl.ds(half * 48, 48), :]
            jobs.append(ExpertReduce(p, m, sums.at[m], bufs, sems, sink))
            continue
        sems.update(ps=pair_sems.at[m - 2, 0], pr=pair_sems.at[m - 2, 1])
        for i, name in enumerate(("fs", "fr", "ss", "sr")):
            sems[name] = plane_sems.at[m - 2, i]
        s = sets[m]
        bufs = {"z": z_dense.at[m - 2], "first": first.at[s], "second": second.at[s], "near": near.at[s]}
        if m in WIDE_AT:
            def sink(half, m=m):
                return done.at[WIDE_AT[m], :, pl.ds(half * 768, 768)]
        else:
            def sink(half):
                return tall_out.at[0, pl.ds(half * 48, 48), :]
        jobs.append(DenseReduce(p, m, refs[m], bufs, sems, sink))
    for m in range(2):
        jobs[m].begin()

    experts = Pump()

    def along(job, half, stop):
        experts.add([functools.partial(job.stage_four, half, stop)])
        if job.m == 2 and (half, stop) == (1, 3):
            for device in (p.sibling, p.across_x, p.across_y):
                pl.semaphore_signal(credit, inc=1, device_id=(device,), device_id_type=MESH_ID)

    dense = Belt(LAG, along)
    units = [(m, half, stop) for stop in range(4) for m in range(2) for half in range(2)]

    def expert_event(i):
        if i + AHEAD < 12:
            m, half, stop = units[i + AHEAD]
            jobs[m].plain_send(half, stop)
        m, half, stop = units[i]
        jobs[m].stage_one(half, stop)

    for m, half, stop in units[:AHEAD]:
        jobs[m].plain_send(half, stop)
    experts.add([functools.partial(expert_event, i) for i in range(16)])
    experts.add([functools.partial(jobs[m].crossed, half) for m in range(2) for half in range(2)])

    def pump(e=1, d=0):
        experts.run(e)
        dense.run(d)

    def load(pairs, sems):
        copies = [pltpu.make_async_copy(src, dst, sems.at[i]) for i, (src, dst) in enumerate(pairs)]
        for copy in copies:
            copy.start()
        return copies

    def attention(w_src, x_src, an_src, qkv_src, o_src, dw, row, ready, pump):
        def scope(w_buf):
            qkv, o = mix_buf.at[:, pl.ds(0, 2304)], mix_buf.at[:, pl.ds(2304, 768)]
            x_to = xf if x_src.dtype == F32 else low
            copies = load([(x_src, x_to), (o_src, o), (an_src, an_buf), (qkv_src, qkv),
                           (w_src.reshape(WIDTH, HIDDEN), w_buf)], load_sems)
            for copy in copies[:2]:
                copy.wait()
            if x_src.dtype != F32:
                xf[...] = low[...].astype(F32)

            def weights_here():
                for copy in copies[2:]:
                    copy.wait()

            attention_backward(
                g_ref, xf, small[row : row + 1, :], w_buf, an_buf, qkv, o, dw, ds, row, images, seq,
                low, do, dqkv, dn, weights_here, ready, pump,
            )

        pl.run_scoped(scope, pltpu.VMEM((WIDTH, HIDDEN), BF16))

    g_ref[...] = g_in[...]
    ds[...] = small_grad_in[...]
    attention(wa1, x2, an1, qkv1, o1, dw_wide.at[0].reshape(WIDTH, HIDDEN), 1, jobs[2].start,
              lambda: pump(*PACE[0]))
    dense.add(jobs[2])

    def feed_forward(wo_buf, wi_buf, slope_buf, ma_buf):
        wo, wi = wmo.reshape(HIDDEN, WIDTH), wmi.reshape(WIDTH, HIDDEN)
        dwo, dwi = dw_tall.reshape(HIDDEN, WIDTH), dw_wide.at[1].reshape(WIDTH, HIDDEN)
        first_loads = load([(x1, xf), (mn, an_buf)], load_sems)

        def chunk(n):
            cols = pl.ds(n * 512, 512)
            slot = n % 2
            return load([(wo.at[cols, :], wo_buf.at[slot]), (wi.at[:, cols], wi_buf.at[slot]),
                         (slope.at[:, cols], slope_buf.at[slot]), (ma.at[:, cols], ma_buf.at[slot])],
                        stream_sems.at[slot])

        coming = chunk(0)
        low[...] = g_ref[...].astype(BF16)
        dn[...] = jnp.zeros_like(dn)
        for copy in first_loads:
            copy.wait()
        for n in range(6):
            for copy in coming:
                copy.wait()
            if n < 5:
                coming = chunk(n + 1)
            slot = n % 2
            cols = pl.ds(n * 512, 512)
            dwo[cols, :] = tn(ma_buf[slot], low[...]).astype(BF16)
            dact = nt(low[...], wo_buf[slot])
            dh = (slope_buf[slot].astype(F32) * dact).astype(BF16)
            dwi[:, cols] = tn(an_buf[...], dh).astype(BF16)
            dn[...] += nt(dh, wi_buf[slot])
            pump(*PACE[1])
        jobs[3].start()
        jobs[4].start()
        norm_back(x1_buf, small[2:3, :], dn, g_ref, ds, 2)

    x1_buf = xf
    rows = g_ref.shape[0]
    pl.run_scoped(
        feed_forward, pltpu.VMEM((2, 512, WIDTH), BF16), pltpu.VMEM((2, WIDTH, 512), BF16),
        pltpu.VMEM((2, rows, 512), BF16), pltpu.VMEM((2, rows, 512), BF16))
    dense.add(jobs[3])
    dense.add(jobs[4])

    def last_ready():
        assert dense.done[3] >= 8
        pl.semaphore_wait(credit, 3)
        jobs[5].start()

    attention(wa0, x0, an0, qkv0, o0, dw_wide.at[2].reshape(WIDTH, HIDDEN), 0, last_ready,
              lambda: pump(*PACE[2]))

    def small_copy(to, i, source):
        return remote(ds.at[:, pl.ds(pl.multiple_of(window(to), 128), 256)], small_got.at[source],
                      small_sems.at[0, i], small_sems.at[1, source], to)

    pl.loop(1, 32)(lambda i: small_copy((p.me + i) % 32, i, p.me).start())
    dense.add(jobs[5])
    while dense.done[3] < len(dense.units) or experts.queue:
        pump(*PACE[3])
    swap = remote(
        done.at[:, pl.ds(pl.multiple_of((1 - p.core) * 24, 8), 24), :], wide_out.at[p.core],
        meet.at[0], meet.at[1], p.sibling)
    swap.start()
    keep = pltpu.make_async_copy(
        done.at[:, pl.ds(pl.multiple_of(p.core * 24, 8), 24), :], wide_out.at[p.core], meet.at[2])
    keep.start()
    pl.loop(1, 32)(lambda i: small_copy((p.me + i) % 32, i, (p.me + i) % 32).wait())
    small_got[p.me] = ds[:, pl.ds(pl.multiple_of(window(p.me), 128), 256)]
    small_out[...] = jnp.sum(small_got[...], 0)
    for m in range(6):
        jobs[m].finish()
    keep.wait()
    swap.wait()


def run_backward_step(images, seq, args):
    any_space = pl.BlockSpec(memory_space=pl.ANY)
    vmem = pl.BlockSpec(memory_space=pltpu.VMEM)
    dma = pltpu.SemaphoreType.DMA
    piece = (48, 768)
    rows = args[0].shape[0]
    act, low = pltpu.VMEM((rows, WIDTH), F32), pltpu.VMEM((rows, WIDTH), BF16)
    return pl.pallas_call(
        functools.partial(backward_step, images, seq),
        out_shape=[struct((rows, WIDTH), F32), struct((8, 256), F32),
                   struct((2, 7, 24, 1536), F32), struct((5, 96, 768), F32)],
        in_specs=[vmem] * 3 + [any_space] * (len(args) - 3),
        out_specs=[vmem, vmem, any_space, vmem],
        scratch_shapes=[
            act, low, low, pltpu.VMEM((rows, 3 * WIDTH), BF16), act, low,
            pltpu.VMEM((rows, HIDDEN), BF16), pltpu.VMEM((8, WIDTH), F32),
            pltpu.VMEM((3, 4, 2, 2, 48, HIDDEN), BF16),
            pltpu.VMEM((4, 2, 2, 192, WIDTH), BF16),
            pltpu.VMEM((3, 4, 2, 2, 2) + piece, BF16),
            pltpu.VMEM((3, 4, 2, 2) + piece, BF16),
            pltpu.VMEM((3, 4, 2) + piece, BF16),
            pltpu.VMEM((4, 2, 5) + piece, BF16),
            pltpu.VMEM((2, 2, 2, 2) + piece, BF16),
            pltpu.VMEM((2, 2, 5, 2, 2) + piece, BF16),
            pltpu.VMEM((2, 2, 3) + piece, BF16),
            pltpu.VMEM((7, 48, 1536), F32),
            pltpu.VMEM((32, 8, 256), F32),
            dma((5,)),
            dma((2, 2)),
            dma((4, 2, 4, 2)),
            dma((4, 4, 4, 2)),
            dma((6, 2, 4)),
            dma((6, 2, 5)),
            dma((2, 2, 2, 3)),
            dma((2, 32)),
            dma((3,)),
            dma((2, 4)),
            pltpu.SemaphoreType.REGULAR,
        ],
        compiler_params=pltpu.CompilerParams(
            collective_id=1, has_side_effects=True, vmem_limit_bytes=63 << 20),
        cost_estimate=pl.CostEstimate(
            flops=20_000_000_000, bytes_accessed=60_000_000, transcendentals=0),
    )(*args)


def fast_backward(images, seq, x0, g4, small, weights, saved, y_back, d_back, sums):
    rows = x0.shape[0]
    act = struct((rows, WIDTH), F32)
    wa0, wmi, wmo, wa1 = weights
    x1, x2, x3, an0, qkv0, o0, mn, slope, ma, an1, qkv1, o1, en, aux, p0, p1 = saved
    x4, g, ds = call(
        combine_kernel, [act, act, struct((8, WIDTH), F32)], [pltpu.VMEM((rows, WIDTH), F32)],
        [g4, small, x3, en, aux, p0, p1, y_back, d_back], 3_000_000_000,
    )
    w = lambda g: g.reshape(4, 2, 2, 48, HIDDEN)
    t = lambda g: g.reshape(4, 2, 2, 192, WIDTH)
    g, dsmall, wide, tall = run_backward_step(images, seq, [
        g, small, ds, x2, x1, x0, an1, qkv1, o1, mn, slope, ma, an0, qkv0, o0,
        w(wa1), t(wmo), w(wmi), w(wa0), sums])
    me = lax.axis_index("fsdp")
    dsmall = lax.dynamic_slice(dsmall, (0, me * 24 - window(me)), (8, 24))
    wide = wide.transpose(1, 2, 0, 3).reshape(7, 24, HIDDEN)
    return x4, g, (dsmall.T, wide[0], wide[1], tall[0], wide[2],
                   wide[3:].transpose(1, 0, 2), tall[1:].transpose(1, 0, 2))


def expert_step(
    rows_x, rows_d, ein, eout,
    y_back, d_back, sums,
    wi, wo, got_x, got_d, active, slope, y_out, d_out, acc, dwi, dwo, near,
    load_sems, own_sems, move_sems, pair_sems, sum_sems,
):
    p = Place()
    greet_all(p, 32)
    chips = [device // 2 % 4 for device in (p.me, p.across_x, p.across_y, p.across_both)]
    devices = (None, p.across_x, p.across_y, p.across_both)
    loads = [pltpu.make_async_copy(src, dst, load_sems.at[i])
             for i, (src, dst) in enumerate(((ein, wi), (eout, wo)))]

    def inward(t, i):
        src, dst = ((rows_x, got_x), (rows_d, got_d))[t]
        if i == 0:
            return pltpu.make_async_copy(src.at[p.chip], dst.at[p.chip], own_sems.at[t])
        return remote(src.at[chips[i]], dst.at[p.chip], move_sems.at[t, 0, i], move_sems.at[t, 1, i],
                      devices[i])

    def outward(t, i):
        src, dst = ((y_out, y_back), (d_out, d_back))[t]
        if i == 0:
            return pltpu.make_async_copy(src.at[p.chip], dst.at[p.chip], own_sems.at[2 + t])
        return remote(src.at[chips[i]], dst.at[p.chip], move_sems.at[2 + t, 0, i],
                      move_sems.at[2 + t, 1, i], devices[i])

    for i in range(4):
        inward(0, i).start()
    for copy in loads:
        copy.start()
    inward(1, 0).start()
    for copy in loads:
        copy.wait()
    wide = wi.reshape(WIDTH, HIDDEN)
    tall = wo.reshape(HIDDEN, WIDTH)
    for i in range(4):
        chip = chips[i]
        if i == 0:
            inward(0, 0).wait()
        else:
            inward(0, i).wait_recv()
        if i == 1:
            for j in range(1, 4):
                inward(1, j).start()
        acc[...] = jnp.zeros_like(acc)

        def forward(n):
            cols = tile(n, 512)
            ea, sl = gelu_both(nn(got_x[chip], wide[:, cols]))
            ea = ea.astype(BF16)
            active[chip, :, cols] = ea
            slope[chip, :, cols] = sl.astype(BF16)
            acc[...] += nn(ea, tall[cols, :])

        loop(6, forward)
        y_out[chip] = acc[...].astype(BF16)
        outward(0, i).start()
    for i in range(4):
        chip = chips[i]
        if i == 0:
            inward(1, 0).wait()
        else:
            inward(1, i).wait_recv()
        acc[...] = jnp.zeros_like(acc)

        def backward(n):
            cols = tile(n, 512)
            dh = slope[chip, :, cols].astype(F32) * nt(got_d[chip], tall[cols, :])
            dh = dh.astype(BF16)
            slope[chip, :, cols] = dh
            acc[...] += nt(dh, wide[:, cols])

        loop(6, backward)
        d_out[chip] = acc[...].astype(BF16)
        outward(1, i).start()
    every = EXPERTS * SLOT
    x_all, d_all = got_x.reshape(every, WIDTH), got_d.reshape(every, WIDTH)
    ea_all, dh_all = active.reshape(every, HIDDEN), slope.reshape(every, HIDDEN)
    dwi_all, dwo_all = dwi.reshape(WIDTH, HIDDEN), dwo.reshape(HIDDEN, WIDTH)

    def weights(n):
        cols = tile(n, 512)
        dwo_all[cols, :] = tn(ea_all[:, cols], d_all[...]).astype(BF16)
        dwi_all[:, cols] = tn(x_all[...], dh_all[:, cols]).astype(BF16)

    loop(6, weights)
    pairs = [(m, z, half) for z in range(4) for m in range(2) for half in range(2)]

    def pair(m, z, half):
        src = plane_part((dwi, dwo)[m], KINDS[m], z, 1 - p.core, half)
        return remote(src, near.at[m, z, half], pair_sems.at[m, z, half, 0],
                      pair_sems.at[m, z, half, 1], p.sibling)

    def result(m, z, half):
        return pltpu.make_async_copy(near.at[m, z, half], sums.at[m, z, half], sum_sems.at[m, z, half])

    for one in pairs:
        pair(*one).start()
    for m, z, half in pairs:
        pair(m, z, half).wait_recv()
        own = plane_part((dwi, dwo)[m], KINDS[m], z, p.core, half)
        came = near.at[m, z, half]
        add_into(lambda i: came.at[i // 2, i % 2], lambda i: own.at[i // 2, i % 2], 4)
        result(m, z, half).start()
    for one in pairs:
        result(*one).wait()
        pair(*one).wait_send()
    for t in range(2):
        outward(t, 0).wait()
        for i in range(1, 4):
            inward(t, i).wait_send()
            outward(t, i).wait()


def run_expert_step(rows_x, rows_d, ein, eout):
    any_space = pl.BlockSpec(memory_space=pl.ANY)
    dma = pltpu.SemaphoreType.DMA
    rows = (EXPERTS, SLOT, WIDTH)
    y, d, sums = pl.pallas_call(
        expert_step,
        out_shape=[struct(rows, BF16)] * 2 + [struct((2, 4, 2, 2, 2, 48, 768), BF16)],
        in_specs=[any_space] * 4,
        out_specs=[any_space] * 3,
        scratch_shapes=[
            pltpu.VMEM((4, 2, 2, 48, HIDDEN), BF16),
            pltpu.VMEM((4, 2, 2, 192, WIDTH), BF16),
            pltpu.VMEM(rows, BF16),
            pltpu.VMEM(rows, BF16),
            pltpu.VMEM((EXPERTS, SLOT, HIDDEN), BF16),
            pltpu.VMEM((EXPERTS, SLOT, HIDDEN), BF16),
            pltpu.VMEM(rows, BF16),
            pltpu.VMEM(rows, BF16),
            pltpu.VMEM((SLOT, WIDTH), F32),
            pltpu.VMEM((4, 2, 2, 48, HIDDEN), BF16),
            pltpu.VMEM((4, 2, 2, 192, WIDTH), BF16),
            pltpu.VMEM((2, 4, 2, 2, 2, 48, 768), BF16),
            dma((2,)),
            dma((4,)),
            dma((4, 2, 4)),
            dma((2, 4, 2, 2)),
            dma((2, 4, 2)),
        ],
        compiler_params=pltpu.CompilerParams(
            collective_id=2, has_side_effects=True, vmem_limit_bytes=VMEM_BYTES),
        cost_estimate=pl.CostEstimate(
            flops=30_000_000_000, bytes_accessed=40_000_000, transcendentals=0),
    )(rows_x.reshape(rows), rows_d.reshape(rows), ein, eout)
    flat = (EXPERTS * SLOT, WIDTH)
    return y.reshape(flat), d.reshape(flat), sums


def local(
    patches, live_count, expert_ids, attn_gain, attn_qkv, attn_out, mlp_gain, mlp_in, mlp_out,
    moe_gain, router, expert_in, expert_out, cotangent,
):
    images, seq, width = patches.shape
    padded = -(-seq // 16) * 16
    n = lax.axis_size("fsdp")
    group_size = n // EXPERTS
    group = lax.axis_index("fsdp") // group_size
    alive = jnp.arange(images, dtype=jnp.int32) < live_count[0]

    def pad(values, fill=0):
        values = values.reshape(images, seq, -1)
        values = jnp.pad(values, ((0, 0), (0, padded - seq), (0, 0)), constant_values=fill)
        return values.reshape(images * padded, -1)

    x0 = pad(patches)
    g4 = pad(jnp.where(alive[:, None, None], cotangent, jnp.zeros_like(cotangent)))
    ids = pad(expert_ids, -1)
    smalls = jnp.concatenate(
        [attn_gain, mlp_gain[:, None], moe_gain[:, None], router], 1
    )
    wide = [jnp.concatenate([attn_qkv[:, 0], attn_out[:, 0]], 1), mlp_in,
            jnp.concatenate([attn_qkv[:, 1], attn_out[:, 1]], 1)]
    if n == 32:
        small, weights, w_in, w_out, saved, rows_x, rows_d = fast_front(
            images, seq, smalls, wide, mlp_out, expert_in, expert_out, x0, g4, ids)
    else:
        small, wides, talls, w_in, w_out = plain_gather(
            smalls, wide, [mlp_out], expert_in, expert_out)
        small = small.astype(F32).T
        small = jnp.concatenate(
            [small[:4], jnp.zeros((4, width), F32), small[4:], jnp.zeros((124, width), F32)], 0
        )
        weights = (wides[0], wides[1], talls[0], wides[2])
        out = run_forward(images, seq, x0, g4, ids, small, *weights)
        saved, rows_x, rows_d = out[:16], out[16], out[17]

    def exchange(rows):
        rows = rows.reshape(EXPERTS, SLOT, width)
        return group_exchange(rows, group_size, group).reshape(EXPERTS * SLOT, width)

    if n == 32:
        y_back, d_back, sums = run_expert_step(rows_x, rows_d, w_in, w_out)
        x4, grad, shards = fast_backward(
            images, seq, x0, g4, small, weights, saved, y_back, d_back, sums)
        dsmall, d0, dmi, dmo, d1, de_in, de_out = shards
    else:
        y, dx, dw_in, dw_out = run_expert(exchange(rows_x), exchange(rows_d), w_in, w_out)
        x4, grad, d0, dmi, dmo, d1, dsmall = run_backward(
            images, seq, x0, g4, small, weights, saved, exchange(y), exchange(dx)
        )
        d0, dmi, dmo, d1 = (plain_reduce(g).astype(F32) for g in (d0, dmi, dmo, d1))
        de_in, de_out = (plain_reduce_expert(g).astype(F32) for g in (dw_in, dw_out))
        dsmall = lax.psum_scatter(dsmall.T, "fsdp", scatter_dimension=0, tiled=True)

    def unpad(values):
        return values.reshape(images, padded, width)[:, :seq]

    block_out = jnp.where(alive[:, None, None], unpad(x4), 0.0).astype(BF16)
    return (
        block_out,
        unpad(grad),
        dsmall[:, 0:2],
        jnp.stack([d0[:, :2304], d1[:, :2304]], 1),
        jnp.stack([d0[:, 2304:], d1[:, 2304:]], 1),
        dsmall[:, 2],
        dmi,
        dmo,
        dsmall[:, 3],
        dsmall[:, 4:8],
        de_in,
        de_out,
    )


def solution(mesh):
    def lead(rank):
        return P("fsdp", *([None] * (rank - 1)))

    return jax.shard_map(
        local,
        mesh=mesh,
        in_specs=tuple(lead(r) for r in (3, 1, 2, 2, 3, 3, 1, 2, 2, 1, 2, 3, 3, 3)),
        out_specs=tuple(lead(r) for r in (3, 3, 2, 3, 3, 1, 2, 2, 1, 2, 3, 3)),
        check_vma=False,
    )
```

```python
import functools

import jax
import jax.numpy as jnp
from jax import lax
from jax.experimental import pallas as pl
from jax.experimental.pallas import tpu as pltpu
from jax.sharding import PartitionSpec as P

HEADS = 12
HEAD_DIM = 64
EXPERTS = 4
CAP = 247
SLOT = 256
WIDTH = 768
HIDDEN = 3072
NORM_EPSILON = 1e-06
VMEM_BYTES = 60 << 20
F32 = jnp.float32
BF16 = jnp.bfloat16


def nn(left, right):
    return lax.dot_general(left, right, (((1,), (0,)), ((), ())), preferred_element_type=F32)


def nt(left, right):
    return lax.dot_general(left, right, (((1,), (1,)), ((), ())), preferred_element_type=F32)


def tn(left, right):
    return lax.dot_general(left, right, (((0,), (0,)), ((), ())), preferred_element_type=F32)


def tile(index, size):
    return pl.ds(pl.multiple_of(index * size, size), size)


def loop(count, body):
    pl.loop(0, count)(body)


def norm_parts(values):
    center = values - jnp.mean(values, -1, keepdims=True)
    spread = jnp.mean(center * center, -1, keepdims=True)
    scale = lax.rsqrt(spread + NORM_EPSILON)
    return center * scale, scale


def norm_rows(x_ref, gain, out_ref, block=32):
    def body(i):
        rows = tile(i, block)
        unit, _ = norm_parts(x_ref[rows, :])
        out_ref[rows, :] = (unit * gain).astype(BF16)

    loop(x_ref.shape[0] // block, body)


def norm_back(x_ref, gain, dn_ref, g_ref, dgain_ref, row, block=32):
    def body(i, total):
        rows = tile(i, block)
        unit, scale = norm_parts(x_ref[rows, :])
        dn = dn_ref[rows, :]
        scaled = dn * gain
        mean_one = jnp.mean(scaled, -1, keepdims=True)
        mean_two = jnp.mean(scaled * unit, -1, keepdims=True)
        g_ref[rows, :] = g_ref[rows, :] + scale * (scaled - mean_one - unit * mean_two)
        return total + jnp.sum((dn * unit).reshape(block // 8, 8, WIDTH), 0)

    total = lax.fori_loop(0, x_ref.shape[0] // block, body, jnp.zeros((8, WIDTH), F32))
    dgain_ref[row : row + 1, :] = jnp.sum(total, 0, keepdims=True)


def gelu_both(u):
    c = 0.7978845608
    square = u * u
    t = jnp.tanh(c * u * (1.0 + 0.044715 * square))
    half = 0.5 * (1.0 + t)
    slope = half + 0.5 * u * (1.0 - t * t) * (c + (3 * 0.044715 * c) * square)
    return u * half, slope


def halves(shape):
    lane = lax.broadcasted_iota(jnp.int32, shape, 1)
    return lane < HEAD_DIM


def head_probs(q, k, seq):
    scores = nt(q, k) * HEAD_DIM ** (-0.5)
    key = lax.broadcasted_iota(jnp.int32, scores.shape, 1)
    scores = jnp.where(key < seq, scores, -1e30)
    top = jnp.max(scores, -1, keepdims=True)
    e = jnp.exp(scores - top)
    return e / jnp.sum(e, -1, keepdims=True)


def attention_heads(qkv_ref, o_ref, images, seq):
    rows_of = qkv_ref.shape[0] // images
    for image in range(images):
        rows = pl.ds(image * rows_of, rows_of)

        def pair(p, rows=rows):
            q = qkv_ref[rows, tile(p, 128)]
            k = qkv_ref[rows, tile(p + 6, 128)]
            v = qkv_ref[rows, tile(p + 12, 128)]
            first = halves(q.shape)
            zero = jnp.zeros_like(q)
            p0 = head_probs(jnp.where(first, q, zero), k, seq).astype(BF16)
            p1 = head_probs(jnp.where(first, zero, q), k, seq).astype(BF16)
            out = nn(p0, jnp.where(first, v, zero)) + nn(p1, jnp.where(first, zero, v))
            o_ref[rows, tile(p, 128)] = out.astype(BF16)

        loop(6, pair)


def attention_forward(x_ref, gain, w_ref, xo_ref, an_ref, qkv_ref, o_ref, images, seq):
    norm_rows(x_ref, gain, an_ref)

    def project(n):
        qkv_ref[:, tile(n, 256)] = nn(an_ref[...], w_ref[:, tile(n, 256)]).astype(BF16)

    loop(9, project)
    attention_heads(qkv_ref, o_ref, images, seq)

    def outward(n):
        cols = tile(n, 256)
        xo_ref[:, cols] = x_ref[:, cols] + nn(o_ref[...], w_ref[:, tile(n + 9, 256)])

    loop(3, outward)


def attention_backward(
    g_ref, x_ref, gain, w_ref, an_ref, qkv_ref, o_ref, dw_ref, dgain_ref, row, images, seq,
    low_ref, do_ref, dqkv_ref, dn_ref, weights_here=lambda: None, ready=lambda: None,
    pump=lambda: None,
):
    rows_of = qkv_ref.shape[0] // images
    low_ref[...] = g_ref[...].astype(BF16)

    def outward(n):
        dw_ref[:, tile(n + 9, 256)] = tn(o_ref[...], low_ref[:, tile(n, 256)]).astype(BF16)

    loop(3, outward)
    pump()
    weights_here()

    def outward_rows(n):
        do_ref[:, tile(n, 256)] = nt(low_ref[...], w_ref[tile(n, 256), 2304:]).astype(BF16)

    loop(3, outward_rows)
    pump()
    for image in range(images):
        rows = pl.ds(image * rows_of, rows_of)

        def pair(p, rows=rows):
            q = qkv_ref[rows, tile(p, 128)]
            k = qkv_ref[rows, tile(p + 6, 128)]
            v = qkv_ref[rows, tile(p + 12, 128)]
            d = do_ref[rows, tile(p, 128)]
            first = halves(q.shape)
            zero = jnp.zeros_like(q)
            dq = dk = dv = None
            for mine in (first, ~first):
                qm, km, dm = (jnp.where(mine, t, zero) for t in (q, k, d))
                probs = head_probs(qm, k, seq)
                dp = nt(dm, v)
                inner = jnp.sum(dp * probs, -1, keepdims=True)
                ds = (probs * (dp - inner)).astype(BF16)
                one = (nn(ds, km), tn(ds, qm), tn(probs.astype(BF16), dm))
                dq, dk, dv = one if dq is None else (dq + one[0], dk + one[1], dv + one[2])
            scale = HEAD_DIM ** (-0.5)
            dqkv_ref[rows, tile(p, 128)] = (dq * scale).astype(BF16)
            dqkv_ref[rows, tile(p + 6, 128)] = (dk * scale).astype(BF16)
            dqkv_ref[rows, tile(p + 12, 128)] = dv.astype(BF16)

        loop(3, pair)
        pump()
        loop(3, lambda p, pair=pair: pair(p + 3))
        pump()

    for third in range(3):

        def inward(n, third=third):
            cols = tile(n + third * 3, 256)
            dw_ref[:, cols] = tn(an_ref[...], dqkv_ref[:, cols]).astype(BF16)

        loop(3, inward)
        pump()
    ready()

    def normed(n):
        dn_ref[:, tile(n, 256)] = nt(dqkv_ref[...], w_ref[tile(n, 256), :2304])

    loop(3, normed)
    pump()
    norm_back(x_ref, gain, dn_ref, g_ref, dgain_ref, row)
    pump()


def route_rows(g4_ref, ids_ref, small_ref, en_ref, aux_ref, g0_ref, g1_ref, rx_ref, rd_ref, pump):
    rows = en_ref.shape[0]
    logits = nt(en_ref[...], small_ref[8:136, :].astype(BF16))
    lane = lax.broadcasted_iota(jnp.int32, logits.shape, 1)
    logits = jnp.where(lane < EXPERTS, logits, -1e30)
    e = jnp.exp(logits - jnp.max(logits, -1, keepdims=True))
    chances = e / jnp.sum(e, -1, keepdims=True)
    ids = ids_ref[...]
    chosen = [(ids[:, j : j + 1] == lane).astype(F32) for j in range(2)]
    row_i = lax.broadcasted_iota(jnp.int32, (rows, rows), 0)
    row_j = lax.broadcasted_iota(jnp.int32, (rows, rows), 1)
    earlier = nn((row_j < row_i).astype(BF16), (chosen[0] + chosen[1]).astype(BF16))
    place = lax.broadcasted_iota(jnp.int32, (rows, EXPERTS * SLOT), 1)
    gates = []
    for j, pick_ref in ((0, g0_ref), (1, g1_ref)):
        gates.append(jnp.sum(chances * chosen[j], -1, keepdims=True))
        inside = jnp.sum(earlier * chosen[j], -1, keepdims=True).astype(jnp.int32)
        slot = jnp.where(ids[:, j : j + 1] >= 0, ids[:, j : j + 1] * SLOT + inside, -1)
        pick_ref[...] = (slot == place).astype(BF16)
    aux = jnp.where(lane < EXPERTS, chances, 0.0)
    aux = jnp.where(lane == 8, gates[0], aux)
    aux_ref[...] = jnp.where(lane == 9, gates[1], aux)

    def fill(n):
        cols = tile(n, 256)
        both = g0_ref[:, cols] + g1_ref[:, cols]
        rx_ref[cols, :] = tn(both, en_ref[...]).astype(BF16)
        g4 = g4_ref[...].astype(F32)
        one = tn(g0_ref[:, cols], (g4 * gates[0]).astype(BF16))
        two = tn(g1_ref[:, cols], (g4 * gates[1]).astype(BF16))
        rd_ref[cols, :] = (one + two).astype(BF16)

    pump()
    loop(2, fill)
    pump()
    loop(2, lambda n: fill(n + 2))
    pump()


def forward_kernel(
    images, seq,
    x0_ref, g4_ref, ids_ref, small_ref, wa0_ref, wmi_ref, wmo_ref, wa1_ref,
    x1_ref, x2_ref, x3_ref, an0_ref, qkv0_ref, o0_ref, mn_ref, slope_ref, ma_ref,
    an1_ref, qkv1_ref, o1_ref, en_ref, aux_ref, g0_ref, g1_ref, rx_ref, rd_ref,
    xf_ref,
):
    xf_ref[...] = x0_ref[...].astype(F32)
    attention_forward(
        xf_ref, small_ref[0:1, :], wa0_ref, x1_ref, an0_ref, qkv0_ref, o0_ref, images, seq
    )
    norm_rows(x1_ref, small_ref[2:3, :], mn_ref)
    x2_ref[...] = x1_ref[...]

    def dense(n):
        cols = tile(n, 512)
        active, slope = gelu_both(nn(mn_ref[...], wmi_ref[:, cols]))
        slope_ref[:, cols] = slope.astype(BF16)
        active = active.astype(BF16)
        ma_ref[:, cols] = active
        x2_ref[...] += nn(active, wmo_ref[cols, :])

    loop(6, dense)
    attention_forward(
        x2_ref, small_ref[1:2, :], wa1_ref, x3_ref, an1_ref, qkv1_ref, o1_ref, images, seq
    )
    norm_rows(x3_ref, small_ref[3:4, :], en_ref)
    route_rows(
        g4_ref, ids_ref, small_ref, en_ref, aux_ref, g0_ref, g1_ref, rx_ref, rd_ref, lambda: None
    )


def expert_kernel(x_ref, d_ref, wi_ref, wo_ref, y_ref, dx_ref, dwi_ref, dwo_ref, yf_ref, df_ref):
    yf_ref[...] = jnp.zeros_like(yf_ref)
    df_ref[...] = jnp.zeros_like(df_ref)

    def body(n):
        cols = tile(n, 512)
        active, slope = gelu_both(nn(x_ref[...], wi_ref[:, cols]))
        active = active.astype(BF16)
        yf_ref[...] += nn(active, wo_ref[cols, :])
        dwo_ref[cols, :] = tn(active, d_ref[...]).astype(BF16)
        dh = (slope * nt(d_ref[...], wo_ref[cols, :])).astype(BF16)
        df_ref[...] += nt(dh, wi_ref[:, cols])
        dwi_ref[:, cols] = tn(x_ref[...], dh).astype(BF16)

    loop(6, body)
    y_ref[...] = yf_ref[...].astype(BF16)
    dx_ref[...] = df_ref[...].astype(BF16)


def combine_kernel(
    g4_ref, small_ref, x3_ref, en_ref, aux_ref, g0_ref, g1_ref, yr_ref, dr_ref,
    x4_ref, g_ref, ds_ref,
    dn_ref,
):
    aux = aux_ref[...]
    lane = lax.broadcasted_iota(jnp.int32, aux.shape, 1)
    g_ref[...] = g4_ref[...].astype(F32)
    x4_ref[...] = x3_ref[...]
    dgates = []
    chosen = []
    expert_of = lax.broadcasted_iota(jnp.int32, (EXPERTS * SLOT, 128), 0) // SLOT
    spread = (expert_of == lax.broadcasted_iota(jnp.int32, expert_of.shape, 1)).astype(BF16)
    for j, pick_ref in ((0, g0_ref), (1, g1_ref)):
        picked = nn(pick_ref[...], yr_ref[...])
        x4_ref[...] += aux[:, 8 + j : 9 + j] * picked
        dgates.append(jnp.sum(g_ref[...] * picked, -1, keepdims=True))
        chosen.append(nn(pick_ref[...], spread))
    dr = dgates[0] * chosen[0] + dgates[1] * chosen[1]
    chances = jnp.where(lane < EXPERTS, aux, 0.0)
    dlogits = chances * (dr - jnp.sum(chances * dr, -1, keepdims=True))
    dlogits = jnp.where(lane < EXPERTS, dlogits, 0.0).astype(BF16)
    ds_ref[...] = jnp.zeros_like(ds_ref)
    ds_ref[4:8, :] = tn(dlogits, en_ref[...])[0:4, :]
    dn_ref[...] = nn(dlogits, small_ref[8:136, :].astype(BF16)) + nn(
        g0_ref[...] + g1_ref[...], dr_ref[...]
    )
    norm_back(x3_ref, small_ref[3:4, :], dn_ref, g_ref, ds_ref, 3)


def attention_back_kernel(
    images, seq, row,
    g_in_ref, small_ref, x_ref, w_ref, an_ref, qkv_ref, o_ref,
    g_ref, dw_ref, ds_ref,
    xf_ref, low_ref, do_ref, dqkv_ref, dn_ref,
):
    g_ref[...] = g_in_ref[...]
    xf_ref[...] = x_ref[...].astype(F32)
    ds_ref[...] = jnp.zeros_like(ds_ref)
    attention_backward(
        g_ref, xf_ref, small_ref[row : row + 1, :], w_ref, an_ref, qkv_ref, o_ref, dw_ref,
        ds_ref, row, images, seq, low_ref, do_ref, dqkv_ref, dn_ref,
    )


def dense_back_kernel(
    g_in_ref, small_ref, x1_ref, wmi_ref, wmo_ref, mn_ref, slope_ref, ma_ref,
    g_ref, dwmi_ref, dwmo_ref, ds_ref,
    low_ref, dn_ref,
):
    g_ref[...] = g_in_ref[...]
    ds_ref[...] = jnp.zeros_like(ds_ref)
    low_ref[...] = g_ref[...].astype(BF16)
    dn_ref[...] = jnp.zeros_like(dn_ref)

    def dense(n):
        cols = tile(n, 512)
        dwmo_ref[cols, :] = tn(ma_ref[:, cols], low_ref[...]).astype(BF16)
        dact = nt(low_ref[...], wmo_ref[cols, :])
        dh = (slope_ref[:, cols].astype(F32) * dact).astype(BF16)
        dwmi_ref[:, cols] = tn(mn_ref[...], dh).astype(BF16)
        dn_ref[...] += nt(dh, wmi_ref[:, cols])

    loop(6, dense)
    norm_back(x1_ref, small_ref[2:3, :], dn_ref, g_ref, ds_ref, 2)


def struct(shape, dtype):
    return jax.ShapeDtypeStruct(shape, dtype)


def call(body, outs, scratch, args, flops):
    total = sum(a.size * a.dtype.itemsize for a in list(args) + list(outs))
    return pl.pallas_call(
        body,
        out_shape=outs,
        in_specs=[pl.BlockSpec(memory_space=pltpu.VMEM)] * len(args),
        out_specs=[pl.BlockSpec(memory_space=pltpu.VMEM)] * len(outs),
        scratch_shapes=scratch,
        compiler_params=pltpu.CompilerParams(vmem_limit_bytes=VMEM_BYTES),
        cost_estimate=pl.CostEstimate(flops=flops, bytes_accessed=total, transcendentals=0),
    )(*args)


def run_forward(images, seq, x0, g4, ids, small, wa0, wmi, wmo, wa1):
    rows = x0.shape[0]
    act = struct((rows, WIDTH), F32)
    low = struct((rows, WIDTH), BF16)
    qkv = struct((rows, 3 * WIDTH), BF16)
    hid = struct((rows, HIDDEN), BF16)
    pick = struct((rows, EXPERTS * SLOT), BF16)
    buf = struct((EXPERTS * SLOT, WIDTH), BF16)
    outs = [act, act, act, low, qkv, low, low, hid, hid, low, qkv, low, low,
            struct((rows, 128), F32), pick, pick, buf, buf]
    return call(
        functools.partial(forward_kernel, images, seq), outs,
        [pltpu.VMEM((rows, WIDTH), F32)],
        [x0, g4, ids, small, wa0, wmi, wmo, wa1], 8_000_000_000,
    )


def run_expert(x, d, wi, wo):
    outs = [struct(x.shape, BF16), struct(x.shape, BF16), struct(wi.shape, BF16), struct(wo.shape, BF16)]
    return call(
        expert_kernel, outs, [pltpu.VMEM(x.shape, F32), pltpu.VMEM(x.shape, F32)],
        [x, d, wi, wo], 30_000_000_000,
    )


def run_backward(images, seq, x0, g4, small, weights, saved, y_back, d_back):
    rows = x0.shape[0]
    act = struct((rows, WIDTH), F32)
    wide, tall = struct((WIDTH, HIDDEN), BF16), struct((HIDDEN, WIDTH), BF16)
    row = struct((8, WIDTH), F32)
    wa0, wmi, wmo, wa1 = weights
    x1, x2, x3, an0, qkv0, o0, mn, slope, ma, an1, qkv1, o1, en, aux, p0, p1 = saved
    full = pltpu.VMEM((rows, WIDTH), F32)
    low = pltpu.VMEM((rows, WIDTH), BF16)
    mixed = pltpu.VMEM((rows, 3 * WIDTH), BF16)
    x4, g, s0 = call(
        combine_kernel, [act, act, row], [full],
        [g4, small, x3, en, aux, p0, p1, y_back, d_back], 3_000_000_000,
    )
    g, dwa1, s1 = call(
        functools.partial(attention_back_kernel, images, seq, 1), [act, wide, row],
        [full, low, low, mixed, full], [g, small, x2, wa1, an1, qkv1, o1], 5_000_000_000,
    )
    g, dwmi, dwmo, s2 = call(
        dense_back_kernel, [act, wide, tall, row], [low, full],
        [g, small, x1, wmi, wmo, mn, slope, ma], 8_000_000_000,
    )
    g, dwa0, s3 = call(
        functools.partial(attention_back_kernel, images, seq, 0), [act, wide, row],
        [full, low, low, mixed, full], [g, small, x0, wa0, an0, qkv0, o0], 5_000_000_000,
    )
    return x4, g, dwa0, dwmi, dwmo, dwa1, s0 + s1 + s2 + s3


def gather_rows(piece):
    return lax.all_gather(piece, "fsdp", axis=0, tiled=True)


def shift(values, steps):
    count = lax.axis_size("fsdp")
    return lax.ppermute(values, "fsdp", [(s, (s + steps) % count) for s in range(count)])


def group_exchange(rows, group_size, group_id):
    out = jnp.zeros_like(rows)
    for offset in range(EXPERTS):
        piece = lax.dynamic_index_in_dim(rows, (group_id + offset) % EXPERTS, 0, keepdims=False)
        if offset:
            piece = shift(piece, offset * group_size)
        out = lax.dynamic_update_index_in_dim(out, piece, (group_id - offset) % EXPERTS, 0)
    return out


def plain_gather(smalls, wide, tall, e_in, e_out):
    n = lax.axis_size("fsdp")
    group_size = n // EXPERTS
    group = lax.axis_index("fsdp") // group_size
    small = gather_rows(smalls)
    wides = [gather_rows(w) for w in wide]
    talls = [gather_rows(w) for w in tall]
    big_in = lax.dynamic_index_in_dim(gather_rows(e_in), group, 1, keepdims=False)
    big_out = lax.dynamic_index_in_dim(gather_rows(e_out), group, 1, keepdims=False)
    return small, wides, talls, big_in, big_out


def plain_reduce(grad):
    return lax.psum_scatter(grad, "fsdp", scatter_dimension=0, tiled=True)


def plain_reduce_expert(grad):
    n = lax.axis_size("fsdp")
    group_size = n // EXPERTS
    group = lax.axis_index("fsdp") // group_size
    full = jnp.zeros((grad.shape[0], EXPERTS, grad.shape[1]), BF16)
    full = lax.dynamic_update_index_in_dim(full, grad, group, 1)
    return plain_reduce(full)

MESH_ID = pl.DeviceIdType.MESH


class Place:
    def __init__(self):
        self.me = lax.axis_index("fsdp")
        self.core = self.me % 2
        self.x = self.me // 2 % 2
        self.y = self.me // 4 % 2
        self.z = self.me // 8
        self.sibling = self.me + 1 - 2 * self.core
        self.across_x = self.me + 2 - 4 * self.x
        self.across_y = self.me + 4 - 8 * self.y
        self.across_both = self.across_x + 4 - 8 * self.y
        self.chip = self.me // 2 % 4


def remote(src, dst, send, recv, device):
    return pltpu.make_async_remote_copy(
        src_ref=src, dst_ref=dst, send_sem=send, recv_sem=recv,
        device_id=(device,), device_id_type=MESH_ID,
    )


def greet_all(place, count):
    barrier = pltpu.get_barrier_semaphore()

    def hello(i):
        pl.semaphore_signal(
            barrier, inc=1, device_id=((place.me + i) % count,), device_id_type=MESH_ID
        )

    pl.loop(1, count)(hello)
    pl.semaphore_wait(barrier, count - 1)


DENSE = ("wide", "wide", "tall", "wide")


def part(ref, kind, z, y, x, core, half):
    if kind == "wide":
        return ref.at[z, y, x, :, pl.ds(pl.multiple_of(core * 1536 + half * 768, 128), 768)]
    return ref.at[z, y, x, pl.ds(pl.multiple_of(core * 96 + half * 48, 16), 48), :]


def own_part(mine, kind, half):
    if kind == "wide":
        return mine.at[:, pl.ds(half * 768, 768)]
    return mine.at[pl.ds(half * 48, 48), :]


class Gather:
    def __init__(self, place, kind, mine, out, sems):
        self.p, self.kind, self.mine, self.out, self.sems = place, kind, mine, out, sems

    def _z(self, half, source, up):
        p = self.p
        where = part(self.out, self.kind, source, p.y, p.x, p.core, half)
        return where, 0 if up else 1

    def _slot(self, half, source):
        return half * 4 + source

    def start_own(self):
        p, s = self.p, self.sems
        for half in range(2):
            there = part(self.out, self.kind, p.z, p.y, p.x, p.core, half)
            src = own_part(self.mine, self.kind, half)
            pltpu.make_async_copy(src, there, s["own"].at[half]).start()
            self._along_z(half, p.z, src, True, True)

    def _copy_z(self, half, source, src, up):
        p, s = self.p, self.sems
        slot = self._slot(half, source)
        there = part(self.out, self.kind, source, p.y, p.x, p.core, half)
        name = "zu" if up else "zd"
        return remote(there if src is None else src, there, s[name].at[slot], s["zr"].at[slot],
                      p.me + 8 if up else p.me - 8)

    def _along_z(self, half, source, src, up, down):
        p = self.p
        if up:
            pl.when(p.z < 3)(lambda: self._copy_z(half, source, src, True).start())
        if down:
            pl.when(p.z > 0)(lambda: self._copy_z(half, source, src, False).start())

    def _first(self, half, source, src=None):
        p, s = self.p, self.sems
        slot = self._slot(half, source)
        there = part(self.out, self.kind, source, p.y, p.x, p.core, half)
        return remote(there if src is None else src, there, s["fs"].at[slot], s["fr"].at[slot],
                      p.across_y if half else p.across_x)

    def _line(self, half, source):
        p = self.p
        if self.kind == "wide":
            rows, cols = slice(None), pl.ds(pl.multiple_of(p.core * 1536 + half * 768, 128), 768)
        else:
            rows, cols = pl.ds(pl.multiple_of(p.core * 96 + half * 48, 16), 48), slice(None)
        if half:
            return self.out.at[source, :, p.x, rows, cols]
        return self.out.at[source, p.y, :, rows, cols]

    def _second(self, half, source):
        p, s = self.p, self.sems
        slot = self._slot(half, source)
        line = self._line(half, source)
        return remote(line, line, s["ss"].at[slot], s["sr"].at[slot],
                      p.across_x if half else p.across_y)

    def _hand(self, half, source):
        p, s = self.p, self.sems
        slot = self._slot(half, source)
        if self.kind == "wide":
            rows, cols = slice(None), pl.ds(pl.multiple_of(p.core * 1536 + half * 768, 128), 768)
        else:
            rows, cols = pl.ds(pl.multiple_of(p.core * 96 + half * 48, 16), 48), slice(None)
        plane = self.out.at[source, :, :, rows, cols]
        return remote(plane, plane, s["hs"].at[slot], s["hr"].at[slot], p.sibling)

    def valid(self, k):
        z = self.p.z + k
        return (z >= 0) & (z <= 3)

    def stage_one(self, half, k):
        source = self.p.z + k

        def run():
            if k == 0:
                src = own_part(self.mine, self.kind, half)
                self._first(half, source, src).start()
                there = part(self.out, self.kind, source, self.p.y, self.p.x, self.p.core, half)
                pltpu.make_async_copy(src, there, self.sems["own"].at[half]).wait()
                return
            self._copy_z(half, source, None, k < 0).wait_recv()
            self._along_z(half, source, None, k < 0, k > 0)
            self._first(half, source).start()

        pl.when(self.valid(k))(run)

    def stage_two(self, half, k):
        source = self.p.z + k

        def run():
            self._first(half, source).wait_recv()
            self._second(half, source).start()

        pl.when(self.valid(k))(run)

    def stage_three(self, half, k):
        source = self.p.z + k

        def run():
            self._second(half, source).wait_recv()
            self._hand(half, source).start()

        pl.when(self.valid(k))(run)

    def arrived(self):
        for half in range(2):
            for source in range(4):
                self._hand(half, source).wait_recv()

    def finish(self):
        p = self.p
        for half in range(2):
            for source in range(4):
                self._first(half, source).wait_send()
                self._second(half, source).wait_send()
                self._hand(half, source).wait_send()
                up = (source <= p.z) & (p.z < 3)
                down = (source >= p.z) & (p.z > 0)
                pl.when(up)(lambda: self._copy_z(half, source, None, True).wait_send())
                pl.when(down)(lambda: self._copy_z(half, source, None, False).wait_send())


GATHER_SEMS = ("zu", "zd", "zr", "fs", "fr", "ss", "sr", "hs", "hr")


def expert_block(ref, kind, z, y, core):
    if kind == "wide":
        return ref.at[z, y, :, :, pl.ds(pl.multiple_of(core * 1536, 128), 1536)]
    return ref.at[z, y, :, pl.ds(pl.multiple_of(core * 96, 16), 96), :]


def expert_piece(ref, kind, z, y, x, core):
    if kind == "wide":
        return ref.at[z, y, x, :, pl.ds(pl.multiple_of(core * 1536, 128), 1536)]
    return ref.at[z, y, x, pl.ds(pl.multiple_of(core * 96, 16), 96), :]


class ExpertGather:
    def __init__(self, place, kind, mine, out, sems):
        self.p, self.kind, self.mine, self.out, self.sems = place, kind, mine, out, sems

    def _cross(self, i):
        p, s = self.p, self.sems
        there = expert_piece(self.out, self.kind, p.z, p.y, p.x, p.core)
        device = (p.across_x, p.across_y, p.across_both)[i]
        expert = device // 2 % 4
        return remote(self.mine.at[expert], there, s["cs"].at[i], s["cr"].at[i], device)

    def _own(self):
        p = self.p
        there = expert_piece(self.out, self.kind, p.z, p.y, p.x, p.core)
        return pltpu.make_async_copy(self.mine.at[p.chip], there, self.sems["own"].at[0])

    def start_own(self):
        self._own().start()
        for i in range(3):
            self._cross(i).start()

    def _copy_z(self, y, source, up):
        p, s = self.p, self.sems
        slot = y * 4 + source
        block = expert_block(self.out, self.kind, source, y, p.core)
        return remote(block, block, s["zu" if up else "zd"].at[slot], s["zr"].at[slot],
                      p.me + 8 if up else p.me - 8)

    def _hand(self, y, source):
        p, s = self.p, self.sems
        slot = y * 4 + source
        block = expert_block(self.out, self.kind, source, y, p.core)
        return remote(block, block, s["hs"].at[slot], s["hr"].at[slot], p.sibling)

    def crossed(self):
        p = self.p
        self._own().wait()
        for i in range(3):
            self._cross(i).wait_recv()
        for y in range(2):
            pl.when(p.z < 3)(lambda: self._copy_z(y, p.z, True).start())
            pl.when(p.z > 0)(lambda: self._copy_z(y, p.z, False).start())
            self._hand(y, p.z).start()

    def stage(self, y, k):
        p = self.p
        source = p.z + k

        def run():
            self._copy_z(y, source, k < 0).wait_recv()
            if k < 0:
                pl.when(p.z < 3)(lambda: self._copy_z(y, source, True).start())
            else:
                pl.when(p.z > 0)(lambda: self._copy_z(y, source, False).start())
            self._hand(y, source).start()

        pl.when((source >= 0) & (source <= 3))(run)

    def arrived(self):
        for y in range(2):
            for source in range(4):
                self._hand(y, source).wait_recv()

    def finish(self):
        p = self.p
        for i in range(3):
            self._cross(i).wait_send()
        for y in range(2):
            for source in range(4):
                self._hand(y, source).wait_send()
                up = (source <= p.z) & (p.z < 3)
                down = (source >= p.z) & (p.z > 0)
                pl.when(up)(lambda: self._copy_z(y, source, True).wait_send())
                pl.when(down)(lambda: self._copy_z(y, source, False).wait_send())


EXPERT_SEMS = ("zu", "zd", "zr", "hs", "hr")
STEPS = (0, -1, 1, -2, 2, -3, 3)

FRONT = (0.05, (0.3, 4.7), (0.4, 7), (0.4, 14), 1)


def front_kernel(
    images, seq,
    small_in, wide_in, tall_in, x0_ref, g4_ref, ids_ref,
    small, wa0, wmi, wmo, wa1, ein, eout, *rest,
):
    outs, mine, tools = rest[:18], rest[18:36], rest[36:]
    (x1, x2, x3, an0, qkv0, o0, mn, slope, ma, an1, qkv1, o1, en, aux_ref, pick0, pick1, rx, rd) = mine
    (xf, va0, vmi, vmo, va1, wide_mine, expert_mine, from_sibling, small_got,
     meet, small_sems, gather_sems, own_sems, expert_sems, cross_sems, out_sems, weight_sems) = tools
    p = Place()
    greet_all(p, 32)
    swap = remote(wide_in.at[1 - p.core], from_sibling, meet.at[0], meet.at[1], p.sibling)
    swap.start()

    def small_copy(to, i, source):
        return remote(small_in, small_got.at[source], small_sems.at[0, i], small_sems.at[1, source], to)

    pl.loop(1, 32)(lambda i: small_copy((p.me + i) % 32, i, p.me).start())
    small_got[p.me] = small_in[...]
    landing, weights = (va0, vmi, vmo, va1), (wa0, wmi, wmo, wa1)
    jobs = []
    for m, kind in enumerate(DENSE):
        sems = {name: gather_sems.at[m, i] for i, name in enumerate(GATHER_SEMS)}
        sems["own"] = own_sems.at[m]
        piece = tall_in.at[0] if kind == "tall" else wide_mine.at[(0, 1, None, 2)[m]]
        jobs.append(Gather(p, kind, piece, landing[m], sems))
    big = []
    for m, kind in enumerate(("wide", "tall")):
        sems = {name: expert_sems.at[m, i] for i, name in enumerate(EXPERT_SEMS)}
        sems["cs"], sems["cr"], sems["own"] = (
            cross_sems.at[m, 0], cross_sems.at[m, 1], cross_sems.at[m, 2])
        piece = tall_in.at[pl.ds(1, 4)] if kind == "tall" else expert_mine
        big.append(ExpertGather(p, kind, piece, (ein, eout)[m], sems))
    jobs[2].start_own()
    swap.wait_recv()

    def merge(m, out):
        cols = pl.ds(m * 1536, 1536)
        kept = wide_in[p.core, :, cols]
        came = from_sibling[:, cols]
        upper = jnp.where(p.core == 0, kept, came)
        lower = jnp.where(p.core == 0, came, kept)
        out[...] = jnp.concatenate([upper, lower], 0).astype(BF16)

    merge(0, wide_mine.at[0])
    jobs[0].start_own()
    big[1].start_own()
    for e in range(4):
        merge(3 + e, expert_mine.at[e])
    big[0].start_own()
    merge(1, wide_mine.at[1])
    jobs[1].start_own()
    merge(2, wide_mine.at[2])
    jobs[3].start_own()

    dense, experts = Pump(), Pump()
    order = [(m, k, half) for m in range(4) for k in STEPS for half in range(2)]
    done_at = {}
    for i in range(len(order) + 24):
        for stage, lag in ((0, 0), (1, 12), (2, 24)):
            if 0 <= i - lag < len(order):
                m, k, half = order[i - lag]
                name = ("stage_one", "stage_two", "stage_three")[stage]
                dense.add([functools.partial(getattr(jobs[m], name), half, k)])
                if stage == 2:
                    done_at[m] = len(dense.queue)
    total = len(dense.queue)

    def crossed():
        big[1].crossed()
        big[0].crossed()

    experts.add([crossed])
    experts.add([functools.partial(big[m].stage, y, k) for k in STEPS[1:] for m in (1, 0) for y in range(2)])

    def pump(pace=(0, 0)):
        experts.run(pace[0])
        dense.run(pace[1])

    def arrive(m):
        while total - len(dense.queue) < done_at[m]:
            pump((FRONT[0], 1))
        jobs[m].arrived()
        pltpu.make_async_copy(landing[m], weights[m], weight_sems.at[m]).start()

    copies = []

    def emit(i):
        copy = pltpu.make_async_copy(mine[i], outs[i], out_sems.at[i])
        copy.start()
        copies.append(copy)

    def attention(x, row, w_ref, xo, an, qkv, o, pace):
        norm_rows(x, small[row : row + 1, :], an)
        pump(pace)
        for third in range(3):

            def project(n, third=third):
                cols = tile(n + third * 3, 256)
                qkv[:, cols] = nn(an[...], w_ref[:, cols]).astype(BF16)

            loop(3, project)
            pump(pace)
        rows_of = qkv.shape[0] // images
        for image in range(images):
            rows = pl.ds(image * rows_of, rows_of)

            def pair(i, rows=rows):
                q = qkv[rows, tile(i, 128)]
                k = qkv[rows, tile(i + 6, 128)]
                v = qkv[rows, tile(i + 12, 128)]
                first = halves(q.shape)
                zero = jnp.zeros_like(q)
                p0 = head_probs(jnp.where(first, q, zero), k, seq).astype(BF16)
                p1 = head_probs(jnp.where(first, zero, q), k, seq).astype(BF16)
                out = nn(p0, jnp.where(first, v, zero)) + nn(p1, jnp.where(first, zero, v))
                o[rows, tile(i, 128)] = out.astype(BF16)

            for part in range(2):
                loop(3, lambda i, pair=pair, part=part: pair(i + 3 * part))
                pump(pace)

        def outward(n):
            cols = tile(n, 256)
            xo[:, cols] = x[:, cols] + nn(o[...], w_ref[:, tile(n + 9, 256)])

        loop(3, outward)
        pump(pace)

    xf[...] = x0_ref[...].astype(F32)
    arrive(0)
    pl.loop(1, 32)(lambda i: small_copy((p.me + i) % 32, i, (p.me + i) % 32).wait())
    small[...] = jnp.zeros_like(small)
    for d in range(32):
        lanes = slice(24 * d, 24 * d + 24)
        small[0:4, lanes] = small_got[d, 0:4, 0:24]
        small[8:12, lanes] = small_got[d, 4:8, 0:24]
    attention(xf, 0, va0.reshape(WIDTH, HIDDEN), x1, an0, qkv0, o0, FRONT[1])
    for i in (0, 3, 4, 5):
        emit(i)
    norm_rows(x1, small[2:3, :], mn)
    emit(6)
    arrive(1)
    wi = vmi.reshape(WIDTH, HIDDEN)
    for n in range(6):
        cols = pl.ds(n * 512, 512)
        active, bend = gelu_both(nn(mn[...], wi[:, cols]))
        slope[:, cols] = bend.astype(BF16)
        ma[:, cols] = active.astype(BF16)
        pump(FRONT[2])
    emit(7)
    emit(8)
    arrive(2)
    wo = vmo.reshape(HIDDEN, WIDTH)
    for n in range(3):
        cols = pl.ds(n * 256, 256)
        x2[:, cols] = x1[:, cols] + nn(ma[...], wo[:, cols])
        pump(FRONT[3])
    emit(1)
    arrive(3)
    attention(x2, 1, va1.reshape(WIDTH, HIDDEN), x3, an1, qkv1, o1, (FRONT[4], 0))
    for i in (2, 9, 10, 11):
        emit(i)
    norm_rows(x3, small[3:4, :], en)
    route_rows(g4_ref, ids_ref, small, en, aux_ref, pick0, pick1, rx, rd, lambda: pump((FRONT[4], 0)))
    for i in range(12, 18):
        emit(i)
    while experts.step():
        pass
    for job in big:
        job.arrived()
    for job in jobs + big:
        job.finish()
    swap.wait_send()
    for m in range(4):
        pltpu.make_async_copy(landing[m], weights[m], weight_sems.at[m]).wait()
    for copy in copies:
        copy.wait()


def run_front(images, seq, small, wide, tall, x0, g4, ids):
    any_space = pl.BlockSpec(memory_space=pl.ANY)
    vmem = pl.BlockSpec(memory_space=pltpu.VMEM)
    wide_out = struct((4, 2, 2, 48, HIDDEN), BF16)
    tall_out = struct((4, 2, 2, 192, WIDTH), BF16)
    dma = pltpu.SemaphoreType.DMA
    rows = x0.shape[0]
    act, low = struct((rows, WIDTH), F32), struct((rows, WIDTH), BF16)
    qkv, hid = struct((rows, 3 * WIDTH), BF16), struct((rows, HIDDEN), BF16)
    pick, buf = struct((rows, EXPERTS * SLOT), BF16), struct((EXPERTS * SLOT, WIDTH), BF16)
    kept = [act, act, act, low, qkv, low, low, hid, hid, low, qkv, low, low,
            struct((rows, 128), F32), pick, pick, buf, buf]

    def scratch(one):
        return pltpu.VMEM(one.shape, one.dtype)

    return pl.pallas_call(
        functools.partial(front_kernel, images, seq),
        out_shape=[struct((136, WIDTH), F32), wide_out, wide_out, tall_out, wide_out, wide_out,
                   tall_out] + kept,
        in_specs=[vmem] * 6,
        out_specs=[vmem] + [any_space] * 24,
        scratch_shapes=[scratch(one) for one in kept] + [
            scratch(act), scratch(wide_out), scratch(wide_out), scratch(tall_out), scratch(wide_out),
            pltpu.VMEM((3, 48, 1536), BF16),
            pltpu.VMEM((4, 48, 1536), BF16),
            pltpu.VMEM((24, 7 * 1536), F32),
            pltpu.VMEM((32, 8, 128), F32),
            dma((2,)),
            dma((2, 32)),
            dma((4, len(GATHER_SEMS), 8)),
            dma((4, 2)),
            dma((2, len(EXPERT_SEMS), 8)),
            dma((2, 3, 3)),
            dma((18,)),
            dma((4,)),
        ],
        compiler_params=pltpu.CompilerParams(
            collective_id=0, has_side_effects=True, vmem_limit_bytes=63 << 20),
        cost_estimate=pl.CostEstimate(
            flops=9_000_000_000, bytes_accessed=60_000_000, transcendentals=0),
    )(small, wide, tall, x0, g4, ids)


def fast_front(images, seq, smalls, wide, mlp_out, expert_in, expert_out, x0, g4, ids):
    small = jnp.pad(smalls.astype(F32).T, ((0, 0), (0, 128 - smalls.shape[0])))
    mixed = [wide[0], wide[2]]
    one = [mixed[0][0][:, :1536], wide[1][:, :1536], mixed[1][0][:, :1536]]
    two = [mixed[0][0][:, 1536:], mixed[0][1], wide[1][:, 1536:], mixed[1][0][:, 1536:], mixed[1][1]]
    one += [expert_in[:, e, :1536] for e in range(EXPERTS)]
    two += [expert_in[:, e, 1536:] for e in range(EXPERTS)]
    packed = jnp.stack([jnp.concatenate(one, 1), jnp.concatenate(two, 1)]).astype(F32)
    tall = jnp.concatenate([mlp_out[None], expert_out.transpose(1, 0, 2)], 0)
    out = run_front(images, seq, small, packed, tall, x0, g4, ids)
    small, wa0, wmi, wmo, wa1, ein, eout = out[:7]
    return small, (wa0, wmi, wmo, wa1), ein, eout, out[7:23], out[23], out[24]

KINDS = ("wide", "tall", "wide", "tall", "wide", "wide")
WIDE_AT = {2: 2, 4: 1, 5: 0}
LAG = 3
AHEAD = 4
PACE = ((0.65, 0), (0.65, 1.2), (0.65, 1.3), (2, 1))


def plane_part(ref, kind, z, core, half):
    if kind == "wide":
        return ref.at[z, :, :, :, pl.ds(pl.multiple_of(core * 1536 + half * 768, 128), 768)]
    return ref.at[z, :, :, pl.ds(pl.multiple_of(core * 96 + half * 48, 16), 48), :]


def add_into(kept, came, pieces):
    def body(i):
        a, b = kept(i), came(i)
        a[...] = a[...] + b[...]

    if pieces == 1:
        body(0)
    else:
        loop(pieces, body)


class Reduce:
    def __init__(self, place, m, ref, bufs, sems, sink):
        self.p, self.m, self.kind, self.ref = place, m, KINDS[m], ref
        self.bufs, self.sems, self.sink = bufs, sems, sink

    def goal(self, stop):
        z = self.p.z
        if stop == 3:
            return z
        table = ((3, 3, 0, 0), (2, 0, 3, 1), (1, 2, 1, 2))[stop]
        low = jnp.where(z == 0, table[0], table[1])
        return jnp.where(z < 2, low, jnp.where(z == 2, table[2], table[3]))

    def joins(self, stop):
        z = self.p.z
        return (z > 0) & (z < 3) if stop < 3 else z >= 0

    def _send_z(self, half, stop, src):
        p, s = self.p, self.sems
        z = self.goal(stop)
        up = z > p.z
        slot = jnp.where(up | (z != p.z - 1), z, 4)
        return remote(src, self.bufs["z"].at[half, slot], s["zs"].at[half, stop],
                      s["zr"].at[half, slot], jnp.where(up, p.me + 8, p.me - 8))

    def _came(self, half, src, slot):
        p, s = self.p, self.sems
        came = self.bufs["z"].at[half, slot]
        remote(src, came, s["zs"].at[half, 0], s["zr"].at[half, slot], p.sibling).wait_recv()
        return came


class DenseReduce(Reduce):
    def _plane(self, half, stop):
        return plane_part(self.ref, self.kind, self.goal(stop), self.p.core, half)

    def _block(self, half, stop):
        return self._plane(half, stop).at[self.p.y, self.p.x]

    def _pair(self, half, stop):
        p, s = self.p, self.sems
        src = plane_part(self.ref, self.kind, self.goal(stop), 1 - p.core, half)
        return remote(src, self.bufs["near"].at[stop, half], s["ps"].at[stop, half],
                      s["pr"].at[stop, half], p.sibling)

    def start(self):
        for unit in range(3):
            self._pair(unit % 2, unit // 2).start()

    def _first(self, half, stop):
        p, s = self.p, self.sems
        plane = self._plane(half, stop)
        src = plane.at[:, 1 - p.x] if half else plane.at[1 - p.y]
        return remote(src, self.bufs["first"].at[stop, half], s["fs"].at[stop, half],
                      s["fr"].at[stop, half], p.across_x if half else p.across_y)

    def _second(self, half, stop):
        p, s = self.p, self.sems
        plane = self._plane(half, stop)
        src = plane.at[1 - p.y, p.x] if half else plane.at[p.y, 1 - p.x]
        return remote(src, self.bufs["second"].at[stop, half], s["ss"].at[stop, half],
                      s["sr"].at[stop, half], p.across_y if half else p.across_x)

    def stage_one(self, half, stop):
        self._pair(half, stop).wait_recv()
        later = stop * 2 + half + 3
        if later < 8:
            self._pair(later % 2, later // 2).start()
        own, near = self._plane(half, stop), self.bufs["near"].at[stop, half]
        add_into(lambda i: own.at[i // 2, i % 2], lambda i: near.at[i // 2, i % 2], 4)
        self._first(half, stop).start()

    def stage_two(self, half, stop):
        p = self.p
        self._first(half, stop).wait_recv()
        own, came = self._plane(half, stop), self.bufs["first"].at[stop, half]
        if half:
            add_into(lambda i: own.at[i, p.x], lambda i: came.at[i], 2)
        else:
            add_into(lambda i: own.at[p.y, i], lambda i: came.at[i], 2)
        self._second(half, stop).start()

    def stage_three(self, half, stop):
        self._second(half, stop).wait_recv()
        kept, came = self._block(half, stop), self.bufs["second"].at[stop, half]
        add_into(lambda i: kept, lambda i: came, 1)

    def stage_four(self, half, stop):
        p = self.p
        block = self._block(half, stop)
        if stop < 3:

            def join():
                came = self._came(half, block, self.goal(stop))
                add_into(lambda i: block, lambda i: came, 1)

            pl.when(self.joins(stop))(join)
            self._send_z(half, stop, block).start()
            return
        out = self.sink(half)
        out[...] = block[...].astype(F32)

        def last(slot):
            out[...] += self._came(half, block, slot)[...].astype(F32)

        pl.when(p.z > 0)(lambda: last(p.z))
        pl.when(p.z < 3)(lambda: last(4))

    def z_events(self):
        return [functools.partial(self.stage_four, half, stop)
                for stop in range(4) for half in range(2)]

    def finish(self):
        for half in range(2):
            for stop in range(4):
                self._pair(half, stop).wait_send()
                self._first(half, stop).wait_send()
                self._second(half, stop).wait_send()
                if stop < 3:
                    self._send_z(half, stop, self._block(half, stop)).wait_send()


class ExpertReduce(Reduce):
    def _source(self, half, stop):
        return self.ref.at[self.goal(stop), half]

    def _load(self, half, stop):
        return pltpu.make_async_copy(
            self._source(half, stop), self.bufs["own"].at[half], self.sems["load"].at[half])

    def start_load(self, half, stop):
        pl.when(self.joins(stop))(lambda: self._load(half, stop).start())

    def begin(self):
        for half in range(2):
            self.start_load(half, 0)

    def plain_send(self, half, stop):
        p = self.p
        pl.when((p.z == 0) | (p.z == 3))(
            lambda: self._send_z(half, stop, self._source(half, stop)).start())

    def stage_one(self, half, stop):
        p = self.p
        own = self.bufs["own"].at[half]

        def join(slot, into_own):
            came = self._came(half, self._source(half, stop), slot)
            kept, added = (own, came) if into_own else (came, own)
            add_into(lambda i: kept.at[i // 2, i % 2], lambda i: added.at[i // 2, i % 2], 4)

        def middle():
            z = self.goal(stop)
            self._load(half, stop).wait()
            join(z, False)
            self._send_z(half, stop, self.bufs["z"].at[half, z]).start()

        if stop < 3:
            pl.when(self.joins(stop))(middle)
            self.start_load(half, stop + 1)
            return
        self._load(half, stop).wait()
        pl.when(p.z > 0)(lambda: join(p.z, True))
        pl.when(p.z < 3)(lambda: join(4, True))
        for i in range(3):
            self._cross(half, i).start()

    def _cross(self, half, i):
        p, s = self.p, self.sems
        device = (p.across_x, p.across_y, p.across_both)[i]
        chip = device // 2 % 4
        src = self.bufs["own"].at[half, chip // 2, chip % 2]
        return remote(src, self.bufs["cross"].at[half, i], s["cs"].at[half, i], s["cr"].at[half, i], device)

    def crossed(self, half):
        p = self.p
        self.sink(half, p.chip)[...] = self.bufs["own"][half, p.y, p.x].astype(F32)
        for i in range(3):
            self._cross(half, i).wait_recv()
            device = (p.across_x, p.across_y, p.across_both)[i]
            self.sink(half, device // 2 % 4)[...] = self.bufs["cross"][half, i].astype(F32)

    def finish(self):
        for half in range(2):
            for i in range(3):
                self._cross(half, i).wait_send()
            for stop in range(3):
                self._send_z(half, stop, self._source(half, stop)).wait_send()


class Pump:
    def __init__(self):
        self.queue, self.due = [], 0.0

    def add(self, events):
        self.queue += events

    def run(self, count):
        self.due = min(self.due + count, count + 4.0)
        while self.due >= 1 and self.step():
            self.due -= 1

    def step(self):
        if self.queue:
            self.queue.pop(0)()
            return True
        return False


class Belt(Pump):
    def __init__(self, lag, after):
        super().__init__()
        self.units, self.done, self.lag, self.after = [], [0, 0, 0, 0], lag, after

    def add(self, job):
        self.units += [(job, half, stop) for stop in range(4) for half in range(2)]

    def step(self):
        moved = False
        for stage in range(4):
            ahead = self.done[stage - 1] if stage else len(self.units)
            mine = self.done[stage]
            flush = ahead == len(self.units)
            if mine < ahead and (stage == 0 or flush or ahead - mine > self.lag):
                job, half, stop = self.units[mine]
                self.done[stage] += 1
                moved = True
                if stage < 3:
                    (job.stage_one, job.stage_two, job.stage_three)[stage](half, stop)
                else:
                    self.after(job, half, stop)
        return moved


def window(device):
    return jnp.minimum(device * 24 // 128, 4) * 128


def backward_step(
    images, seq,
    g4, small, x3, en_src, aux_src, p0_src, p1_src, y_src, d_src, x2, x1, x0, an1, qkv1, o1, mn, slope, ma, an0, qkv0, o0,
    wa1, wmo, wmi, wa0, sums,
    x4_ref, g_ref, small_out, wide_out, tall_out,
    xf, low, do, dqkv, dn, an_buf, mix_buf, ds,
    dw_wide, dw_tall, near, first, second, z_dense, own, z_expert, cross, done, small_got,
    load_sems, expert_load_sems, pair_sems, plane_sems, zs_sems, zr_sems, cross_sems, small_sems,
    meet, stream_sems, combine_sems, credit,
):
    p = Place()
    greet_all(p, 32)
    jobs = []
    sets = {2: 0, 3: 1, 4: 2, 5: 0}
    refs = {2: dw_wide.at[0], 3: dw_tall, 4: dw_wide.at[1], 5: dw_wide.at[2]}
    for m in range(6):
        sems = {"zs": zs_sems.at[m], "zr": zr_sems.at[m]}
        if m < 2:
            sems.update(cs=cross_sems.at[m, 0], cr=cross_sems.at[m, 1], load=expert_load_sems.at[m])
            bufs = {"z": z_expert.at[m], "cross": cross.at[m], "own": own.at[m]}
            if m == 0:
                def sink(half, e):
                    return done.at[3 + e, :, pl.ds(half * 768, 768)]
            else:
                def sink(half, e):
                    return tall_out.at[1 + e, pl.ds(half * 48, 48), :]
            jobs.append(ExpertReduce(p, m, sums.at[m], bufs, sems, sink))
            continue
        sems.update(ps=pair_sems.at[m - 2, 0], pr=pair_sems.at[m - 2, 1])
        for i, name in enumerate(("fs", "fr", "ss", "sr")):
            sems[name] = plane_sems.at[m - 2, i]
        s = sets[m]
        bufs = {"z": z_dense.at[m - 2], "first": first.at[s], "second": second.at[s], "near": near.at[s]}
        if m in WIDE_AT:
            def sink(half, m=m):
                return done.at[WIDE_AT[m], :, pl.ds(half * 768, 768)]
        else:
            def sink(half):
                return tall_out.at[0, pl.ds(half * 48, 48), :]
        jobs.append(DenseReduce(p, m, refs[m], bufs, sems, sink))
    for m in range(2):
        jobs[m].begin()

    experts = Pump()

    def along(job, half, stop):
        experts.add([functools.partial(job.stage_four, half, stop)])
        if job.m == 2 and (half, stop) == (1, 3):
            for device in (p.sibling, p.across_x, p.across_y):
                pl.semaphore_signal(credit, inc=1, device_id=(device,), device_id_type=MESH_ID)

    dense = Belt(LAG, along)
    units = [(m, half, stop) for stop in range(4) for m in range(2) for half in range(2)]

    def expert_event(i):
        if i + AHEAD < 12:
            m, half, stop = units[i + AHEAD]
            jobs[m].plain_send(half, stop)
        m, half, stop = units[i]
        jobs[m].stage_one(half, stop)

    for m, half, stop in units[:AHEAD]:
        jobs[m].plain_send(half, stop)
    experts.add([functools.partial(expert_event, i) for i in range(16)])
    experts.add([functools.partial(jobs[m].crossed, half) for m in range(2) for half in range(2)])

    def pump(e=1, d=0):
        experts.run(e)
        dense.run(d)

    def load(pairs, sems):
        copies = [pltpu.make_async_copy(src, dst, sems.at[i]) for i, (src, dst) in enumerate(pairs)]
        for copy in copies:
            copy.start()
        return copies

    def attention(w_src, x_src, an_src, qkv_src, o_src, dw, row, ready, pump):
        def scope(w_buf):
            qkv, o = mix_buf.at[:, pl.ds(0, 2304)], mix_buf.at[:, pl.ds(2304, 768)]
            x_to = xf if x_src.dtype == F32 else low
            copies = load([(x_src, x_to), (o_src, o), (an_src, an_buf), (qkv_src, qkv),
                           (w_src.reshape(WIDTH, HIDDEN), w_buf)], load_sems)
            for copy in copies[:2]:
                copy.wait()
            if x_src.dtype != F32:
                xf[...] = low[...].astype(F32)

            def weights_here():
                for copy in copies[2:]:
                    copy.wait()

            attention_backward(
                g_ref, xf, small[row : row + 1, :], w_buf, an_buf, qkv, o, dw, ds, row, images, seq,
                low, do, dqkv, dn, weights_here, ready, pump,
            )

        pl.run_scoped(scope, pltpu.VMEM((WIDTH, HIDDEN), BF16))

    def combine(en, aux_ref, p0, p1, y, d):
        copies = load([(y_src, y), (p0_src, p0), (p1_src, p1), (x3, xf), (aux_src, aux_ref),
                       (en_src, en), (d_src, d)], combine_sems)
        g_ref[...] = g4[...].astype(F32)
        ds[...] = jnp.zeros_like(ds)
        expert_of = lax.broadcasted_iota(jnp.int32, (EXPERTS * SLOT, 128), 0) // SLOT
        spread = (expert_of == lax.broadcasted_iota(jnp.int32, expert_of.shape, 1)).astype(BF16)
        for copy in copies:
            copy.wait()
        aux = aux_ref[...]
        lane = lax.broadcasted_iota(jnp.int32, aux.shape, 1)
        dr = jnp.zeros(aux.shape, F32)
        dn[...] = xf[...]
        for j, pick in ((0, p0), (1, p1)):
            picked = nn(pick[...], y[...])
            dn[...] += aux[:, 8 + j : 9 + j] * picked
            dr += jnp.sum(g_ref[...] * picked, -1, keepdims=True) * nn(pick[...], spread)
            pump(*PACE[0])
        x4_ref[...] = dn[...].astype(BF16)
        chances = jnp.where(lane < EXPERTS, aux, 0.0)
        dlogits = chances * (dr - jnp.sum(chances * dr, -1, keepdims=True))
        dlogits = jnp.where(lane < EXPERTS, dlogits, 0.0).astype(BF16)
        ds[4:8, :] = tn(dlogits, en[...])[0:4, :]
        dn[...] = nn(dlogits, small[8:136, :].astype(BF16)) + nn(p0[...] + p1[...], d[...])
        pump(*PACE[0])
        norm_back(xf, small[3:4, :], dn, g_ref, ds, 3)
        pump(*PACE[0])

    rows = g_ref.shape[0]
    pl.run_scoped(
        combine, pltpu.VMEM((rows, WIDTH), BF16), pltpu.VMEM((rows, 128), F32),
        pltpu.VMEM((rows, EXPERTS * SLOT), BF16), pltpu.VMEM((rows, EXPERTS * SLOT), BF16),
        pltpu.VMEM((EXPERTS * SLOT, WIDTH), BF16), pltpu.VMEM((EXPERTS * SLOT, WIDTH), BF16))
    attention(wa1, x2, an1, qkv1, o1, dw_wide.at[0].reshape(WIDTH, HIDDEN), 1, jobs[2].start,
              lambda: pump(*PACE[0]))
    dense.add(jobs[2])

    def feed_forward(wo_buf, wi_buf, slope_buf, ma_buf):
        wo, wi = wmo.reshape(HIDDEN, WIDTH), wmi.reshape(WIDTH, HIDDEN)
        dwo, dwi = dw_tall.reshape(HIDDEN, WIDTH), dw_wide.at[1].reshape(WIDTH, HIDDEN)
        first_loads = load([(x1, xf), (mn, an_buf)], load_sems)

        def chunk(n):
            cols = pl.ds(n * 512, 512)
            slot = n % 2
            return load([(wo.at[cols, :], wo_buf.at[slot]), (wi.at[:, cols], wi_buf.at[slot]),
                         (slope.at[:, cols], slope_buf.at[slot]), (ma.at[:, cols], ma_buf.at[slot])],
                        stream_sems.at[slot])

        coming = chunk(0)
        low[...] = g_ref[...].astype(BF16)
        dn[...] = jnp.zeros_like(dn)
        for copy in first_loads:
            copy.wait()
        for n in range(6):
            for copy in coming:
                copy.wait()
            if n < 5:
                coming = chunk(n + 1)
            slot = n % 2
            cols = pl.ds(n * 512, 512)
            dwo[cols, :] = tn(ma_buf[slot], low[...]).astype(BF16)
            dact = nt(low[...], wo_buf[slot])
            dh = (slope_buf[slot].astype(F32) * dact).astype(BF16)
            dwi[:, cols] = tn(an_buf[...], dh).astype(BF16)
            dn[...] += nt(dh, wi_buf[slot])
            pump(*PACE[1])
        jobs[3].start()
        jobs[4].start()
        norm_back(x1_buf, small[2:3, :], dn, g_ref, ds, 2)

    x1_buf = xf
    pl.run_scoped(
        feed_forward, pltpu.VMEM((2, 512, WIDTH), BF16), pltpu.VMEM((2, WIDTH, 512), BF16),
        pltpu.VMEM((2, rows, 512), BF16), pltpu.VMEM((2, rows, 512), BF16))
    dense.add(jobs[3])
    dense.add(jobs[4])

    def last_ready():
        assert dense.done[3] >= 8
        pl.semaphore_wait(credit, 3)
        jobs[5].start()

    attention(wa0, x0, an0, qkv0, o0, dw_wide.at[2].reshape(WIDTH, HIDDEN), 0, last_ready,
              lambda: pump(*PACE[2]))

    def small_copy(to, i, source):
        return remote(ds.at[:, pl.ds(pl.multiple_of(window(to), 128), 256)], small_got.at[source],
                      small_sems.at[0, i], small_sems.at[1, source], to)

    pl.loop(1, 32)(lambda i: small_copy((p.me + i) % 32, i, p.me).start())
    dense.add(jobs[5])
    while dense.done[3] < len(dense.units) or experts.queue:
        pump(*PACE[3])
    mine = pl.ds(pl.multiple_of(p.core * 1536, 128), 1536)
    swap = remote(
        done.at[:, pl.ds(pl.multiple_of((1 - p.core) * 24, 8), 24), :], wide_out.at[:, :, mine],
        meet.at[0], meet.at[1], p.sibling)
    swap.start()
    keep = pltpu.make_async_copy(
        done.at[:, pl.ds(pl.multiple_of(p.core * 24, 8), 24), :], wide_out.at[:, :, mine],
        meet.at[2])
    keep.start()
    pl.loop(1, 32)(lambda i: small_copy((p.me + i) % 32, i, (p.me + i) % 32).wait())
    small_got[p.me] = ds[:, pl.ds(pl.multiple_of(window(p.me), 128), 256)]
    small_out[...] = jnp.sum(small_got[...], 0)
    for m in range(6):
        jobs[m].finish()
    keep.wait()
    swap.wait()


def run_backward_step(images, seq, args):
    any_space = pl.BlockSpec(memory_space=pl.ANY)
    vmem = pl.BlockSpec(memory_space=pltpu.VMEM)
    dma = pltpu.SemaphoreType.DMA
    piece = (48, 768)
    rows = args[0].shape[0]
    act, low = pltpu.VMEM((rows, WIDTH), F32), pltpu.VMEM((rows, WIDTH), BF16)
    return pl.pallas_call(
        functools.partial(backward_step, images, seq),
        out_shape=[struct((rows, WIDTH), BF16), struct((rows, WIDTH), F32), struct((8, 256), F32),
                   struct((7, 24, HIDDEN), F32), struct((5, 96, 768), F32)],
        in_specs=[vmem] * 2 + [any_space] * (len(args) - 2),
        out_specs=[vmem, vmem, vmem, any_space, vmem],
        scratch_shapes=[
            act, low, low, pltpu.VMEM((rows, 3 * WIDTH), BF16), act, low,
            pltpu.VMEM((rows, HIDDEN), BF16), pltpu.VMEM((8, WIDTH), F32),
            pltpu.VMEM((3, 4, 2, 2, 48, HIDDEN), BF16),
            pltpu.VMEM((4, 2, 2, 192, WIDTH), BF16),
            pltpu.VMEM((3, 4, 2, 2, 2) + piece, BF16),
            pltpu.VMEM((3, 4, 2, 2) + piece, BF16),
            pltpu.VMEM((3, 4, 2) + piece, BF16),
            pltpu.VMEM((4, 2, 5) + piece, BF16),
            pltpu.VMEM((2, 2, 2, 2) + piece, BF16),
            pltpu.VMEM((2, 2, 5, 2, 2) + piece, BF16),
            pltpu.VMEM((2, 2, 3) + piece, BF16),
            pltpu.VMEM((7, 48, 1536), F32),
            pltpu.VMEM((32, 8, 256), F32),
            dma((5,)),
            dma((2, 2)),
            dma((4, 2, 4, 2)),
            dma((4, 4, 4, 2)),
            dma((6, 2, 4)),
            dma((6, 2, 5)),
            dma((2, 2, 2, 3)),
            dma((2, 32)),
            dma((3,)),
            dma((2, 4)),
            dma((7,)),
            pltpu.SemaphoreType.REGULAR,
        ],
        compiler_params=pltpu.CompilerParams(
            collective_id=1, has_side_effects=True, vmem_limit_bytes=63 << 20),
        cost_estimate=pl.CostEstimate(
            flops=20_000_000_000, bytes_accessed=60_000_000, transcendentals=0),
    )(*args)


def fast_backward(images, seq, x0, g4, small, weights, saved, y_back, d_back, sums):
    wa0, wmi, wmo, wa1 = weights
    x1, x2, x3, an0, qkv0, o0, mn, slope, ma, an1, qkv1, o1, en, aux, p0, p1 = saved
    x4, g, dsmall, wide, tall = run_backward_step(images, seq, [
        g4, small, x3, en, aux, p0, p1, y_back, d_back, x2, x1, x0, an1, qkv1, o1, mn, slope, ma,
        an0, qkv0, o0, wa1, wmo, wmi, wa0, sums])
    me = lax.axis_index("fsdp")
    dsmall = lax.dynamic_slice(dsmall, (0, me * 24 - window(me)), (8, 24))
    return x4, g, (dsmall.T, wide[0], wide[1], tall[0], wide[2],
                   wide[3:].transpose(1, 0, 2), tall[1:].transpose(1, 0, 2))


def expert_step(
    rows_x, rows_d, ein, eout,
    y_back, d_back, sums,
    wi, wo, got_x, got_d, active, slope, y_out, d_out, acc, dwi, dwo, near,
    load_sems, own_sems, move_sems, pair_sems, sum_sems,
):
    p = Place()
    greet_all(p, 32)
    chips = [device // 2 % 4 for device in (p.me, p.across_x, p.across_y, p.across_both)]
    devices = (None, p.across_x, p.across_y, p.across_both)
    loads = [pltpu.make_async_copy(src, dst, load_sems.at[i])
             for i, (src, dst) in enumerate(((ein, wi), (eout, wo)))]

    def inward(t, i):
        src, dst = ((rows_x, got_x), (rows_d, got_d))[t]
        if i == 0:
            return pltpu.make_async_copy(src.at[p.chip], dst.at[p.chip], own_sems.at[t])
        return remote(src.at[chips[i]], dst.at[p.chip], move_sems.at[t, 0, i], move_sems.at[t, 1, i],
                      devices[i])

    def outward(t, i):
        src, dst = ((y_out, y_back), (d_out, d_back))[t]
        if i == 0:
            return pltpu.make_async_copy(src.at[p.chip], dst.at[p.chip], own_sems.at[2 + t])
        return remote(src.at[chips[i]], dst.at[p.chip], move_sems.at[2 + t, 0, i],
                      move_sems.at[2 + t, 1, i], devices[i])

    for i in range(4):
        inward(0, i).start()
    for copy in loads:
        copy.start()
    inward(1, 0).start()
    for copy in loads:
        copy.wait()
    wide = wi.reshape(WIDTH, HIDDEN)
    tall = wo.reshape(HIDDEN, WIDTH)
    for i in range(4):
        chip = chips[i]
        if i == 0:
            inward(0, 0).wait()
        else:
            inward(0, i).wait_recv()
        if i == 1:
            for j in range(1, 4):
                inward(1, j).start()
        acc[...] = jnp.zeros_like(acc)

        def forward(n):
            cols = tile(n, 512)
            ea, sl = gelu_both(nn(got_x[chip], wide[:, cols]))
            ea = ea.astype(BF16)
            active[chip, :, cols] = ea
            slope[chip, :, cols] = sl.astype(BF16)
            acc[...] += nn(ea, tall[cols, :])

        loop(6, forward)
        y_out[chip] = acc[...].astype(BF16)
        outward(0, i).start()
    for i in range(4):
        chip = chips[i]
        if i == 0:
            inward(1, 0).wait()
        else:
            inward(1, i).wait_recv()
        acc[...] = jnp.zeros_like(acc)

        def backward(n):
            cols = tile(n, 512)
            dh = slope[chip, :, cols].astype(F32) * nt(got_d[chip], tall[cols, :])
            dh = dh.astype(BF16)
            slope[chip, :, cols] = dh
            acc[...] += nt(dh, wide[:, cols])

        loop(6, backward)
        d_out[chip] = acc[...].astype(BF16)
        outward(1, i).start()
    every = EXPERTS * SLOT
    x_all, d_all = got_x.reshape(every, WIDTH), got_d.reshape(every, WIDTH)
    ea_all, dh_all = active.reshape(every, HIDDEN), slope.reshape(every, HIDDEN)
    dwi_all, dwo_all = dwi.reshape(WIDTH, HIDDEN), dwo.reshape(HIDDEN, WIDTH)

    def weights(n):
        cols = tile(n, 512)
        dwo_all[cols, :] = tn(ea_all[:, cols], d_all[...]).astype(BF16)
        dwi_all[:, cols] = tn(x_all[...], dh_all[:, cols]).astype(BF16)

    loop(6, weights)
    pairs = [(m, z, half) for z in range(4) for m in range(2) for half in range(2)]

    def pair(m, z, half):
        src = plane_part((dwi, dwo)[m], KINDS[m], z, 1 - p.core, half)
        return remote(src, near.at[m, z, half], pair_sems.at[m, z, half, 0],
                      pair_sems.at[m, z, half, 1], p.sibling)

    def result(m, z, half):
        return pltpu.make_async_copy(near.at[m, z, half], sums.at[m, z, half], sum_sems.at[m, z, half])

    for one in pairs:
        pair(*one).start()
    for m, z, half in pairs:
        pair(m, z, half).wait_recv()
        own = plane_part((dwi, dwo)[m], KINDS[m], z, p.core, half)
        came = near.at[m, z, half]
        add_into(lambda i: came.at[i // 2, i % 2], lambda i: own.at[i // 2, i % 2], 4)
        result(m, z, half).start()
    for one in pairs:
        result(*one).wait()
        pair(*one).wait_send()
    for t in range(2):
        outward(t, 0).wait()
        for i in range(1, 4):
            inward(t, i).wait_send()
            outward(t, i).wait()


def run_expert_step(rows_x, rows_d, ein, eout):
    any_space = pl.BlockSpec(memory_space=pl.ANY)
    dma = pltpu.SemaphoreType.DMA
    rows = (EXPERTS, SLOT, WIDTH)
    y, d, sums = pl.pallas_call(
        expert_step,
        out_shape=[struct(rows, BF16)] * 2 + [struct((2, 4, 2, 2, 2, 48, 768), BF16)],
        in_specs=[any_space] * 4,
        out_specs=[any_space] * 3,
        scratch_shapes=[
            pltpu.VMEM((4, 2, 2, 48, HIDDEN), BF16),
            pltpu.VMEM((4, 2, 2, 192, WIDTH), BF16),
            pltpu.VMEM(rows, BF16),
            pltpu.VMEM(rows, BF16),
            pltpu.VMEM((EXPERTS, SLOT, HIDDEN), BF16),
            pltpu.VMEM((EXPERTS, SLOT, HIDDEN), BF16),
            pltpu.VMEM(rows, BF16),
            pltpu.VMEM(rows, BF16),
            pltpu.VMEM((SLOT, WIDTH), F32),
            pltpu.VMEM((4, 2, 2, 48, HIDDEN), BF16),
            pltpu.VMEM((4, 2, 2, 192, WIDTH), BF16),
            pltpu.VMEM((2, 4, 2, 2, 2, 48, 768), BF16),
            dma((2,)),
            dma((4,)),
            dma((4, 2, 4)),
            dma((2, 4, 2, 2)),
            dma((2, 4, 2)),
        ],
        compiler_params=pltpu.CompilerParams(
            collective_id=2, has_side_effects=True, vmem_limit_bytes=VMEM_BYTES),
        cost_estimate=pl.CostEstimate(
            flops=30_000_000_000, bytes_accessed=40_000_000, transcendentals=0),
    )(rows_x.reshape(rows), rows_d.reshape(rows), ein, eout)
    flat = (EXPERTS * SLOT, WIDTH)
    return y.reshape(flat), d.reshape(flat), sums


def local(
    patches, live_count, expert_ids, attn_gain, attn_qkv, attn_out, mlp_gain, mlp_in, mlp_out,
    moe_gain, router, expert_in, expert_out, cotangent,
):
    images, seq, width = patches.shape
    padded = -(-seq // 16) * 16
    n = lax.axis_size("fsdp")
    group_size = n // EXPERTS
    group = lax.axis_index("fsdp") // group_size
    alive = jnp.arange(images, dtype=jnp.int32) < live_count[0]

    def pad(values, fill=0):
        values = values.reshape(images, seq, -1)
        values = jnp.pad(values, ((0, 0), (0, padded - seq), (0, 0)), constant_values=fill)
        return values.reshape(images * padded, -1)

    x0 = pad(patches)
    g4 = pad(jnp.where(alive[:, None, None], cotangent, jnp.zeros_like(cotangent)))
    ids = pad(expert_ids, -1)
    smalls = jnp.concatenate(
        [attn_gain, mlp_gain[:, None], moe_gain[:, None], router], 1
    )
    wide = [(attn_qkv[:, 0], attn_out[:, 0]), mlp_in, (attn_qkv[:, 1], attn_out[:, 1])]
    if n == 32:
        small, weights, w_in, w_out, saved, rows_x, rows_d = fast_front(
            images, seq, smalls, wide, mlp_out, expert_in, expert_out, x0, g4, ids)
    else:
        small, wides, talls, w_in, w_out = plain_gather(
            smalls, [jnp.concatenate(wide[0], 1), mlp_in, jnp.concatenate(wide[2], 1)],
            [mlp_out], expert_in, expert_out)
        small = small.astype(F32).T
        small = jnp.concatenate(
            [small[:4], jnp.zeros((4, width), F32), small[4:], jnp.zeros((124, width), F32)], 0
        )
        weights = (wides[0], wides[1], talls[0], wides[2])
        out = run_forward(images, seq, x0, g4, ids, small, *weights)
        saved, rows_x, rows_d = out[:16], out[16], out[17]

    def exchange(rows):
        rows = rows.reshape(EXPERTS, SLOT, width)
        return group_exchange(rows, group_size, group).reshape(EXPERTS * SLOT, width)

    if n == 32:
        y_back, d_back, sums = run_expert_step(rows_x, rows_d, w_in, w_out)
        x4, grad, shards = fast_backward(
            images, seq, x0, g4, small, weights, saved, y_back, d_back, sums)
        dsmall, d0, dmi, dmo, d1, de_in, de_out = shards
    else:
        y, dx, dw_in, dw_out = run_expert(exchange(rows_x), exchange(rows_d), w_in, w_out)
        x4, grad, d0, dmi, dmo, d1, dsmall = run_backward(
            images, seq, x0, g4, small, weights, saved, exchange(y), exchange(dx)
        )
        d0, dmi, dmo, d1 = (plain_reduce(g).astype(F32) for g in (d0, dmi, dmo, d1))
        de_in, de_out = (plain_reduce_expert(g).astype(F32) for g in (dw_in, dw_out))
        dsmall = lax.psum_scatter(dsmall.T, "fsdp", scatter_dimension=0, tiled=True)

    def unpad(values):
        return values.reshape(images, padded, width)[:, :seq]

    block_out = jnp.where(alive[:, None, None], unpad(x4), 0.0).astype(BF16)
    return (
        block_out,
        unpad(grad),
        dsmall[:, 0:2],
        jnp.stack([d0[:, :2304], d1[:, :2304]], 1),
        jnp.stack([d0[:, 2304:], d1[:, 2304:]], 1),
        dsmall[:, 2],
        dmi,
        dmo,
        dsmall[:, 3],
        dsmall[:, 4:8],
        de_in,
        de_out,
    )


def solution(mesh):
    def lead(rank):
        return P("fsdp", *([None] * (rank - 1)))

    return jax.shard_map(
        local,
        mesh=mesh,
        in_specs=tuple(lead(r) for r in (3, 1, 2, 2, 3, 3, 1, 2, 2, 1, 2, 3, 3, 3)),
        out_specs=tuple(lead(r) for r in (3, 3, 2, 3, 3, 1, 2, 2, 1, 2, 3, 3)),
        check_vma=False,
    )
```

```python
import functools

import jax
import jax.numpy as jnp
from jax import lax
from jax.experimental import pallas as pl
from jax.experimental.pallas import tpu as pltpu
from jax.sharding import PartitionSpec as P

HEADS = 12
HEAD_DIM = 64
EXPERTS = 4
CAP = 247
SLOT = 256
WIDTH = 768
HIDDEN = 3072
NORM_EPSILON = 1e-06
VMEM_BYTES = 60 << 20
F32 = jnp.float32
BF16 = jnp.bfloat16


def nn(left, right):
    return lax.dot_general(left, right, (((1,), (0,)), ((), ())), preferred_element_type=F32)


def nt(left, right):
    return lax.dot_general(left, right, (((1,), (1,)), ((), ())), preferred_element_type=F32)


def tn(left, right):
    return lax.dot_general(left, right, (((0,), (0,)), ((), ())), preferred_element_type=F32)


def tile(index, size):
    return pl.ds(pl.multiple_of(index * size, size), size)


def loop(count, body):
    pl.loop(0, count)(body)


def norm_parts(values):
    center = values - jnp.mean(values, -1, keepdims=True)
    spread = jnp.mean(center * center, -1, keepdims=True)
    scale = lax.rsqrt(spread + NORM_EPSILON)
    return center * scale, scale


def norm_rows(x_ref, gain, out_ref, block=32):
    def body(i):
        rows = tile(i, block)
        unit, _ = norm_parts(x_ref[rows, :])
        out_ref[rows, :] = (unit * gain).astype(BF16)

    loop(x_ref.shape[0] // block, body)


def norm_back(x_ref, gain, dn_ref, g_ref, dgain_ref, row, block=32):
    def body(i, total):
        rows = tile(i, block)
        unit, scale = norm_parts(x_ref[rows, :])
        dn = dn_ref[rows, :]
        scaled = dn * gain
        mean_one = jnp.mean(scaled, -1, keepdims=True)
        mean_two = jnp.mean(scaled * unit, -1, keepdims=True)
        g_ref[rows, :] = g_ref[rows, :] + scale * (scaled - mean_one - unit * mean_two)
        return total + jnp.sum((dn * unit).reshape(block // 8, 8, WIDTH), 0)

    total = lax.fori_loop(0, x_ref.shape[0] // block, body, jnp.zeros((8, WIDTH), F32))
    dgain_ref[row : row + 1, :] = jnp.sum(total, 0, keepdims=True)


def gelu_both(u):
    c = 0.7978845608
    square = u * u
    t = jnp.tanh(c * u * (1.0 + 0.044715 * square))
    half = 0.5 * (1.0 + t)
    slope = half + 0.5 * u * (1.0 - t * t) * (c + (3 * 0.044715 * c) * square)
    return u * half, slope


def halves(shape):
    lane = lax.broadcasted_iota(jnp.int32, shape, 1)
    return lane < HEAD_DIM


def head_probs(q, k, seq):
    scores = nt(q, k) * HEAD_DIM ** (-0.5)
    key = lax.broadcasted_iota(jnp.int32, scores.shape, 1)
    scores = jnp.where(key < seq, scores, -1e30)
    top = jnp.max(scores, -1, keepdims=True)
    e = jnp.exp(scores - top)
    return e / jnp.sum(e, -1, keepdims=True)


def attention_heads(qkv_ref, o_ref, images, seq):
    rows_of = qkv_ref.shape[0] // images
    for image in range(images):
        rows = pl.ds(image * rows_of, rows_of)

        def pair(p, rows=rows):
            q = qkv_ref[rows, tile(p, 128)]
            k = qkv_ref[rows, tile(p + 6, 128)]
            v = qkv_ref[rows, tile(p + 12, 128)]
            first = halves(q.shape)
            zero = jnp.zeros_like(q)
            p0 = head_probs(jnp.where(first, q, zero), k, seq).astype(BF16)
            p1 = head_probs(jnp.where(first, zero, q), k, seq).astype(BF16)
            out = nn(p0, jnp.where(first, v, zero)) + nn(p1, jnp.where(first, zero, v))
            o_ref[rows, tile(p, 128)] = out.astype(BF16)

        loop(6, pair)


def attention_forward(x_ref, gain, w_ref, xo_ref, an_ref, qkv_ref, o_ref, images, seq):
    norm_rows(x_ref, gain, an_ref)

    def project(n):
        qkv_ref[:, tile(n, 256)] = nn(an_ref[...], w_ref[:, tile(n, 256)]).astype(BF16)

    loop(9, project)
    attention_heads(qkv_ref, o_ref, images, seq)

    def outward(n):
        cols = tile(n, 256)
        xo_ref[:, cols] = x_ref[:, cols] + nn(o_ref[...], w_ref[:, tile(n + 9, 256)])

    loop(3, outward)


def attention_backward(
    g_ref, x_ref, gain, w_ref, an_ref, qkv_ref, o_ref, dw_ref, dgain_ref, row, images, seq,
    low_ref, do_ref, dqkv_ref, dn_ref, weights_here=lambda: None, ready=lambda: None,
    pump=lambda: None,
):
    rows_of = qkv_ref.shape[0] // images
    low_ref[...] = g_ref[...].astype(BF16)

    def outward(n):
        dw_ref[:, tile(n + 9, 256)] = tn(o_ref[...], low_ref[:, tile(n, 256)]).astype(BF16)

    loop(3, outward)
    pump()
    weights_here()

    def outward_rows(n):
        do_ref[:, tile(n, 256)] = nt(low_ref[...], w_ref[tile(n, 256), 2304:]).astype(BF16)

    loop(3, outward_rows)
    pump()
    for image in range(images):
        rows = pl.ds(image * rows_of, rows_of)

        def pair(p, rows=rows):
            q = qkv_ref[rows, tile(p, 128)]
            k = qkv_ref[rows, tile(p + 6, 128)]
            v = qkv_ref[rows, tile(p + 12, 128)]
            d = do_ref[rows, tile(p, 128)]
            first = halves(q.shape)
            zero = jnp.zeros_like(q)
            dq = dk = dv = None
            for mine in (first, ~first):
                qm, km, dm = (jnp.where(mine, t, zero) for t in (q, k, d))
                probs = head_probs(qm, k, seq)
                dp = nt(dm, v)
                inner = jnp.sum(dp * probs, -1, keepdims=True)
                ds = (probs * (dp - inner)).astype(BF16)
                one = (nn(ds, km), tn(ds, qm), tn(probs.astype(BF16), dm))
                dq, dk, dv = one if dq is None else (dq + one[0], dk + one[1], dv + one[2])
            scale = HEAD_DIM ** (-0.5)
            dqkv_ref[rows, tile(p, 128)] = (dq * scale).astype(BF16)
            dqkv_ref[rows, tile(p + 6, 128)] = (dk * scale).astype(BF16)
            dqkv_ref[rows, tile(p + 12, 128)] = dv.astype(BF16)

        loop(3, pair)
        pump()
        loop(3, lambda p, pair=pair: pair(p + 3))
        pump()

    for third in range(3):

        def inward(n, third=third):
            cols = tile(n + third * 3, 256)
            dw_ref[:, cols] = tn(an_ref[...], dqkv_ref[:, cols]).astype(BF16)

        loop(3, inward)
        pump()
    ready()

    def normed(n):
        dn_ref[:, tile(n, 256)] = nt(dqkv_ref[...], w_ref[tile(n, 256), :2304])

    loop(3, normed)
    pump()
    norm_back(x_ref, gain, dn_ref, g_ref, dgain_ref, row)
    pump()


def route_rows(g4_ref, ids_ref, small_ref, en_ref, aux_ref, g0_ref, g1_ref, rx_ref, rd_ref, pump):
    rows = en_ref.shape[0]
    logits = nt(en_ref[...], small_ref[8:136, :].astype(BF16))
    lane = lax.broadcasted_iota(jnp.int32, logits.shape, 1)
    logits = jnp.where(lane < EXPERTS, logits, -1e30)
    e = jnp.exp(logits - jnp.max(logits, -1, keepdims=True))
    chances = e / jnp.sum(e, -1, keepdims=True)
    ids = ids_ref[...]
    chosen = [(ids[:, j : j + 1] == lane).astype(F32) for j in range(2)]
    row_i = lax.broadcasted_iota(jnp.int32, (rows, rows), 0)
    row_j = lax.broadcasted_iota(jnp.int32, (rows, rows), 1)
    earlier = nn((row_j < row_i).astype(BF16), (chosen[0] + chosen[1]).astype(BF16))
    place = lax.broadcasted_iota(jnp.int32, (rows, EXPERTS * SLOT), 1)
    gates = []
    for j, pick_ref in ((0, g0_ref), (1, g1_ref)):
        gates.append(jnp.sum(chances * chosen[j], -1, keepdims=True))
        inside = jnp.sum(earlier * chosen[j], -1, keepdims=True).astype(jnp.int32)
        slot = jnp.where(ids[:, j : j + 1] >= 0, ids[:, j : j + 1] * SLOT + inside, -1)
        pick_ref[...] = (slot == place).astype(BF16)
    aux = jnp.where(lane < EXPERTS, chances, 0.0)
    aux = jnp.where(lane == 8, gates[0], aux)
    aux_ref[...] = jnp.where(lane == 9, gates[1], aux)

    def fill(n):
        cols = tile(n, 256)
        both = g0_ref[:, cols] + g1_ref[:, cols]
        rx_ref[cols, :] = tn(both, en_ref[...]).astype(BF16)
        g4 = g4_ref[...].astype(F32)
        one = tn(g0_ref[:, cols], (g4 * gates[0]).astype(BF16))
        two = tn(g1_ref[:, cols], (g4 * gates[1]).astype(BF16))
        rd_ref[cols, :] = (one + two).astype(BF16)

    pump()
    loop(2, fill)
    pump()
    loop(2, lambda n: fill(n + 2))
    pump()


def forward_kernel(
    images, seq,
    x0_ref, g4_ref, ids_ref, small_ref, wa0_ref, wmi_ref, wmo_ref, wa1_ref,
    x1_ref, x2_ref, x3_ref, an0_ref, qkv0_ref, o0_ref, mn_ref, slope_ref, ma_ref,
    an1_ref, qkv1_ref, o1_ref, en_ref, aux_ref, g0_ref, g1_ref, rx_ref, rd_ref,
    xf_ref,
):
    xf_ref[...] = x0_ref[...].astype(F32)
    attention_forward(
        xf_ref, small_ref[0:1, :], wa0_ref, x1_ref, an0_ref, qkv0_ref, o0_ref, images, seq
    )
    norm_rows(x1_ref, small_ref[2:3, :], mn_ref)
    x2_ref[...] = x1_ref[...]

    def dense(n):
        cols = tile(n, 512)
        active, slope = gelu_both(nn(mn_ref[...], wmi_ref[:, cols]))
        slope_ref[:, cols] = slope.astype(BF16)
        active = active.astype(BF16)
        ma_ref[:, cols] = active
        x2_ref[...] += nn(active, wmo_ref[cols, :])

    loop(6, dense)
    attention_forward(
        x2_ref, small_ref[1:2, :], wa1_ref, x3_ref, an1_ref, qkv1_ref, o1_ref, images, seq
    )
    norm_rows(x3_ref, small_ref[3:4, :], en_ref)
    route_rows(
        g4_ref, ids_ref, small_ref, en_ref, aux_ref, g0_ref, g1_ref, rx_ref, rd_ref, lambda: None
    )


def expert_kernel(x_ref, d_ref, wi_ref, wo_ref, y_ref, dx_ref, dwi_ref, dwo_ref, yf_ref, df_ref):
    yf_ref[...] = jnp.zeros_like(yf_ref)
    df_ref[...] = jnp.zeros_like(df_ref)

    def body(n):
        cols = tile(n, 512)
        active, slope = gelu_both(nn(x_ref[...], wi_ref[:, cols]))
        active = active.astype(BF16)
        yf_ref[...] += nn(active, wo_ref[cols, :])
        dwo_ref[cols, :] = tn(active, d_ref[...]).astype(BF16)
        dh = (slope * nt(d_ref[...], wo_ref[cols, :])).astype(BF16)
        df_ref[...] += nt(dh, wi_ref[:, cols])
        dwi_ref[:, cols] = tn(x_ref[...], dh).astype(BF16)

    loop(6, body)
    y_ref[...] = yf_ref[...].astype(BF16)
    dx_ref[...] = df_ref[...].astype(BF16)


def combine_kernel(
    g4_ref, small_ref, x3_ref, en_ref, aux_ref, g0_ref, g1_ref, yr_ref, dr_ref,
    x4_ref, g_ref, ds_ref,
    dn_ref,
):
    aux = aux_ref[...]
    lane = lax.broadcasted_iota(jnp.int32, aux.shape, 1)
    g_ref[...] = g4_ref[...].astype(F32)
    x4_ref[...] = x3_ref[...]
    dgates = []
    chosen = []
    expert_of = lax.broadcasted_iota(jnp.int32, (EXPERTS * SLOT, 128), 0) // SLOT
    spread = (expert_of == lax.broadcasted_iota(jnp.int32, expert_of.shape, 1)).astype(BF16)
    for j, pick_ref in ((0, g0_ref), (1, g1_ref)):
        picked = nn(pick_ref[...], yr_ref[...])
        x4_ref[...] += aux[:, 8 + j : 9 + j] * picked
        dgates.append(jnp.sum(g_ref[...] * picked, -1, keepdims=True))
        chosen.append(nn(pick_ref[...], spread))
    dr = dgates[0] * chosen[0] + dgates[1] * chosen[1]
    chances = jnp.where(lane < EXPERTS, aux, 0.0)
    dlogits = chances * (dr - jnp.sum(chances * dr, -1, keepdims=True))
    dlogits = jnp.where(lane < EXPERTS, dlogits, 0.0).astype(BF16)
    ds_ref[...] = jnp.zeros_like(ds_ref)
    ds_ref[4:8, :] = tn(dlogits, en_ref[...])[0:4, :]
    dn_ref[...] = nn(dlogits, small_ref[8:136, :].astype(BF16)) + nn(
        g0_ref[...] + g1_ref[...], dr_ref[...]
    )
    norm_back(x3_ref, small_ref[3:4, :], dn_ref, g_ref, ds_ref, 3)


def attention_back_kernel(
    images, seq, row,
    g_in_ref, small_ref, x_ref, w_ref, an_ref, qkv_ref, o_ref,
    g_ref, dw_ref, ds_ref,
    xf_ref, low_ref, do_ref, dqkv_ref, dn_ref,
):
    g_ref[...] = g_in_ref[...]
    xf_ref[...] = x_ref[...].astype(F32)
    ds_ref[...] = jnp.zeros_like(ds_ref)
    attention_backward(
        g_ref, xf_ref, small_ref[row : row + 1, :], w_ref, an_ref, qkv_ref, o_ref, dw_ref,
        ds_ref, row, images, seq, low_ref, do_ref, dqkv_ref, dn_ref,
    )


def dense_back_kernel(
    g_in_ref, small_ref, x1_ref, wmi_ref, wmo_ref, mn_ref, slope_ref, ma_ref,
    g_ref, dwmi_ref, dwmo_ref, ds_ref,
    low_ref, dn_ref,
):
    g_ref[...] = g_in_ref[...]
    ds_ref[...] = jnp.zeros_like(ds_ref)
    low_ref[...] = g_ref[...].astype(BF16)
    dn_ref[...] = jnp.zeros_like(dn_ref)

    def dense(n):
        cols = tile(n, 512)
        dwmo_ref[cols, :] = tn(ma_ref[:, cols], low_ref[...]).astype(BF16)
        dact = nt(low_ref[...], wmo_ref[cols, :])
        dh = (slope_ref[:, cols].astype(F32) * dact).astype(BF16)
        dwmi_ref[:, cols] = tn(mn_ref[...], dh).astype(BF16)
        dn_ref[...] += nt(dh, wmi_ref[:, cols])

    loop(6, dense)
    norm_back(x1_ref, small_ref[2:3, :], dn_ref, g_ref, ds_ref, 2)


def struct(shape, dtype):
    return jax.ShapeDtypeStruct(shape, dtype)


def call(body, outs, scratch, args, flops):
    total = sum(a.size * a.dtype.itemsize for a in list(args) + list(outs))
    return pl.pallas_call(
        body,
        out_shape=outs,
        in_specs=[pl.BlockSpec(memory_space=pltpu.VMEM)] * len(args),
        out_specs=[pl.BlockSpec(memory_space=pltpu.VMEM)] * len(outs),
        scratch_shapes=scratch,
        compiler_params=pltpu.CompilerParams(vmem_limit_bytes=VMEM_BYTES),
        cost_estimate=pl.CostEstimate(flops=flops, bytes_accessed=total, transcendentals=0),
    )(*args)


def run_forward(images, seq, x0, g4, ids, small, wa0, wmi, wmo, wa1):
    rows = x0.shape[0]
    act = struct((rows, WIDTH), F32)
    low = struct((rows, WIDTH), BF16)
    qkv = struct((rows, 3 * WIDTH), BF16)
    hid = struct((rows, HIDDEN), BF16)
    pick = struct((rows, EXPERTS * SLOT), BF16)
    buf = struct((EXPERTS * SLOT, WIDTH), BF16)
    outs = [act, act, act, low, qkv, low, low, hid, hid, low, qkv, low, low,
            struct((rows, 128), F32), pick, pick, buf, buf]
    return call(
        functools.partial(forward_kernel, images, seq), outs,
        [pltpu.VMEM((rows, WIDTH), F32)],
        [x0, g4, ids, small, wa0, wmi, wmo, wa1], 8_000_000_000,
    )


def run_expert(x, d, wi, wo):
    outs = [struct(x.shape, BF16), struct(x.shape, BF16), struct(wi.shape, BF16), struct(wo.shape, BF16)]
    return call(
        expert_kernel, outs, [pltpu.VMEM(x.shape, F32), pltpu.VMEM(x.shape, F32)],
        [x, d, wi, wo], 30_000_000_000,
    )


def run_backward(images, seq, x0, g4, small, weights, saved, y_back, d_back):
    rows = x0.shape[0]
    act = struct((rows, WIDTH), F32)
    wide, tall = struct((WIDTH, HIDDEN), BF16), struct((HIDDEN, WIDTH), BF16)
    row = struct((8, WIDTH), F32)
    wa0, wmi, wmo, wa1 = weights
    x1, x2, x3, an0, qkv0, o0, mn, slope, ma, an1, qkv1, o1, en, aux, p0, p1 = saved
    full = pltpu.VMEM((rows, WIDTH), F32)
    low = pltpu.VMEM((rows, WIDTH), BF16)
    mixed = pltpu.VMEM((rows, 3 * WIDTH), BF16)
    x4, g, s0 = call(
        combine_kernel, [act, act, row], [full],
        [g4, small, x3, en, aux, p0, p1, y_back, d_back], 3_000_000_000,
    )
    g, dwa1, s1 = call(
        functools.partial(attention_back_kernel, images, seq, 1), [act, wide, row],
        [full, low, low, mixed, full], [g, small, x2, wa1, an1, qkv1, o1], 5_000_000_000,
    )
    g, dwmi, dwmo, s2 = call(
        dense_back_kernel, [act, wide, tall, row], [low, full],
        [g, small, x1, wmi, wmo, mn, slope, ma], 8_000_000_000,
    )
    g, dwa0, s3 = call(
        functools.partial(attention_back_kernel, images, seq, 0), [act, wide, row],
        [full, low, low, mixed, full], [g, small, x0, wa0, an0, qkv0, o0], 5_000_000_000,
    )
    return x4, g, dwa0, dwmi, dwmo, dwa1, s0 + s1 + s2 + s3


def gather_rows(piece):
    return lax.all_gather(piece, "fsdp", axis=0, tiled=True)


def shift(values, steps):
    count = lax.axis_size("fsdp")
    return lax.ppermute(values, "fsdp", [(s, (s + steps) % count) for s in range(count)])


def group_exchange(rows, group_size, group_id):
    out = jnp.zeros_like(rows)
    for offset in range(EXPERTS):
        piece = lax.dynamic_index_in_dim(rows, (group_id + offset) % EXPERTS, 0, keepdims=False)
        if offset:
            piece = shift(piece, offset * group_size)
        out = lax.dynamic_update_index_in_dim(out, piece, (group_id - offset) % EXPERTS, 0)
    return out


def plain_gather(smalls, wide, tall, e_in, e_out):
    n = lax.axis_size("fsdp")
    group_size = n // EXPERTS
    group = lax.axis_index("fsdp") // group_size
    small = gather_rows(smalls)
    wides = [gather_rows(w) for w in wide]
    talls = [gather_rows(w) for w in tall]
    big_in = lax.dynamic_index_in_dim(gather_rows(e_in), group, 1, keepdims=False)
    big_out = lax.dynamic_index_in_dim(gather_rows(e_out), group, 1, keepdims=False)
    return small, wides, talls, big_in, big_out


def plain_reduce(grad):
    return lax.psum_scatter(grad, "fsdp", scatter_dimension=0, tiled=True)


def plain_reduce_expert(grad):
    n = lax.axis_size("fsdp")
    group_size = n // EXPERTS
    group = lax.axis_index("fsdp") // group_size
    full = jnp.zeros((grad.shape[0], EXPERTS, grad.shape[1]), BF16)
    full = lax.dynamic_update_index_in_dim(full, grad, group, 1)
    return plain_reduce(full)

MESH_ID = pl.DeviceIdType.MESH


class Place:
    def __init__(self):
        self.me = lax.axis_index("fsdp")
        self.core = self.me % 2
        self.x = self.me // 2 % 2
        self.y = self.me // 4 % 2
        self.z = self.me // 8
        self.sibling = self.me + 1 - 2 * self.core
        self.across_x = self.me + 2 - 4 * self.x
        self.across_y = self.me + 4 - 8 * self.y
        self.across_both = self.across_x + 4 - 8 * self.y
        self.chip = self.me // 2 % 4


def remote(src, dst, send, recv, device):
    return pltpu.make_async_remote_copy(
        src_ref=src, dst_ref=dst, send_sem=send, recv_sem=recv,
        device_id=(device,), device_id_type=MESH_ID,
    )


def greet_all(place, count):
    barrier = pltpu.get_barrier_semaphore()

    def hello(i):
        pl.semaphore_signal(
            barrier, inc=1, device_id=((place.me + i) % count,), device_id_type=MESH_ID
        )

    pl.loop(1, count)(hello)
    pl.semaphore_wait(barrier, count - 1)


DENSE = ("wide", "wide", "tall", "wide")


def part(ref, kind, z, y, x, core, half):
    if kind == "wide":
        return ref.at[z, y, x, :, pl.ds(pl.multiple_of(core * 1536 + half * 768, 128), 768)]
    return ref.at[z, y, x, pl.ds(pl.multiple_of(core * 96 + half * 48, 16), 48), :]


def own_part(mine, kind, half):
    if kind == "wide":
        return mine.at[:, pl.ds(half * 768, 768)]
    return mine.at[pl.ds(half * 48, 48), :]


class Gather:
    def __init__(self, place, kind, mine, out, sems):
        self.p, self.kind, self.mine, self.out, self.sems = place, kind, mine, out, sems

    def _z(self, half, source, up):
        p = self.p
        where = part(self.out, self.kind, source, p.y, p.x, p.core, half)
        return where, 0 if up else 1

    def _slot(self, half, source):
        return half * 4 + source

    def start_own(self):
        p, s = self.p, self.sems
        for half in range(2):
            there = part(self.out, self.kind, p.z, p.y, p.x, p.core, half)
            src = own_part(self.mine, self.kind, half)
            pltpu.make_async_copy(src, there, s["own"].at[half]).start()
            self._along_z(half, p.z, src, True, True)

    def _copy_z(self, half, source, src, up):
        p, s = self.p, self.sems
        slot = self._slot(half, source)
        there = part(self.out, self.kind, source, p.y, p.x, p.core, half)
        name = "zu" if up else "zd"
        return remote(there if src is None else src, there, s[name].at[slot], s["zr"].at[slot],
                      p.me + 8 if up else p.me - 8)

    def _along_z(self, half, source, src, up, down):
        p = self.p
        if up:
            pl.when(p.z < 3)(lambda: self._copy_z(half, source, src, True).start())
        if down:
            pl.when(p.z > 0)(lambda: self._copy_z(half, source, src, False).start())

    def _first(self, half, source, src=None):
        p, s = self.p, self.sems
        slot = self._slot(half, source)
        there = part(self.out, self.kind, source, p.y, p.x, p.core, half)
        return remote(there if src is None else src, there, s["fs"].at[slot], s["fr"].at[slot],
                      p.across_y if half else p.across_x)

    def _line(self, half, source):
        p = self.p
        if self.kind == "wide":
            rows, cols = slice(None), pl.ds(pl.multiple_of(p.core * 1536 + half * 768, 128), 768)
        else:
            rows, cols = pl.ds(pl.multiple_of(p.core * 96 + half * 48, 16), 48), slice(None)
        if half:
            return self.out.at[source, :, p.x, rows, cols]
        return self.out.at[source, p.y, :, rows, cols]

    def _second(self, half, source):
        p, s = self.p, self.sems
        slot = self._slot(half, source)
        line = self._line(half, source)
        return remote(line, line, s["ss"].at[slot], s["sr"].at[slot],
                      p.across_x if half else p.across_y)

    def _hand(self, half, source):
        p, s = self.p, self.sems
        slot = self._slot(half, source)
        if self.kind == "wide":
            rows, cols = slice(None), pl.ds(pl.multiple_of(p.core * 1536 + half * 768, 128), 768)
        else:
            rows, cols = pl.ds(pl.multiple_of(p.core * 96 + half * 48, 16), 48), slice(None)
        plane = self.out.at[source, :, :, rows, cols]
        return remote(plane, plane, s["hs"].at[slot], s["hr"].at[slot], p.sibling)

    def valid(self, k):
        z = self.p.z + k
        return (z >= 0) & (z <= 3)

    def stage_one(self, half, k):
        source = self.p.z + k

        def run():
            if k == 0:
                src = own_part(self.mine, self.kind, half)
                self._first(half, source, src).start()
                there = part(self.out, self.kind, source, self.p.y, self.p.x, self.p.core, half)
                pltpu.make_async_copy(src, there, self.sems["own"].at[half]).wait()
                return
            self._copy_z(half, source, None, k < 0).wait_recv()
            self._along_z(half, source, None, k < 0, k > 0)
            self._first(half, source).start()

        pl.when(self.valid(k))(run)

    def stage_two(self, half, k):
        source = self.p.z + k

        def run():
            self._first(half, source).wait_recv()
            self._second(half, source).start()

        pl.when(self.valid(k))(run)

    def stage_three(self, half, k):
        source = self.p.z + k

        def run():
            self._second(half, source).wait_recv()
            self._hand(half, source).start()

        pl.when(self.valid(k))(run)

    def arrived(self):
        for half in range(2):
            for source in range(4):
                self._hand(half, source).wait_recv()

    def finish(self):
        p = self.p
        for half in range(2):
            for source in range(4):
                self._first(half, source).wait_send()
                self._second(half, source).wait_send()
                self._hand(half, source).wait_send()
                up = (source <= p.z) & (p.z < 3)
                down = (source >= p.z) & (p.z > 0)
                pl.when(up)(lambda: self._copy_z(half, source, None, True).wait_send())
                pl.when(down)(lambda: self._copy_z(half, source, None, False).wait_send())


GATHER_SEMS = ("zu", "zd", "zr", "fs", "fr", "ss", "sr", "hs", "hr")


def expert_block(ref, kind, z, y, core):
    if kind == "wide":
        return ref.at[z, y, :, :, pl.ds(pl.multiple_of(core * 1536, 128), 1536)]
    return ref.at[z, y, :, pl.ds(pl.multiple_of(core * 96, 16), 96), :]


def expert_piece(ref, kind, z, y, x, core):
    if kind == "wide":
        return ref.at[z, y, x, :, pl.ds(pl.multiple_of(core * 1536, 128), 1536)]
    return ref.at[z, y, x, pl.ds(pl.multiple_of(core * 96, 16), 96), :]


class ExpertGather:
    def __init__(self, place, kind, mine, out, sems):
        self.p, self.kind, self.mine, self.out, self.sems = place, kind, mine, out, sems

    def _cross(self, i):
        p, s = self.p, self.sems
        there = expert_piece(self.out, self.kind, p.z, p.y, p.x, p.core)
        device = (p.across_x, p.across_y, p.across_both)[i]
        expert = device // 2 % 4
        return remote(self.mine.at[expert], there, s["cs"].at[i], s["cr"].at[i], device)

    def _own(self):
        p = self.p
        there = expert_piece(self.out, self.kind, p.z, p.y, p.x, p.core)
        return pltpu.make_async_copy(self.mine.at[p.chip], there, self.sems["own"].at[0])

    def start_own(self):
        self._own().start()
        for i in range(3):
            self._cross(i).start()

    def _copy_z(self, y, source, up):
        p, s = self.p, self.sems
        slot = y * 4 + source
        block = expert_block(self.out, self.kind, source, y, p.core)
        return remote(block, block, s["zu" if up else "zd"].at[slot], s["zr"].at[slot],
                      p.me + 8 if up else p.me - 8)

    def _hand(self, y, source):
        p, s = self.p, self.sems
        slot = y * 4 + source
        block = expert_block(self.out, self.kind, source, y, p.core)
        return remote(block, block, s["hs"].at[slot], s["hr"].at[slot], p.sibling)

    def crossed(self):
        p = self.p
        self._own().wait()
        for i in range(3):
            self._cross(i).wait_recv()
        for y in range(2):
            pl.when(p.z < 3)(lambda: self._copy_z(y, p.z, True).start())
            pl.when(p.z > 0)(lambda: self._copy_z(y, p.z, False).start())
            self._hand(y, p.z).start()

    def stage(self, y, k):
        p = self.p
        source = p.z + k

        def run():
            self._copy_z(y, source, k < 0).wait_recv()
            if k < 0:
                pl.when(p.z < 3)(lambda: self._copy_z(y, source, True).start())
            else:
                pl.when(p.z > 0)(lambda: self._copy_z(y, source, False).start())
            self._hand(y, source).start()

        pl.when((source >= 0) & (source <= 3))(run)

    def arrived(self):
        for y in range(2):
            for source in range(4):
                self._hand(y, source).wait_recv()

    def finish(self):
        p = self.p
        for i in range(3):
            self._cross(i).wait_send()
        for y in range(2):
            for source in range(4):
                self._hand(y, source).wait_send()
                up = (source <= p.z) & (p.z < 3)
                down = (source >= p.z) & (p.z > 0)
                pl.when(up)(lambda: self._copy_z(y, source, True).wait_send())
                pl.when(down)(lambda: self._copy_z(y, source, False).wait_send())


EXPERT_SEMS = ("zu", "zd", "zr", "hs", "hr")
STEPS = (0, -1, 1, -2, 2, -3, 3)

FRONT = (0.05, (0.3, 4.7), (0.4, 7), (0.4, 14), 1)


def front_kernel(
    images, seq,
    small_in, wide_in, tall_in, x0_ref, g4_ref, ids_ref,
    small, wa0, wmi, wmo, wa1, ein, eout, *rest,
):
    outs, mine, tools = rest[:18], rest[18:36], rest[36:]
    (x1, x2, x3, an0, qkv0, o0, mn, slope, ma, an1, qkv1, o1, en, aux_ref, pick0, pick1, rx, rd) = mine
    (xf, va0, vmi, vmo, va1, wide_mine, expert_mine, from_sibling, small_got,
     meet, small_sems, gather_sems, own_sems, expert_sems, cross_sems, out_sems, weight_sems) = tools
    p = Place()
    greet_all(p, 32)
    swap = remote(wide_in.at[1 - p.core], from_sibling, meet.at[0], meet.at[1], p.sibling)
    swap.start()

    def small_copy(to, i, source):
        return remote(small_in, small_got.at[source], small_sems.at[0, i], small_sems.at[1, source], to)

    pl.loop(1, 32)(lambda i: small_copy((p.me + i) % 32, i, p.me).start())
    small_got[p.me] = small_in[...]
    landing, weights = (va0, vmi, vmo, va1), (wa0, wmi, wmo, wa1)
    jobs = []
    for m, kind in enumerate(DENSE):
        sems = {name: gather_sems.at[m, i] for i, name in enumerate(GATHER_SEMS)}
        sems["own"] = own_sems.at[m]
        piece = tall_in.at[0] if kind == "tall" else wide_mine.at[(0, 1, None, 2)[m]]
        jobs.append(Gather(p, kind, piece, landing[m], sems))
    big = []
    for m, kind in enumerate(("wide", "tall")):
        sems = {name: expert_sems.at[m, i] for i, name in enumerate(EXPERT_SEMS)}
        sems["cs"], sems["cr"], sems["own"] = (
            cross_sems.at[m, 0], cross_sems.at[m, 1], cross_sems.at[m, 2])
        piece = tall_in.at[pl.ds(1, 4)] if kind == "tall" else expert_mine
        big.append(ExpertGather(p, kind, piece, (ein, eout)[m], sems))
    jobs[2].start_own()
    swap.wait_recv()

    def merge(m, out):
        cols = pl.ds(m * 1536, 1536)
        kept = wide_in[p.core, :, cols]
        came = from_sibling[:, cols]
        upper = jnp.where(p.core == 0, kept, came)
        lower = jnp.where(p.core == 0, came, kept)
        out[...] = jnp.concatenate([upper, lower], 0).astype(BF16)

    merge(0, wide_mine.at[0])
    jobs[0].start_own()
    big[1].start_own()
    for e in range(4):
        merge(3 + e, expert_mine.at[e])
    big[0].start_own()
    merge(1, wide_mine.at[1])
    jobs[1].start_own()
    merge(2, wide_mine.at[2])
    jobs[3].start_own()

    dense, experts = Pump(), Pump()
    order = [(m, k, half) for m in range(4) for k in STEPS for half in range(2)]
    done_at = {}
    for i in range(len(order) + 24):
        for stage, lag in ((0, 0), (1, 12), (2, 24)):
            if 0 <= i - lag < len(order):
                m, k, half = order[i - lag]
                name = ("stage_one", "stage_two", "stage_three")[stage]
                dense.add([functools.partial(getattr(jobs[m], name), half, k)])
                if stage == 2:
                    done_at[m] = len(dense.queue)
    total = len(dense.queue)

    def crossed():
        big[1].crossed()
        big[0].crossed()

    experts.add([crossed])
    experts.add([functools.partial(big[m].stage, y, k) for k in STEPS[1:] for m in (1, 0) for y in range(2)])

    def pump(pace=(0, 0)):
        experts.run(pace[0])
        dense.run(pace[1])

    def arrive(m):
        while total - len(dense.queue) < done_at[m]:
            pump((FRONT[0], 1))
        jobs[m].arrived()
        pltpu.make_async_copy(landing[m], weights[m], weight_sems.at[m]).start()

    copies = []

    def emit(i):
        copy = pltpu.make_async_copy(mine[i], outs[i], out_sems.at[i])
        copy.start()
        copies.append(copy)

    def attention(x, row, w_ref, xo, an, qkv, o, pace):
        norm_rows(x, small[row : row + 1, :], an)
        pump(pace)
        for third in range(3):

            def project(n, third=third):
                cols = tile(n + third * 3, 256)
                qkv[:, cols] = nn(an[...], w_ref[:, cols]).astype(BF16)

            loop(3, project)
            pump(pace)
        rows_of = qkv.shape[0] // images
        for image in range(images):
            rows = pl.ds(image * rows_of, rows_of)

            def pair(i, rows=rows):
                q = qkv[rows, tile(i, 128)]
                k = qkv[rows, tile(i + 6, 128)]
                v = qkv[rows, tile(i + 12, 128)]
                first = halves(q.shape)
                zero = jnp.zeros_like(q)
                p0 = head_probs(jnp.where(first, q, zero), k, seq).astype(BF16)
                p1 = head_probs(jnp.where(first, zero, q), k, seq).astype(BF16)
                out = nn(p0, jnp.where(first, v, zero)) + nn(p1, jnp.where(first, zero, v))
                o[rows, tile(i, 128)] = out.astype(BF16)

            for part in range(2):
                loop(3, lambda i, pair=pair, part=part: pair(i + 3 * part))
                pump(pace)

        def outward(n):
            cols = tile(n, 256)
            xo[:, cols] = x[:, cols] + nn(o[...], w_ref[:, tile(n + 9, 256)])

        loop(3, outward)
        pump(pace)

    xf[...] = x0_ref[...].astype(F32)
    arrive(0)
    pl.loop(1, 32)(lambda i: small_copy((p.me + i) % 32, i, (p.me + i) % 32).wait())
    small[...] = jnp.zeros_like(small)
    for d in range(32):
        lanes = slice(24 * d, 24 * d + 24)
        small[0:4, lanes] = small_got[d, 0:4, 0:24]
        small[8:12, lanes] = small_got[d, 4:8, 0:24]
    attention(xf, 0, va0.reshape(WIDTH, HIDDEN), x1, an0, qkv0, o0, FRONT[1])
    for i in (0, 3, 4, 5):
        emit(i)
    norm_rows(x1, small[2:3, :], mn)
    emit(6)
    arrive(1)
    wi = vmi.reshape(WIDTH, HIDDEN)
    for n in range(6):
        cols = pl.ds(n * 512, 512)
        active, bend = gelu_both(nn(mn[...], wi[:, cols]))
        slope[:, cols] = bend.astype(BF16)
        ma[:, cols] = active.astype(BF16)
        pump(FRONT[2])
    emit(7)
    emit(8)
    arrive(2)
    wo = vmo.reshape(HIDDEN, WIDTH)
    for n in range(3):
        cols = pl.ds(n * 256, 256)
        x2[:, cols] = x1[:, cols] + nn(ma[...], wo[:, cols])
        pump(FRONT[3])
    emit(1)
    arrive(3)
    attention(x2, 1, va1.reshape(WIDTH, HIDDEN), x3, an1, qkv1, o1, (FRONT[4], 0))
    for i in (2, 9, 10, 11):
        emit(i)
    norm_rows(x3, small[3:4, :], en)
    route_rows(g4_ref, ids_ref, small, en, aux_ref, pick0, pick1, rx, rd, lambda: pump((FRONT[4], 0)))
    for i in range(12, 18):
        emit(i)
    while experts.step():
        pass
    for job in big:
        job.arrived()
    for job in jobs + big:
        job.finish()
    swap.wait_send()
    for m in range(4):
        pltpu.make_async_copy(landing[m], weights[m], weight_sems.at[m]).wait()
    for copy in copies:
        copy.wait()


def run_front(images, seq, small, wide, tall, x0, g4, ids):
    any_space = pl.BlockSpec(memory_space=pl.ANY)
    vmem = pl.BlockSpec(memory_space=pltpu.VMEM)
    wide_out = struct((4, 2, 2, 48, HIDDEN), BF16)
    tall_out = struct((4, 2, 2, 192, WIDTH), BF16)
    dma = pltpu.SemaphoreType.DMA
    rows = x0.shape[0]
    act, low = struct((rows, WIDTH), F32), struct((rows, WIDTH), BF16)
    qkv, hid = struct((rows, 3 * WIDTH), BF16), struct((rows, HIDDEN), BF16)
    pick, buf = struct((rows, EXPERTS * SLOT), BF16), struct((EXPERTS * SLOT, WIDTH), BF16)
    kept = [act, act, act, low, qkv, low, low, hid, hid, low, qkv, low, low,
            struct((rows, 128), F32), pick, pick, buf, buf]

    def scratch(one):
        return pltpu.VMEM(one.shape, one.dtype)

    return pl.pallas_call(
        functools.partial(front_kernel, images, seq),
        out_shape=[struct((136, WIDTH), F32), wide_out, wide_out, tall_out, wide_out, wide_out,
                   tall_out] + kept,
        in_specs=[vmem] * 6,
        out_specs=[vmem] + [any_space] * 24,
        scratch_shapes=[scratch(one) for one in kept] + [
            scratch(act), scratch(wide_out), scratch(wide_out), scratch(tall_out), scratch(wide_out),
            pltpu.VMEM((3, 48, 1536), BF16),
            pltpu.VMEM((4, 48, 1536), BF16),
            pltpu.VMEM((24, 7 * 1536), F32),
            pltpu.VMEM((32, 8, 128), F32),
            dma((2,)),
            dma((2, 32)),
            dma((4, len(GATHER_SEMS), 8)),
            dma((4, 2)),
            dma((2, len(EXPERT_SEMS), 8)),
            dma((2, 3, 3)),
            dma((18,)),
            dma((4,)),
        ],
        compiler_params=pltpu.CompilerParams(
            collective_id=0, has_side_effects=True, vmem_limit_bytes=63 << 20),
        cost_estimate=pl.CostEstimate(
            flops=9_000_000_000, bytes_accessed=60_000_000, transcendentals=0),
    )(small, wide, tall, x0, g4, ids)


def fast_front(images, seq, smalls, wide, mlp_out, expert_in, expert_out, x0, g4, ids):
    small = jnp.pad(smalls.astype(F32).T, ((0, 0), (0, 128 - smalls.shape[0])))
    mixed = [wide[0], wide[2]]
    one = [mixed[0][0][:, :1536], wide[1][:, :1536], mixed[1][0][:, :1536]]
    two = [mixed[0][0][:, 1536:], mixed[0][1], wide[1][:, 1536:], mixed[1][0][:, 1536:], mixed[1][1]]
    one += [expert_in[:, e, :1536] for e in range(EXPERTS)]
    two += [expert_in[:, e, 1536:] for e in range(EXPERTS)]
    packed = jnp.stack([jnp.concatenate(one, 1), jnp.concatenate(two, 1)]).astype(F32)
    tall = jnp.concatenate([mlp_out[None], expert_out.transpose(1, 0, 2)], 0)
    out = run_front(images, seq, small, packed, tall, x0, g4, ids)
    small, wa0, wmi, wmo, wa1, ein, eout = out[:7]
    return small, (wa0, wmi, wmo, wa1), ein, eout, out[7:23], out[23], out[24]

KINDS = ("wide", "tall", "wide", "tall", "wide", "wide")
WIDE_AT = {2: 2, 4: 1, 5: 0}
LAG = 3
AHEAD = 4
PACE = ((0.65, 0), (0.8, 1.2), (1.0, 1.3), (2, 1))


def plane_part(ref, kind, z, core, half):
    if kind == "wide":
        return ref.at[z, :, :, :, pl.ds(pl.multiple_of(core * 1536 + half * 768, 128), 768)]
    return ref.at[z, :, :, pl.ds(pl.multiple_of(core * 96 + half * 48, 16), 48), :]


def add_into(kept, came, pieces):
    def body(i):
        a, b = kept(i), came(i)
        a[...] = a[...] + b[...]

    if pieces == 1:
        body(0)
    else:
        loop(pieces, body)


class Reduce:
    def __init__(self, place, m, ref, bufs, sems, sink):
        self.p, self.m, self.kind, self.ref = place, m, KINDS[m], ref
        self.bufs, self.sems, self.sink = bufs, sems, sink

    def goal(self, stop):
        z = self.p.z
        if stop == 3:
            return z
        table = ((3, 3, 0, 0), (2, 0, 3, 1), (1, 2, 1, 2))[stop]
        low = jnp.where(z == 0, table[0], table[1])
        return jnp.where(z < 2, low, jnp.where(z == 2, table[2], table[3]))

    def joins(self, stop):
        z = self.p.z
        return (z > 0) & (z < 3) if stop < 3 else z >= 0

    def _send_z(self, half, stop, src):
        p, s = self.p, self.sems
        z = self.goal(stop)
        up = z > p.z
        slot = jnp.where(up | (z != p.z - 1), z, 4)
        return remote(src, self.bufs["z"].at[half, slot], s["zs"].at[half, stop],
                      s["zr"].at[half, slot], jnp.where(up, p.me + 8, p.me - 8))

    def _came(self, half, src, slot):
        p, s = self.p, self.sems
        came = self.bufs["z"].at[half, slot]
        remote(src, came, s["zs"].at[half, 0], s["zr"].at[half, slot], p.sibling).wait_recv()
        return came


class DenseReduce(Reduce):
    def _plane(self, half, stop):
        return plane_part(self.ref, self.kind, self.goal(stop), self.p.core, half)

    def _block(self, half, stop):
        return self._plane(half, stop).at[self.p.y, self.p.x]

    def _pair(self, half, stop):
        p, s = self.p, self.sems
        src = plane_part(self.ref, self.kind, self.goal(stop), 1 - p.core, half)
        return remote(src, self.bufs["near"].at[stop, half], s["ps"].at[stop, half],
                      s["pr"].at[stop, half], p.sibling)

    def start(self):
        for unit in range(3):
            self._pair(unit % 2, unit // 2).start()

    def _first(self, half, stop):
        p, s = self.p, self.sems
        plane = self._plane(half, stop)
        src = plane.at[:, 1 - p.x] if half else plane.at[1 - p.y]
        return remote(src, self.bufs["first"].at[stop, half], s["fs"].at[stop, half],
                      s["fr"].at[stop, half], p.across_x if half else p.across_y)

    def _second(self, half, stop):
        p, s = self.p, self.sems
        plane = self._plane(half, stop)
        src = plane.at[1 - p.y, p.x] if half else plane.at[p.y, 1 - p.x]
        return remote(src, self.bufs["second"].at[stop, half], s["ss"].at[stop, half],
                      s["sr"].at[stop, half], p.across_y if half else p.across_x)

    def stage_one(self, half, stop):
        self._pair(half, stop).wait_recv()
        later = stop * 2 + half + 3
        if later < 8:
            self._pair(later % 2, later // 2).start()
        own, near = self._plane(half, stop), self.bufs["near"].at[stop, half]
        add_into(lambda i: own.at[i // 2, i % 2], lambda i: near.at[i // 2, i % 2], 4)
        self._first(half, stop).start()

    def stage_two(self, half, stop):
        p = self.p
        self._first(half, stop).wait_recv()
        own, came = self._plane(half, stop), self.bufs["first"].at[stop, half]
        if half:
            add_into(lambda i: own.at[i, p.x], lambda i: came.at[i], 2)
        else:
            add_into(lambda i: own.at[p.y, i], lambda i: came.at[i], 2)
        self._second(half, stop).start()

    def stage_three(self, half, stop):
        self._second(half, stop).wait_recv()
        kept, came = self._block(half, stop), self.bufs["second"].at[stop, half]
        add_into(lambda i: kept, lambda i: came, 1)

    def stage_four(self, half, stop):
        p = self.p
        block = self._block(half, stop)
        if stop < 3:

            def join():
                came = self._came(half, block, self.goal(stop))
                add_into(lambda i: block, lambda i: came, 1)

            pl.when(self.joins(stop))(join)
            self._send_z(half, stop, block).start()
            return
        out = self.sink(half)
        out[...] = block[...].astype(F32)

        def last(slot):
            out[...] += self._came(half, block, slot)[...].astype(F32)

        pl.when(p.z > 0)(lambda: last(p.z))
        pl.when(p.z < 3)(lambda: last(4))

    def z_events(self):
        return [functools.partial(self.stage_four, half, stop)
                for stop in range(4) for half in range(2)]

    def finish(self):
        for half in range(2):
            for stop in range(4):
                self._pair(half, stop).wait_send()
                self._first(half, stop).wait_send()
                self._second(half, stop).wait_send()
                if stop < 3:
                    self._send_z(half, stop, self._block(half, stop)).wait_send()


class ExpertReduce(Reduce):
    def _source(self, half, stop):
        return self.ref.at[self.goal(stop), half]

    def _load(self, half, stop):
        return pltpu.make_async_copy(
            self._source(half, stop), self.bufs["own"].at[half], self.sems["load"].at[half])

    def start_load(self, half, stop):
        pl.when(self.joins(stop))(lambda: self._load(half, stop).start())

    def begin(self):
        for half in range(2):
            self.start_load(half, 0)

    def plain_send(self, half, stop):
        p = self.p
        pl.when((p.z == 0) | (p.z == 3))(
            lambda: self._send_z(half, stop, self._source(half, stop)).start())

    def stage_one(self, half, stop):
        p = self.p
        own = self.bufs["own"].at[half]

        def join(slot, into_own):
            came = self._came(half, self._source(half, stop), slot)
            kept, added = (own, came) if into_own else (came, own)
            add_into(lambda i: kept.at[i // 2, i % 2], lambda i: added.at[i // 2, i % 2], 4)

        def middle():
            z = self.goal(stop)
            self._load(half, stop).wait()
            join(z, False)
            self._send_z(half, stop, self.bufs["z"].at[half, z]).start()

        if stop < 3:
            pl.when(self.joins(stop))(middle)
            self.start_load(half, stop + 1)
            return
        self._load(half, stop).wait()
        pl.when(p.z > 0)(lambda: join(p.z, True))
        pl.when(p.z < 3)(lambda: join(4, True))
        for i in range(3):
            self._cross(half, i).start()

    def _cross(self, half, i):
        p, s = self.p, self.sems
        device = (p.across_x, p.across_y, p.across_both)[i]
        chip = device // 2 % 4
        src = self.bufs["own"].at[half, chip // 2, chip % 2]
        return remote(src, self.bufs["cross"].at[half, i], s["cs"].at[half, i], s["cr"].at[half, i], device)

    def crossed(self, half):
        p = self.p
        self.sink(half, p.chip)[...] = self.bufs["own"][half, p.y, p.x].astype(F32)
        for i in range(3):
            self._cross(half, i).wait_recv()
            device = (p.across_x, p.across_y, p.across_both)[i]
            self.sink(half, device // 2 % 4)[...] = self.bufs["cross"][half, i].astype(F32)

    def finish(self):
        for half in range(2):
            for i in range(3):
                self._cross(half, i).wait_send()
            for stop in range(3):
                self._send_z(half, stop, self._source(half, stop)).wait_send()


class Pump:
    def __init__(self):
        self.queue, self.due = [], 0.0

    def add(self, events):
        self.queue += events

    def run(self, count):
        self.due = min(self.due + count, count + 4.0)
        while self.due >= 1 and self.step():
            self.due -= 1

    def step(self):
        if self.queue:
            self.queue.pop(0)()
            return True
        return False


class Belt(Pump):
    def __init__(self, lag, after):
        super().__init__()
        self.units, self.done, self.lag, self.after = [], [0, 0, 0, 0], lag, after

    def add(self, job):
        self.units += [(job, half, stop) for stop in range(4) for half in range(2)]

    def step(self):
        moved = False
        for stage in range(4):
            ahead = self.done[stage - 1] if stage else len(self.units)
            mine = self.done[stage]
            flush = ahead == len(self.units)
            if mine < ahead and (stage == 0 or flush or ahead - mine > self.lag):
                job, half, stop = self.units[mine]
                self.done[stage] += 1
                moved = True
                if stage < 3:
                    (job.stage_one, job.stage_two, job.stage_three)[stage](half, stop)
                else:
                    self.after(job, half, stop)
        return moved


def backward_step(
    images, seq,
    g4, small, x3, en_src, aux_src, p0_src, p1_src, y_src, d_src, x2, x1, x0, an1, qkv1, o1, mn, slope, ma, an0, qkv0, o0,
    wa1, wmo, wmi, wa0, sums,
    x4_ref, g_ref, small_out, wide_out, tall_out,
    xf, low, do, dqkv, dn, an_buf, mix_buf, ds,
    dw_wide, dw_tall, near, first, second, z_dense, own, z_expert, cross, done, small_got, tiles,
    load_sems, expert_load_sems, pair_sems, plane_sems, zs_sems, zr_sems, cross_sems, small_sems,
    meet, stream_sems, combine_sems, credit,
):
    p = Place()
    greet_all(p, 32)
    jobs = []
    sets = {2: 0, 3: 1, 4: 2, 5: 0}
    refs = {2: dw_wide.at[0], 3: dw_tall, 4: dw_wide.at[1], 5: dw_wide.at[2]}
    for m in range(6):
        sems = {"zs": zs_sems.at[m], "zr": zr_sems.at[m]}
        if m < 2:
            sems.update(cs=cross_sems.at[m, 0], cr=cross_sems.at[m, 1], load=expert_load_sems.at[m])
            bufs = {"z": z_expert.at[m], "cross": cross.at[m], "own": own.at[m]}
            if m == 0:
                def sink(half, e):
                    return done.at[3 + e, :, pl.ds(half * 768, 768)]
            else:
                def sink(half, e):
                    return tall_out.at[1 + e, pl.ds(half * 48, 48), :]
            jobs.append(ExpertReduce(p, m, sums.at[m], bufs, sems, sink))
            continue
        sems.update(ps=pair_sems.at[m - 2, 0], pr=pair_sems.at[m - 2, 1])
        for i, name in enumerate(("fs", "fr", "ss", "sr")):
            sems[name] = plane_sems.at[m - 2, i]
        s = sets[m]
        bufs = {"z": z_dense.at[m - 2], "first": first.at[s], "second": second.at[s], "near": near.at[s]}
        if m in WIDE_AT:
            def sink(half, m=m):
                return done.at[WIDE_AT[m], :, pl.ds(half * 768, 768)]
        else:
            def sink(half):
                return tall_out.at[0, pl.ds(half * 48, 48), :]
        jobs.append(DenseReduce(p, m, refs[m], bufs, sems, sink))
    for m in range(2):
        jobs[m].begin()

    experts = Pump()

    def along(job, half, stop):
        experts.add([functools.partial(job.stage_four, half, stop)])
        if job.m == 2 and (half, stop) == (1, 3):
            for device in (p.sibling, p.across_x, p.across_y):
                pl.semaphore_signal(credit, inc=1, device_id=(device,), device_id_type=MESH_ID)

    dense = Belt(LAG, along)
    units = [(m, half, stop) for stop in range(4) for m in range(2) for half in range(2)]

    def expert_event(i):
        if i + AHEAD < 12:
            m, half, stop = units[i + AHEAD]
            jobs[m].plain_send(half, stop)
        m, half, stop = units[i]
        jobs[m].stage_one(half, stop)

    for m, half, stop in units[:AHEAD]:
        jobs[m].plain_send(half, stop)
    experts.add([functools.partial(expert_event, i) for i in range(16)])

    def pump(e=1, d=0):
        experts.run(e)
        dense.run(d)

    def load(pairs, sems):
        copies = [pltpu.make_async_copy(src, dst, sems.at[i]) for i, (src, dst) in enumerate(pairs)]
        for copy in copies:
            copy.start()
        return copies

    def attention(w_src, x_src, an_src, qkv_src, o_src, dw, row, ready, pump):
        def scope(w_buf):
            qkv, o = mix_buf.at[:, pl.ds(0, 2304)], mix_buf.at[:, pl.ds(2304, 768)]
            x_to = xf if x_src.dtype == F32 else low
            copies = load([(x_src, x_to), (o_src, o), (an_src, an_buf), (qkv_src, qkv),
                           (w_src.reshape(WIDTH, HIDDEN), w_buf)], load_sems)
            for copy in copies[:2]:
                copy.wait()
            if x_src.dtype != F32:
                xf[...] = low[...].astype(F32)

            def weights_here():
                for copy in copies[2:]:
                    copy.wait()

            attention_backward(
                g_ref, xf, small[row : row + 1, :], w_buf, an_buf, qkv, o, dw, ds, row, images, seq,
                low, do, dqkv, dn, weights_here, ready, pump,
            )

        pl.run_scoped(scope, pltpu.VMEM((WIDTH, HIDDEN), BF16))

    def combine(en, aux_ref, p0, p1, y, d):
        copies = load([(y_src, y), (p0_src, p0), (p1_src, p1), (x3, xf), (aux_src, aux_ref),
                       (en_src, en), (d_src, d)], combine_sems)
        g_ref[...] = g4[...].astype(F32)
        ds[...] = jnp.zeros_like(ds)
        expert_of = lax.broadcasted_iota(jnp.int32, (EXPERTS * SLOT, 128), 0) // SLOT
        spread = (expert_of == lax.broadcasted_iota(jnp.int32, expert_of.shape, 1)).astype(BF16)
        for copy in copies:
            copy.wait()
        aux = aux_ref[...]
        lane = lax.broadcasted_iota(jnp.int32, aux.shape, 1)
        dr = jnp.zeros(aux.shape, F32)
        dn[...] = xf[...]
        for j, pick in ((0, p0), (1, p1)):
            picked = nn(pick[...], y[...])
            dn[...] += aux[:, 8 + j : 9 + j] * picked
            dr += jnp.sum(g_ref[...] * picked, -1, keepdims=True) * nn(pick[...], spread)
            pump(*PACE[0])
        x4_ref[...] = dn[...].astype(BF16)
        chances = jnp.where(lane < EXPERTS, aux, 0.0)
        dlogits = chances * (dr - jnp.sum(chances * dr, -1, keepdims=True))
        dlogits = jnp.where(lane < EXPERTS, dlogits, 0.0).astype(BF16)
        ds[4:8, :] = tn(dlogits, en[...])[0:4, :]
        dn[...] = nn(dlogits, small[8:136, :].astype(BF16)) + nn(p0[...] + p1[...], d[...])
        pump(*PACE[0])
        norm_back(xf, small[3:4, :], dn, g_ref, ds, 3)
        pump(*PACE[0])

    rows = g_ref.shape[0]
    pl.run_scoped(
        combine, pltpu.VMEM((rows, WIDTH), BF16), pltpu.VMEM((rows, 128), F32),
        pltpu.VMEM((rows, EXPERTS * SLOT), BF16), pltpu.VMEM((rows, EXPERTS * SLOT), BF16),
        pltpu.VMEM((EXPERTS * SLOT, WIDTH), BF16), pltpu.VMEM((EXPERTS * SLOT, WIDTH), BF16))
    attention(wa1, x2, an1, qkv1, o1, dw_wide.at[0].reshape(WIDTH, HIDDEN), 1, jobs[2].start,
              lambda: pump(*PACE[0]))
    dense.add(jobs[2])

    def feed_forward(wo_buf, wi_buf, slope_buf, ma_buf):
        wo, wi = wmo.reshape(HIDDEN, WIDTH), wmi.reshape(WIDTH, HIDDEN)
        dwo, dwi = dw_tall.reshape(HIDDEN, WIDTH), dw_wide.at[1].reshape(WIDTH, HIDDEN)
        first_loads = load([(x1, xf), (mn, an_buf)], load_sems)

        def chunk(n):
            cols = pl.ds(n * 512, 512)
            slot = n % 2
            return load([(wo.at[cols, :], wo_buf.at[slot]), (wi.at[:, cols], wi_buf.at[slot]),
                         (slope.at[:, cols], slope_buf.at[slot]), (ma.at[:, cols], ma_buf.at[slot])],
                        stream_sems.at[slot])

        coming = chunk(0)
        low[...] = g_ref[...].astype(BF16)
        dn[...] = jnp.zeros_like(dn)
        for copy in first_loads:
            copy.wait()
        for n in range(6):
            for copy in coming:
                copy.wait()
            if n < 5:
                coming = chunk(n + 1)
            slot = n % 2
            cols = pl.ds(n * 512, 512)
            dwo[cols, :] = tn(ma_buf[slot], low[...]).astype(BF16)
            dact = nt(low[...], wo_buf[slot])
            dh = (slope_buf[slot].astype(F32) * dact).astype(BF16)
            dwi[:, cols] = tn(an_buf[...], dh).astype(BF16)
            dn[...] += nt(dh, wi_buf[slot])
            pump(*PACE[1])
        jobs[3].start()
        jobs[4].start()
        norm_back(x1_buf, small[2:3, :], dn, g_ref, ds, 2)

    x1_buf = xf
    pl.run_scoped(
        feed_forward, pltpu.VMEM((2, 512, WIDTH), BF16), pltpu.VMEM((2, WIDTH, 512), BF16),
        pltpu.VMEM((2, rows, 512), BF16), pltpu.VMEM((2, rows, 512), BF16))
    dense.add(jobs[3])
    dense.add(jobs[4])

    def last_ready():
        assert dense.done[3] >= 8
        pl.semaphore_wait(credit, 3)
        jobs[5].start()

    attention(wa0, x0, an0, qkv0, o0, dw_wide.at[2].reshape(WIDTH, HIDDEN), 0, last_ready,
              lambda: pump(*PACE[2]))

    def small_copy(to, i, source):
        return remote(tiles.at[to], small_got.at[source],
                      small_sems.at[0, i], small_sems.at[1, source], to)

    tiles[...] = jnp.zeros_like(tiles)
    for d in range(32):
        tiles[d, :, 0:24] = ds[:, 24 * d : 24 * d + 24]
    pl.loop(1, 32)(lambda i: small_copy((p.me + i) % 32, i, p.me).start())
    dense.add(jobs[5])
    while dense.done[3] < len(dense.units) or experts.queue:
        pump(*PACE[3])
    for m in range(2):
        for half in range(2):
            jobs[m].crossed(half)
    mine = pl.ds(pl.multiple_of(p.core * 1536, 128), 1536)
    swap = remote(
        done.at[:, pl.ds(pl.multiple_of((1 - p.core) * 24, 8), 24), :], wide_out.at[:, :, mine],
        meet.at[0], meet.at[1], p.sibling)
    swap.start()
    keep = pltpu.make_async_copy(
        done.at[:, pl.ds(pl.multiple_of(p.core * 24, 8), 24), :], wide_out.at[:, :, mine],
        meet.at[2])
    keep.start()
    pl.loop(1, 32)(lambda i: small_copy((p.me + i) % 32, i, (p.me + i) % 32).wait())
    small_got[p.me] = tiles[p.me]
    small_out[...] = jnp.sum(small_got[...], 0)
    for m in range(6):
        jobs[m].finish()
    keep.wait()
    swap.wait()


def run_backward_step(images, seq, args):
    any_space = pl.BlockSpec(memory_space=pl.ANY)
    vmem = pl.BlockSpec(memory_space=pltpu.VMEM)
    dma = pltpu.SemaphoreType.DMA
    piece = (48, 768)
    rows = args[0].shape[0]
    act, low = pltpu.VMEM((rows, WIDTH), F32), pltpu.VMEM((rows, WIDTH), BF16)
    return pl.pallas_call(
        functools.partial(backward_step, images, seq),
        out_shape=[struct((rows, WIDTH), BF16), struct((rows, WIDTH), F32), struct((8, 128), F32),
                   struct((7, 24, HIDDEN), F32), struct((5, 96, 768), F32)],
        in_specs=[vmem] * 2 + [any_space] * (len(args) - 2),
        out_specs=[vmem, vmem, vmem, any_space, vmem],
        scratch_shapes=[
            act, low, low, pltpu.VMEM((rows, 3 * WIDTH), BF16), act, low,
            pltpu.VMEM((rows, HIDDEN), BF16), pltpu.VMEM((8, WIDTH), F32),
            pltpu.VMEM((3, 4, 2, 2, 48, HIDDEN), BF16),
            pltpu.VMEM((4, 2, 2, 192, WIDTH), BF16),
            pltpu.VMEM((3, 4, 2, 2, 2) + piece, BF16),
            pltpu.VMEM((3, 4, 2, 2) + piece, BF16),
            pltpu.VMEM((3, 4, 2) + piece, BF16),
            pltpu.VMEM((4, 2, 5) + piece, BF16),
            pltpu.VMEM((2, 2, 2, 2) + piece, BF16),
            pltpu.VMEM((2, 2, 5, 2, 2) + piece, BF16),
            pltpu.VMEM((2, 2, 3) + piece, BF16),
            pltpu.VMEM((7, 48, 1536), F32),
            pltpu.VMEM((32, 8, 128), F32),
            pltpu.VMEM((32, 8, 128), F32),
            dma((5,)),
            dma((2, 2)),
            dma((4, 2, 4, 2)),
            dma((4, 4, 4, 2)),
            dma((6, 2, 4)),
            dma((6, 2, 5)),
            dma((2, 2, 2, 3)),
            dma((2, 32)),
            dma((3,)),
            dma((2, 4)),
            dma((7,)),
            pltpu.SemaphoreType.REGULAR,
        ],
        compiler_params=pltpu.CompilerParams(
            collective_id=1, has_side_effects=True, vmem_limit_bytes=63 << 20),
        cost_estimate=pl.CostEstimate(
            flops=20_000_000_000, bytes_accessed=60_000_000, transcendentals=0),
    )(*args)


def fast_backward(images, seq, x0, g4, small, weights, saved, y_back, d_back, sums):
    wa0, wmi, wmo, wa1 = weights
    x1, x2, x3, an0, qkv0, o0, mn, slope, ma, an1, qkv1, o1, en, aux, p0, p1 = saved
    x4, g, dsmall, wide, tall = run_backward_step(images, seq, [
        g4, small, x3, en, aux, p0, p1, y_back, d_back, x2, x1, x0, an1, qkv1, o1, mn, slope, ma,
        an0, qkv0, o0, wa1, wmo, wmi, wa0, sums])
    dsmall = dsmall[:, :24]
    return x4, g, (dsmall.T, wide[0], wide[1], tall[0], wide[2],
                   wide[3:].transpose(1, 0, 2), tall[1:].transpose(1, 0, 2))


def expert_step(
    rows_x, rows_d, ein, eout,
    y_back, d_back, sums,
    wi, wo, got_x, got_d, active, slope, y_out, d_out, acc, dwi, dwo, near,
    load_sems, own_sems, move_sems, pair_sems, sum_sems,
):
    p = Place()
    greet_all(p, 32)
    chips = [device // 2 % 4 for device in (p.me, p.across_x, p.across_y, p.across_both)]
    devices = (None, p.across_x, p.across_y, p.across_both)
    loads = [pltpu.make_async_copy(src, dst, load_sems.at[i])
             for i, (src, dst) in enumerate(((ein, wi), (eout, wo)))]

    def inward(t, i):
        src, dst = ((rows_x, got_x), (rows_d, got_d))[t]
        if i == 0:
            return pltpu.make_async_copy(src.at[p.chip], dst.at[p.chip], own_sems.at[t])
        return remote(src.at[chips[i]], dst.at[p.chip], move_sems.at[t, 0, i], move_sems.at[t, 1, i],
                      devices[i])

    def outward(t, i):
        src, dst = ((y_out, y_back), (d_out, d_back))[t]
        if i == 0:
            return pltpu.make_async_copy(src.at[p.chip], dst.at[p.chip], own_sems.at[2 + t])
        return remote(src.at[chips[i]], dst.at[p.chip], move_sems.at[2 + t, 0, i],
                      move_sems.at[2 + t, 1, i], devices[i])

    for i in range(4):
        inward(0, i).start()
    for copy in loads:
        copy.start()
    inward(1, 0).start()
    for copy in loads:
        copy.wait()
    wide = wi.reshape(WIDTH, HIDDEN)
    tall = wo.reshape(HIDDEN, WIDTH)
    for i in range(4):
        chip = chips[i]
        if i == 0:
            inward(0, 0).wait()
        else:
            inward(0, i).wait_recv()
        if i == 1:
            for j in range(1, 4):
                inward(1, j).start()
        acc[...] = jnp.zeros_like(acc)

        def forward(n):
            cols = tile(n, 512)
            ea, sl = gelu_both(nn(got_x[chip], wide[:, cols]))
            ea = ea.astype(BF16)
            active[chip, :, cols] = ea
            slope[chip, :, cols] = sl.astype(BF16)
            acc[...] += nn(ea, tall[cols, :])

        loop(6, forward)
        y_out[chip] = acc[...].astype(BF16)
        outward(0, i).start()
    for i in range(4):
        chip = chips[i]
        if i == 0:
            inward(1, 0).wait()
        else:
            inward(1, i).wait_recv()
        acc[...] = jnp.zeros_like(acc)

        def backward(n):
            cols = tile(n, 512)
            dh = slope[chip, :, cols].astype(F32) * nt(got_d[chip], tall[cols, :])
            dh = dh.astype(BF16)
            slope[chip, :, cols] = dh
            acc[...] += nt(dh, wide[:, cols])

        loop(6, backward)
        d_out[chip] = acc[...].astype(BF16)
        outward(1, i).start()
    every = EXPERTS * SLOT
    x_all, d_all = got_x.reshape(every, WIDTH), got_d.reshape(every, WIDTH)
    ea_all, dh_all = active.reshape(every, HIDDEN), slope.reshape(every, HIDDEN)
    dwi_all, dwo_all = dwi.reshape(WIDTH, HIDDEN), dwo.reshape(HIDDEN, WIDTH)

    def weights(n):
        cols = tile(n, 512)
        dwo_all[cols, :] = tn(ea_all[:, cols], d_all[...]).astype(BF16)
        dwi_all[:, cols] = tn(x_all[...], dh_all[:, cols]).astype(BF16)

    loop(6, weights)
    pairs = [(m, z, half) for z in range(4) for m in range(2) for half in range(2)]

    def pair(m, z, half):
        src = plane_part((dwi, dwo)[m], KINDS[m], z, 1 - p.core, half)
        return remote(src, near.at[m, z, half], pair_sems.at[m, z, half, 0],
                      pair_sems.at[m, z, half, 1], p.sibling)

    def result(m, z, half):
        return pltpu.make_async_copy(near.at[m, z, half], sums.at[m, z, half], sum_sems.at[m, z, half])

    for one in pairs:
        pair(*one).start()
    for m, z, half in pairs:
        pair(m, z, half).wait_recv()
        own = plane_part((dwi, dwo)[m], KINDS[m], z, p.core, half)
        came = near.at[m, z, half]
        add_into(lambda i: came.at[i // 2, i % 2], lambda i: own.at[i // 2, i % 2], 4)
        result(m, z, half).start()
    for one in pairs:
        result(*one).wait()
        pair(*one).wait_send()
    for t in range(2):
        outward(t, 0).wait()
        for i in range(1, 4):
            inward(t, i).wait_send()
            outward(t, i).wait()


def run_expert_step(rows_x, rows_d, ein, eout):
    any_space = pl.BlockSpec(memory_space=pl.ANY)
    dma = pltpu.SemaphoreType.DMA
    rows = (EXPERTS, SLOT, WIDTH)
    y, d, sums = pl.pallas_call(
        expert_step,
        out_shape=[struct(rows, BF16)] * 2 + [struct((2, 4, 2, 2, 2, 48, 768), BF16)],
        in_specs=[any_space] * 4,
        out_specs=[any_space] * 3,
        scratch_shapes=[
            pltpu.VMEM((4, 2, 2, 48, HIDDEN), BF16),
            pltpu.VMEM((4, 2, 2, 192, WIDTH), BF16),
            pltpu.VMEM(rows, BF16),
            pltpu.VMEM(rows, BF16),
            pltpu.VMEM((EXPERTS, SLOT, HIDDEN), BF16),
            pltpu.VMEM((EXPERTS, SLOT, HIDDEN), BF16),
            pltpu.VMEM(rows, BF16),
            pltpu.VMEM(rows, BF16),
            pltpu.VMEM((SLOT, WIDTH), F32),
            pltpu.VMEM((4, 2, 2, 48, HIDDEN), BF16),
            pltpu.VMEM((4, 2, 2, 192, WIDTH), BF16),
            pltpu.VMEM((2, 4, 2, 2, 2, 48, 768), BF16),
            dma((2,)),
            dma((4,)),
            dma((4, 2, 4)),
            dma((2, 4, 2, 2)),
            dma((2, 4, 2)),
        ],
        compiler_params=pltpu.CompilerParams(
            collective_id=2, has_side_effects=True, vmem_limit_bytes=VMEM_BYTES),
        cost_estimate=pl.CostEstimate(
            flops=30_000_000_000, bytes_accessed=40_000_000, transcendentals=0),
    )(rows_x.reshape(rows), rows_d.reshape(rows), ein, eout)
    flat = (EXPERTS * SLOT, WIDTH)
    return y.reshape(flat), d.reshape(flat), sums


def local(
    patches, live_count, expert_ids, attn_gain, attn_qkv, attn_out, mlp_gain, mlp_in, mlp_out,
    moe_gain, router, expert_in, expert_out, cotangent,
):
    images, seq, width = patches.shape
    padded = -(-seq // 16) * 16
    n = lax.axis_size("fsdp")
    group_size = n // EXPERTS
    group = lax.axis_index("fsdp") // group_size
    alive = jnp.arange(images, dtype=jnp.int32) < live_count[0]

    def pad(values, fill=0):
        values = values.reshape(images, seq, -1)
        values = jnp.pad(values, ((0, 0), (0, padded - seq), (0, 0)), constant_values=fill)
        return values.reshape(images * padded, -1)

    x0 = pad(patches)
    g4 = pad(jnp.where(alive[:, None, None], cotangent, jnp.zeros_like(cotangent)))
    ids = pad(expert_ids, -1)
    smalls = jnp.concatenate(
        [attn_gain, mlp_gain[:, None], moe_gain[:, None], router], 1
    )
    wide = [(attn_qkv[:, 0], attn_out[:, 0]), mlp_in, (attn_qkv[:, 1], attn_out[:, 1])]
    if n == 32:
        small, weights, w_in, w_out, saved, rows_x, rows_d = fast_front(
            images, seq, smalls, wide, mlp_out, expert_in, expert_out, x0, g4, ids)
    else:
        small, wides, talls, w_in, w_out = plain_gather(
            smalls, [jnp.concatenate(wide[0], 1), mlp_in, jnp.concatenate(wide[2], 1)],
            [mlp_out], expert_in, expert_out)
        small = small.astype(F32).T
        small = jnp.concatenate(
            [small[:4], jnp.zeros((4, width), F32), small[4:], jnp.zeros((124, width), F32)], 0
        )
        weights = (wides[0], wides[1], talls[0], wides[2])
        out = run_forward(images, seq, x0, g4, ids, small, *weights)
        saved, rows_x, rows_d = out[:16], out[16], out[17]

    def exchange(rows):
        rows = rows.reshape(EXPERTS, SLOT, width)
        return group_exchange(rows, group_size, group).reshape(EXPERTS * SLOT, width)

    if n == 32:
        y_back, d_back, sums = run_expert_step(rows_x, rows_d, w_in, w_out)
        x4, grad, shards = fast_backward(
            images, seq, x0, g4, small, weights, saved, y_back, d_back, sums)
        dsmall, d0, dmi, dmo, d1, de_in, de_out = shards
    else:
        y, dx, dw_in, dw_out = run_expert(exchange(rows_x), exchange(rows_d), w_in, w_out)
        x4, grad, d0, dmi, dmo, d1, dsmall = run_backward(
            images, seq, x0, g4, small, weights, saved, exchange(y), exchange(dx)
        )
        d0, dmi, dmo, d1 = (plain_reduce(g).astype(F32) for g in (d0, dmi, dmo, d1))
        de_in, de_out = (plain_reduce_expert(g).astype(F32) for g in (dw_in, dw_out))
        dsmall = lax.psum_scatter(dsmall.T, "fsdp", scatter_dimension=0, tiled=True)

    def unpad(values):
        return values.reshape(images, padded, width)[:, :seq]

    block_out = jnp.where(alive[:, None, None], unpad(x4), 0.0).astype(BF16)
    return (
        block_out,
        unpad(grad),
        dsmall[:, 0:2],
        jnp.stack([d0[:, :2304], d1[:, :2304]], 1),
        jnp.stack([d0[:, 2304:], d1[:, 2304:]], 1),
        dsmall[:, 2],
        dmi,
        dmo,
        dsmall[:, 3],
        dsmall[:, 4:8],
        de_in,
        de_out,
    )


def solution(mesh):
    def lead(rank):
        return P("fsdp", *([None] * (rank - 1)))

    return jax.shard_map(
        local,
        mesh=mesh,
        in_specs=tuple(lead(r) for r in (3, 1, 2, 2, 3, 3, 1, 2, 2, 1, 2, 3, 3, 3)),
        out_specs=tuple(lead(r) for r in (3, 3, 2, 3, 3, 1, 2, 2, 1, 2, 3, 3)),
        check_vma=False,
    )
```

```python
import functools

import jax
import jax.numpy as jnp
from jax import lax
from jax.experimental import pallas as pl
from jax.experimental.pallas import tpu as pltpu
from jax.sharding import PartitionSpec as P

HEADS = 12
HEAD_DIM = 64
EXPERTS = 4
CAP = 247
SLOT = 256
WIDTH = 768
HIDDEN = 3072
NORM_EPSILON = 1e-06
VMEM_BYTES = 60 << 20
F32 = jnp.float32
BF16 = jnp.bfloat16


def nn(left, right):
    return lax.dot_general(left, right, (((1,), (0,)), ((), ())), preferred_element_type=F32)


def nt(left, right):
    return lax.dot_general(left, right, (((1,), (1,)), ((), ())), preferred_element_type=F32)


def tn(left, right):
    return lax.dot_general(left, right, (((0,), (0,)), ((), ())), preferred_element_type=F32)


def tile(index, size):
    return pl.ds(pl.multiple_of(index * size, size), size)


def loop(count, body):
    pl.loop(0, count)(body)


def norm_parts(values):
    center = values - jnp.mean(values, -1, keepdims=True)
    spread = jnp.mean(center * center, -1, keepdims=True)
    scale = lax.rsqrt(spread + NORM_EPSILON)
    return center * scale, scale


def norm_rows(x_ref, gain, out_ref, block=32):
    def body(i):
        rows = tile(i, block)
        unit, _ = norm_parts(x_ref[rows, :])
        out_ref[rows, :] = (unit * gain).astype(BF16)

    loop(x_ref.shape[0] // block, body)


def norm_back(x_ref, gain, dn_ref, g_ref, dgain_ref, row, block=32):
    def body(i, total):
        rows = tile(i, block)
        unit, scale = norm_parts(x_ref[rows, :])
        dn = dn_ref[rows, :]
        scaled = dn * gain
        mean_one = jnp.mean(scaled, -1, keepdims=True)
        mean_two = jnp.mean(scaled * unit, -1, keepdims=True)
        g_ref[rows, :] = g_ref[rows, :] + scale * (scaled - mean_one - unit * mean_two)
        return total + jnp.sum((dn * unit).reshape(block // 8, 8, WIDTH), 0)

    total = lax.fori_loop(0, x_ref.shape[0] // block, body, jnp.zeros((8, WIDTH), F32))
    dgain_ref[row : row + 1, :] = jnp.sum(total, 0, keepdims=True)


def gelu_both(u):
    c = 0.7978845608
    square = u * u
    t = jnp.tanh(c * u * (1.0 + 0.044715 * square))
    half = 0.5 * (1.0 + t)
    slope = half + 0.5 * u * (1.0 - t * t) * (c + (3 * 0.044715 * c) * square)
    return u * half, slope


def halves(shape):
    lane = lax.broadcasted_iota(jnp.int32, shape, 1)
    return lane < HEAD_DIM


def head_probs(q, k, seq):
    scores = nt(q, k) * HEAD_DIM ** (-0.5)
    key = lax.broadcasted_iota(jnp.int32, scores.shape, 1)
    scores = jnp.where(key < seq, scores, -1e30)
    top = jnp.max(scores, -1, keepdims=True)
    e = jnp.exp(scores - top)
    return e / jnp.sum(e, -1, keepdims=True)


def attention_heads(qkv_ref, o_ref, images, seq):
    rows_of = qkv_ref.shape[0] // images
    for image in range(images):
        rows = pl.ds(image * rows_of, rows_of)

        def pair(p, rows=rows):
            q = qkv_ref[rows, tile(p, 128)]
            k = qkv_ref[rows, tile(p + 6, 128)]
            v = qkv_ref[rows, tile(p + 12, 128)]
            first = halves(q.shape)
            zero = jnp.zeros_like(q)
            p0 = head_probs(jnp.where(first, q, zero), k, seq).astype(BF16)
            p1 = head_probs(jnp.where(first, zero, q), k, seq).astype(BF16)
            out = nn(p0, jnp.where(first, v, zero)) + nn(p1, jnp.where(first, zero, v))
            o_ref[rows, tile(p, 128)] = out.astype(BF16)

        loop(6, pair)


def attention_forward(x_ref, gain, w_ref, xo_ref, an_ref, qkv_ref, o_ref, images, seq):
    norm_rows(x_ref, gain, an_ref)

    def project(n):
        qkv_ref[:, tile(n, 256)] = nn(an_ref[...], w_ref[:, tile(n, 256)]).astype(BF16)

    loop(9, project)
    attention_heads(qkv_ref, o_ref, images, seq)

    def outward(n):
        cols = tile(n, 256)
        xo_ref[:, cols] = x_ref[:, cols] + nn(o_ref[...], w_ref[:, tile(n + 9, 256)])

    loop(3, outward)


def attention_backward(
    g_ref, x_ref, gain, w_ref, an_ref, qkv_ref, o_ref, dw_ref, dgain_ref, row, images, seq,
    low_ref, do_ref, dqkv_ref, dn_ref, weights_here=lambda: None, ready=lambda: None,
    pump=lambda: None,
):
    rows_of = qkv_ref.shape[0] // images
    low_ref[...] = g_ref[...].astype(BF16)

    def outward(n):
        dw_ref[:, tile(n + 9, 256)] = tn(o_ref[...], low_ref[:, tile(n, 256)]).astype(BF16)

    loop(3, outward)
    pump()
    weights_here()

    def outward_rows(n):
        do_ref[:, tile(n, 256)] = nt(low_ref[...], w_ref[tile(n, 256), 2304:]).astype(BF16)

    loop(3, outward_rows)
    pump()
    for image in range(images):
        rows = pl.ds(image * rows_of, rows_of)

        def pair(p, rows=rows):
            q = qkv_ref[rows, tile(p, 128)]
            k = qkv_ref[rows, tile(p + 6, 128)]
            v = qkv_ref[rows, tile(p + 12, 128)]
            d = do_ref[rows, tile(p, 128)]
            first = halves(q.shape)
            zero = jnp.zeros_like(q)
            dq = dk = dv = None
            for mine in (first, ~first):
                qm, km, dm = (jnp.where(mine, t, zero) for t in (q, k, d))
                probs = head_probs(qm, k, seq)
                dp = nt(dm, v)
                inner = jnp.sum(dp * probs, -1, keepdims=True)
                ds = (probs * (dp - inner)).astype(BF16)
                one = (nn(ds, km), tn(ds, qm), tn(probs.astype(BF16), dm))
                dq, dk, dv = one if dq is None else (dq + one[0], dk + one[1], dv + one[2])
            scale = HEAD_DIM ** (-0.5)
            dqkv_ref[rows, tile(p, 128)] = (dq * scale).astype(BF16)
            dqkv_ref[rows, tile(p + 6, 128)] = (dk * scale).astype(BF16)
            dqkv_ref[rows, tile(p + 12, 128)] = dv.astype(BF16)

        loop(3, pair)
        pump()
        loop(3, lambda p, pair=pair: pair(p + 3))
        pump()

    for third in range(3):

        def inward(n, third=third):
            cols = tile(n + third * 3, 256)
            dw_ref[:, cols] = tn(an_ref[...], dqkv_ref[:, cols]).astype(BF16)

        loop(3, inward)
        pump()
    ready()

    def normed(n):
        dn_ref[:, tile(n, 256)] = nt(dqkv_ref[...], w_ref[tile(n, 256), :2304])

    loop(3, normed)
    pump()
    norm_back(x_ref, gain, dn_ref, g_ref, dgain_ref, row)
    pump()


def route_rows(g4_ref, ids_ref, small_ref, en_ref, aux_ref, g0_ref, g1_ref, rx_ref, rd_ref, pump):
    rows = en_ref.shape[0]
    logits = nt(en_ref[...], small_ref[8:136, :].astype(BF16))
    lane = lax.broadcasted_iota(jnp.int32, logits.shape, 1)
    logits = jnp.where(lane < EXPERTS, logits, -1e30)
    e = jnp.exp(logits - jnp.max(logits, -1, keepdims=True))
    chances = e / jnp.sum(e, -1, keepdims=True)
    ids = ids_ref[...]
    chosen = [(ids[:, j : j + 1] == lane).astype(F32) for j in range(2)]
    row_i = lax.broadcasted_iota(jnp.int32, (rows, rows), 0)
    row_j = lax.broadcasted_iota(jnp.int32, (rows, rows), 1)
    earlier = nn((row_j < row_i).astype(BF16), (chosen[0] + chosen[1]).astype(BF16))
    place = lax.broadcasted_iota(jnp.int32, (rows, EXPERTS * SLOT), 1)
    gates = []
    for j, pick_ref in ((0, g0_ref), (1, g1_ref)):
        gates.append(jnp.sum(chances * chosen[j], -1, keepdims=True))
        inside = jnp.sum(earlier * chosen[j], -1, keepdims=True).astype(jnp.int32)
        slot = jnp.where(ids[:, j : j + 1] >= 0, ids[:, j : j + 1] * SLOT + inside, -1)
        pick_ref[...] = (slot == place).astype(BF16)
    aux = jnp.where(lane < EXPERTS, chances, 0.0)
    aux = jnp.where(lane == 8, gates[0], aux)
    aux_ref[...] = jnp.where(lane == 9, gates[1], aux)

    def fill(n):
        cols = tile(n, 256)
        both = g0_ref[:, cols] + g1_ref[:, cols]
        rx_ref[cols, :] = tn(both, en_ref[...]).astype(BF16)
        g4 = g4_ref[...].astype(F32)
        one = tn(g0_ref[:, cols], (g4 * gates[0]).astype(BF16))
        two = tn(g1_ref[:, cols], (g4 * gates[1]).astype(BF16))
        rd_ref[cols, :] = (one + two).astype(BF16)

    pump()
    loop(2, fill)
    pump()
    loop(2, lambda n: fill(n + 2))
    pump()


def forward_kernel(
    images, seq,
    x0_ref, g4_ref, ids_ref, small_ref, wa0_ref, wmi_ref, wmo_ref, wa1_ref,
    x1_ref, x2_ref, x3_ref, an0_ref, qkv0_ref, o0_ref, mn_ref, slope_ref, ma_ref,
    an1_ref, qkv1_ref, o1_ref, en_ref, aux_ref, g0_ref, g1_ref, rx_ref, rd_ref,
    xf_ref,
):
    xf_ref[...] = x0_ref[...].astype(F32)
    attention_forward(
        xf_ref, small_ref[0:1, :], wa0_ref, x1_ref, an0_ref, qkv0_ref, o0_ref, images, seq
    )
    norm_rows(x1_ref, small_ref[2:3, :], mn_ref)
    x2_ref[...] = x1_ref[...]

    def dense(n):
        cols = tile(n, 512)
        active, slope = gelu_both(nn(mn_ref[...], wmi_ref[:, cols]))
        slope_ref[:, cols] = slope.astype(BF16)
        active = active.astype(BF16)
        ma_ref[:, cols] = active
        x2_ref[...] += nn(active, wmo_ref[cols, :])

    loop(6, dense)
    attention_forward(
        x2_ref, small_ref[1:2, :], wa1_ref, x3_ref, an1_ref, qkv1_ref, o1_ref, images, seq
    )
    norm_rows(x3_ref, small_ref[3:4, :], en_ref)
    route_rows(
        g4_ref, ids_ref, small_ref, en_ref, aux_ref, g0_ref, g1_ref, rx_ref, rd_ref, lambda: None
    )


def expert_kernel(x_ref, d_ref, wi_ref, wo_ref, y_ref, dx_ref, dwi_ref, dwo_ref, yf_ref, df_ref):
    yf_ref[...] = jnp.zeros_like(yf_ref)
    df_ref[...] = jnp.zeros_like(df_ref)

    def body(n):
        cols = tile(n, 512)
        active, slope = gelu_both(nn(x_ref[...], wi_ref[:, cols]))
        active = active.astype(BF16)
        yf_ref[...] += nn(active, wo_ref[cols, :])
        dwo_ref[cols, :] = tn(active, d_ref[...]).astype(BF16)
        dh = (slope * nt(d_ref[...], wo_ref[cols, :])).astype(BF16)
        df_ref[...] += nt(dh, wi_ref[:, cols])
        dwi_ref[:, cols] = tn(x_ref[...], dh).astype(BF16)

    loop(6, body)
    y_ref[...] = yf_ref[...].astype(BF16)
    dx_ref[...] = df_ref[...].astype(BF16)


def combine_kernel(
    g4_ref, small_ref, x3_ref, en_ref, aux_ref, g0_ref, g1_ref, yr_ref, dr_ref,
    x4_ref, g_ref, ds_ref,
    dn_ref,
):
    aux = aux_ref[...]
    lane = lax.broadcasted_iota(jnp.int32, aux.shape, 1)
    g_ref[...] = g4_ref[...].astype(F32)
    x4_ref[...] = x3_ref[...]
    dgates = []
    chosen = []
    expert_of = lax.broadcasted_iota(jnp.int32, (EXPERTS * SLOT, 128), 0) // SLOT
    spread = (expert_of == lax.broadcasted_iota(jnp.int32, expert_of.shape, 1)).astype(BF16)
    for j, pick_ref in ((0, g0_ref), (1, g1_ref)):
        picked = nn(pick_ref[...], yr_ref[...])
        x4_ref[...] += aux[:, 8 + j : 9 + j] * picked
        dgates.append(jnp.sum(g_ref[...] * picked, -1, keepdims=True))
        chosen.append(nn(pick_ref[...], spread))
    dr = dgates[0] * chosen[0] + dgates[1] * chosen[1]
    chances = jnp.where(lane < EXPERTS, aux, 0.0)
    dlogits = chances * (dr - jnp.sum(chances * dr, -1, keepdims=True))
    dlogits = jnp.where(lane < EXPERTS, dlogits, 0.0).astype(BF16)
    ds_ref[...] = jnp.zeros_like(ds_ref)
    ds_ref[4:8, :] = tn(dlogits, en_ref[...])[0:4, :]
    dn_ref[...] = nn(dlogits, small_ref[8:136, :].astype(BF16)) + nn(
        g0_ref[...] + g1_ref[...], dr_ref[...]
    )
    norm_back(x3_ref, small_ref[3:4, :], dn_ref, g_ref, ds_ref, 3)


def attention_back_kernel(
    images, seq, row,
    g_in_ref, small_ref, x_ref, w_ref, an_ref, qkv_ref, o_ref,
    g_ref, dw_ref, ds_ref,
    xf_ref, low_ref, do_ref, dqkv_ref, dn_ref,
):
    g_ref[...] = g_in_ref[...]
    xf_ref[...] = x_ref[...].astype(F32)
    ds_ref[...] = jnp.zeros_like(ds_ref)
    attention_backward(
        g_ref, xf_ref, small_ref[row : row + 1, :], w_ref, an_ref, qkv_ref, o_ref, dw_ref,
        ds_ref, row, images, seq, low_ref, do_ref, dqkv_ref, dn_ref,
    )


def dense_back_kernel(
    g_in_ref, small_ref, x1_ref, wmi_ref, wmo_ref, mn_ref, slope_ref, ma_ref,
    g_ref, dwmi_ref, dwmo_ref, ds_ref,
    low_ref, dn_ref,
):
    g_ref[...] = g_in_ref[...]
    ds_ref[...] = jnp.zeros_like(ds_ref)
    low_ref[...] = g_ref[...].astype(BF16)
    dn_ref[...] = jnp.zeros_like(dn_ref)

    def dense(n):
        cols = tile(n, 512)
        dwmo_ref[cols, :] = tn(ma_ref[:, cols], low_ref[...]).astype(BF16)
        dact = nt(low_ref[...], wmo_ref[cols, :])
        dh = (slope_ref[:, cols].astype(F32) * dact).astype(BF16)
        dwmi_ref[:, cols] = tn(mn_ref[...], dh).astype(BF16)
        dn_ref[...] += nt(dh, wmi_ref[:, cols])

    loop(6, dense)
    norm_back(x1_ref, small_ref[2:3, :], dn_ref, g_ref, ds_ref, 2)


def struct(shape, dtype):
    return jax.ShapeDtypeStruct(shape, dtype)


def call(body, outs, scratch, args, flops):
    total = sum(a.size * a.dtype.itemsize for a in list(args) + list(outs))
    return pl.pallas_call(
        body,
        out_shape=outs,
        in_specs=[pl.BlockSpec(memory_space=pltpu.VMEM)] * len(args),
        out_specs=[pl.BlockSpec(memory_space=pltpu.VMEM)] * len(outs),
        scratch_shapes=scratch,
        compiler_params=pltpu.CompilerParams(vmem_limit_bytes=VMEM_BYTES),
        cost_estimate=pl.CostEstimate(flops=flops, bytes_accessed=total, transcendentals=0),
    )(*args)


def run_forward(images, seq, x0, g4, ids, small, wa0, wmi, wmo, wa1):
    rows = x0.shape[0]
    act = struct((rows, WIDTH), F32)
    low = struct((rows, WIDTH), BF16)
    qkv = struct((rows, 3 * WIDTH), BF16)
    hid = struct((rows, HIDDEN), BF16)
    pick = struct((rows, EXPERTS * SLOT), BF16)
    buf = struct((EXPERTS * SLOT, WIDTH), BF16)
    outs = [act, act, act, low, qkv, low, low, hid, hid, low, qkv, low, low,
            struct((rows, 128), F32), pick, pick, buf, buf]
    return call(
        functools.partial(forward_kernel, images, seq), outs,
        [pltpu.VMEM((rows, WIDTH), F32)],
        [x0, g4, ids, small, wa0, wmi, wmo, wa1], 8_000_000_000,
    )


def run_expert(x, d, wi, wo):
    outs = [struct(x.shape, BF16), struct(x.shape, BF16), struct(wi.shape, BF16), struct(wo.shape, BF16)]
    return call(
        expert_kernel, outs, [pltpu.VMEM(x.shape, F32), pltpu.VMEM(x.shape, F32)],
        [x, d, wi, wo], 30_000_000_000,
    )


def run_backward(images, seq, x0, g4, small, weights, saved, y_back, d_back):
    rows = x0.shape[0]
    act = struct((rows, WIDTH), F32)
    wide, tall = struct((WIDTH, HIDDEN), BF16), struct((HIDDEN, WIDTH), BF16)
    row = struct((8, WIDTH), F32)
    wa0, wmi, wmo, wa1 = weights
    x1, x2, x3, an0, qkv0, o0, mn, slope, ma, an1, qkv1, o1, en, aux, p0, p1 = saved
    full = pltpu.VMEM((rows, WIDTH), F32)
    low = pltpu.VMEM((rows, WIDTH), BF16)
    mixed = pltpu.VMEM((rows, 3 * WIDTH), BF16)
    x4, g, s0 = call(
        combine_kernel, [act, act, row], [full],
        [g4, small, x3, en, aux, p0, p1, y_back, d_back], 3_000_000_000,
    )
    g, dwa1, s1 = call(
        functools.partial(attention_back_kernel, images, seq, 1), [act, wide, row],
        [full, low, low, mixed, full], [g, small, x2, wa1, an1, qkv1, o1], 5_000_000_000,
    )
    g, dwmi, dwmo, s2 = call(
        dense_back_kernel, [act, wide, tall, row], [low, full],
        [g, small, x1, wmi, wmo, mn, slope, ma], 8_000_000_000,
    )
    g, dwa0, s3 = call(
        functools.partial(attention_back_kernel, images, seq, 0), [act, wide, row],
        [full, low, low, mixed, full], [g, small, x0, wa0, an0, qkv0, o0], 5_000_000_000,
    )
    return x4, g, dwa0, dwmi, dwmo, dwa1, s0 + s1 + s2 + s3


def gather_rows(piece):
    return lax.all_gather(piece, "fsdp", axis=0, tiled=True)


def shift(values, steps):
    count = lax.axis_size("fsdp")
    return lax.ppermute(values, "fsdp", [(s, (s + steps) % count) for s in range(count)])


def group_exchange(rows, group_size, group_id):
    out = jnp.zeros_like(rows)
    for offset in range(EXPERTS):
        piece = lax.dynamic_index_in_dim(rows, (group_id + offset) % EXPERTS, 0, keepdims=False)
        if offset:
            piece = shift(piece, offset * group_size)
        out = lax.dynamic_update_index_in_dim(out, piece, (group_id - offset) % EXPERTS, 0)
    return out


def plain_gather(smalls, wide, tall, e_in, e_out):
    n = lax.axis_size("fsdp")
    group_size = n // EXPERTS
    group = lax.axis_index("fsdp") // group_size
    small = gather_rows(smalls)
    wides = [gather_rows(w) for w in wide]
    talls = [gather_rows(w) for w in tall]
    big_in = lax.dynamic_index_in_dim(gather_rows(e_in), group, 1, keepdims=False)
    big_out = lax.dynamic_index_in_dim(gather_rows(e_out), group, 1, keepdims=False)
    return small, wides, talls, big_in, big_out


def plain_reduce(grad):
    return lax.psum_scatter(grad, "fsdp", scatter_dimension=0, tiled=True)


def plain_reduce_expert(grad):
    n = lax.axis_size("fsdp")
    group_size = n // EXPERTS
    group = lax.axis_index("fsdp") // group_size
    full = jnp.zeros((grad.shape[0], EXPERTS, grad.shape[1]), BF16)
    full = lax.dynamic_update_index_in_dim(full, grad, group, 1)
    return plain_reduce(full)

MESH_ID = pl.DeviceIdType.MESH


class Place:
    def __init__(self):
        self.me = lax.axis_index("fsdp")
        self.core = self.me % 2
        self.x = self.me // 2 % 2
        self.y = self.me // 4 % 2
        self.z = self.me // 8
        self.sibling = self.me + 1 - 2 * self.core
        self.across_x = self.me + 2 - 4 * self.x
        self.across_y = self.me + 4 - 8 * self.y
        self.across_both = self.across_x + 4 - 8 * self.y
        self.chip = self.me // 2 % 4


def remote(src, dst, send, recv, device):
    return pltpu.make_async_remote_copy(
        src_ref=src, dst_ref=dst, send_sem=send, recv_sem=recv,
        device_id=(device,), device_id_type=MESH_ID,
    )


def greet_all(place, count):
    barrier = pltpu.get_barrier_semaphore()

    def hello(i):
        pl.semaphore_signal(
            barrier, inc=1, device_id=((place.me + i) % count,), device_id_type=MESH_ID
        )

    pl.loop(1, count)(hello)
    pl.semaphore_wait(barrier, count - 1)


DENSE = ("wide", "wide", "tall", "wide")


def part(ref, kind, z, y, x, core, half):
    if kind == "wide":
        return ref.at[z, y, x, :, pl.ds(pl.multiple_of(core * 1536 + half * 768, 128), 768)]
    return ref.at[z, y, x, pl.ds(pl.multiple_of(core * 96 + half * 48, 16), 48), :]


def own_part(mine, kind, half):
    if kind == "wide":
        return mine.at[:, pl.ds(half * 768, 768)]
    return mine.at[pl.ds(half * 48, 48), :]


class Gather:
    def __init__(self, place, kind, mine, out, sems):
        self.p, self.kind, self.mine, self.out, self.sems = place, kind, mine, out, sems

    def _z(self, half, source, up):
        p = self.p
        where = part(self.out, self.kind, source, p.y, p.x, p.core, half)
        return where, 0 if up else 1

    def _slot(self, half, source):
        return half * 4 + source

    def start_own(self):
        p, s = self.p, self.sems
        for half in range(2):
            there = part(self.out, self.kind, p.z, p.y, p.x, p.core, half)
            src = own_part(self.mine, self.kind, half)
            pltpu.make_async_copy(src, there, s["own"].at[half]).start()
            self._along_z(half, p.z, src, True, True)

    def _copy_z(self, half, source, src, up):
        p, s = self.p, self.sems
        slot = self._slot(half, source)
        there = part(self.out, self.kind, source, p.y, p.x, p.core, half)
        name = "zu" if up else "zd"
        return remote(there if src is None else src, there, s[name].at[slot], s["zr"].at[slot],
                      p.me + 8 if up else p.me - 8)

    def _along_z(self, half, source, src, up, down):
        p = self.p
        if up:
            pl.when(p.z < 3)(lambda: self._copy_z(half, source, src, True).start())
        if down:
            pl.when(p.z > 0)(lambda: self._copy_z(half, source, src, False).start())

    def _first(self, half, source, src=None):
        p, s = self.p, self.sems
        slot = self._slot(half, source)
        there = part(self.out, self.kind, source, p.y, p.x, p.core, half)
        return remote(there if src is None else src, there, s["fs"].at[slot], s["fr"].at[slot],
                      p.across_y if half else p.across_x)

    def _line(self, half, source):
        p = self.p
        if self.kind == "wide":
            rows, cols = slice(None), pl.ds(pl.multiple_of(p.core * 1536 + half * 768, 128), 768)
        else:
            rows, cols = pl.ds(pl.multiple_of(p.core * 96 + half * 48, 16), 48), slice(None)
        if half:
            return self.out.at[source, :, p.x, rows, cols]
        return self.out.at[source, p.y, :, rows, cols]

    def _second(self, half, source):
        p, s = self.p, self.sems
        slot = self._slot(half, source)
        line = self._line(half, source)
        return remote(line, line, s["ss"].at[slot], s["sr"].at[slot],
                      p.across_x if half else p.across_y)

    def _hand(self, half, source):
        p, s = self.p, self.sems
        slot = self._slot(half, source)
        if self.kind == "wide":
            rows, cols = slice(None), pl.ds(pl.multiple_of(p.core * 1536 + half * 768, 128), 768)
        else:
            rows, cols = pl.ds(pl.multiple_of(p.core * 96 + half * 48, 16), 48), slice(None)
        plane = self.out.at[source, :, :, rows, cols]
        return remote(plane, plane, s["hs"].at[slot], s["hr"].at[slot], p.sibling)

    def valid(self, k):
        z = self.p.z + k
        return (z >= 0) & (z <= 3)

    def stage_one(self, half, k):
        source = self.p.z + k

        def run():
            if k == 0:
                src = own_part(self.mine, self.kind, half)
                self._first(half, source, src).start()
                there = part(self.out, self.kind, source, self.p.y, self.p.x, self.p.core, half)
                pltpu.make_async_copy(src, there, self.sems["own"].at[half]).wait()
                return
            self._copy_z(half, source, None, k < 0).wait_recv()
            self._along_z(half, source, None, k < 0, k > 0)
            self._first(half, source).start()

        pl.when(self.valid(k))(run)

    def stage_two(self, half, k):
        source = self.p.z + k

        def run():
            self._first(half, source).wait_recv()
            self._second(half, source).start()

        pl.when(self.valid(k))(run)

    def stage_three(self, half, k):
        source = self.p.z + k

        def run():
            self._second(half, source).wait_recv()
            self._hand(half, source).start()

        pl.when(self.valid(k))(run)

    def arrived(self):
        for half in range(2):
            for source in range(4):
                self._hand(half, source).wait_recv()

    def finish(self):
        p = self.p
        for half in range(2):
            for source in range(4):
                self._first(half, source).wait_send()
                self._second(half, source).wait_send()
                self._hand(half, source).wait_send()
                up = (source <= p.z) & (p.z < 3)
                down = (source >= p.z) & (p.z > 0)
                pl.when(up)(lambda: self._copy_z(half, source, None, True).wait_send())
                pl.when(down)(lambda: self._copy_z(half, source, None, False).wait_send())


GATHER_SEMS = ("zu", "zd", "zr", "fs", "fr", "ss", "sr", "hs", "hr")


def expert_block(ref, kind, z, y, core):
    if kind == "wide":
        return ref.at[z, y, :, :, pl.ds(pl.multiple_of(core * 1536, 128), 1536)]
    return ref.at[z, y, :, pl.ds(pl.multiple_of(core * 96, 16), 96), :]


def expert_piece(ref, kind, z, y, x, core):
    if kind == "wide":
        return ref.at[z, y, x, :, pl.ds(pl.multiple_of(core * 1536, 128), 1536)]
    return ref.at[z, y, x, pl.ds(pl.multiple_of(core * 96, 16), 96), :]


class ExpertGather:
    def __init__(self, place, kind, mine, out, sems):
        self.p, self.kind, self.mine, self.out, self.sems = place, kind, mine, out, sems

    def _cross(self, i):
        p, s = self.p, self.sems
        there = expert_piece(self.out, self.kind, p.z, p.y, p.x, p.core)
        device = (p.across_x, p.across_y, p.across_both)[i]
        expert = device // 2 % 4
        return remote(self.mine.at[expert], there, s["cs"].at[i], s["cr"].at[i], device)

    def _own(self):
        p = self.p
        there = expert_piece(self.out, self.kind, p.z, p.y, p.x, p.core)
        return pltpu.make_async_copy(self.mine.at[p.chip], there, self.sems["own"].at[0])

    def start_own(self):
        self._own().start()
        for i in range(3):
            self._cross(i).start()

    def _copy_z(self, y, source, up):
        p, s = self.p, self.sems
        slot = y * 4 + source
        block = expert_block(self.out, self.kind, source, y, p.core)
        return remote(block, block, s["zu" if up else "zd"].at[slot], s["zr"].at[slot],
                      p.me + 8 if up else p.me - 8)

    def _hand(self, y, source):
        p, s = self.p, self.sems
        slot = y * 4 + source
        block = expert_block(self.out, self.kind, source, y, p.core)
        return remote(block, block, s["hs"].at[slot], s["hr"].at[slot], p.sibling)

    def crossed(self):
        p = self.p
        self._own().wait()
        for i in range(3):
            self._cross(i).wait_recv()
        for y in range(2):
            pl.when(p.z < 3)(lambda: self._copy_z(y, p.z, True).start())
            pl.when(p.z > 0)(lambda: self._copy_z(y, p.z, False).start())
            self._hand(y, p.z).start()

    def stage(self, y, k):
        p = self.p
        source = p.z + k

        def run():
            self._copy_z(y, source, k < 0).wait_recv()
            if k < 0:
                pl.when(p.z < 3)(lambda: self._copy_z(y, source, True).start())
            else:
                pl.when(p.z > 0)(lambda: self._copy_z(y, source, False).start())
            self._hand(y, source).start()

        pl.when((source >= 0) & (source <= 3))(run)

    def arrived(self):
        for y in range(2):
            for source in range(4):
                self._hand(y, source).wait_recv()

    def finish(self):
        p = self.p
        for i in range(3):
            self._cross(i).wait_send()
        for y in range(2):
            for source in range(4):
                self._hand(y, source).wait_send()
                up = (source <= p.z) & (p.z < 3)
                down = (source >= p.z) & (p.z > 0)
                pl.when(up)(lambda: self._copy_z(y, source, True).wait_send())
                pl.when(down)(lambda: self._copy_z(y, source, False).wait_send())


EXPERT_SEMS = ("zu", "zd", "zr", "hs", "hr")
STEPS = (0, -1, 1, -2, 2, -3, 3)

FRONT = (0.05, (0.3, 4.7), (0.4, 7), (0.4, 14), 1)


def front_kernel(
    images, seq,
    small_in, wide_in, tall_in, x0_ref, g4_ref, ids_ref,
    small, wa0, wmi, wmo, wa1, ein, eout, *rest,
):
    outs, mine, tools = rest[:18], rest[18:36], rest[36:]
    (x1, x2, x3, an0, qkv0, o0, mn, slope, ma, an1, qkv1, o1, en, aux_ref, pick0, pick1, rx, rd) = mine
    (xf, va0, vmi, vmo, va1, wide_mine, expert_mine, from_sibling, small_got,
     meet, small_sems, gather_sems, own_sems, expert_sems, cross_sems, out_sems, weight_sems) = tools
    p = Place()
    greet_all(p, 32)
    swap = remote(wide_in.at[1 - p.core], from_sibling, meet.at[0], meet.at[1], p.sibling)
    swap.start()

    def small_copy(to, i, source):
        return remote(small_in, small_got.at[source], small_sems.at[0, i], small_sems.at[1, source], to)

    pl.loop(1, 32)(lambda i: small_copy((p.me + i) % 32, i, p.me).start())
    small_got[p.me] = small_in[...]
    landing, weights = (va0, vmi, vmo, va1), (wa0, wmi, wmo, wa1)
    jobs = []
    for m, kind in enumerate(DENSE):
        sems = {name: gather_sems.at[m, i] for i, name in enumerate(GATHER_SEMS)}
        sems["own"] = own_sems.at[m]
        piece = tall_in.at[0] if kind == "tall" else wide_mine.at[(0, 1, None, 2)[m]]
        jobs.append(Gather(p, kind, piece, landing[m], sems))
    big = []
    for m, kind in enumerate(("wide", "tall")):
        sems = {name: expert_sems.at[m, i] for i, name in enumerate(EXPERT_SEMS)}
        sems["cs"], sems["cr"], sems["own"] = (
            cross_sems.at[m, 0], cross_sems.at[m, 1], cross_sems.at[m, 2])
        piece = tall_in.at[pl.ds(1, 4)] if kind == "tall" else expert_mine
        big.append(ExpertGather(p, kind, piece, (ein, eout)[m], sems))
    jobs[2].start_own()
    swap.wait_recv()

    def merge(m, out):
        cols = pl.ds(m * 1536, 1536)
        kept = wide_in[p.core, :, cols]
        came = from_sibling[:, cols]
        upper = jnp.where(p.core == 0, kept, came)
        lower = jnp.where(p.core == 0, came, kept)
        out[...] = jnp.concatenate([upper, lower], 0).astype(BF16)

    merge(0, wide_mine.at[0])
    jobs[0].start_own()
    big[1].start_own()
    for e in range(4):
        merge(3 + e, expert_mine.at[e])
    big[0].start_own()
    merge(1, wide_mine.at[1])
    jobs[1].start_own()
    merge(2, wide_mine.at[2])
    jobs[3].start_own()

    dense, experts = Pump(), Pump()
    order = [(m, k, half) for m in range(4) for k in STEPS for half in range(2)]
    done_at = {}
    for i in range(len(order) + 24):
        for stage, lag in ((0, 0), (1, 12), (2, 24)):
            if 0 <= i - lag < len(order):
                m, k, half = order[i - lag]
                name = ("stage_one", "stage_two", "stage_three")[stage]
                dense.add([functools.partial(getattr(jobs[m], name), half, k)])
                if stage == 2:
                    done_at[m] = len(dense.queue)
    total = len(dense.queue)

    def crossed():
        big[1].crossed()
        big[0].crossed()

    experts.add([crossed])
    experts.add([functools.partial(big[m].stage, y, k) for k in STEPS[1:] for m in (1, 0) for y in range(2)])

    def pump(pace=(0, 0)):
        experts.run(pace[0])
        dense.run(pace[1])

    def arrive(m):
        while total - len(dense.queue) < done_at[m]:
            pump((FRONT[0], 1))
        jobs[m].arrived()
        pltpu.make_async_copy(landing[m], weights[m], weight_sems.at[m]).start()

    copies = []

    def emit(i):
        copy = pltpu.make_async_copy(mine[i], outs[i], out_sems.at[i])
        copy.start()
        copies.append(copy)

    def attention(x, row, w_ref, xo, an, qkv, o, pace):
        norm_rows(x, small[row : row + 1, :], an)
        pump(pace)
        for third in range(3):

            def project(n, third=third):
                cols = tile(n + third * 3, 256)
                qkv[:, cols] = nn(an[...], w_ref[:, cols]).astype(BF16)

            loop(3, project)
            pump(pace)
        rows_of = qkv.shape[0] // images
        for image in range(images):
            rows = pl.ds(image * rows_of, rows_of)

            def pair(i, rows=rows):
                q = qkv[rows, tile(i, 128)]
                k = qkv[rows, tile(i + 6, 128)]
                v = qkv[rows, tile(i + 12, 128)]
                first = halves(q.shape)
                zero = jnp.zeros_like(q)
                p0 = head_probs(jnp.where(first, q, zero), k, seq).astype(BF16)
                p1 = head_probs(jnp.where(first, zero, q), k, seq).astype(BF16)
                out = nn(p0, jnp.where(first, v, zero)) + nn(p1, jnp.where(first, zero, v))
                o[rows, tile(i, 128)] = out.astype(BF16)

            for part in range(2):
                loop(3, lambda i, pair=pair, part=part: pair(i + 3 * part))
                pump(pace)

        def outward(n):
            cols = tile(n, 256)
            xo[:, cols] = x[:, cols] + nn(o[...], w_ref[:, tile(n + 9, 256)])

        loop(3, outward)
        pump(pace)

    xf[...] = x0_ref[...].astype(F32)
    arrive(0)
    pl.loop(1, 32)(lambda i: small_copy((p.me + i) % 32, i, (p.me + i) % 32).wait())
    small[...] = jnp.zeros_like(small)
    for d in range(32):
        lanes = slice(24 * d, 24 * d + 24)
        small[0:4, lanes] = small_got[d, 0:4, 0:24]
        small[8:12, lanes] = small_got[d, 4:8, 0:24]
    attention(xf, 0, va0.reshape(WIDTH, HIDDEN), x1, an0, qkv0, o0, FRONT[1])
    for i in (0, 3, 4, 5):
        emit(i)
    norm_rows(x1, small[2:3, :], mn)
    emit(6)
    arrive(1)
    wi = vmi.reshape(WIDTH, HIDDEN)
    for n in range(6):
        cols = pl.ds(n * 512, 512)
        active, bend = gelu_both(nn(mn[...], wi[:, cols]))
        slope[:, cols] = bend.astype(BF16)
        ma[:, cols] = active.astype(BF16)
        pump(FRONT[2])
    emit(7)
    emit(8)
    arrive(2)
    wo = vmo.reshape(HIDDEN, WIDTH)
    for n in range(3):
        cols = pl.ds(n * 256, 256)
        x2[:, cols] = x1[:, cols] + nn(ma[...], wo[:, cols])
        pump(FRONT[3])
    emit(1)
    arrive(3)
    attention(x2, 1, va1.reshape(WIDTH, HIDDEN), x3, an1, qkv1, o1, (FRONT[4], 0))
    for i in (2, 9, 10, 11):
        emit(i)
    norm_rows(x3, small[3:4, :], en)
    route_rows(g4_ref, ids_ref, small, en, aux_ref, pick0, pick1, rx, rd, lambda: pump((FRONT[4], 0)))
    for i in range(12, 18):
        emit(i)
    while experts.step():
        pass
    for job in big:
        job.arrived()
    for job in jobs + big:
        job.finish()
    swap.wait_send()
    for m in range(4):
        pltpu.make_async_copy(landing[m], weights[m], weight_sems.at[m]).wait()
    for copy in copies:
        copy.wait()


def run_front(images, seq, small, wide, tall, x0, g4, ids):
    any_space = pl.BlockSpec(memory_space=pl.ANY)
    vmem = pl.BlockSpec(memory_space=pltpu.VMEM)
    wide_out = struct((4, 2, 2, 48, HIDDEN), BF16)
    tall_out = struct((4, 2, 2, 192, WIDTH), BF16)
    dma = pltpu.SemaphoreType.DMA
    rows = x0.shape[0]
    act, low = struct((rows, WIDTH), F32), struct((rows, WIDTH), BF16)
    qkv, hid = struct((rows, 3 * WIDTH), BF16), struct((rows, HIDDEN), BF16)
    pick, buf = struct((rows, EXPERTS * SLOT), BF16), struct((EXPERTS * SLOT, WIDTH), BF16)
    kept = [act, act, act, low, qkv, low, low, hid, hid, low, qkv, low, low,
            struct((rows, 128), F32), pick, pick, buf, buf]

    def scratch(one):
        return pltpu.VMEM(one.shape, one.dtype)

    return pl.pallas_call(
        functools.partial(front_kernel, images, seq),
        out_shape=[struct((136, WIDTH), F32), wide_out, wide_out, tall_out, wide_out, wide_out,
                   tall_out] + kept,
        in_specs=[vmem] * 6,
        out_specs=[vmem] + [any_space] * 24,
        scratch_shapes=[scratch(one) for one in kept] + [
            scratch(act), scratch(wide_out), scratch(wide_out), scratch(tall_out), scratch(wide_out),
            pltpu.VMEM((3, 48, 1536), BF16),
            pltpu.VMEM((4, 48, 1536), BF16),
            pltpu.VMEM((24, 7 * 1536), F32),
            pltpu.VMEM((32, 8, 128), F32),
            dma((2,)),
            dma((2, 32)),
            dma((4, len(GATHER_SEMS), 8)),
            dma((4, 2)),
            dma((2, len(EXPERT_SEMS), 8)),
            dma((2, 3, 3)),
            dma((18,)),
            dma((4,)),
        ],
        compiler_params=pltpu.CompilerParams(
            collective_id=0, has_side_effects=True, vmem_limit_bytes=63 << 20),
        cost_estimate=pl.CostEstimate(
            flops=9_000_000_000, bytes_accessed=60_000_000, transcendentals=0),
    )(small, wide, tall, x0, g4, ids)


def fast_front(images, seq, smalls, wide, mlp_out, expert_in, expert_out, x0, g4, ids):
    small = jnp.pad(smalls.astype(F32).T, ((0, 0), (0, 128 - smalls.shape[0])))
    mixed = [wide[0], wide[2]]
    one = [mixed[0][0][:, :1536], wide[1][:, :1536], mixed[1][0][:, :1536]]
    two = [mixed[0][0][:, 1536:], mixed[0][1], wide[1][:, 1536:], mixed[1][0][:, 1536:], mixed[1][1]]
    one += [expert_in[:, e, :1536] for e in range(EXPERTS)]
    two += [expert_in[:, e, 1536:] for e in range(EXPERTS)]
    packed = jnp.stack([jnp.concatenate(one, 1), jnp.concatenate(two, 1)]).astype(F32)
    tall = jnp.concatenate([mlp_out[None], expert_out.transpose(1, 0, 2)], 0)
    out = run_front(images, seq, small, packed, tall, x0, g4, ids)
    small, wa0, wmi, wmo, wa1, ein, eout = out[:7]
    return small, (wa0, wmi, wmo, wa1), ein, eout, out[7:23], out[23], out[24]

KINDS = ("wide", "tall", "wide", "tall", "wide", "wide")
WIDE_AT = {2: 2, 4: 1, 5: 0}
LAG = 3
AHEAD = 4
PACE = ((0.65, 0), (0.8, 1.2), (1.0, 1.3), (2, 1))


def plane_part(ref, kind, z, core, half):
    if kind == "wide":
        return ref.at[z, :, :, :, pl.ds(pl.multiple_of(core * 1536 + half * 768, 128), 768)]
    return ref.at[z, :, :, pl.ds(pl.multiple_of(core * 96 + half * 48, 16), 48), :]


def add_into(kept, came, pieces):
    def body(i):
        a, b = kept(i), came(i)
        a[...] = a[...] + b[...]

    if pieces == 1:
        body(0)
    else:
        loop(pieces, body)


class Reduce:
    def __init__(self, place, m, ref, bufs, sems, sink):
        self.p, self.m, self.kind, self.ref = place, m, KINDS[m], ref
        self.bufs, self.sems, self.sink = bufs, sems, sink

    def goal(self, stop):
        z = self.p.z
        if stop == 3:
            return z
        table = ((3, 3, 0, 0), (2, 0, 3, 1), (1, 2, 1, 2))[stop]
        low = jnp.where(z == 0, table[0], table[1])
        return jnp.where(z < 2, low, jnp.where(z == 2, table[2], table[3]))

    def joins(self, stop):
        z = self.p.z
        return (z > 0) & (z < 3) if stop < 3 else z >= 0

    def _send_z(self, half, stop, src):
        p, s = self.p, self.sems
        z = self.goal(stop)
        up = z > p.z
        slot = jnp.where(up | (z != p.z - 1), z, 4)
        return remote(src, self.bufs["z"].at[half, slot], s["zs"].at[half, stop],
                      s["zr"].at[half, slot], jnp.where(up, p.me + 8, p.me - 8))

    def _came(self, half, src, slot):
        p, s = self.p, self.sems
        came = self.bufs["z"].at[half, slot]
        remote(src, came, s["zs"].at[half, 0], s["zr"].at[half, slot], p.sibling).wait_recv()
        return came


class DenseReduce(Reduce):
    def _plane(self, half, stop):
        return plane_part(self.ref, self.kind, self.goal(stop), self.p.core, half)

    def _block(self, half, stop):
        return self._plane(half, stop).at[self.p.y, self.p.x]

    def _pair(self, half, stop):
        p, s = self.p, self.sems
        src = plane_part(self.ref, self.kind, self.goal(stop), 1 - p.core, half)
        return remote(src, self.bufs["near"].at[stop, half], s["ps"].at[stop, half],
                      s["pr"].at[stop, half], p.sibling)

    def start(self):
        for unit in range(3):
            self._pair(unit % 2, unit // 2).start()

    def _first(self, half, stop):
        p, s = self.p, self.sems
        plane = self._plane(half, stop)
        src = plane.at[:, 1 - p.x] if half else plane.at[1 - p.y]
        return remote(src, self.bufs["first"].at[stop, half], s["fs"].at[stop, half],
                      s["fr"].at[stop, half], p.across_x if half else p.across_y)

    def _second(self, half, stop):
        p, s = self.p, self.sems
        plane = self._plane(half, stop)
        src = plane.at[1 - p.y, p.x] if half else plane.at[p.y, 1 - p.x]
        return remote(src, self.bufs["second"].at[stop, half], s["ss"].at[stop, half],
                      s["sr"].at[stop, half], p.across_y if half else p.across_x)

    def stage_one(self, half, stop):
        self._pair(half, stop).wait_recv()
        later = stop * 2 + half + 3
        if later < 8:
            self._pair(later % 2, later // 2).start()
        own, near = self._plane(half, stop), self.bufs["near"].at[stop, half]
        add_into(lambda i: own.at[i // 2, i % 2], lambda i: near.at[i // 2, i % 2], 4)
        self._first(half, stop).start()

    def stage_two(self, half, stop):
        p = self.p
        self._first(half, stop).wait_recv()
        own, came = self._plane(half, stop), self.bufs["first"].at[stop, half]
        if half:
            add_into(lambda i: own.at[i, p.x], lambda i: came.at[i], 2)
        else:
            add_into(lambda i: own.at[p.y, i], lambda i: came.at[i], 2)
        self._second(half, stop).start()

    def stage_three(self, half, stop):
        self._second(half, stop).wait_recv()
        kept, came = self._block(half, stop), self.bufs["second"].at[stop, half]
        add_into(lambda i: kept, lambda i: came, 1)

    def stage_four(self, half, stop):
        p = self.p
        block = self._block(half, stop)
        if stop < 3:

            def join():
                came = self._came(half, block, self.goal(stop))
                add_into(lambda i: block, lambda i: came, 1)

            pl.when(self.joins(stop))(join)
            self._send_z(half, stop, block).start()
            return
        out = self.sink(half)
        out[...] = block[...].astype(F32)

        def last(slot):
            out[...] += self._came(half, block, slot)[...].astype(F32)

        pl.when(p.z > 0)(lambda: last(p.z))
        pl.when(p.z < 3)(lambda: last(4))

    def z_events(self):
        return [functools.partial(self.stage_four, half, stop)
                for stop in range(4) for half in range(2)]

    def finish(self):
        for half in range(2):
            for stop in range(4):
                self._pair(half, stop).wait_send()
                self._first(half, stop).wait_send()
                self._second(half, stop).wait_send()
                if stop < 3:
                    self._send_z(half, stop, self._block(half, stop)).wait_send()


class ExpertReduce(Reduce):
    def _source(self, half, stop):
        return self.ref.at[self.goal(stop), half]

    def _load(self, half, stop):
        return pltpu.make_async_copy(
            self._source(half, stop), self.bufs["own"].at[half], self.sems["load"].at[half])

    def start_load(self, half, stop):
        pl.when(self.joins(stop))(lambda: self._load(half, stop).start())

    def begin(self):
        for half in range(2):
            self.start_load(half, 0)

    def plain_send(self, half, stop):
        p = self.p
        pl.when((p.z == 0) | (p.z == 3))(
            lambda: self._send_z(half, stop, self._source(half, stop)).start())

    def stage_one(self, half, stop):
        p = self.p
        own = self.bufs["own"].at[half]

        def join(slot, into_own):
            came = self._came(half, self._source(half, stop), slot)
            kept, added = (own, came) if into_own else (came, own)
            add_into(lambda i: kept.at[i // 2, i % 2], lambda i: added.at[i // 2, i % 2], 4)

        def middle():
            z = self.goal(stop)
            self._load(half, stop).wait()
            join(z, False)
            self._send_z(half, stop, self.bufs["z"].at[half, z]).start()

        if stop < 3:
            pl.when(self.joins(stop))(middle)
            self.start_load(half, stop + 1)
            return
        self._load(half, stop).wait()
        pl.when(p.z > 0)(lambda: join(p.z, True))
        pl.when(p.z < 3)(lambda: join(4, True))
        for i in range(3):
            self._cross(half, i).start()

    def _cross(self, half, i):
        p, s = self.p, self.sems
        device = (p.across_x, p.across_y, p.across_both)[i]
        chip = device // 2 % 4
        src = self.bufs["own"].at[half, chip // 2, chip % 2]
        return remote(src, self.bufs["cross"].at[half, i], s["cs"].at[half, i], s["cr"].at[half, i], device)

    def crossed(self, half):
        p = self.p
        self.sink(half, p.chip)[...] = self.bufs["own"][half, p.y, p.x].astype(F32)
        for i in range(3):
            self._cross(half, i).wait_recv()
            device = (p.across_x, p.across_y, p.across_both)[i]
            self.sink(half, device // 2 % 4)[...] = self.bufs["cross"][half, i].astype(F32)

    def finish(self):
        for half in range(2):
            for i in range(3):
                self._cross(half, i).wait_send()
            for stop in range(3):
                self._send_z(half, stop, self._source(half, stop)).wait_send()


class Pump:
    def __init__(self):
        self.queue, self.due = [], 0.0

    def add(self, events):
        self.queue += events

    def run(self, count):
        self.due = min(self.due + count, count + 4.0)
        while self.due >= 1 and self.step():
            self.due -= 1

    def step(self):
        if self.queue:
            self.queue.pop(0)()
            return True
        return False


class Belt(Pump):
    def __init__(self, lag, after):
        super().__init__()
        self.units, self.done, self.lag, self.after = [], [0, 0, 0, 0], lag, after

    def add(self, job):
        self.units += [(job, half, stop) for stop in range(4) for half in range(2)]

    def step(self):
        moved = False
        for stage in range(4):
            ahead = self.done[stage - 1] if stage else len(self.units)
            mine = self.done[stage]
            flush = ahead == len(self.units)
            if mine < ahead and (stage == 0 or flush or ahead - mine > self.lag):
                job, half, stop = self.units[mine]
                self.done[stage] += 1
                moved = True
                if stage < 3:
                    (job.stage_one, job.stage_two, job.stage_three)[stage](half, stop)
                else:
                    self.after(job, half, stop)
        return moved


def backward_step(
    images, seq,
    g4, small, x3, en_src, aux_src, p0_src, p1_src, y_src, d_src, x2, x1, x0, an1, qkv1, o1, mn, slope, ma, an0, qkv0, o0,
    wa1, wmo, wmi, wa0, sums,
    x4_ref, g_ref, small_out, wide_out, tall_out,
    xf, low, do, dqkv, dn, an_buf, mix_buf, ds,
    dw_wide, dw_tall, near, first, second, z_dense, own, z_expert, cross, done, small_got, tiles,
    load_sems, expert_load_sems, pair_sems, plane_sems, zs_sems, zr_sems, cross_sems, small_sems,
    meet, stream_sems, combine_sems, credit,
):
    p = Place()
    greet_all(p, 32)
    jobs = []
    sets = {2: 0, 3: 1, 4: 2, 5: 0}
    refs = {2: dw_wide.at[0], 3: dw_tall, 4: dw_wide.at[1], 5: dw_wide.at[2]}
    for m in range(6):
        sems = {"zs": zs_sems.at[m], "zr": zr_sems.at[m]}
        if m < 2:
            sems.update(cs=cross_sems.at[m, 0], cr=cross_sems.at[m, 1], load=expert_load_sems.at[m])
            bufs = {"z": z_expert.at[m], "cross": cross.at[m], "own": own.at[m]}
            if m == 0:
                def sink(half, e):
                    return done.at[3 + e, :, pl.ds(half * 768, 768)]
            else:
                def sink(half, e):
                    return tall_out.at[1 + e, pl.ds(half * 48, 48), :]
            jobs.append(ExpertReduce(p, m, sums.at[m], bufs, sems, sink))
            continue
        sems.update(ps=pair_sems.at[m - 2, 0], pr=pair_sems.at[m - 2, 1])
        for i, name in enumerate(("fs", "fr", "ss", "sr")):
            sems[name] = plane_sems.at[m - 2, i]
        s = sets[m]
        bufs = {"z": z_dense.at[m - 2], "first": first.at[s], "second": second.at[s], "near": near.at[s]}
        if m in WIDE_AT:
            def sink(half, m=m):
                return done.at[WIDE_AT[m], :, pl.ds(half * 768, 768)]
        else:
            def sink(half):
                return tall_out.at[0, pl.ds(half * 48, 48), :]
        jobs.append(DenseReduce(p, m, refs[m], bufs, sems, sink))
    for m in range(2):
        jobs[m].begin()

    experts = Pump()

    def along(job, half, stop):
        experts.add([functools.partial(job.stage_four, half, stop)])
        if job.m == 2 and (half, stop) == (1, 3):
            for device in (p.sibling, p.across_x, p.across_y):
                pl.semaphore_signal(credit, inc=1, device_id=(device,), device_id_type=MESH_ID)

    dense = Belt(LAG, along)
    units = [(m, half, stop) for stop in range(4) for m in range(2) for half in range(2)]

    def expert_event(i):
        if i + AHEAD < 12:
            m, half, stop = units[i + AHEAD]
            jobs[m].plain_send(half, stop)
        m, half, stop = units[i]
        jobs[m].stage_one(half, stop)

    for m, half, stop in units[:AHEAD]:
        jobs[m].plain_send(half, stop)
    experts.add([functools.partial(expert_event, i) for i in range(16)])

    def pump(e=1, d=0):
        experts.run(e)
        dense.run(d)

    def load(pairs, sems):
        copies = [pltpu.make_async_copy(src, dst, sems.at[i]) for i, (src, dst) in enumerate(pairs)]
        for copy in copies:
            copy.start()
        return copies

    def attention(w_src, x_src, an_src, qkv_src, o_src, dw, row, ready, pump):
        def scope(w_buf):
            qkv, o = mix_buf.at[:, pl.ds(0, 2304)], mix_buf.at[:, pl.ds(2304, 768)]
            x_to = xf if x_src.dtype == F32 else low
            copies = load([(x_src, x_to), (o_src, o), (an_src, an_buf), (qkv_src, qkv),
                           (w_src.reshape(WIDTH, HIDDEN), w_buf)], load_sems)
            for copy in copies[:2]:
                copy.wait()
            if x_src.dtype != F32:
                xf[...] = low[...].astype(F32)

            def weights_here():
                for copy in copies[2:]:
                    copy.wait()

            attention_backward(
                g_ref, xf, small[row : row + 1, :], w_buf, an_buf, qkv, o, dw, ds, row, images, seq,
                low, do, dqkv, dn, weights_here, ready, pump,
            )

        pl.run_scoped(scope, pltpu.VMEM((WIDTH, HIDDEN), BF16))

    def combine(en, aux_ref, p0, p1, y, d):
        copies = load([(y_src, y), (p0_src, p0), (p1_src, p1), (x3, xf), (aux_src, aux_ref),
                       (en_src, en), (d_src, d)], combine_sems)
        g_ref[...] = g4[...].astype(F32)
        ds[...] = jnp.zeros_like(ds)
        expert_of = lax.broadcasted_iota(jnp.int32, (EXPERTS * SLOT, 128), 0) // SLOT
        spread = (expert_of == lax.broadcasted_iota(jnp.int32, expert_of.shape, 1)).astype(BF16)
        for copy in copies:
            copy.wait()
        aux = aux_ref[...]
        lane = lax.broadcasted_iota(jnp.int32, aux.shape, 1)
        dr = jnp.zeros(aux.shape, F32)
        dn[...] = xf[...]
        for j, pick in ((0, p0), (1, p1)):
            picked = nn(pick[...], y[...])
            dn[...] += aux[:, 8 + j : 9 + j] * picked
            dr += jnp.sum(g_ref[...] * picked, -1, keepdims=True) * nn(pick[...], spread)
            pump(*PACE[0])
        x4_ref[...] = dn[...].astype(BF16)
        chances = jnp.where(lane < EXPERTS, aux, 0.0)
        dlogits = chances * (dr - jnp.sum(chances * dr, -1, keepdims=True))
        dlogits = jnp.where(lane < EXPERTS, dlogits, 0.0).astype(BF16)
        ds[4:8, :] = tn(dlogits, en[...])[0:4, :]
        dn[...] = nn(dlogits, small[8:136, :].astype(BF16)) + nn(p0[...] + p1[...], d[...])
        pump(*PACE[0])
        norm_back(xf, small[3:4, :], dn, g_ref, ds, 3)
        pump(*PACE[0])

    rows = g_ref.shape[0]
    pl.run_scoped(
        combine, pltpu.VMEM((rows, WIDTH), BF16), pltpu.VMEM((rows, 128), F32),
        pltpu.VMEM((rows, EXPERTS * SLOT), BF16), pltpu.VMEM((rows, EXPERTS * SLOT), BF16),
        pltpu.VMEM((EXPERTS * SLOT, WIDTH), BF16), pltpu.VMEM((EXPERTS * SLOT, WIDTH), BF16))
    attention(wa1, x2, an1, qkv1, o1, dw_wide.at[0].reshape(WIDTH, HIDDEN), 1, jobs[2].start,
              lambda: pump(*PACE[0]))
    dense.add(jobs[2])

    def feed_forward(wo_buf, wi_buf, slope_buf, ma_buf):
        wo, wi = wmo.reshape(HIDDEN, WIDTH), wmi.reshape(WIDTH, HIDDEN)
        dwo, dwi = dw_tall.reshape(HIDDEN, WIDTH), dw_wide.at[1].reshape(WIDTH, HIDDEN)
        first_loads = load([(x1, xf), (mn, an_buf)], load_sems)

        def chunk(n):
            cols = pl.ds(n * 512, 512)
            slot = n % 2
            return load([(wo.at[cols, :], wo_buf.at[slot]), (wi.at[:, cols], wi_buf.at[slot]),
                         (slope.at[:, cols], slope_buf.at[slot]), (ma.at[:, cols], ma_buf.at[slot])],
                        stream_sems.at[slot])

        coming = chunk(0)
        low[...] = g_ref[...].astype(BF16)
        dn[...] = jnp.zeros_like(dn)
        for copy in first_loads:
            copy.wait()
        for n in range(6):
            for copy in coming:
                copy.wait()
            if n < 5:
                coming = chunk(n + 1)
            slot = n % 2
            cols = pl.ds(n * 512, 512)
            dwo[cols, :] = tn(ma_buf[slot], low[...]).astype(BF16)
            dact = nt(low[...], wo_buf[slot])
            dh = (slope_buf[slot].astype(F32) * dact).astype(BF16)
            dwi[:, cols] = tn(an_buf[...], dh).astype(BF16)
            dn[...] += nt(dh, wi_buf[slot])
            pump(*PACE[1])
        jobs[3].start()
        jobs[4].start()
        norm_back(x1_buf, small[2:3, :], dn, g_ref, ds, 2)

    x1_buf = xf
    pl.run_scoped(
        feed_forward, pltpu.VMEM((2, 512, WIDTH), BF16), pltpu.VMEM((2, WIDTH, 512), BF16),
        pltpu.VMEM((2, rows, 512), BF16), pltpu.VMEM((2, rows, 512), BF16))
    dense.add(jobs[3])
    dense.add(jobs[4])

    def last_ready():
        assert dense.done[3] >= 8
        pl.semaphore_wait(credit, 3)
        jobs[5].start()

    attention(wa0, x0, an0, qkv0, o0, dw_wide.at[2].reshape(WIDTH, HIDDEN), 0, last_ready,
              lambda: pump(*PACE[2]))

    def small_copy(to, i, source):
        return remote(tiles.at[to], small_got.at[source],
                      small_sems.at[0, i], small_sems.at[1, source], to)

    tiles[...] = jnp.zeros_like(tiles)
    for d in range(32):
        tiles[d, :, 0:24] = ds[:, 24 * d : 24 * d + 24]
    pl.loop(1, 32)(lambda i: small_copy((p.me + i) % 32, i, p.me).start())
    dense.add(jobs[5])
    while dense.done[3] < len(dense.units) or experts.queue:
        pump(*PACE[3])
    for m in range(2):
        for half in range(2):
            jobs[m].crossed(half)
    mine = pl.ds(pl.multiple_of(p.core * 1536, 128), 1536)
    swap = remote(
        done.at[:, pl.ds(pl.multiple_of((1 - p.core) * 24, 8), 24), :], wide_out.at[:, :, mine],
        meet.at[0], meet.at[1], p.sibling)
    swap.start()
    keep = pltpu.make_async_copy(
        done.at[:, pl.ds(pl.multiple_of(p.core * 24, 8), 24), :], wide_out.at[:, :, mine],
        meet.at[2])
    keep.start()
    pl.loop(1, 32)(lambda i: small_copy((p.me + i) % 32, i, (p.me + i) % 32).wait())
    small_got[p.me] = tiles[p.me]
    small_out[...] = jnp.sum(small_got[...], 0)
    for m in range(6):
        jobs[m].finish()
    keep.wait()
    swap.wait()


def run_backward_step(images, seq, args):
    any_space = pl.BlockSpec(memory_space=pl.ANY)
    vmem = pl.BlockSpec(memory_space=pltpu.VMEM)
    dma = pltpu.SemaphoreType.DMA
    piece = (48, 768)
    rows = args[0].shape[0]
    act, low = pltpu.VMEM((rows, WIDTH), F32), pltpu.VMEM((rows, WIDTH), BF16)
    return pl.pallas_call(
        functools.partial(backward_step, images, seq),
        out_shape=[struct((rows, WIDTH), BF16), struct((rows, WIDTH), F32), struct((8, 128), F32),
                   struct((7, 24, HIDDEN), F32), struct((5, 96, 768), F32)],
        in_specs=[vmem] * 2 + [any_space] * (len(args) - 2),
        out_specs=[vmem, vmem, vmem, any_space, vmem],
        scratch_shapes=[
            act, low, low, pltpu.VMEM((rows, 3 * WIDTH), BF16), act, low,
            pltpu.VMEM((rows, HIDDEN), BF16), pltpu.VMEM((8, WIDTH), F32),
            pltpu.VMEM((3, 4, 2, 2, 48, HIDDEN), BF16),
            pltpu.VMEM((4, 2, 2, 192, WIDTH), BF16),
            pltpu.VMEM((3, 4, 2, 2, 2) + piece, BF16),
            pltpu.VMEM((3, 4, 2, 2) + piece, BF16),
            pltpu.VMEM((3, 4, 2) + piece, BF16),
            pltpu.VMEM((4, 2, 5) + piece, BF16),
            pltpu.VMEM((2, 2, 2, 2) + piece, BF16),
            pltpu.VMEM((2, 2, 5, 2, 2) + piece, BF16),
            pltpu.VMEM((2, 2, 3) + piece, BF16),
            pltpu.VMEM((7, 48, 1536), F32),
            pltpu.VMEM((32, 8, 128), F32),
            pltpu.VMEM((32, 8, 128), F32),
            dma((5,)),
            dma((2, 2)),
            dma((4, 2, 4, 2)),
            dma((4, 4, 4, 2)),
            dma((6, 2, 4)),
            dma((6, 2, 5)),
            dma((2, 2, 2, 3)),
            dma((2, 32)),
            dma((3,)),
            dma((2, 4)),
            dma((7,)),
            pltpu.SemaphoreType.REGULAR,
        ],
        compiler_params=pltpu.CompilerParams(
            collective_id=1, has_side_effects=True, vmem_limit_bytes=63 << 20),
        cost_estimate=pl.CostEstimate(
            flops=20_000_000_000, bytes_accessed=60_000_000, transcendentals=0),
    )(*args)


def fast_backward(images, seq, x0, g4, small, weights, saved, y_back, d_back, sums):
    wa0, wmi, wmo, wa1 = weights
    x1, x2, x3, an0, qkv0, o0, mn, slope, ma, an1, qkv1, o1, en, aux, p0, p1 = saved
    x4, g, dsmall, wide, tall = run_backward_step(images, seq, [
        g4, small, x3, en, aux, p0, p1, y_back, d_back, x2, x1, x0, an1, qkv1, o1, mn, slope, ma,
        an0, qkv0, o0, wa1, wmo, wmi, wa0, sums])
    dsmall = dsmall[:, :24]
    return x4, g, (dsmall.T, wide[0], wide[1], tall[0], wide[2],
                   wide[3:].transpose(1, 0, 2), tall[1:].transpose(1, 0, 2))


def expert_step(
    rows_x, rows_d, ein, eout,
    y_back, d_back, sums,
    wi, wo, got_x, got_d, active, slope, y_out, d_out, acc, dwi, dwo, near,
    load_sems, own_sems, move_sems, pair_sems, sum_sems,
):
    p = Place()
    barrier = pltpu.get_barrier_semaphore()
    for device in (p.sibling, p.across_x, p.across_y, p.across_both):
        pl.semaphore_signal(barrier, inc=1, device_id=(device,), device_id_type=MESH_ID)
    pl.semaphore_wait(barrier, 4)
    chips = [device // 2 % 4 for device in (p.me, p.across_x, p.across_y, p.across_both)]
    devices = (None, p.across_x, p.across_y, p.across_both)
    loads = [pltpu.make_async_copy(src, dst, load_sems.at[i])
             for i, (src, dst) in enumerate(((ein, wi), (eout, wo)))]

    def inward(t, i):
        src, dst = ((rows_x, got_x), (rows_d, got_d))[t]
        if i == 0:
            return pltpu.make_async_copy(src.at[p.chip], dst.at[p.chip], own_sems.at[t])
        return remote(src.at[chips[i]], dst.at[p.chip], move_sems.at[t, 0, i], move_sems.at[t, 1, i],
                      devices[i])

    def outward(t, i):
        src, dst = ((y_out, y_back), (d_out, d_back))[t]
        if i == 0:
            return pltpu.make_async_copy(src.at[p.chip], dst.at[p.chip], own_sems.at[2 + t])
        return remote(src.at[chips[i]], dst.at[p.chip], move_sems.at[2 + t, 0, i],
                      move_sems.at[2 + t, 1, i], devices[i])

    for i in range(4):
        inward(0, i).start()
    for copy in loads:
        copy.start()
    inward(1, 0).start()
    for copy in loads:
        copy.wait()
    wide = wi.reshape(WIDTH, HIDDEN)
    tall = wo.reshape(HIDDEN, WIDTH)
    for i in range(4):
        chip = chips[i]
        if i == 0:
            inward(0, 0).wait()
        else:
            inward(0, i).wait_recv()
        if i == 1:
            for j in range(1, 4):
                inward(1, j).start()
        acc[...] = jnp.zeros_like(acc)

        def forward(n):
            cols = tile(n, 512)
            ea, sl = gelu_both(nn(got_x[chip], wide[:, cols]))
            ea = ea.astype(BF16)
            active[chip, :, cols] = ea
            slope[chip, :, cols] = sl.astype(BF16)
            acc[...] += nn(ea, tall[cols, :])

        loop(6, forward)
        y_out[chip] = acc[...].astype(BF16)
        outward(0, i).start()
    for i in range(4):
        chip = chips[i]
        if i == 0:
            inward(1, 0).wait()
        else:
            inward(1, i).wait_recv()
        acc[...] = jnp.zeros_like(acc)

        def backward(n):
            cols = tile(n, 512)
            dh = slope[chip, :, cols].astype(F32) * nt(got_d[chip], tall[cols, :])
            dh = dh.astype(BF16)
            slope[chip, :, cols] = dh
            acc[...] += nt(dh, wide[:, cols])

        loop(6, backward)
        d_out[chip] = acc[...].astype(BF16)
        outward(1, i).start()
    every = EXPERTS * SLOT
    x_all, d_all = got_x.reshape(every, WIDTH), got_d.reshape(every, WIDTH)
    ea_all, dh_all = active.reshape(every, HIDDEN), slope.reshape(every, HIDDEN)
    dwi_all, dwo_all = dwi.reshape(WIDTH, HIDDEN), dwo.reshape(HIDDEN, WIDTH)

    def weights(n):
        cols = tile(n, 512)
        dwo_all[cols, :] = tn(ea_all[:, cols], d_all[...]).astype(BF16)
        dwi_all[:, cols] = tn(x_all[...], dh_all[:, cols]).astype(BF16)

    loop(6, weights)
    pairs = [(m, z, half) for z in range(4) for m in range(2) for half in range(2)]

    def pair(m, z, half):
        src = plane_part((dwi, dwo)[m], KINDS[m], z, 1 - p.core, half)
        return remote(src, near.at[m, z, half], pair_sems.at[m, z, half, 0],
                      pair_sems.at[m, z, half, 1], p.sibling)

    def result(m, z, half):
        return pltpu.make_async_copy(near.at[m, z, half], sums.at[m, z, half], sum_sems.at[m, z, half])

    for one in pairs:
        pair(*one).start()
    for m, z, half in pairs:
        pair(m, z, half).wait_recv()
        own = plane_part((dwi, dwo)[m], KINDS[m], z, p.core, half)
        came = near.at[m, z, half]
        add_into(lambda i: came.at[i // 2, i % 2], lambda i: own.at[i // 2, i % 2], 4)
        result(m, z, half).start()
    for one in pairs:
        result(*one).wait()
        pair(*one).wait_send()
    for t in range(2):
        outward(t, 0).wait()
        for i in range(1, 4):
            inward(t, i).wait_send()
            outward(t, i).wait()


def run_expert_step(rows_x, rows_d, ein, eout):
    any_space = pl.BlockSpec(memory_space=pl.ANY)
    dma = pltpu.SemaphoreType.DMA
    rows = (EXPERTS, SLOT, WIDTH)
    y, d, sums = pl.pallas_call(
        expert_step,
        out_shape=[struct(rows, BF16)] * 2 + [struct((2, 4, 2, 2, 2, 48, 768), BF16)],
        in_specs=[any_space] * 4,
        out_specs=[any_space] * 3,
        scratch_shapes=[
            pltpu.VMEM((4, 2, 2, 48, HIDDEN), BF16),
            pltpu.VMEM((4, 2, 2, 192, WIDTH), BF16),
            pltpu.VMEM(rows, BF16),
            pltpu.VMEM(rows, BF16),
            pltpu.VMEM((EXPERTS, SLOT, HIDDEN), BF16),
            pltpu.VMEM((EXPERTS, SLOT, HIDDEN), BF16),
            pltpu.VMEM(rows, BF16),
            pltpu.VMEM(rows, BF16),
            pltpu.VMEM((SLOT, WIDTH), F32),
            pltpu.VMEM((4, 2, 2, 48, HIDDEN), BF16),
            pltpu.VMEM((4, 2, 2, 192, WIDTH), BF16),
            pltpu.VMEM((2, 4, 2, 2, 2, 48, 768), BF16),
            dma((2,)),
            dma((4,)),
            dma((4, 2, 4)),
            dma((2, 4, 2, 2)),
            dma((2, 4, 2)),
        ],
        compiler_params=pltpu.CompilerParams(
            collective_id=2, has_side_effects=True, vmem_limit_bytes=VMEM_BYTES),
        cost_estimate=pl.CostEstimate(
            flops=30_000_000_000, bytes_accessed=40_000_000, transcendentals=0),
    )(rows_x.reshape(rows), rows_d.reshape(rows), ein, eout)
    flat = (EXPERTS * SLOT, WIDTH)
    return y.reshape(flat), d.reshape(flat), sums


def local(
    patches, live_count, expert_ids, attn_gain, attn_qkv, attn_out, mlp_gain, mlp_in, mlp_out,
    moe_gain, router, expert_in, expert_out, cotangent,
):
    images, seq, width = patches.shape
    padded = -(-seq // 16) * 16
    n = lax.axis_size("fsdp")
    group_size = n // EXPERTS
    group = lax.axis_index("fsdp") // group_size
    alive = jnp.arange(images, dtype=jnp.int32) < live_count[0]

    def pad(values, fill=0):
        values = values.reshape(images, seq, -1)
        values = jnp.pad(values, ((0, 0), (0, padded - seq), (0, 0)), constant_values=fill)
        return values.reshape(images * padded, -1)

    x0 = pad(patches)
    g4 = pad(jnp.where(alive[:, None, None], cotangent, jnp.zeros_like(cotangent)))
    ids = pad(expert_ids, -1)
    smalls = jnp.concatenate(
        [attn_gain, mlp_gain[:, None], moe_gain[:, None], router], 1
    )
    wide = [(attn_qkv[:, 0], attn_out[:, 0]), mlp_in, (attn_qkv[:, 1], attn_out[:, 1])]
    if n == 32:
        small, weights, w_in, w_out, saved, rows_x, rows_d = fast_front(
            images, seq, smalls, wide, mlp_out, expert_in, expert_out, x0, g4, ids)
    else:
        small, wides, talls, w_in, w_out = plain_gather(
            smalls, [jnp.concatenate(wide[0], 1), mlp_in, jnp.concatenate(wide[2], 1)],
            [mlp_out], expert_in, expert_out)
        small = small.astype(F32).T
        small = jnp.concatenate(
            [small[:4], jnp.zeros((4, width), F32), small[4:], jnp.zeros((124, width), F32)], 0
        )
        weights = (wides[0], wides[1], talls[0], wides[2])
        out = run_forward(images, seq, x0, g4, ids, small, *weights)
        saved, rows_x, rows_d = out[:16], out[16], out[17]

    def exchange(rows):
        rows = rows.reshape(EXPERTS, SLOT, width)
        return group_exchange(rows, group_size, group).reshape(EXPERTS * SLOT, width)

    if n == 32:
        y_back, d_back, sums = run_expert_step(rows_x, rows_d, w_in, w_out)
        x4, grad, shards = fast_backward(
            images, seq, x0, g4, small, weights, saved, y_back, d_back, sums)
        dsmall, d0, dmi, dmo, d1, de_in, de_out = shards
    else:
        y, dx, dw_in, dw_out = run_expert(exchange(rows_x), exchange(rows_d), w_in, w_out)
        x4, grad, d0, dmi, dmo, d1, dsmall = run_backward(
            images, seq, x0, g4, small, weights, saved, exchange(y), exchange(dx)
        )
        d0, dmi, dmo, d1 = (plain_reduce(g).astype(F32) for g in (d0, dmi, dmo, d1))
        de_in, de_out = (plain_reduce_expert(g).astype(F32) for g in (dw_in, dw_out))
        dsmall = lax.psum_scatter(dsmall.T, "fsdp", scatter_dimension=0, tiled=True)

    def unpad(values):
        return values.reshape(images, padded, width)[:, :seq]

    block_out = jnp.where(alive[:, None, None], unpad(x4), 0.0).astype(BF16)
    return (
        block_out,
        unpad(grad),
        dsmall[:, 0:2],
        jnp.stack([d0[:, :2304], d1[:, :2304]], 1),
        jnp.stack([d0[:, 2304:], d1[:, 2304:]], 1),
        dsmall[:, 2],
        dmi,
        dmo,
        dsmall[:, 3],
        dsmall[:, 4:8],
        de_in,
        de_out,
    )


def solution(mesh):
    def lead(rank):
        return P("fsdp", *([None] * (rank - 1)))

    return jax.shard_map(
        local,
        mesh=mesh,
        in_specs=tuple(lead(r) for r in (3, 1, 2, 2, 3, 3, 1, 2, 2, 1, 2, 3, 3, 3)),
        out_specs=tuple(lead(r) for r in (3, 3, 2, 3, 3, 1, 2, 2, 1, 2, 3, 3)),
        check_vma=False,
    )
```
